128 devices in a mesh: ctx: 16 (over x, y_lo, core), head: 8 (over y_hi, z).
Axes of the slice: x: 4, y: 4 (y_hi: 2, y_lo: 2; y = y_hi * 2 + y_lo), z: 4, core: 2. Of those that a mesh axis runs over, the one named last changes fastest.
Arguments:
- clean_q: bfloat16 [8192, 2048], P('ctx', 'head')
- clean_k: bfloat16 [8192, 2048], P('ctx', 'head')
- clean_v: bfloat16 [8192, 2048], P('ctx', 'head'), may hold values from -6 to 6
- noisy_q: bfloat16 [8192, 2048], P('ctx', 'head')
- noisy_k: bfloat16 [8192, 2048], P('ctx', 'head')
- noisy_v: bfloat16 [8192, 2048], P('ctx', 'head'), may hold values from -6 to 6
- q_gain: float32 [2048], P('head'), may hold values from 0.5 to 4
- k_gain: float32 [2048], P('head'), may hold values from 0.5 to 4
- grad_clean: bfloat16 [8192, 2048], P('ctx', 'head'), may hold values from -6 to 6
- grad_noisy: bfloat16 [8192, 2048], P('ctx', 'head'), may hold values from -6 to 6
- owned_blocks: int32 [32], P('ctx'), may hold values from 0 to 31, as said below
- block_doc: int32 [32], replicated, may hold values from 0 to 7, never falling along the last dimension, each value on 1 to 16 neighbouring positions
Outputs:
- out_clean: float32 [8192, 2048], P('ctx', 'head')
- out_noisy: float32 [8192, 2048], P('ctx', 'head')
- dq_clean: float32 [8192, 2048], P('ctx', 'head')
- dk_clean: float32 [8192, 2048], P('ctx', 'head')
- dv_clean: float32 [8192, 2048], P('ctx', 'head')
- dq_noisy: float32 [8192, 2048], P('ctx', 'head')
- dk_noisy: float32 [8192, 2048], P('ctx', 'head')
- dv_noisy: float32 [8192, 2048], P('ctx', 'head')
The draws below stay inside these ranges and needn't reach their ends.
Inputs may be any that keep to these rules, and one draw needn't show every extreme that they name: `owned_blocks`: every block appears once; entries 2i and 2i+1 sum to 31.
All inputs are finite; a program needn't handle non-finite values.
Results may differ from the reference program's by a relative error of at most 0.035.
The reference program's roundings to bfloat16 on the way count: a program that leaves them out, or rounds other values in their place, can miss the bound.
Values may be sent and summed in bfloat16 or wider, within the bound.
A program may use at most 128 MiB of HBM per device.

```python
import math
import jax
import jax.numpy as jnp
import numpy as np
from jax import lax

HEADS = 16
HD = 128
BLK = 256
NB = 32
ROWS = 8192
FEAT = 2048


def query_key_pair(key, salt, align):
    key = jax.random.fold_in(key, salt)
    key_draw, query_draw = jax.random.split(key, 2)
    key_rows = jax.random.normal(key_draw, (NB * BLK, HEADS * HD))
    query_rows = jax.random.normal(query_draw, (NB * BLK, HEADS * HD))
    positions = jnp.arange(NB * BLK)
    chosen = (positions % 61 == 7).astype(jnp.float32)[:, None] * align
    follow = (positions % 61 == 8).astype(jnp.float32)[:, None] * align
    key_rows = key_rows * (1.0 - follow)
    query_rows = query_rows * (1.0 - chosen)
    return (query_rows, key_rows)


def draw_clean_q(key, part):
    drawn = query_key_pair(key, 5, 0.0)
    return drawn[0].astype(jnp.bfloat16)


def draw_clean_k(key, part):
    drawn = query_key_pair(key, 5, 0.0)
    return drawn[1].astype(jnp.bfloat16)


def draw_noisy_q(key, part):
    drawn = query_key_pair(key, 6, 0.0)
    return drawn[0].astype(jnp.bfloat16)


def draw_noisy_k(key, part):
    drawn = query_key_pair(key, 6, 0.0)
    return drawn[1].astype(jnp.bfloat16)


def draw_q_gain(key, part):
    key = jax.random.fold_in(key, 21)
    return jnp.exp(jax.random.uniform(key, (HEADS * HD,), minval=math.log(0.5), maxval=math.log(2.0))).astype(jnp.float32)


def draw_k_gain(key, part):
    key = jax.random.fold_in(key, 22)
    return jnp.exp(jax.random.uniform(key, (HEADS * HD,), minval=math.log(0.5), maxval=math.log(2.0))).astype(jnp.float32)


def draw_owned_blocks(key, part):
    key = jax.random.fold_in(key, 31)
    order_key, flip_key = jax.random.split(key)
    pair_order = jax.random.permutation(order_key, NB // 2).astype(jnp.int32)
    flips = jax.random.randint(flip_key, (NB // 2,), 0, 2).astype(jnp.int32)
    first = jnp.where(flips == 1, NB - 1 - pair_order, pair_order)
    second = NB - 1 - first
    return jnp.stack([first, second], axis=1).reshape(NB).astype(jnp.int32)


def levels(stream_key, extent, cuts, low, high):
    def one(position, blocks):
        draws = jax.random.uniform(jax.random.fold_in(jax.random.fold_in(stream_key, 6), position), (blocks,), jnp.float32, low / len(cuts), high / len(cuts))
        return jnp.repeat(jnp.exp(draws), extent[position] // blocks).reshape((-1,) + (1,) * (len(extent) - position - 1))

    factor_of = one(*cuts[0])
    for cut in cuts[1:]:
        factor_of = factor_of * one(*cut)
    return factor_of


def length_profile(amount, total, most, lean):
    portions = [(1 << 20) // math.isqrt(rank ** lean) + 1 for rank in range(2, amount + 1)]
    rest, counts = total - most - (amount - 1), [1] * (amount - 1)
    while rest > 0:
        movable = [i for i in range(amount - 1) if counts[i] < most]
        mass, budget = sum([portions[i] for i in movable]), rest
        for i in movable:
            extra = min(most - counts[i], max(1, budget * portions[i] // mass), rest)
            counts[i] = counts[i] + extra
            rest = rest - extra
    return np.array([most] + counts)


def ragged(own_key, amount, total, bound, lean):
    if amount == 2:
        one = jax.random.randint(own_key, (), max(1, total - bound), min(bound, total - 1) + 1)
        return jnp.stack([one, total - one])
    tallies = jnp.asarray(length_profile(amount, total, bound, lean), jnp.int32)
    couples = (amount - 1) // 2
    donor, receiver = tallies[1:1 + 2 * couples:2], tallies[2:2 + 2 * couples:2]
    room = jnp.minimum(donor - 1, bound - receiver)
    passed = jax.random.randint(jax.random.fold_in(own_key, 1), (couples,), 0, 1 << 20) % (room + 1)
    tallies = tallies.at[1:1 + 2 * couples:2].set(donor - passed).at[2:2 + 2 * couples:2].set(receiver + passed)
    return tallies[jax.random.permutation(jax.random.fold_in(own_key, 2), amount)]


def noise(rng, shape, deviation, most, cuts=(), kind=jnp.bfloat16):
    values = deviation * jax.random.normal(rng, shape, jnp.float32)
    if cuts:
        values = values * levels(rng, shape, cuts, -0.22, 0.18)
    return jnp.clip(values, -most, most).astype(kind)


def setup_inputs(seed: int = 0) -> dict:
    streams_of = jax.random.split(jax.random.key(seed), 13)
    return {
        "clean_q": draw_clean_q(jax.random.fold_in(streams_of[12], 71), 0),
        "clean_k": draw_clean_k(jax.random.fold_in(streams_of[12], 71), 0),
        "clean_v": noise(streams_of[2], (ROWS, FEAT), 1.0, 6.0, ((0, 16), (1, 8))),
        "noisy_q": draw_noisy_q(jax.random.fold_in(streams_of[12], 71), 0),
        "noisy_k": draw_noisy_k(jax.random.fold_in(streams_of[12], 71), 0),
        "noisy_v": noise(streams_of[5], (ROWS, FEAT), 1.0, 6.0, ((0, 16), (1, 8))),
        "q_gain": draw_q_gain(jax.random.fold_in(streams_of[12], 71), 0),
        "k_gain": draw_k_gain(jax.random.fold_in(streams_of[12], 71), 0),
        "grad_clean": noise(streams_of[8], (ROWS, FEAT), 1.0, 6.0, ((0, 16), (1, 8))),
        "grad_noisy": noise(streams_of[9], (ROWS, FEAT), 1.0, 6.0, ((0, 16), (1, 8))),
        "owned_blocks": draw_owned_blocks(jax.random.fold_in(streams_of[12], 71), 0),
        "block_doc": jnp.searchsorted(jnp.cumsum(ragged(streams_of[11], NB // 4, NB, NB // 2, 0)), jnp.arange(NB), side="right").astype(jnp.int32),
    }


NEGATIVE = -1e+30
EPSILON = 1e-06

def normalize(source, gain_row):
    raw_input = source.astype(jnp.float32)
    inverse = lax.rsqrt(lax.optimization_barrier(jnp.mean(raw_input * raw_input, axis=1, keepdims=True)) + EPSILON)
    return ((raw_input * inverse * gain_row).astype(jnp.bfloat16), raw_input, inverse)

def head_pass(clean_qn, clean_kn, clean_vals, noisy_qn, noisy_kn, noisy_vals, clean_grad, noisy_grad, row_block, row_doc):
    score_scale = 1.0 / math.sqrt(HD)
    queries = jnp.concatenate([clean_qn, noisy_qn], axis=0)
    cotangents = jnp.concatenate([clean_grad, noisy_grad], axis=0)

    def advance(running, block_index):
        key_clean, value_clean, key_noisy, value_noisy = running
        slot_rows = block_index % NB * BLK
        kind = (block_index >= NB).astype(jnp.int32)
        query_rows = lax.dynamic_slice_in_dim(queries, block_index * BLK, BLK, 0)
        grad_rows = lax.dynamic_slice_in_dim(cotangents, block_index * BLK, BLK, 0)
        own_keys = lax.dynamic_slice_in_dim(noisy_kn, slot_rows, BLK, 0)
        own_values = lax.dynamic_slice_in_dim(noisy_vals, slot_rows, BLK, 0)
        query_block = row_block[slot_rows]
        query_doc = row_doc[slot_rows]
        clean_seen = (row_doc == query_doc) & (row_block + kind <= query_block)
        own_seen = kind == 1
        first = jnp.dot(query_rows, clean_kn.T, preferred_element_type=jnp.float32) * score_scale
        second = jnp.dot(query_rows, own_keys.T, preferred_element_type=jnp.float32) * score_scale
        first = jnp.where(clean_seen[None, :], first, NEGATIVE)
        second = jnp.where(own_seen, second, NEGATIVE)
        row_peak = jnp.maximum(lax.optimization_barrier(jnp.max(first, axis=1)), lax.optimization_barrier(jnp.max(second, axis=1)))
        part_one = jnp.where(clean_seen[None, :], jnp.exp(first - row_peak[:, None]), 0.0)
        part_two = jnp.where(own_seen, jnp.exp(second - row_peak[:, None]), 0.0)
        log_total = row_peak + jnp.log(lax.optimization_barrier(jnp.sum(part_one, axis=1)) + lax.optimization_barrier(jnp.sum(part_two, axis=1)))
        prob_one = jnp.where(clean_seen[None, :], jnp.exp(first - log_total[:, None]), 0.0)
        prob_two = jnp.where(own_seen, jnp.exp(second - log_total[:, None]), 0.0)
        round_one = prob_one.astype(jnp.bfloat16)
        round_two = prob_two.astype(jnp.bfloat16)
        output = jnp.dot(round_one, clean_vals, preferred_element_type=jnp.float32) + jnp.dot(round_two, own_values, preferred_element_type=jnp.float32)
        delta_rows = lax.optimization_barrier(jnp.sum(grad_rows.astype(jnp.float32) * output, axis=1))
        grad_one = jnp.dot(grad_rows, clean_vals.T, preferred_element_type=jnp.float32)
        grad_two = jnp.dot(grad_rows, own_values.T, preferred_element_type=jnp.float32)
        score_one = (prob_one * (grad_one - delta_rows[:, None])).astype(jnp.bfloat16)
        score_two = (prob_two * (grad_two - delta_rows[:, None])).astype(jnp.bfloat16)
        query_grad = (jnp.dot(score_one, clean_kn, preferred_element_type=jnp.float32) + jnp.dot(score_two, own_keys, preferred_element_type=jnp.float32)) * score_scale
        key_clean = key_clean + jnp.dot(score_one.T, query_rows, preferred_element_type=jnp.float32) * score_scale
        value_clean = value_clean + jnp.dot(round_one.T, grad_rows, preferred_element_type=jnp.float32)
        own_key_grad = jnp.dot(score_two.T, query_rows, preferred_element_type=jnp.float32) * score_scale
        own_value_grad = jnp.dot(round_two.T, grad_rows, preferred_element_type=jnp.float32)
        key_noisy = lax.dynamic_update_slice_in_dim(key_noisy, lax.dynamic_slice_in_dim(key_noisy, slot_rows, BLK, 0) + own_key_grad, slot_rows, 0)
        value_noisy = lax.dynamic_update_slice_in_dim(value_noisy, lax.dynamic_slice_in_dim(value_noisy, slot_rows, BLK, 0) + own_value_grad, slot_rows, 0)
        return ((key_clean, value_clean, key_noisy, value_noisy), (output, query_grad))
    zeros_rows = jnp.zeros((ROWS, HD), jnp.float32)
    running, (outputs, query_grads) = lax.scan(advance, (zeros_rows, zeros_rows, zeros_rows, zeros_rows), jnp.arange(2 * NB, dtype=jnp.int32))
    return (outputs.reshape(2 * ROWS, HD), query_grads.reshape(2 * ROWS, HD)) + running

def norm_backward(raw_input, inverse, gain_row, upstream):
    scaled = gain_row * upstream
    inner = lax.optimization_barrier(jnp.mean(raw_input * scaled, axis=1, keepdims=True))
    return inverse * scaled - raw_input * inverse * inverse * inverse * inner

def reference(clean_q, clean_k, clean_v, noisy_q, noisy_k, noisy_v, q_gain, k_gain, grad_clean, grad_noisy, owned_blocks, block_doc):
    row_block = jnp.repeat(owned_blocks, BLK)
    row_doc = block_doc[row_block]
    cq_norm, cq_raw, cq_inverse = normalize(clean_q, q_gain)
    ck_norm, ck_raw, ck_inverse = normalize(clean_k, k_gain)
    nq_norm, nq_raw, nq_inverse = normalize(noisy_q, q_gain)
    nk_norm, nk_raw, nk_inverse = normalize(noisy_k, k_gain)

    def split_heads(source):
        return source.reshape(ROWS, HEADS, HD).transpose(1, 0, 2)
    stacked = (split_heads(cq_norm), split_heads(ck_norm), split_heads(clean_v), split_heads(nq_norm), split_heads(nk_norm), split_heads(noisy_v), split_heads(grad_clean), split_heads(grad_noisy))

    def one_head(pieces):
        return head_pass(pieces[0], pieces[1], pieces[2], pieces[3], pieces[4], pieces[5], pieces[6], pieces[7], row_block, row_doc)
    outputs, query_grads, key_clean, value_clean, key_noisy, value_noisy = lax.map(one_head, stacked)

    def merge_heads(source):
        return source.transpose(1, 0, 2).reshape(source.shape[1], FEAT)
    outputs = merge_heads(outputs)
    query_grads = merge_heads(query_grads)
    out_clean = outputs[:ROWS]
    out_noisy = outputs[ROWS:]
    dq_clean = norm_backward(cq_raw, cq_inverse, q_gain, query_grads[:ROWS])
    dq_noisy = norm_backward(nq_raw, nq_inverse, q_gain, query_grads[ROWS:])
    dk_clean = norm_backward(ck_raw, ck_inverse, k_gain, merge_heads(key_clean))
    dk_noisy = norm_backward(nk_raw, nk_inverse, k_gain, merge_heads(key_noisy))
    dv_clean = merge_heads(value_clean)
    dv_noisy = merge_heads(value_noisy)
    return (out_clean, out_noisy, dq_clean, dk_clean, dv_clean, dq_noisy, dk_noisy, dv_noisy)
```

```python
import math

import jax
import jax.numpy as jnp
from jax import lax
from jax.experimental import pallas as pl
from jax.experimental.pallas import tpu as pltpu
from jax.sharding import PartitionSpec as P

HD = 128
BLK = 256
FEAT = 2048
EPSILON = 1e-06
NEGATIVE = -1e30
MESH = pl.DeviceIdType.MESH
F32 = jnp.float32
BF16 = jnp.bfloat16
VMEM = pl.BlockSpec(memory_space=pltpu.VMEM)
SMEM = pl.BlockSpec(memory_space=pltpu.SMEM)
ANY = pl.BlockSpec(memory_space=pl.ANY)
LAST = (((1,), (1,)), ((), ()))
FIRST = (((0,), (0,)), ((), ()))
PLAIN = (((1,), (0,)), ((), ()))
PACKET = 528


def dot(a, b, dims):
    return lax.dot_general(a, b, dims, preferred_element_type=F32)


def row_sums(products):
    high = products.astype(BF16)
    low = (products - high.astype(F32)).astype(BF16)
    ones = jnp.ones((8, products.shape[1]), BF16)
    return dot(ones, high, LAST) + dot(ones, low, LAST)


def place():
    ctx = lax.axis_index("ctx")
    head = lax.axis_index("head")
    core = ctx % 2
    y = (ctx // 2) % 2
    x = ctx // 4
    return ctx, head, core, y, x


def ctx_of(x, y, core):
    return (x * 2 + y) * 2 + core


def chip_of(x, y):
    return x * 2 + y


class Copies:
    def __init__(self, send, recv, head):
        self.send, self.recv, self.head = send, recv, head
        self.started = []
        self.count = 0

    def start(self, src, dst, ctx, head=None):
        copy = pltpu.make_async_remote_copy(
            src_ref=src,
            dst_ref=dst,
            send_sem=self.send.at[self.count],
            recv_sem=self.recv.at[self.count],
            device_id={"ctx": ctx, "head": self.head if head is None else head},
            device_id_type=MESH,
        )
        self.count += 1
        copy.start()
        self.started.append(copy)
        return copy


class Locals:
    def __init__(self, sems):
        self.sems = sems
        self.count = 0

    def start(self, src, dst):
        copy = pltpu.make_async_copy(src, dst, self.sems.at[self.count])
        self.count += 1
        copy.start()
        return copy


def enter(ctx, head, core, y, x):
    barrier = pltpu.get_barrier_semaphore()
    right, left = (x + 1) % 4, (x + 3) % 4
    for other in (
        ctx_of(x, y, 1 - core),
        ctx_of(x, 1 - y, core),
        ctx_of(right, y, core),
        ctx_of(left, y, core),
    ):
        pl.semaphore_signal(barrier, inc=1, device_id={"ctx": other, "head": head}, device_id_type=MESH)
    for step in range(1, 8):
        pl.semaphore_signal(
            barrier, inc=1, device_id={"ctx": ctx, "head": (head + step) % 8}, device_id_type=MESH
        )
    pl.semaphore_wait(barrier, 11)


def gather_kernel(
    cq, ck, nq, nk, qg, kg, cv, nv, gc, gn, owned,
    kall, vall, loc, inv_out, ids_out,
    normed, id_rows, id_all, sums, send, recv, lsem,
):
    ctx, head, core, y, x = place()
    right, left = (x + 1) % 4, (x + 3) % 4
    mine = pl.ds(pl.multiple_of(core * HD, HD), HD)
    theirs = pl.ds(pl.multiple_of((1 - core) * HD, HD), HD)
    partner = ctx_of(x, y, 1 - core)
    lane = lax.broadcasted_iota(jnp.int32, (16, HD), 1)
    id_rows[...] = jnp.where(lane == 0, owned[0], owned[1]).astype(F32).astype(BF16)
    enter(ctx, head, core, y, x)
    remote = Copies(send, recv, head)
    local = Locals(lsem)

    own_v = vall.at[ctx, pl.ds(0, 512)]
    own_i = vall.at[ctx, pl.ds(512, 16)]
    v_swap = [remote.start(cv.at[:, theirs], own_v, partner), remote.start(id_rows, own_i, partner)]
    v_own = [local.start(cv.at[:, mine], own_v), local.start(id_rows, own_i)]

    row = lax.broadcasted_iota(jnp.int32, (8, 512), 0)
    total = jnp.zeros((8, 512), F32)
    for index, ref in enumerate((cq, ck, nq, nk)):
        raw = ref[...].astype(F32)
        total = jnp.where(row == index, row_sums(raw * raw), total)
    sums[0] = total
    exchange = [
        remote.start(sums.at[0], sums.at[step], ctx, (head + step) % 8) for step in range(1, 8)
    ]

    for copy in v_own:
        copy.wait()
    for copy in v_swap:
        copy.wait_recv()

    def slot(buf, sx, sy):
        return buf.at[pl.ds(2 * chip_of(sx, sy), 2)]

    def part(buf, sx, sy, half):
        return buf.at[2 * chip_of(sx, sy) + half]

    def to(px, py):
        return ctx_of(px, py, core)

    def spread(buf, sx, sy, px, py):
        view = slot(buf, sx, sy)
        return remote.start(view, view, to(px, py))

    def spread_part(buf, sx, sy, half, px, py):
        view = part(buf, sx, sy, half)
        return remote.start(view, view, to(px, py))

    v_right = spread(vall, x, y, right, y)
    v_left = spread(vall, x, y, left, y)
    v_y = [spread(vall, x, y, x, 1 - y)]

    late = []
    for index, ref in ((3, nv), (4, gc), (5, gn)):
        late.append(remote.start(ref.at[:, theirs], loc.at[index, core], partner))
    late_own = [
        local.start(ref.at[:, mine], loc.at[index, core]) for index, ref in ((3, nv), (4, gc), (5, gn))
    ]

    for copy in exchange:
        copy.wait_recv()
    total = sums[0]
    for step in range(1, 8):
        total = total + sums[step]
    inverse = lax.rsqrt(total / FEAT + EPSILON)
    inv_out[...] = inverse
    columns = jnp.transpose(inverse)

    def normalize(index, ref, gain, where):
        normed[where] = (ref[...].astype(F32) * columns[:, index : index + 1] * gain[...]).astype(BF16)

    normalize(1, ck, kg, 0)
    k_swap = remote.start(normed.at[0, :, theirs], kall.at[ctx], partner)
    k_own = local.start(normed.at[0, :, mine], kall.at[ctx])
    normalize(0, cq, qg, 1)
    normalize(2, nq, qg, 2)
    normalize(3, nk, kg, 3)
    k_own.wait()
    k_swap.wait_recv()
    k_y = spread(kall, x, y, x, 1 - y)
    k_right = [spread(kall, x, y, right, y)]
    k_left = [spread(kall, x, y, left, y)]
    for index in range(3):
        late.append(remote.start(normed.at[index + 1, :, theirs], loc.at[index, core], partner))
        late_own.append(local.start(normed.at[index + 1, :, mine], loc.at[index, core]))

    v_right.wait_recv()
    v_half = [spread_part(vall, left, y, 0, right, y)]
    v_y.append(spread(vall, left, y, x, 1 - y))
    v_left.wait_recv()
    v_half.append(spread_part(vall, right, y, 1, left, y))
    v_y.append(spread(vall, right, y, x, 1 - y))
    k_y.wait_recv()
    k_right.append(spread(kall, x, 1 - y, right, y))
    k_left.append(spread(kall, x, 1 - y, left, y))
    k_half = []
    opposite = (x + 2) % 4
    k_right[0].wait_recv()
    k_half.append(spread_part(kall, left, y, 0, right, y))
    k_left[0].wait_recv()
    k_half.append(spread_part(kall, right, y, 1, left, y))
    v_half[0].wait_recv()
    v_y.append(spread_part(vall, opposite, y, 0, x, 1 - y))
    v_half[1].wait_recv()
    v_y.append(spread_part(vall, opposite, y, 1, x, 1 - y))
    k_right[1].wait_recv()
    k_half.append(spread_part(kall, left, 1 - y, 0, right, y))
    k_left[1].wait_recv()
    k_half.append(spread_part(kall, right, 1 - y, 1, left, y))

    for copy in late_own:
        copy.wait()
    for copy in late + v_y + k_half:
        copy.wait_recv()
    gathered = local.start(vall.at[:, pl.ds(512, 16)], id_all)
    gathered.wait()
    ids_out[...] = jnp.max(id_all[...].astype(F32), axis=1).astype(jnp.int32)
    for copy in remote.started:
        copy.wait_send()


def gather_call(cq, ck, nq, nk, qg, kg, cv, nv, gc, gn, owned):
    return pl.pallas_call(
        gather_kernel,
        name="gather_keys",
        out_shape=(
            jax.ShapeDtypeStruct((16, 512, HD), BF16),
            jax.ShapeDtypeStruct((16, PACKET, HD), BF16),
            jax.ShapeDtypeStruct((6, 2, 512, HD), BF16),
            jax.ShapeDtypeStruct((8, 512), F32),
            jax.ShapeDtypeStruct((16, HD), jnp.int32),
        ),
        in_specs=[VMEM] * 6 + [ANY] * 4 + [SMEM],
        out_specs=(ANY, ANY, ANY, VMEM, VMEM),
        scratch_shapes=[
            pltpu.VMEM((4, 512, 256), BF16),
            pltpu.VMEM((16, HD), BF16),
            pltpu.VMEM((16, 16, HD), BF16),
            pltpu.VMEM((8, 8, 512), F32),
            pltpu.SemaphoreType.DMA((40,)),
            pltpu.SemaphoreType.DMA((40,)),
            pltpu.SemaphoreType.DMA((16,)),
        ],
        compiler_params=pltpu.CompilerParams(
            collective_id=0, has_side_effects=True, vmem_limit_bytes=48 * 2**20
        ),
    )(cq, ck, nq, nk, qg, kg, cv, nv, gc, gn, owned)


def attention_kernel(
    ids, docs, loc, kall, vall,
    res, dkp, dvp,
    where_is, first_of, weights, dk_acc, dv_acc, out_acc, dq_acc,
):
    ctx = lax.axis_index("ctx")
    chip = ctx // 2
    scale = 1.0 / math.sqrt(HD)
    scale2 = scale * math.log2(math.e)

    @pl.loop(0, 16)
    def _(packet):
        where_is[ids[packet, 0]] = packet * 2
        where_is[ids[packet, 1]] = packet * 2 + 1

    first_of[0] = 0

    @pl.loop(1, 32)
    def _(block):
        first_of[block] = jnp.where(docs[block] == docs[block - 1], first_of[block - 1], block)

    @pl.loop(0, 32)
    def _(block):
        dk_acc[block] = jnp.zeros((BLK, HD), F32)
        dv_acc[block] = jnp.zeros((BLK, HD), F32)

    def key_rows(buf, stored):
        start = pl.multiple_of((stored % 2) * BLK, BLK)
        return buf[stored // 2, pl.ds(start, BLK), :]

    def tops(scores):
        return jnp.max(scores.reshape(BLK // 8, 8, scores.shape[1]), axis=0)

    def totals(values):
        return jnp.sum(values.reshape(BLK // 8, 8, values.shape[1]), axis=0)

    @pl.loop(0, 4)
    def _(index):
        stored_own = chip * 4 + index
        side = index // 2
        block = ids[chip * 2 + side, index % 2]
        rows = pl.ds(pl.multiple_of((index % 2) * BLK, BLK), BLK)
        begin = first_of[block]
        count = block - begin
        query_clean = loc[0, side, rows, :]
        query_noisy = loc[1, side, rows, :]
        key_noisy = loc[2, side, rows, :]
        value_noisy = loc[3, side, rows, :]
        grad_clean = loc[4, side, rows, :]
        grad_noisy = loc[5, side, rows, :]
        queries = jnp.concatenate([query_clean, query_noisy], axis=0)
        grads = jnp.concatenate([grad_clean, grad_noisy], axis=0)
        key_own = key_rows(kall, stored_own)
        value_own = key_rows(vall, stored_own)

        own_scores = jnp.concatenate(
            [dot(key_own, query_clean, LAST), dot(key_noisy, query_noisy, LAST)], axis=1
        )
        weights[0] = own_scores

        def score_step(step, peak):
            keys = key_rows(kall, where_is[begin + step])
            scores = dot(keys, queries, LAST)
            weights[step + 1] = scores
            return jnp.maximum(peak, tops(scores))

        peak = lax.fori_loop(0, count, score_step, tops(own_scores))
        peak = jnp.max(peak, axis=0, keepdims=True) * scale2

        own = jnp.exp2(weights[0] * scale2 - peak)
        weights[0] = own
        own_low = own.astype(BF16)
        out_acc[...] = jnp.concatenate(
            [
                dot(value_own, own_low[:, :BLK], FIRST),
                dot(value_noisy, own_low[:, BLK:], FIRST),
            ],
            axis=1,
        )

        def value_step(step, total):
            values = key_rows(vall, where_is[begin + step])
            weight = jnp.exp2(weights[step + 1] * scale2 - peak)
            weights[step + 1] = weight
            out_acc[...] += dot(values, weight.astype(BF16), FIRST)
            return total + totals(weight)

        total = lax.fori_loop(0, count, value_step, totals(own))
        inverse_total = 1.0 / jnp.sum(total, axis=0, keepdims=True)
        out = out_acc[...] * inverse_total
        grads_t = jnp.transpose(grads.astype(F32))
        delta = jnp.sum(out * grads_t, axis=0, keepdims=True)
        out_rows = jnp.transpose(out)
        res[0, side, rows, :] = out_rows[:BLK]
        res[1, side, rows, :] = out_rows[BLK:]

        own = weights[0] * inverse_total
        own_low = own.astype(BF16)
        own_dp = jnp.concatenate(
            [dot(value_own, grad_clean, LAST), dot(value_noisy, grad_noisy, LAST)], axis=1
        )
        own_ds = (own * (own_dp - delta)).astype(BF16)
        dv_acc[stored_own] += dot(own_low[:, :BLK], grad_clean, PLAIN)
        dk_acc[stored_own] += dot(own_ds[:, :BLK], query_clean, PLAIN)
        res[5, side, rows, :] = dot(own_low[:, BLK:], grad_noisy, PLAIN)
        res[4, side, rows, :] = dot(own_ds[:, BLK:], query_noisy, PLAIN) * scale
        dq_acc[...] = jnp.concatenate(
            [dot(key_own, own_ds[:, :BLK], FIRST), dot(key_noisy, own_ds[:, BLK:], FIRST)], axis=1
        )

        @pl.loop(0, count)
        def _(step):
            stored = where_is[begin + step]
            keys = key_rows(kall, stored)
            values = key_rows(vall, stored)
            probs = weights[step + 1] * inverse_total
            dv_acc[stored] += dot(probs.astype(BF16), grads, PLAIN)
            dp = dot(values, grads, LAST)
            ds = (probs * (dp - delta)).astype(BF16)
            dk_acc[stored] += dot(ds, queries, PLAIN)
            dq_acc[...] += dot(keys, ds, FIRST)

        dq_rows = jnp.transpose(dq_acc[...] * scale)
        res[2, side, rows, :] = dq_rows[:BLK]
        res[3, side, rows, :] = dq_rows[BLK:]

    @pl.loop(0, 32)
    def _(stored):
        start = pl.multiple_of((stored % 2) * BLK, BLK)
        dkp[stored // 4, (stored // 2) % 2, pl.ds(start, BLK), :] = (dk_acc[stored] * scale).astype(BF16)
        dvp[stored // 4, (stored // 2) % 2, pl.ds(start, BLK), :] = dv_acc[stored].astype(BF16)


def attention_call(ids, docs, loc, kall, vall):
    return pl.pallas_call(
        attention_kernel,
        name="attention",
        out_shape=(
            jax.ShapeDtypeStruct((6, 2, 512, HD), F32),
            jax.ShapeDtypeStruct((8, 2, 512, HD), BF16),
            jax.ShapeDtypeStruct((8, 2, 512, HD), BF16),
        ),
        in_specs=[SMEM, SMEM, VMEM, VMEM, VMEM],
        out_specs=(VMEM, VMEM, VMEM),
        scratch_shapes=[
            pltpu.SMEM((32,), jnp.int32),
            pltpu.SMEM((32,), jnp.int32),
            pltpu.VMEM((17, BLK, 2 * BLK), F32),
            pltpu.VMEM((32, BLK, HD), F32),
            pltpu.VMEM((32, BLK, HD), F32),
            pltpu.VMEM((HD, 2 * BLK), F32),
            pltpu.VMEM((HD, 2 * BLK), F32),
        ],
        compiler_params=pltpu.CompilerParams(vmem_limit_bytes=56 * 2**20),
    )(ids, docs, loc, kall, vall)


def scatter_kernel(
    cq, ck, nq, nk, qg, kg, res, dkp, dvp,
    back, fin, inner_out,
    va, vy, vh, vx, ka, kh, kx, ks, ky, sums, ksums, send, recv, lsem,
):
    ctx, head, core, y, x = place()
    right, left = (x + 1) % 4, (x + 3) % 4
    partner = ctx_of(x, y, 1 - core)
    to_right, to_left = ctx_of(right, y, core), ctx_of(left, y, core)
    to_y = ctx_of(x, 1 - y, core)
    enter(ctx, head, core, y, x)
    remote = Copies(send, recv, head)
    local = Locals(lsem)

    def chip(step, row):
        return chip_of((x + step) % 4, y if row == 0 else 1 - y)

    v_y = {}
    k_half = {}
    v_y[2] = remote.start(dvp.at[chip(2, 1)], vy.at[2], to_y)
    for row in (1, 0):
        k_half[row, 0] = remote.start(dkp.at[chip(2, row), 0], kh.at[row, 0], to_left)
        k_half[row, 1] = remote.start(dkp.at[chip(2, row), 1], kh.at[row, 1], to_right)
    for step in (3, 1, 0):
        v_y[step] = remote.start(dvp.at[chip(step, 1)], vy.at[step], to_y)
    k_own = {}
    for row in (1, 0):
        for step in (3, 1, 0):
            k_own[row, step] = local.start(dkp.at[chip(step, row)], ka.at[row, step])
    v_own = {step: local.start(dvp.at[chip(step, 0)], va.at[step]) for step in (2, 3, 1, 0)}
    order = (2, 3, 4, 0, 1, 5)
    back_swap = {i: remote.start(res.at[i, 1 - core], back.at[i, core], partner) for i in order}
    back_own = {i: local.start(res.at[i, core], back.at[i, core]) for i in order}

    row = lax.broadcasted_iota(jnp.int32, (8, 512), 0)

    def inner(raw, gain, first, second):
        products = 0.0
        for half, values in ((0, first), (1, second)):
            columns = slice(half * HD, half * HD + HD)
            products = products + raw[:, columns].astype(F32) * (gain[:, columns] * values)
        return row_sums(products)

    for i in (2, 3, 4):
        back_own[i].wait()
        back_swap[i].wait_recv()
    total = jnp.zeros((8, 512), F32)
    for index, raw, gain, i in ((0, cq, qg, 2), (2, nq, qg, 3), (3, nk, kg, 4)):
        total = jnp.where(row == index, inner(raw, gain, back[i, 0], back[i, 1]), total)
    sums[0] = total
    exchange = [
        remote.start(sums.at[0], sums.at[step], ctx, (head + step) % 8) for step in range(1, 8)
    ]

    def add(target, other):
        target[...] = (target[...].astype(F32) + other[...].astype(F32)).astype(BF16)

    k_x = {}

    def k_forward(row):
        k_own[row, 3].wait()
        k_half[row, 0].wait_recv()
        add(ka.at[row, 3, 0], kh.at[row, 0])
        k_x[row, 0] = remote.start(ka.at[row, 3], kx.at[row, 0], to_left)
        k_own[row, 1].wait()
        k_half[row, 1].wait_recv()
        add(ka.at[row, 1, 1], kh.at[row, 1])
        k_x[row, 1] = remote.start(ka.at[row, 1], kx.at[row, 1], to_right)

    k_forward(1)
    v_own[2].wait()
    v_y[2].wait_recv()
    add(va.at[2], vy.at[2])
    v_half = [
        remote.start(va.at[2, 0], vh.at[0], to_left),
        remote.start(va.at[2, 1], vh.at[1], to_right),
    ]
    k_forward(0)
    k_own[1, 0].wait()
    k_x[1, 0].wait_recv()
    k_x[1, 1].wait_recv()
    ks[...] = (ka[1, 0].astype(F32) + kx[1, 0].astype(F32) + kx[1, 1].astype(F32)).astype(BF16)
    k_y = remote.start(ks, ky, to_y)

    v_own[3].wait()
    v_y[3].wait_recv()
    add(va.at[3], vy.at[3])
    v_half[0].wait_recv()
    add(va.at[3, 0], vh.at[0])
    v_x = [remote.start(va.at[3], vx.at[0], to_left)]
    v_own[1].wait()
    v_y[1].wait_recv()
    add(va.at[1], vy.at[1])
    v_half[1].wait_recv()
    add(va.at[1, 1], vh.at[1])
    v_x.append(remote.start(va.at[1], vx.at[1], to_right))

    k_own[0, 0].wait()
    k_x[0, 0].wait_recv()
    k_x[0, 1].wait_recv()
    k_y.wait_recv()

    def finish(index, terms):
        values = [
            sum(term[half].astype(F32) for term in terms[1:]) + terms[0][half].astype(F32)
            for half in range(2)
        ]
        first_core = core == 0
        fin[index, core] = jnp.where(first_core, values[0], values[1])
        away[index] = jnp.where(first_core, values[1], values[0])
        return remote.start(away.at[index], fin.at[index, core], partner)

    away = ksums
    k_fin = finish(0, (ka.at[0, 0], kx.at[0, 0], kx.at[0, 1], ky))
    k_fin.wait_recv()
    sums[8] = inner(ck, kg, fin[0, 0], fin[0, 1])
    k_exchange = [
        remote.start(sums.at[8], sums.at[8 + step], ctx, (head + step) % 8) for step in range(1, 8)
    ]
    v_own[0].wait()
    v_y[0].wait_recv()
    v_x[0].wait_recv()
    v_x[1].wait_recv()
    v_fin = finish(1, (va.at[0], vy.at[0], vx.at[0], vx.at[1]))

    for copy in exchange + k_exchange:
        copy.wait_recv()
    total = sums[0]
    k_total = sums[8]
    for step in range(1, 8):
        total = total + sums[step]
        k_total = k_total + sums[8 + step]
    inner_out[...] = jnp.where(row == 1, k_total, total)
    v_fin.wait_recv()
    for i in (0, 1, 5):
        back_own[i].wait()
        back_swap[i].wait_recv()
    for copy in remote.started:
        copy.wait_send()


def scatter_call(cq, ck, nq, nk, qg, kg, res, dkp, dvp):
    return pl.pallas_call(
        scatter_kernel,
        name="scatter_grads",
        out_shape=(
            jax.ShapeDtypeStruct((6, 2, 512, HD), F32),
            jax.ShapeDtypeStruct((2, 2, 512, HD), F32),
            jax.ShapeDtypeStruct((8, 512), F32),
        ),
        in_specs=[VMEM] * 6 + [ANY] * 3,
        out_specs=(VMEM, VMEM, VMEM),
        scratch_shapes=[
            pltpu.VMEM((4, 2, 512, HD), BF16),
            pltpu.VMEM((4, 2, 512, HD), BF16),
            pltpu.VMEM((2, 512, HD), BF16),
            pltpu.VMEM((2, 2, 512, HD), BF16),
            pltpu.VMEM((2, 4, 2, 512, HD), BF16),
            pltpu.VMEM((2, 2, 512, HD), BF16),
            pltpu.VMEM((2, 2, 2, 512, HD), BF16),
            pltpu.VMEM((2, 512, HD), BF16),
            pltpu.VMEM((2, 512, HD), BF16),
            pltpu.VMEM((16, 8, 512), F32),
            pltpu.VMEM((2, 512, HD), F32),
            pltpu.SemaphoreType.DMA((44,)),
            pltpu.SemaphoreType.DMA((44,)),
            pltpu.SemaphoreType.DMA((20,)),
        ],
        compiler_params=pltpu.CompilerParams(
            collective_id=1, has_side_effects=True, vmem_limit_bytes=56 * 2**20
        ),
    )(cq, ck, nq, nk, qg, kg, res, dkp, dvp)


def finish_kernel(
    cq, ck, nq, nk, qg, kg, inv, inner, back, fin,
    out_clean, out_noisy, dq_clean, dk_clean, dv_clean, dq_noisy, dk_noisy, dv_noisy,
):
    inverse = jnp.transpose(inv[...])
    means = jnp.transpose(inner[...]) / FEAT
    for half in range(2):
        columns = slice(half * HD, half * HD + HD)
        out_clean[:, columns] = back[0, half]
        out_noisy[:, columns] = back[1, half]
        dv_noisy[:, columns] = back[5, half]
        dv_clean[:, columns] = fin[1, half]
        for index, raw, gain, grad, target in (
            (0, cq, qg, back[2, half], dq_clean),
            (1, ck, kg, fin[0, half], dk_clean),
            (2, nq, qg, back[3, half], dq_noisy),
            (3, nk, kg, back[4, half], dk_noisy),
        ):
            scale = inverse[:, index : index + 1]
            factor = scale * scale * scale * means[:, index : index + 1]
            target[:, columns] = scale * (gain[:, columns] * grad) - raw[:, columns].astype(F32) * factor


def finish_call(cq, ck, nq, nk, qg, kg, inv, inner, back, fin):
    rows = 128
    wide = pl.BlockSpec((rows, 256), lambda i: (i, 0))
    gain = pl.BlockSpec((1, 256), lambda i: (0, 0))
    stat = pl.BlockSpec((8, rows), lambda i: (0, i))
    return pl.pallas_call(
        finish_kernel,
        name="finish",
        grid=(512 // rows,),
        out_shape=tuple(jax.ShapeDtypeStruct((512, 256), F32) for _ in range(8)),
        in_specs=[wide] * 4
        + [gain] * 2
        + [stat] * 2
        + [
            pl.BlockSpec((6, 2, rows, HD), lambda i: (0, 0, i, 0)),
            pl.BlockSpec((2, 2, rows, HD), lambda i: (0, 0, i, 0)),
        ],
        out_specs=tuple([wide] * 8),
        compiler_params=pltpu.CompilerParams(vmem_limit_bytes=32 * 2**20),
    )(cq, ck, nq, nk, qg, kg, inv, inner, back, fin)


def local(
    clean_q, clean_k, clean_v, noisy_q, noisy_k, noisy_v,
    q_gain, k_gain, grad_clean, grad_noisy, owned_blocks, block_doc,
):
    qg = q_gain.reshape(1, 256)
    kg = k_gain.reshape(1, 256)
    raws = (clean_q, clean_k, noisy_q, noisy_k, qg, kg)
    kall, vall, loc, inv, ids = gather_call(
        *raws, clean_v, noisy_v, grad_clean, grad_noisy, owned_blocks
    )
    res, dkp, dvp = attention_call(ids, block_doc, loc, kall, vall)
    back, fin, inner = scatter_call(*raws, res, dkp, dvp)
    return finish_call(*raws, inv, inner, back, fin)


def solution(mesh):
    placed = (P("ctx", "head"),) * 6 + (P("head"),) * 2 + (P("ctx", "head"),) * 2 + (P("ctx"), P())
    return jax.shard_map(
        local,
        mesh=mesh,
        in_specs=placed,
        out_specs=(P("ctx", "head"),) * 8,
        check_vma=False,
    )
```

```python
import math

import jax
import jax.numpy as jnp
from jax import lax
from jax.experimental import pallas as pl
from jax.experimental.pallas import tpu as pltpu
from jax.sharding import PartitionSpec as P

HD = 128
BLK = 256
FEAT = 2048
EPSILON = 1e-06
NEGATIVE = -1e30
MESH = pl.DeviceIdType.MESH
F32 = jnp.float32
BF16 = jnp.bfloat16
VMEM = pl.BlockSpec(memory_space=pltpu.VMEM)
SMEM = pl.BlockSpec(memory_space=pltpu.SMEM)
ANY = pl.BlockSpec(memory_space=pl.ANY)
HBM = pl.BlockSpec(memory_space=pltpu.HBM)
LAST = (((1,), (1,)), ((), ()))
FIRST = (((0,), (0,)), ((), ()))
PLAIN = (((1,), (0,)), ((), ()))
PACKET = 528


def dot(a, b, dims):
    return lax.dot_general(a, b, dims, preferred_element_type=F32)


def row_sums(products):
    high = products.astype(BF16)
    low = (products - high.astype(F32)).astype(BF16)
    ones = jnp.ones((8, products.shape[1]), BF16)
    return dot(ones, high, LAST) + dot(ones, low, LAST)


def place():
    ctx = lax.axis_index("ctx")
    head = lax.axis_index("head")
    core = ctx % 2
    y = (ctx // 2) % 2
    x = ctx // 4
    return ctx, head, core, y, x


def ctx_of(x, y, core):
    return (x * 2 + y) * 2 + core


def chip_of(x, y):
    return x * 2 + y


class Copies:
    def __init__(self, send, recv, head):
        self.send, self.recv, self.head = send, recv, head
        self.started = []
        self.count = 0

    def start(self, src, dst, ctx, head=None):
        copy = pltpu.make_async_remote_copy(
            src_ref=src,
            dst_ref=dst,
            send_sem=self.send.at[self.count],
            recv_sem=self.recv.at[self.count],
            device_id={"ctx": ctx, "head": self.head if head is None else head},
            device_id_type=MESH,
        )
        self.count += 1
        copy.start()
        self.started.append(copy)
        return copy


class Locals:
    def __init__(self, sems):
        self.sems = sems
        self.count = 0

    def start(self, src, dst):
        copy = pltpu.make_async_copy(src, dst, self.sems.at[self.count])
        self.count += 1
        copy.start()
        return copy


def enter(ctx, head, core, y, x):
    barrier = pltpu.get_barrier_semaphore()
    right, left = (x + 1) % 4, (x + 3) % 4
    for other in (
        ctx_of(x, y, 1 - core),
        ctx_of(x, 1 - y, core),
        ctx_of(right, y, core),
        ctx_of(left, y, core),
    ):
        pl.semaphore_signal(barrier, inc=1, device_id={"ctx": other, "head": head}, device_id_type=MESH)
    for step in range(1, 8):
        pl.semaphore_signal(
            barrier, inc=1, device_id={"ctx": ctx, "head": (head + step) % 8}, device_id_type=MESH
        )
    pl.semaphore_wait(barrier, 11)


def gather_kernel(
    cq_h, ck_h, nq_h, nk_h, qg_h, kg_h, cv, nv, gc, gn, owned,
    kall, vall, loc, own_s, own_d, grads_t, inv_out, ids_out,
    owned_s, raws, qg, kg, normed, id_rows, id_all, sums, send, recv, lsem,
):
    ctx, head, core, y, x = place()
    right, left = (x + 1) % 4, (x + 3) % 4
    mine = pl.ds(pl.multiple_of(core * HD, HD), HD)
    theirs = pl.ds(pl.multiple_of((1 - core) * HD, HD), HD)
    partner = ctx_of(x, y, 1 - core)
    local = Locals(lsem)
    owned_load = local.start(owned, owned_s)
    loads = [local.start(ref, raws.at[i]) for i, ref in enumerate((cq_h, ck_h, nq_h, nk_h))]
    loads += [local.start(qg_h, qg), local.start(kg_h, kg)]
    cq, ck, nq, nk = [raws.at[i] for i in range(4)]
    owned_load.wait()
    lane = lax.broadcasted_iota(jnp.int32, (16, HD), 1)
    id_rows[...] = jnp.where(lane == 0, owned_s[0], owned_s[1]).astype(F32).astype(BF16)
    enter(ctx, head, core, y, x)
    remote = Copies(send, recv, head)

    own_v = vall.at[ctx, pl.ds(0, 512)]
    own_i = vall.at[ctx, pl.ds(512, 16)]
    v_swap = [remote.start(cv.at[:, theirs], own_v, partner), remote.start(id_rows, own_i, partner)]
    v_own = [local.start(cv.at[:, mine], own_v), local.start(id_rows, own_i)]

    for copy in loads:
        copy.wait()
    row = lax.broadcasted_iota(jnp.int32, (8, 512), 0)
    total = jnp.zeros((8, 512), F32)
    for index, ref in enumerate((cq, ck, nq, nk)):
        raw = ref[...].astype(F32)
        total = jnp.where(row == index, row_sums(raw * raw), total)
    sums[0] = total
    exchange = [
        remote.start(sums.at[0], sums.at[step], ctx, (head + step) % 8) for step in range(1, 8)
    ]

    for copy in v_own:
        copy.wait()
    for copy in v_swap:
        copy.wait_recv()

    def slot(buf, sx, sy):
        return buf.at[pl.ds(2 * chip_of(sx, sy), 2)]

    def part(buf, sx, sy, half):
        return buf.at[2 * chip_of(sx, sy) + half]

    def to(px, py):
        return ctx_of(px, py, core)

    def spread(buf, sx, sy, px, py):
        view = slot(buf, sx, sy)
        return remote.start(view, view, to(px, py))

    def spread_part(buf, sx, sy, half, px, py):
        view = part(buf, sx, sy, half)
        return remote.start(view, view, to(px, py))

    v_right = spread(vall, x, y, right, y)
    v_left = spread(vall, x, y, left, y)
    v_y = [spread(vall, x, y, x, 1 - y)]

    late = []
    for index, ref in ((3, nv), (4, gc), (5, gn)):
        late.append(remote.start(ref.at[:, theirs], loc.at[index, core], partner))
    late_own = [
        local.start(ref.at[:, mine], loc.at[index, core]) for index, ref in ((3, nv), (4, gc), (5, gn))
    ]

    for copy in exchange:
        copy.wait_recv()
    total = sums[0]
    for step in range(1, 8):
        total = total + sums[step]
    inverse = lax.rsqrt(total / FEAT + EPSILON)
    inv_out[...] = inverse
    columns = jnp.transpose(inverse)

    def normalize(index, ref, gain, where):
        normed[where] = (ref[...].astype(F32) * columns[:, index : index + 1] * gain[...]).astype(BF16)

    normalize(1, ck, kg, 0)
    k_swap = remote.start(normed.at[0, :, theirs], kall.at[ctx], partner)
    k_own = local.start(normed.at[0, :, mine], kall.at[ctx])
    normalize(0, cq, qg, 1)
    normalize(2, nq, qg, 2)
    normalize(3, nk, kg, 3)
    k_own.wait()
    k_swap.wait_recv()
    k_y = spread(kall, x, y, x, 1 - y)
    k_right = [spread(kall, x, y, right, y)]
    k_left = [spread(kall, x, y, left, y)]
    for index in range(3):
        late.append(remote.start(normed.at[index + 1, :, theirs], loc.at[index, core], partner))
        late_own.append(local.start(normed.at[index + 1, :, mine], loc.at[index, core]))

    for copy in late_own:
        copy.wait()
    for copy in late:
        copy.wait_recv()
    for index in range(4):
        side, rows = index // 2, slice(index % 2 * BLK, index % 2 * BLK + BLK)
        packet = 2 * chip_of(x, y) + side
        grad_clean, grad_noisy = loc[4, side, rows, :], loc[5, side, rows, :]
        own_s[index, :, :BLK] = dot(kall[packet, rows, :], loc[0, side, rows, :], LAST)
        own_s[index, :, BLK:] = dot(loc[2, side, rows, :], loc[1, side, rows, :], LAST)
        own_d[index, :, :BLK] = dot(vall[packet, rows, :], grad_clean, LAST)
        own_d[index, :, BLK:] = dot(loc[3, side, rows, :], grad_noisy, LAST)
        grads_t[index, :, :BLK] = jnp.transpose(grad_clean.astype(F32))
        grads_t[index, :, BLK:] = jnp.transpose(grad_noisy.astype(F32))

    v_right.wait_recv()
    v_half = [spread_part(vall, left, y, 0, right, y)]
    v_y.append(spread(vall, left, y, x, 1 - y))
    v_left.wait_recv()
    v_half.append(spread_part(vall, right, y, 1, left, y))
    v_y.append(spread(vall, right, y, x, 1 - y))
    k_y.wait_recv()
    k_right.append(spread(kall, x, 1 - y, right, y))
    k_left.append(spread(kall, x, 1 - y, left, y))
    k_half = []
    opposite = (x + 2) % 4
    k_right[0].wait_recv()
    k_half.append(spread_part(kall, left, y, 0, right, y))
    k_left[0].wait_recv()
    k_half.append(spread_part(kall, right, y, 1, left, y))
    v_half[0].wait_recv()
    v_y.append(spread_part(vall, opposite, y, 0, x, 1 - y))
    v_half[1].wait_recv()
    v_y.append(spread_part(vall, opposite, y, 1, x, 1 - y))
    k_right[1].wait_recv()
    k_half.append(spread_part(kall, left, 1 - y, 0, right, y))
    k_left[1].wait_recv()
    k_half.append(spread_part(kall, right, 1 - y, 1, left, y))

    for copy in v_y + k_half:
        copy.wait_recv()
    gathered = local.start(vall.at[:, pl.ds(512, 16)], id_all)
    gathered.wait()
    ids_out[...] = jnp.max(id_all[...].astype(F32), axis=1).astype(jnp.int32)
    for copy in remote.started:
        copy.wait_send()


def gather_call(cq, ck, nq, nk, qg, kg, cv, nv, gc, gn, owned):
    return pl.pallas_call(
        gather_kernel,
        name="gather_keys",
        out_shape=(
            jax.ShapeDtypeStruct((16, 512, HD), BF16),
            jax.ShapeDtypeStruct((16, PACKET, HD), BF16),
            jax.ShapeDtypeStruct((6, 2, 512, HD), BF16),
            jax.ShapeDtypeStruct((4, BLK, 2 * BLK), F32),
            jax.ShapeDtypeStruct((4, BLK, 2 * BLK), F32),
            jax.ShapeDtypeStruct((4, HD, 2 * BLK), F32),
            jax.ShapeDtypeStruct((8, 512), F32),
            jax.ShapeDtypeStruct((16, HD), jnp.int32),
        ),
        in_specs=[HBM] * 11,
        out_specs=(VMEM,) * 8,
        scratch_shapes=[
            pltpu.SMEM((2,), jnp.int32),
            pltpu.VMEM((4, 512, 256), BF16),
            pltpu.VMEM((1, 256), F32),
            pltpu.VMEM((1, 256), F32),
            pltpu.VMEM((4, 512, 256), BF16),
            pltpu.VMEM((16, HD), BF16),
            pltpu.VMEM((16, 16, HD), BF16),
            pltpu.VMEM((8, 8, 512), F32),
            pltpu.SemaphoreType.DMA((40,)),
            pltpu.SemaphoreType.DMA((40,)),
            pltpu.SemaphoreType.DMA((24,)),
        ],
        compiler_params=pltpu.CompilerParams(
            collective_id=0, has_side_effects=True, vmem_limit_bytes=20 * 2**20
        ),
    )(cq, ck, nq, nk, qg, kg, cv, nv, gc, gn, owned)


def attention_kernel(
    ids, docs, loc, kall, vall, own_s, own_d, grads_t,
    out_t, dq_t, dk_noisy, dv_noisy, dk_acc, dv_acc,
    where_is, first_of, weights,
):
    ctx = lax.axis_index("ctx")
    chip = ctx // 2
    scale = 1.0 / math.sqrt(HD)
    scale2 = scale * math.log2(math.e)

    @pl.loop(0, 16)
    def _(packet):
        where_is[ids[packet, 0]] = packet * 2
        where_is[ids[packet, 1]] = packet * 2 + 1

    first_of[0] = 0

    @pl.loop(1, 32)
    def _(block):
        first_of[block] = jnp.where(docs[block] == docs[block - 1], first_of[block - 1], block)

    @pl.loop(0, 32)
    def _(block):
        dk_acc[block] = jnp.zeros((BLK, HD), F32)
        dv_acc[block] = jnp.zeros((BLK, HD), F32)

    def key_rows(buf, stored):
        start = pl.multiple_of((stored % 2) * BLK, BLK)
        return buf[stored // 2, pl.ds(start, BLK), :]

    def tops(scores):
        return jnp.max(scores.reshape(BLK // 8, 8, scores.shape[1]), axis=0)

    def totals(values):
        return jnp.sum(values.reshape(BLK // 8, 8, values.shape[1]), axis=0)

    def in_pairs(count, body, carry):
        pairs = count // 2
        carry = lax.fori_loop(0, pairs, lambda i, c: body((2 * i, 2 * i + 1), c), carry)
        return lax.fori_loop(2 * pairs, count, lambda i, c: body((i,), c), carry)

    def join(parts):
        return parts[0] if len(parts) == 1 else jnp.concatenate(parts, axis=0)

    @pl.loop(0, 4)
    def _(index):
        stored_own = chip * 4 + index
        side = index // 2
        block = ids[chip * 2 + side, index % 2]
        rows = pl.ds(pl.multiple_of((index % 2) * BLK, BLK), BLK)
        begin = first_of[block]
        count = block - begin
        query_clean = loc[0, side, rows, :]
        query_noisy = loc[1, side, rows, :]
        key_noisy = loc[2, side, rows, :]
        value_noisy = loc[3, side, rows, :]
        grad_clean = loc[4, side, rows, :]
        grad_noisy = loc[5, side, rows, :]
        queries = jnp.concatenate([query_clean, query_noisy], axis=0)
        grads = jnp.concatenate([grad_clean, grad_noisy], axis=0)

        def score_step(steps, peak):
            scores = [dot(key_rows(kall, where_is[begin + step]), queries, LAST) for step in steps]
            for step, score in zip(steps, scores):
                weights[step] = score
                peak = jnp.maximum(peak, tops(score))
            return peak

        peak = in_pairs(count, score_step, tops(own_s[index]))
        peak = jnp.max(peak, axis=0, keepdims=True) * scale2

        own = jnp.exp2(own_s[index] * scale2 - peak)
        own_low = own.astype(BF16)
        value_own = key_rows(vall, stored_own)
        out_t[index, :, :BLK] = dot(value_own, own_low[:, :BLK], FIRST)
        out_t[index, :, BLK:] = dot(value_noisy, own_low[:, BLK:], FIRST)

        def value_step(steps, total):
            values = join([key_rows(vall, where_is[begin + step]) for step in steps])
            scores = [weights[step] for step in steps]
            probs = [jnp.exp2(score * scale2 - peak) for score in scores]
            out_t[index] += dot(values, join([prob.astype(BF16) for prob in probs]), FIRST)
            for step, prob in zip(steps, probs):
                weights[step] = prob
                total = total + totals(prob)
            return total

        total = in_pairs(count, value_step, totals(own))
        inverse_total = 1.0 / jnp.sum(total, axis=0, keepdims=True)
        out = out_t[index] * inverse_total
        out_t[index] = out
        delta = jnp.sum(out * grads_t[index], axis=0, keepdims=True)

        own = jnp.exp2(own_s[index] * scale2 - peak) * inverse_total
        own_low = own.astype(BF16)
        own_ds = (own * (own_d[index] - delta)).astype(BF16)
        key_own = key_rows(kall, stored_own)
        dv_acc[stored_own] += dot(own_low[:, :BLK], grad_clean, PLAIN)
        dk_acc[stored_own] += dot(own_ds[:, :BLK], query_clean, PLAIN)
        dv_noisy[side, rows, :] = dot(own_low[:, BLK:], grad_noisy, PLAIN)
        dk_noisy[side, rows, :] = dot(own_ds[:, BLK:], query_noisy, PLAIN) * scale
        dq_t[index, :, :BLK] = dot(key_own, own_ds[:, :BLK], FIRST)
        dq_t[index, :, BLK:] = dot(key_noisy, own_ds[:, BLK:], FIRST)

        def grad_step(steps, carry):
            stored = [where_is[begin + step] for step in steps]
            keys = [key_rows(kall, place) for place in stored]
            probs = [weights[step] * inverse_total for step in steps]
            dv_old = [dv_acc[place] for place in stored]
            dk_old = [dk_acc[place] for place in stored]
            dps = [dot(key_rows(vall, place), grads, LAST) for place in stored]
            dvs = [dot(prob.astype(BF16), grads, PLAIN) for prob in probs]
            dss = [(prob * (dp - delta)).astype(BF16) for prob, dp in zip(probs, dps)]
            dks = [dot(ds, queries, PLAIN) for ds in dss]
            dq_t[index] += dot(join(keys), join(dss), FIRST)
            for i, place in enumerate(stored):
                dv_acc[place] = dv_old[i] + dvs[i]
                dk_acc[place] = dk_old[i] + dks[i]
            return carry

        in_pairs(count, grad_step, 0)


def attention_call(ids, docs, loc, kall, vall, own_s, own_d, grads_t):
    return pl.pallas_call(
        attention_kernel,
        name="attention",
        out_shape=(
            jax.ShapeDtypeStruct((4, HD, 2 * BLK), F32),
            jax.ShapeDtypeStruct((4, HD, 2 * BLK), F32),
            jax.ShapeDtypeStruct((2, 512, HD), F32),
            jax.ShapeDtypeStruct((2, 512, HD), F32),
            jax.ShapeDtypeStruct((32, BLK, HD), F32),
            jax.ShapeDtypeStruct((32, BLK, HD), F32),
        ),
        in_specs=[SMEM, SMEM] + [VMEM] * 6,
        out_specs=(VMEM,) * 6,
        scratch_shapes=[
            pltpu.SMEM((32,), jnp.int32),
            pltpu.SMEM((32,), jnp.int32),
            pltpu.VMEM((16, BLK, 2 * BLK), F32),
        ],
        compiler_params=pltpu.CompilerParams(vmem_limit_bytes=18 * 2**20),
    )(ids, docs, loc, kall, vall, own_s, own_d, grads_t)


def scatter_kernel(
    cq_h, ck_h, nq_h, nk_h, qg_h, kg_h, out_t, dq_t, dk_noisy, dv_noisy, dk, dv,
    back, fin, inner_out,
    raws, qg, kg, stage, k_out, v_out, vy, vh, vx, kh, kx, ky, away, sums, send, recv, lsem,
):
    ctx, head, core, y, x = place()
    right, left = (x + 1) % 4, (x + 3) % 4
    partner = ctx_of(x, y, 1 - core)
    to_right, to_left = ctx_of(right, y, core), ctx_of(left, y, core)
    to_y = ctx_of(x, 1 - y, core)
    score_scale = 1.0 / math.sqrt(HD)
    local = Locals(lsem)
    loads = [local.start(ref, raws.at[i]) for i, ref in enumerate((cq_h, ck_h, nq_h, nk_h))]
    loads += [local.start(qg_h, qg), local.start(kg_h, kg)]
    cq, ck, nq, nk = [raws.at[i] for i in range(4)]
    remote = Copies(send, recv, head)

    def mine(ref, step, row, half):
        chip = chip_of((x + step) % 4, y if row == 0 else 1 - y)
        return ref[pl.ds(chip * 4 + half * 2, 2)].reshape(512, HD)

    def pack_v(step):
        for half in range(2):
            v_out[step, half] = mine(dv, step, 1, half).astype(BF16)

    def pack_k(row, step, half, *others):
        value = mine(dk, step, row, half) * score_scale
        for other in others:
            value = value + other[...].astype(F32)
        k_out[row, step, half] = value.astype(BF16)

    pack_v(2)
    pack_k(1, 2, 0)
    pack_k(1, 2, 1)
    enter(ctx, head, core, y, x)
    v_y = {2: remote.start(v_out.at[2], vy.at[2], to_y)}
    k_half = {}

    def start_half(row):
        k_half[row, 0] = remote.start(k_out.at[row, 2, 0], kh.at[row, 0], to_left)
        k_half[row, 1] = remote.start(k_out.at[row, 2, 1], kh.at[row, 1], to_right)

    start_half(1)
    pack_k(0, 2, 0)
    pack_k(0, 2, 1)
    start_half(0)
    pack_v(3)
    v_y[3] = remote.start(v_out.at[3], vy.at[3], to_y)
    pack_v(1)
    for row in (1, 0):
        pack_k(row, 3, 1)
        pack_k(row, 1, 0)

    swap = {}
    swap[4] = remote.start(dk_noisy.at[1 - core], back.at[4, core], partner)
    own_noisy = [
        local.start(dk_noisy.at[core], back.at[4, core]),
        local.start(dv_noisy.at[core], back.at[5, core]),
    ]

    def turn(ref, first, factor):
        for part in range(2):
            rows = slice(part * BLK, part * BLK + BLK)
            values = jnp.transpose(ref[2 * core + part]) * factor
            back[first, core, rows, :] = values[:BLK]
            back[first + 1, core, rows, :] = values[BLK:]
            values = jnp.transpose(ref[2 * (1 - core) + part]) * factor
            stage[first, rows, :] = values[:BLK]
            stage[first + 1, rows, :] = values[BLK:]
        for i in (first, first + 1):
            swap[i] = remote.start(stage.at[i], back.at[i, core], partner)

    turn(dq_t, 2, score_scale)

    k_x = {}

    def k_forward(row):
        k_half[row, 0].wait_recv()
        pack_k(row, 3, 0, kh.at[row, 0])
        k_x[row, 0] = remote.start(k_out.at[row, 3], kx.at[row, 0], to_left)
        k_half[row, 1].wait_recv()
        pack_k(row, 1, 1, kh.at[row, 1])
        k_x[row, 1] = remote.start(k_out.at[row, 1], kx.at[row, 1], to_right)

    k_forward(1)

    row = lax.broadcasted_iota(jnp.int32, (8, 512), 0)

    def inner(raw, gain, first, second):
        products = 0.0
        for half, values in ((0, first), (1, second)):
            columns = slice(half * HD, half * HD + HD)
            products = products + raw[:, columns].astype(F32) * (gain[:, columns] * values)
        return row_sums(products)

    for copy in loads + own_noisy:
        copy.wait()
    for i in (2, 3, 4):
        swap[i].wait_recv()
    total = jnp.zeros((8, 512), F32)
    for index, raw, gain, i in ((0, cq, qg, 2), (2, nq, qg, 3), (3, nk, kg, 4)):
        total = jnp.where(row == index, inner(raw, gain, back[i, 0], back[i, 1]), total)
    sums[0] = total
    exchange = [
        remote.start(sums.at[0], sums.at[step], ctx, (head + step) % 8) for step in range(1, 8)
    ]

    def pack_x(step, half, *others):
        value = mine(dv, step, 0, half) + vy[step, half].astype(F32)
        for other in others:
            value = value + other[...].astype(F32)
        vx_out[step, half] = value.astype(BF16)

    vx_out = k_out.at[2]
    v_y[2].wait_recv()
    pack_x(2, 0)
    v_half = [remote.start(vx_out.at[2, 0], vh.at[0], to_left)]
    pack_x(2, 1)
    v_half.append(remote.start(vx_out.at[2, 1], vh.at[1], to_right))
    v_y[1] = remote.start(v_out.at[1], vy.at[1], to_y)
    k_forward(0)
    turn(out_t, 0, 1.0)
    swap[5] = remote.start(dv_noisy.at[1 - core], back.at[5, core], partner)
    pack_v(0)
    k_x[1, 0].wait_recv()
    k_x[1, 1].wait_recv()
    for half in range(2):
        pack_k(1, 0, half, kx.at[1, 0, half], kx.at[1, 1, half])
    k_y = remote.start(k_out.at[1, 0], ky, to_y)
    v_y[0] = remote.start(v_out.at[0], vy.at[0], to_y)

    v_y[3].wait_recv()
    v_half[0].wait_recv()
    pack_x(3, 0, vh.at[0])
    pack_x(3, 1)
    v_x = [remote.start(vx_out.at[3], vx.at[0], to_left)]
    v_y[1].wait_recv()
    v_half[1].wait_recv()
    pack_x(1, 0)
    pack_x(1, 1, vh.at[1])
    v_x.append(remote.start(vx_out.at[1], vx.at[1], to_right))

    def finish(index, ref, factor, terms):
        values = []
        for half in range(2):
            value = mine(ref, 0, 0, half) * factor
            for term in terms:
                value = value + term[half].astype(F32)
            values.append(value)
        first_core = core == 0
        fin[index, core] = jnp.where(first_core, values[0], values[1])
        away[index] = jnp.where(first_core, values[1], values[0])
        return remote.start(away.at[index], fin.at[index, core], partner)

    k_x[0, 0].wait_recv()
    k_x[0, 1].wait_recv()
    k_y.wait_recv()
    k_fin = finish(0, dk, score_scale, (kx.at[0, 0], kx.at[0, 1], ky))
    k_fin.wait_recv()
    sums[8] = inner(ck, kg, fin[0, 0], fin[0, 1])
    k_exchange = [
        remote.start(sums.at[8], sums.at[8 + step], ctx, (head + step) % 8) for step in range(1, 8)
    ]
    v_y[0].wait_recv()
    v_x[0].wait_recv()
    v_x[1].wait_recv()
    v_fin = finish(1, dv, 1.0, (vy.at[0], vx.at[0], vx.at[1]))

    for copy in exchange + k_exchange:
        copy.wait_recv()
    total = sums[0]
    k_total = sums[8]
    for step in range(1, 8):
        total = total + sums[step]
        k_total = k_total + sums[8 + step]
    inner_out[...] = jnp.where(row == 1, k_total, total)
    v_fin.wait_recv()
    for i in (0, 1, 5):
        swap[i].wait_recv()
    for copy in remote.started:
        copy.wait_send()


def scatter_call(cq, ck, nq, nk, qg, kg, out_t, dq_t, dk_noisy, dv_noisy, dk, dv):
    return pl.pallas_call(
        scatter_kernel,
        name="scatter_grads",
        out_shape=(
            jax.ShapeDtypeStruct((6, 2, 512, HD), F32),
            jax.ShapeDtypeStruct((2, 2, 512, HD), F32),
            jax.ShapeDtypeStruct((8, 512), F32),
        ),
        in_specs=[HBM] * 6 + [VMEM] * 6,
        out_specs=(VMEM, VMEM, VMEM),
        scratch_shapes=[
            pltpu.VMEM((4, 512, 256), BF16),
            pltpu.VMEM((1, 256), F32),
            pltpu.VMEM((1, 256), F32),
            pltpu.VMEM((4, 512, HD), F32),
            pltpu.VMEM((3, 4, 2, 512, HD), BF16),
            pltpu.VMEM((4, 2, 512, HD), BF16),
            pltpu.VMEM((4, 2, 512, HD), BF16),
            pltpu.VMEM((2, 512, HD), BF16),
            pltpu.VMEM((2, 2, 512, HD), BF16),
            pltpu.VMEM((2, 2, 512, HD), BF16),
            pltpu.VMEM((2, 2, 2, 512, HD), BF16),
            pltpu.VMEM((2, 512, HD), BF16),
            pltpu.VMEM((2, 512, HD), F32),
            pltpu.VMEM((16, 8, 512), F32),
            pltpu.SemaphoreType.DMA((44,)),
            pltpu.SemaphoreType.DMA((44,)),
            pltpu.SemaphoreType.DMA((8,)),
        ],
        compiler_params=pltpu.CompilerParams(
            collective_id=1, has_side_effects=True, vmem_limit_bytes=18 * 2**20
        ),
    )(cq, ck, nq, nk, qg, kg, out_t, dq_t, dk_noisy, dv_noisy, dk, dv)


def finish_kernel(
    cq, ck, nq, nk, qg, kg, inv, inner, back, fin,
    out_clean, out_noisy, dq_clean, dk_clean, dv_clean, dq_noisy, dk_noisy, dv_noisy,
):
    inverse = jnp.transpose(inv[...])
    means = jnp.transpose(inner[...]) / FEAT
    for half in range(2):
        columns = slice(half * HD, half * HD + HD)
        out_clean[:, columns] = back[0, half]
        out_noisy[:, columns] = back[1, half]
        dv_noisy[:, columns] = back[5, half]
        dv_clean[:, columns] = fin[1, half]
        for index, raw, gain, grad, target in (
            (0, cq, qg, back[2, half], dq_clean),
            (1, ck, kg, fin[0, half], dk_clean),
            (2, nq, qg, back[3, half], dq_noisy),
            (3, nk, kg, back[4, half], dk_noisy),
        ):
            scale = inverse[:, index : index + 1]
            factor = scale * scale * scale * means[:, index : index + 1]
            target[:, columns] = scale * (gain[:, columns] * grad) - raw[:, columns].astype(F32) * factor


def finish_call(cq, ck, nq, nk, qg, kg, inv, inner, back, fin):
    rows = 128
    wide = pl.BlockSpec((rows, 256), lambda i: (i, 0))
    gain = pl.BlockSpec((1, 256), lambda i: (0, 0))
    stat = pl.BlockSpec((8, rows), lambda i: (0, i))
    return pl.pallas_call(
        finish_kernel,
        name="finish",
        grid=(512 // rows,),
        out_shape=tuple(jax.ShapeDtypeStruct((512, 256), F32) for _ in range(8)),
        in_specs=[wide] * 4
        + [gain] * 2
        + [stat] * 2
        + [
            pl.BlockSpec((6, 2, rows, HD), lambda i: (0, 0, i, 0)),
            pl.BlockSpec((2, 2, rows, HD), lambda i: (0, 0, i, 0)),
        ],
        out_specs=tuple([wide] * 8),
        compiler_params=pltpu.CompilerParams(vmem_limit_bytes=32 * 2**20),
    )(cq, ck, nq, nk, qg, kg, inv, inner, back, fin)


def local(
    clean_q, clean_k, clean_v, noisy_q, noisy_k, noisy_v,
    q_gain, k_gain, grad_clean, grad_noisy, owned_blocks, block_doc,
):
    qg = q_gain.reshape(1, 256)
    kg = k_gain.reshape(1, 256)
    raws = (clean_q, clean_k, noisy_q, noisy_k, qg, kg)
    pinned = [
        pltpu.with_memory_space_constraint(a, pltpu.HBM)
        for a in raws + (clean_v, noisy_v, grad_clean, grad_noisy, owned_blocks)
    ]
    *parts, inv, ids = gather_call(*pinned)
    kall, vall, loc, own_s, own_d, grads_t = parts
    docs = pltpu.with_memory_space_constraint(block_doc, pltpu.HBM)
    grads = attention_call(ids, docs, loc, kall, vall, own_s, own_d, grads_t)
    back, fin, inner = scatter_call(*pinned[:6], *grads)
    return finish_call(*raws, inv, inner, back, fin)


def solution(mesh):
    placed = (P("ctx", "head"),) * 6 + (P("head"),) * 2 + (P("ctx", "head"),) * 2 + (P("ctx"), P())
    return jax.shard_map(
        local,
        mesh=mesh,
        in_specs=placed,
        out_specs=(P("ctx", "head"),) * 8,
        check_vma=False,
    )
```

```python
import math

import jax
import jax.numpy as jnp
from jax import lax
from jax.experimental import pallas as pl
from jax.experimental.pallas import tpu as pltpu
from jax.sharding import PartitionSpec as P

HD = 128
BLK = 256
FEAT = 2048
EPSILON = 1e-06
NEGATIVE = -1e30
MESH = pl.DeviceIdType.MESH
F32 = jnp.float32
BF16 = jnp.bfloat16
VMEM = pl.BlockSpec(memory_space=pltpu.VMEM)
SMEM = pl.BlockSpec(memory_space=pltpu.SMEM)
ANY = pl.BlockSpec(memory_space=pl.ANY)
HBM = pl.BlockSpec(memory_space=pltpu.HBM)
LAST = (((1,), (1,)), ((), ()))
FIRST = (((0,), (0,)), ((), ()))
PLAIN = (((1,), (0,)), ((), ()))
PACKET = 528
SHIFT = 160
GROUP = 2


def dot(a, b, dims):
    return lax.dot_general(a, b, dims, preferred_element_type=F32)


def row_sums(products):
    high = products.astype(BF16)
    low = (products - high.astype(F32)).astype(BF16)
    ones = jnp.ones((8, products.shape[1]), BF16)
    return dot(ones, high, LAST) + dot(ones, low, LAST)


def place():
    ctx = lax.axis_index("ctx")
    head = lax.axis_index("head")
    core = ctx % 2
    y = (ctx // 2) % 2
    x = ctx // 4
    return ctx, head, core, y, x


def ctx_of(x, y, core):
    return (x * 2 + y) * 2 + core


def chip_of(x, y):
    return x * 2 + y


class Copies:
    def __init__(self, send, recv, head):
        self.send, self.recv, self.head = send, recv, head
        self.started = []
        self.count = 0

    def start(self, src, dst, ctx, head=None):
        copy = pltpu.make_async_remote_copy(
            src_ref=src,
            dst_ref=dst,
            send_sem=self.send.at[self.count],
            recv_sem=self.recv.at[self.count],
            device_id={"ctx": ctx, "head": self.head if head is None else head},
            device_id_type=MESH,
        )
        self.count += 1
        copy.start()
        self.started.append(copy)
        return copy


class Locals:
    def __init__(self, sems):
        self.sems = sems
        self.count = 0

    def start(self, src, dst):
        copy = pltpu.make_async_copy(src, dst, self.sems.at[self.count])
        self.count += 1
        copy.start()
        return copy


def enter(ctx, head, others):
    barrier = pltpu.get_barrier_semaphore()
    for other in others:
        pl.semaphore_signal(barrier, inc=1, device_id={"ctx": other, "head": head}, device_id_type=MESH)
    for step in range(1, 8):
        pl.semaphore_signal(
            barrier, inc=1, device_id={"ctx": ctx, "head": (head + step) % 8}, device_id_type=MESH
        )
    pl.semaphore_wait(barrier, 7 + len(others))


def gather_kernel(
    cq_h, ck_h, nq_h, nk_h, qg_h, kg_h, cv, nv, gc, gn, owned,
    kall, vall, qq, gg, kn, vn, own_s, own_d, grads_t, inv_out, ids_out,
    owned_s, raws, qg, kg, k_packet, normed, sums, send, recv, wide_send, wide_recv, lsem,
):
    ctx, head, core, y, x = place()
    right, left = (x + 1) % 4, (x + 3) % 4
    opposite = (x + 2) % 4
    mine = pl.ds(pl.multiple_of(core * HD, HD), HD)
    theirs = pl.ds(pl.multiple_of((1 - core) * HD, HD), HD)
    partner = ctx_of(x, y, 1 - core)
    local = Locals(lsem)
    owned_load = local.start(owned, owned_s)
    loads = [local.start(ref, raws.at[i]) for i, ref in enumerate((cq_h, ck_h, nq_h, nk_h))]
    loads += [local.start(qg_h, qg), local.start(kg_h, kg)]
    remote = Copies(send, recv, head)
    chips = ((x, 1 - y), (right, y), (left, y))
    enter(ctx, head, [partner] + [ctx_of(*chip, c) for chip in chips for c in range(2)])
    wide = []

    def first_hop(base, columns_of, buf):
        for number, chip in enumerate(chips):
            for target in range(2):
                copy = pltpu.make_async_remote_copy(
                    src_ref=columns_of(target),
                    dst_ref=buf.at[ctx],
                    send_sem=wide_send.at[base + number, target],
                    recv_sem=wide_recv.at[base + number, core],
                    device_id={"ctx": ctx_of(*chip, target), "head": head},
                    device_id_type=MESH,
                )
                copy.start()
                wide.append(copy)

    def arrived(base, number, buf, source):
        chip = ((x, 1 - y), (left, y), (right, y))[number]
        pltpu.make_async_remote_copy(
            src_ref=buf.at[ctx],
            dst_ref=buf.at[ctx_of(*chip, source)],
            send_sem=wide_send.at[base + number, source],
            recv_sem=wide_recv.at[base + number, source],
            device_id={"ctx": partner, "head": head},
            device_id_type=MESH,
        ).wait_recv()

    first_hop(0, lambda target: cv.at[:, target * HD : target * HD + HD], vall)
    v_swap = remote.start(cv.at[:, theirs], vall.at[ctx], partner)
    v_own = local.start(cv.at[:, mine], vall.at[ctx])

    for copy in loads:
        copy.wait()
    row = lax.broadcasted_iota(jnp.int32, (8, 512), 0)
    total = jnp.zeros((8, 512), F32)
    for index in range(4):
        raw = raws[index].astype(F32)
        total = jnp.where(row == index, row_sums(raw * raw), total)
    sums[0] = total
    exchange = [
        remote.start(sums.at[0], sums.at[step], ctx, (head + step) % 8) for step in range(1, 8)
    ]
    owned_load.wait()
    lane = lax.broadcasted_iota(jnp.int32, (16, 2 * HD), 1)
    k_packet[512:, :] = jnp.where(lane % HD == 0, owned_s[0], owned_s[1]).astype(F32).astype(BF16)

    pair = pl.ds(core * 2, 2)
    late, late_own = [], []

    def swap(src, dst):
        late.append(remote.start(src.at[:, :, theirs], dst, partner))
        late_own.append(local.start(src.at[:, :, mine], dst))

    swap(gc, gg.at[pair, 0])
    swap(gn, gg.at[pair, 1])
    swap(nv, vn.at[pair])

    for copy in exchange:
        copy.wait_recv()
    total = sums[0]
    for step in range(1, 8):
        total = total + sums[step]
    inverse = lax.rsqrt(total / FEAT + EPSILON)
    inv_out[...] = inverse
    columns = jnp.transpose(inverse)

    def normalized(index, gain):
        values = raws[index].astype(F32) * columns[:, index : index + 1] * gain[...]
        return values.astype(BF16)

    k_packet[:512, :] = normalized(1, kg)
    first_hop(3, lambda target: k_packet.at[:, target * HD : target * HD + HD], kall)
    k_swap = remote.start(k_packet.at[:, theirs], kall.at[ctx], partner)
    k_own = local.start(k_packet.at[:, mine], kall.at[ctx])
    for index, raw, gain, dst in (
        (0, 0, qg, qq.at[pair, 0]),
        (1, 2, qg, qq.at[pair, 1]),
        (2, 3, kg, kn.at[pair]),
    ):
        normed[index] = normalized(raw, gain).reshape(2, BLK, 2 * HD)
        swap(normed.at[index], dst)

    def slot(buf, sx, sy):
        return buf.at[pl.ds(2 * chip_of(sx, sy), 2)]

    def part(buf, sx, sy, half):
        return buf.at[2 * chip_of(sx, sy) + half]

    def rows_of(sx, sy, half, first, count):
        return vall.at[2 * chip_of(sx, sy) + half, pl.ds(first, count)]

    def spread(view, px, py):
        return remote.start(view, view, ctx_of(px, py, core))

    v_half, v_y = [], []
    for number, near, far, half in ((1, left, right, 0), (2, right, left, 1)):
        arrived(0, number, vall, half)
        v_half.append(spread(part(vall, near, y, half), far, y))
        arrived(0, number, vall, 1 - half)
        v_y.append(spread(slot(vall, near, y), x, 1 - y))
    arrived(3, 0, kall, 0)
    arrived(3, 0, kall, 1)
    k_right = spread(slot(kall, x, 1 - y), right, y)
    k_left = spread(slot(kall, x, 1 - y), left, y)

    v_own.wait()
    k_own.wait()
    v_swap.wait_recv()
    k_swap.wait_recv()
    for copy in late_own:
        copy.wait()
    for copy in late:
        copy.wait_recv()

    def own_block(index):
        side, rows = index // 2, slice(index % 2 * BLK, index % 2 * BLK + BLK)
        packet = 2 * chip_of(x, y) + side
        grad_clean, grad_noisy = gg[index, 0], gg[index, 1]
        own_s[index, :, :BLK] = dot(kall[packet, rows, :], qq[index, 0], LAST)
        own_s[index, :, BLK:] = dot(kn[index], qq[index, 1], LAST)
        own_d[index, :, :BLK] = dot(vall[packet, rows, :], grad_clean, LAST)
        own_d[index, :, BLK:] = dot(vn[index], grad_noisy, LAST)
        grads_t[index, :, :BLK] = jnp.transpose(grad_clean.astype(F32))
        grads_t[index, :, BLK:] = jnp.transpose(grad_noisy.astype(F32))

    own_block(0)
    own_block(1)
    k_half = []
    for number, near, far, half in ((1, left, right, 0), (2, right, left, 1)):
        arrived(3, number, kall, half)
        k_half.append(spread(part(kall, near, y, half), far, y))
        arrived(3, number, kall, 1 - half)
    own_block(2)
    own_block(3)
    for half in range(2):
        v_half[half].wait_recv()
        v_y.append(spread(rows_of(opposite, y, half, SHIFT, 512 - SHIFT), x, 1 - y))
    arrived(0, 0, vall, 0)
    arrived(0, 0, vall, 1)
    v_far = []
    for half, near, far in ((0, left, right), (1, right, left)):
        v_y[half].wait_recv()
        v_far.append(spread(rows_of(near, 1 - y, half, 0, SHIFT), far, y))
    k_right.wait_recv()
    k_half.append(spread(part(kall, left, 1 - y, 0), right, y))
    k_left.wait_recv()
    k_half.append(spread(part(kall, right, 1 - y, 1), left, y))

    for copy in v_y[2:] + v_far + k_half:
        copy.wait_recv()
    names = jnp.max(kall[:, 512:, :].astype(F32), axis=1)
    ids_out[...] = names.astype(jnp.int32)
    for copy in remote.started + wide:
        copy.wait_send()


def gather_call(cq, ck, nq, nk, qg, kg, cv, nv, gc, gn, owned):
    return pl.pallas_call(
        gather_kernel,
        name="gather_keys",
        out_shape=(
            jax.ShapeDtypeStruct((16, PACKET, HD), BF16),
            jax.ShapeDtypeStruct((16, 512, HD), BF16),
            jax.ShapeDtypeStruct((4, 2, BLK, HD), BF16),
            jax.ShapeDtypeStruct((4, 2, BLK, HD), BF16),
            jax.ShapeDtypeStruct((4, BLK, HD), BF16),
            jax.ShapeDtypeStruct((4, BLK, HD), BF16),
            jax.ShapeDtypeStruct((4, BLK, 2 * BLK), F32),
            jax.ShapeDtypeStruct((4, BLK, 2 * BLK), F32),
            jax.ShapeDtypeStruct((4, HD, 2 * BLK), F32),
            jax.ShapeDtypeStruct((8, 512), F32),
            jax.ShapeDtypeStruct((16, HD), jnp.int32),
        ),
        in_specs=[HBM] * 11,
        out_specs=(VMEM,) * 11,
        scratch_shapes=[
            pltpu.SMEM((2,), jnp.int32),
            pltpu.VMEM((4, 512, 256), BF16),
            pltpu.VMEM((1, 256), F32),
            pltpu.VMEM((1, 256), F32),
            pltpu.VMEM((PACKET, 256), BF16),
            pltpu.VMEM((3, 2, BLK, 2 * HD), BF16),
            pltpu.VMEM((8, 8, 512), F32),
            pltpu.SemaphoreType.DMA((32,)),
            pltpu.SemaphoreType.DMA((32,)),
            pltpu.SemaphoreType.DMA((6, 2)),
            pltpu.SemaphoreType.DMA((6, 2)),
            pltpu.SemaphoreType.DMA((16,)),
        ],
        compiler_params=pltpu.CompilerParams(
            collective_id=0, has_side_effects=True, vmem_limit_bytes=20 * 2**20
        ),
    )(cq, ck, nq, nk, qg, kg, cv, nv, gc, gn, owned)


def attention_kernel(
    ids, docs, kall, vall, qq, gg, kn, vn, own_s, own_d, grads_t,
    out_t, dq_t, dk_noisy, dv_noisy, dk_acc, dv_acc,
    where_is, first_of, tile_query, tile_key, weights, peaks, totals_of, deltas,
):
    chip = lax.axis_index("ctx") // 2
    scale = 1.0 / math.sqrt(HD)
    scale2 = scale * math.log2(math.e)

    @pl.loop(0, 16)
    def _(packet):
        where_is[ids[packet, 0]] = packet * 2
        where_is[ids[packet, 1]] = packet * 2 + 1

    first_of[0] = 0

    @pl.loop(1, 32)
    def _(block):
        first_of[block] = jnp.where(docs[block] == docs[block - 1], first_of[block - 1], block)

    @pl.loop(0, 32)
    def _(block):
        dk_acc[block] = jnp.zeros((BLK, HD), F32)
        dv_acc[block] = jnp.zeros((BLK, HD), F32)

    def key_rows(buf, stored):
        start = pl.multiple_of((stored % 2) * BLK, BLK)
        return buf[stored // 2, pl.ds(start, BLK), :]

    def both(ref, index):
        return ref[index].reshape(2 * BLK, HD)

    def tops(scores):
        return jnp.max(scores.reshape(BLK // 8, 8, scores.shape[1]), axis=0)

    def totals(values):
        return jnp.sum(values.reshape(BLK // 8, 8, values.shape[1]), axis=0)

    def two_blocks(side):
        indices = [2 * side, 2 * side + 1]
        count = 0
        for half, index in enumerate(indices):
            block = ids[chip * 2 + side, half]

            def enlist(key_block, count, index=index):
                tile_query[count] = index
                tile_key[count] = where_is[key_block]
                return count + 1

            count = lax.fori_loop(first_of[block], block, enlist, count)

        def over_tiles(body):
            groups = count // GROUP

            @pl.loop(0, groups)
            def _(group):
                body([group * GROUP + i for i in range(GROUP)])

            @pl.loop(groups * GROUP, count)
            def _(tile):
                body([tile])

        for index in indices:
            peaks[index] = tops(own_s[index])

        def score_tiles(tiles):
            queries = [tile_query[tile] for tile in tiles]
            scores = [
                dot(key_rows(kall, tile_key[tile]), both(qq, query), LAST)
                for tile, query in zip(tiles, queries)
            ]
            for tile, query, score in zip(tiles, queries, scores):
                weights[tile] = score
                peaks[query] = jnp.maximum(peaks[query], tops(score))

        over_tiles(score_tiles)

        for index in indices:
            peak = jnp.max(peaks[index], axis=0, keepdims=True) * scale2
            peaks[index] = jnp.broadcast_to(peak, (8, 2 * BLK))
            own = jnp.exp2(own_s[index] * scale2 - peak)
            totals_of[index] = totals(own)
            own_low = own.astype(BF16)
            out_t[index, :, :BLK] = dot(key_rows(vall, chip * 4 + index), own_low[:, :BLK], FIRST)
            out_t[index, :, BLK:] = dot(vn[index], own_low[:, BLK:], FIRST)

        def value_tiles(tiles):
            queries = [tile_query[tile] for tile in tiles]
            probs = [
                jnp.exp2(weights[tile] * scale2 - peaks[query, :1])
                for tile, query in zip(tiles, queries)
            ]
            outs = [
                dot(key_rows(vall, tile_key[tile]), prob.astype(BF16), FIRST)
                for tile, prob in zip(tiles, probs)
            ]
            for tile, query, prob, out in zip(tiles, queries, probs, outs):
                weights[tile] = prob
                totals_of[query] += totals(prob)
                out_t[query] += out

        over_tiles(value_tiles)

        for index in indices:
            stored_own = chip * 4 + index
            inverse_total = 1.0 / jnp.sum(totals_of[index], axis=0, keepdims=True)
            out = out_t[index] * inverse_total
            out_t[index] = out
            delta = jnp.sum(out * grads_t[index], axis=0, keepdims=True)
            totals_of[index] = jnp.broadcast_to(inverse_total, (8, 2 * BLK))
            deltas[index] = jnp.broadcast_to(delta, (8, 2 * BLK))
            own = jnp.exp2(own_s[index] * scale2 - peaks[index, :1]) * inverse_total
            own_low = own.astype(BF16)
            own_ds = (own * (own_d[index] - delta)).astype(BF16)
            dv_acc[stored_own] += dot(own_low[:, :BLK], gg[index, 0], PLAIN)
            dk_acc[stored_own] += dot(own_ds[:, :BLK], qq[index, 0], PLAIN)
            dv_noisy[index] = dot(own_low[:, BLK:], gg[index, 1], PLAIN)
            dk_noisy[index] = dot(own_ds[:, BLK:], qq[index, 1], PLAIN) * scale
            dq_t[index, :, :BLK] = dot(key_rows(kall, stored_own), own_ds[:, :BLK], FIRST)
            dq_t[index, :, BLK:] = dot(kn[index], own_ds[:, BLK:], FIRST)

        def grad_tiles(tiles):
            queries = [tile_query[tile] for tile in tiles]
            stored = [tile_key[tile] for tile in tiles]
            probs = [weights[tile] * totals_of[query, :1] for tile, query in zip(tiles, queries)]
            dps = [
                dot(key_rows(vall, key), both(gg, query), LAST) for key, query in zip(stored, queries)
            ]
            dvs = [dot(prob.astype(BF16), both(gg, query), PLAIN) for prob, query in zip(probs, queries)]
            dss = [
                (prob * (dp - deltas[query, :1])).astype(BF16)
                for prob, dp, query in zip(probs, dps, queries)
            ]
            dks = [dot(ds, both(qq, query), PLAIN) for ds, query in zip(dss, queries)]
            dqs = [dot(key_rows(kall, key), ds, FIRST) for key, ds in zip(stored, dss)]
            for key, query, dv, dk, dq in zip(stored, queries, dvs, dks, dqs):
                dv_acc[key] += dv
                dk_acc[key] += dk
                dq_t[query] += dq

        over_tiles(grad_tiles)

    @pl.loop(0, 2)
    def _(side):
        two_blocks(side)


def attention_call(ids, docs, *parts):
    return pl.pallas_call(
        attention_kernel,
        name="attention",
        out_shape=(
            jax.ShapeDtypeStruct((4, HD, 2 * BLK), F32),
            jax.ShapeDtypeStruct((4, HD, 2 * BLK), F32),
            jax.ShapeDtypeStruct((4, BLK, HD), F32),
            jax.ShapeDtypeStruct((4, BLK, HD), F32),
            jax.ShapeDtypeStruct((32, BLK, HD), F32),
            jax.ShapeDtypeStruct((32, BLK, HD), F32),
        ),
        in_specs=[SMEM, SMEM] + [VMEM] * 9,
        out_specs=(VMEM,) * 6,
        scratch_shapes=[
            pltpu.SMEM((32,), jnp.int32),
            pltpu.SMEM((32,), jnp.int32),
            pltpu.SMEM((32,), jnp.int32),
            pltpu.SMEM((32,), jnp.int32),
            pltpu.VMEM((30, BLK, 2 * BLK), F32),
            pltpu.VMEM((4, 8, 2 * BLK), F32),
            pltpu.VMEM((4, 8, 2 * BLK), F32),
            pltpu.VMEM((4, 8, 2 * BLK), F32),
        ],
        compiler_params=pltpu.CompilerParams(vmem_limit_bytes=28 * 2**20),
    )(ids, docs, *parts)


def scatter_kernel(
    cq_h, ck_h, nq_h, nk_h, qg_h, kg_h, inv, out_t, dq_t, dk_noisy, dv_noisy, dk, dv,
    back, fin, inner_out,
    raws, qg, kg, stage, k_out, v_out, x_out, vy, vq, vh, vx, kh, kx, ky, away, sums,
    send, recv, lsem,
):
    ctx, head, core, y, x = place()
    right, left = (x + 1) % 4, (x + 3) % 4
    partner = ctx_of(x, y, 1 - core)
    to_right, to_left = ctx_of(right, y, core), ctx_of(left, y, core)
    to_y = ctx_of(x, 1 - y, core)
    score_scale = 1.0 / math.sqrt(HD)
    own_columns = pl.ds(pl.multiple_of(core * HD, HD), HD)
    local = Locals(lsem)
    loads = [local.start(ref, raws.at[i]) for i, ref in enumerate((cq_h, ck_h, nq_h, nk_h))]
    loads += [local.start(qg_h, qg), local.start(kg_h, kg)]
    cq, ck, nq, nk = [raws.at[i] for i in range(4)]
    remote = Copies(send, recv, head)

    def mine(ref, step, row, half):
        chip = chip_of((x + step) % 4, y if row == 0 else 1 - y)
        return ref[pl.ds(chip * 4 + half * 2, 2)].reshape(512, HD)

    def pack_v(step):
        for half in range(2):
            v_out[step, half] = mine(dv, step, 1, half).astype(BF16)

    def pack_k(row, step, half, *others):
        value = mine(dk, step, row, half) * score_scale
        for other in others:
            value = value + other[...].astype(F32)
        k_out[row, step, half] = value.astype(BF16)

    pack_v(2)
    pack_k(1, 2, 0)
    pack_k(1, 2, 1)
    enter(ctx, head, [partner, to_right, to_left, to_y])
    first, rest = pl.ds(0, SHIFT), pl.ds(SHIFT, 512 - SHIFT)
    v_far = [
        remote.start(v_out.at[2, 0, first], vq.at[0], to_left),
        remote.start(v_out.at[2, 1, first], vq.at[1], to_right),
    ]
    v_opposite = [
        remote.start(v_out.at[2, half, rest], vy.at[2, half, rest], to_y) for half in range(2)
    ]
    k_half = {}

    def start_half(row):
        k_half[row, 0] = remote.start(k_out.at[row, 2, 0], kh.at[row, 0], to_left)
        k_half[row, 1] = remote.start(k_out.at[row, 2, 1], kh.at[row, 1], to_right)

    start_half(1)
    pack_k(0, 2, 0)
    pack_k(0, 2, 1)
    start_half(0)
    v_y = {}

    def send_v(step, half):
        pack_v(step)
        if half is not None:
            v_far[half].wait_recv()
            v_out[step, half, :SHIFT] = (
                mine(dv, step, 1, half)[:SHIFT] + vq[half].astype(F32)
            ).astype(BF16)
        v_y[step] = remote.start(v_out.at[step], vy.at[step], to_y)

    send_v(3, 0)
    for row in (1, 0):
        pack_k(row, 3, 1)
        pack_k(row, 1, 0)

    def landing(i):
        return back.at[i, :, own_columns]

    swap = {}
    dk_pair, dv_pair = [
        [ref.at[pl.ds(c * 2, 2)] for c in (core, 1 - core)] for ref in (dk_noisy, dv_noisy)
    ]

    def turn(index, ref, first, factor):
        for part in range(2):
            rows = slice(part * BLK, part * BLK + BLK)
            for c, own in ((core, True), (1 - core, False)):
                values = jnp.transpose(ref[2 * c + part]) * factor
                for kind in range(2):
                    if own:
                        back[first + kind, rows, own_columns] = values[kind * BLK : kind * BLK + BLK]
                    else:
                        stage[first + kind, rows, :] = values[kind * BLK : kind * BLK + BLK]
        for i in (first, first + 1):
            swap[i] = remote.start(stage.at[i], landing(i), partner)

    def turn_noisy(ref, i):
        for part in range(2):
            rows = slice(part * BLK, part * BLK + BLK)
            back[i, rows, own_columns] = ref[2 * core + part]
            stage[i, rows, :] = ref[2 * (1 - core) + part]
        swap[i] = remote.start(stage.at[i], landing(i), partner)

    turn(0, dq_t, 2, score_scale)
    turn_noisy(dk_noisy, 4)

    k_x = {}

    def k_forward(row):
        k_half[row, 0].wait_recv()
        pack_k(row, 3, 0, kh.at[row, 0])
        k_x[row, 0] = remote.start(k_out.at[row, 3], kx.at[row, 0], to_left)
        k_half[row, 1].wait_recv()
        pack_k(row, 1, 1, kh.at[row, 1])
        k_x[row, 1] = remote.start(k_out.at[row, 1], kx.at[row, 1], to_right)

    k_forward(1)

    row = lax.broadcasted_iota(jnp.int32, (8, 512), 0)

    def inner(raw, gain, values):
        return row_sums(raw[...].astype(F32) * (gain[...] * values))

    for copy in loads:
        copy.wait()
    for i in (2, 3, 4):
        swap[i].wait_recv()
    total = jnp.zeros((8, 512), F32)
    normal = ((0, cq, qg, 2), (2, nq, qg, 3), (3, nk, kg, 4))
    for index, raw, gain, i in normal:
        total = jnp.where(row == index, inner(raw, gain, back[i]), total)
    sums[0] = total
    exchange = [
        remote.start(sums.at[0], sums.at[step], ctx, (head + step) % 8) for step in range(1, 8)
    ]

    def pack_x(step, half, *others):
        value = mine(dv, step, 0, half)
        for other in others:
            value = value + other[...].astype(F32)
        x_out[step, half] = value.astype(BF16)

    v_half = []
    for half, target in ((0, to_left), (1, to_right)):
        v_opposite[half].wait_recv()
        pack_x(2, half)
        x_out[2, half, SHIFT:] = (
            mine(dv, 2, 0, half)[SHIFT:] + vy[2, half, SHIFT:].astype(F32)
        ).astype(BF16)
        v_half.append(remote.start(x_out.at[2, half], vh.at[half], target))
    send_v(1, 1)
    k_forward(0)
    turn(0, out_t, 0, 1.0)
    turn_noisy(dv_noisy, 5)
    k_x[1, 0].wait_recv()
    k_x[1, 1].wait_recv()
    for half in range(2):
        pack_k(1, 0, half, kx.at[1, 0, half], kx.at[1, 1, half])
    k_y = remote.start(k_out.at[1, 0], ky, to_y)
    send_v(0, None)

    v_y[3].wait_recv()
    v_half[0].wait_recv()
    pack_x(3, 0, vy.at[3, 0], vh.at[0])
    pack_x(3, 1, vy.at[3, 1])
    v_x = [remote.start(x_out.at[3], vx.at[0], to_left)]
    v_y[1].wait_recv()
    v_half[1].wait_recv()
    pack_x(1, 0, vy.at[1, 0])
    pack_x(1, 1, vy.at[1, 1], vh.at[1])
    v_x.append(remote.start(x_out.at[1], vx.at[1], to_right))

    for copy in exchange:
        copy.wait_recv()
    total = sums[0]
    for step in range(1, 8):
        total = total + sums[step]
    inverses = jnp.transpose(inv[...])
    means = jnp.transpose(total) / FEAT
    for index, raw, gain, i in normal:
        inverse = inverses[:, index : index + 1]
        factor = inverse * inverse * inverse * means[:, index : index + 1]
        back[i] = inverse * (gain[...] * back[i]) - raw[...].astype(F32) * factor

    def finish(index, ref, factor, terms):
        values = []
        for half in range(2):
            value = mine(ref, 0, 0, half) * factor
            for term in terms:
                value = value + term[half].astype(F32)
            values.append(value)
        first_core = core == 0
        fin[index, :, own_columns] = jnp.where(first_core, values[0], values[1])
        away[index] = jnp.where(first_core, values[1], values[0])
        return remote.start(away.at[index], fin.at[index, :, own_columns], partner)

    k_x[0, 0].wait_recv()
    k_x[0, 1].wait_recv()
    k_y.wait_recv()
    k_fin = finish(0, dk, score_scale, (kx.at[0, 0], kx.at[0, 1], ky))
    k_fin.wait_recv()
    sums[8] = inner(ck, kg, fin[0])
    k_exchange = [
        remote.start(sums.at[8], sums.at[8 + step], ctx, (head + step) % 8) for step in range(1, 8)
    ]
    v_y[0].wait_recv()
    v_x[0].wait_recv()
    v_x[1].wait_recv()
    v_fin = finish(1, dv, 1.0, (vy.at[0], vx.at[0], vx.at[1]))

    for copy in k_exchange:
        copy.wait_recv()
    total = sums[8]
    for step in range(1, 8):
        total = total + sums[8 + step]
    inner_out[...] = total
    v_fin.wait_recv()
    for i in (0, 1, 5):
        swap[i].wait_recv()
    for copy in remote.started:
        copy.wait_send()


def scatter_call(*operands):
    return pl.pallas_call(
        scatter_kernel,
        name="scatter_grads",
        out_shape=(
            jax.ShapeDtypeStruct((6, 512, 256), F32),
            jax.ShapeDtypeStruct((2, 512, 256), F32),
            jax.ShapeDtypeStruct((8, 512), F32),
        ),
        in_specs=[HBM] * 6 + [VMEM] * 7,
        out_specs=(VMEM, VMEM, VMEM),
        scratch_shapes=[
            pltpu.VMEM((4, 512, 256), BF16),
            pltpu.VMEM((1, 256), F32),
            pltpu.VMEM((1, 256), F32),
            pltpu.VMEM((6, 512, HD), F32),
            pltpu.VMEM((2, 4, 2, 512, HD), BF16),
            pltpu.VMEM((4, 2, 512, HD), BF16),
            pltpu.VMEM((4, 2, 512, HD), BF16),
            pltpu.VMEM((4, 2, 512, HD), BF16),
            pltpu.VMEM((2, SHIFT, HD), BF16),
            pltpu.VMEM((2, 512, HD), BF16),
            pltpu.VMEM((2, 2, 512, HD), BF16),
            pltpu.VMEM((2, 2, 512, HD), BF16),
            pltpu.VMEM((2, 2, 2, 512, HD), BF16),
            pltpu.VMEM((2, 512, HD), BF16),
            pltpu.VMEM((2, 512, HD), F32),
            pltpu.VMEM((16, 8, 512), F32),
            pltpu.SemaphoreType.DMA((48,)),
            pltpu.SemaphoreType.DMA((48,)),
            pltpu.SemaphoreType.DMA((8,)),
        ],
        compiler_params=pltpu.CompilerParams(
            collective_id=1, has_side_effects=True, vmem_limit_bytes=20 * 2**20
        ),
    )(*operands)


def finish_kernel(
    ck, kg, inv, inner, back, fin,
    out_clean, out_noisy, dq_clean, dk_clean, dv_clean, dq_noisy, dk_noisy, dv_noisy,
    dk, sems,
):
    local = Locals(sems)
    copies = [
        local.start(source, target)
        for source, target in (
            (back.at[0], out_clean),
            (back.at[1], out_noisy),
            (back.at[2], dq_clean),
            (back.at[3], dq_noisy),
            (back.at[4], dk_noisy),
            (back.at[5], dv_noisy),
            (fin.at[1], dv_clean),
        )
    ]
    inverse = jnp.transpose(inv[...])[:, 1:2]
    mean = jnp.transpose(inner[...])[:, :1] / FEAT
    factor = inverse * inverse * inverse * mean
    dk[...] = inverse * (kg[...] * fin[0]) - ck[...].astype(F32) * factor
    copies.append(local.start(dk, dk_clean))
    for copy in copies:
        copy.wait()


def finish_call(*operands):
    return pl.pallas_call(
        finish_kernel,
        name="finish",
        out_shape=tuple(jax.ShapeDtypeStruct((512, 256), F32) for _ in range(8)),
        in_specs=[VMEM] * 6,
        out_specs=(HBM,) * 8,
        scratch_shapes=[pltpu.VMEM((512, 256), F32), pltpu.SemaphoreType.DMA((8,))],
        compiler_params=pltpu.CompilerParams(vmem_limit_bytes=16 * 2**20),
    )(*operands)


def local(
    clean_q, clean_k, clean_v, noisy_q, noisy_k, noisy_v,
    q_gain, k_gain, grad_clean, grad_noisy, owned_blocks, block_doc,
):
    qg = q_gain.reshape(1, 256)
    kg = k_gain.reshape(1, 256)
    blocks = [a.reshape(2, BLK, 2 * HD) for a in (noisy_v, grad_clean, grad_noisy)]
    *pinned, docs = [
        pltpu.with_memory_space_constraint(a, pltpu.HBM)
        for a in (
            clean_q, clean_k, noisy_q, noisy_k, qg, kg, clean_v, *blocks, owned_blocks, block_doc,
        )
    ]
    *parts, inv, ids = gather_call(*pinned)
    grads = attention_call(ids, docs, *parts)
    back, fin, inner = scatter_call(*pinned[:6], inv, *grads)
    return finish_call(clean_k, kg, inv, inner, back, fin)


def solution(mesh):
    placed = (P("ctx", "head"),) * 6 + (P("head"),) * 2 + (P("ctx", "head"),) * 2 + (P("ctx"), P())
    return jax.shard_map(
        local,
        mesh=mesh,
        in_specs=placed,
        out_specs=(P("ctx", "head"),) * 8,
        check_vma=False,
    )
```

```python
import math

import jax
import jax.numpy as jnp
from jax import lax
from jax.experimental import pallas as pl
from jax.experimental.pallas import tpu as pltpu
from jax.sharding import PartitionSpec as P

HD = 128
BLK = 256
FEAT = 2048
EPSILON = 1e-06
NEGATIVE = -1e30
MESH = pl.DeviceIdType.MESH
F32 = jnp.float32
BF16 = jnp.bfloat16
VMEM = pl.BlockSpec(memory_space=pltpu.VMEM)
SMEM = pl.BlockSpec(memory_space=pltpu.SMEM)
ANY = pl.BlockSpec(memory_space=pl.ANY)
HBM = pl.BlockSpec(memory_space=pltpu.HBM)
LAST = (((1,), (1,)), ((), ()))
FIRST = (((0,), (0,)), ((), ()))
PLAIN = (((1,), (0,)), ((), ()))
PACKET = 528
SHIFT = 160
GROUP = 2


def dot(a, b, dims):
    return lax.dot_general(a, b, dims, preferred_element_type=F32)


def row_sums(products):
    high = products.astype(BF16)
    low = (products - high.astype(F32)).astype(BF16)
    ones = jnp.ones((8, products.shape[1]), BF16)
    return dot(ones, high, LAST) + dot(ones, low, LAST)


def place():
    ctx = lax.axis_index("ctx")
    head = lax.axis_index("head")
    core = ctx % 2
    y = (ctx // 2) % 2
    x = ctx // 4
    return ctx, head, core, y, x


def ctx_of(x, y, core):
    return (x * 2 + y) * 2 + core


def chip_of(x, y):
    return x * 2 + y


class Copies:
    def __init__(self, send, recv, head):
        self.send, self.recv, self.head = send, recv, head
        self.started = []
        self.count = 0

    def start(self, src, dst, ctx, head=None):
        copy = pltpu.make_async_remote_copy(
            src_ref=src,
            dst_ref=dst,
            send_sem=self.send.at[self.count],
            recv_sem=self.recv.at[self.count],
            device_id={"ctx": ctx, "head": self.head if head is None else head},
            device_id_type=MESH,
        )
        self.count += 1
        copy.start()
        self.started.append(copy)
        return copy


class Locals:
    def __init__(self, sems):
        self.sems = sems
        self.count = 0

    def start(self, src, dst):
        copy = pltpu.make_async_copy(src, dst, self.sems.at[self.count])
        self.count += 1
        copy.start()
        return copy


def enter(ctx, head, others):
    barrier = pltpu.get_barrier_semaphore()
    for other in others:
        pl.semaphore_signal(barrier, inc=1, device_id={"ctx": other, "head": head}, device_id_type=MESH)
    for step in range(1, 8):
        pl.semaphore_signal(
            barrier, inc=1, device_id={"ctx": ctx, "head": (head + step) % 8}, device_id_type=MESH
        )
    pl.semaphore_wait(barrier, 7 + len(others))


def gather_kernel(
    cq_h, ck_h, nq_h, nk_h, qg_h, kg_h, cv, nv, gc, gn, owned,
    kall, vall, qq, gg, kn, vn, own_s, grads_t, inv_out, ids_out,
    owned_s, raws, qg, kg, k_packet, normed, sums, send, recv, wide_send, wide_recv, lsem,
):
    ctx, head, core, y, x = place()
    right, left = (x + 1) % 4, (x + 3) % 4
    opposite = (x + 2) % 4
    mine = pl.ds(pl.multiple_of(core * HD, HD), HD)
    theirs = pl.ds(pl.multiple_of((1 - core) * HD, HD), HD)
    partner = ctx_of(x, y, 1 - core)
    local = Locals(lsem)
    owned_load = local.start(owned, owned_s)
    loads = [local.start(ref, raws.at[i]) for i, ref in enumerate((cq_h, ck_h, nq_h, nk_h))]
    loads += [local.start(qg_h, qg), local.start(kg_h, kg)]
    remote = Copies(send, recv, head)
    chips = ((x, 1 - y), (right, y), (left, y))
    enter(ctx, head, [partner] + [ctx_of(*chip, c) for chip in chips for c in range(2)])
    wide = []

    def first_hop(base, columns_of, buf):
        for number, chip in enumerate(chips):
            for target in range(2):
                copy = pltpu.make_async_remote_copy(
                    src_ref=columns_of(target),
                    dst_ref=buf.at[ctx],
                    send_sem=wide_send.at[base + number, target],
                    recv_sem=wide_recv.at[base + number, core],
                    device_id={"ctx": ctx_of(*chip, target), "head": head},
                    device_id_type=MESH,
                )
                copy.start()
                wide.append(copy)

    def arrived(base, number, buf, source):
        chip = ((x, 1 - y), (left, y), (right, y))[number]
        pltpu.make_async_remote_copy(
            src_ref=buf.at[ctx],
            dst_ref=buf.at[ctx_of(*chip, source)],
            send_sem=wide_send.at[base + number, source],
            recv_sem=wide_recv.at[base + number, source],
            device_id={"ctx": partner, "head": head},
            device_id_type=MESH,
        ).wait_recv()

    first_hop(0, lambda target: cv.at[:, target * HD : target * HD + HD], vall)
    v_swap = remote.start(cv.at[:, theirs], vall.at[ctx], partner)
    v_own = local.start(cv.at[:, mine], vall.at[ctx])

    for copy in loads:
        copy.wait()
    row = lax.broadcasted_iota(jnp.int32, (8, 512), 0)
    total = jnp.zeros((8, 512), F32)
    for index in range(4):
        raw = raws[index].astype(F32)
        total = jnp.where(row == index, row_sums(raw * raw), total)
    sums[0] = total
    exchange = [
        remote.start(sums.at[0], sums.at[step], ctx, (head + step) % 8) for step in range(1, 8)
    ]
    owned_load.wait()
    lane = lax.broadcasted_iota(jnp.int32, (16, 2 * HD), 1)
    k_packet[512:, :] = jnp.where(lane % HD == 0, owned_s[0], owned_s[1]).astype(F32).astype(BF16)

    pair = pl.ds(core * 2, 2)
    late, late_own = [], []

    def swap(src, dst):
        late.append(remote.start(src.at[:, :, theirs], dst, partner))
        late_own.append(local.start(src.at[:, :, mine], dst))

    swap(gc, gg.at[pair, 0])
    swap(gn, gg.at[pair, 1])
    swap(nv, vn.at[pair])

    for copy in exchange:
        copy.wait_recv()
    total = sums[0]
    for step in range(1, 8):
        total = total + sums[step]
    inverse = lax.rsqrt(total / FEAT + EPSILON)
    inv_out[...] = inverse
    columns = jnp.transpose(inverse)

    def normalized(index, gain):
        values = raws[index].astype(F32) * columns[:, index : index + 1] * gain[...]
        return values.astype(BF16)

    k_packet[:512, :] = normalized(1, kg)
    first_hop(3, lambda target: k_packet.at[:, target * HD : target * HD + HD], kall)
    k_swap = remote.start(k_packet.at[:, theirs], kall.at[ctx], partner)
    k_own = local.start(k_packet.at[:, mine], kall.at[ctx])
    for index, raw, gain, dst in (
        (0, 0, qg, qq.at[pair, 0]),
        (1, 2, qg, qq.at[pair, 1]),
        (2, 3, kg, kn.at[pair]),
    ):
        normed[index] = normalized(raw, gain).reshape(2, BLK, 2 * HD)
        swap(normed.at[index], dst)

    def slot(buf, sx, sy):
        return buf.at[pl.ds(2 * chip_of(sx, sy), 2)]

    def part(buf, sx, sy, half):
        return buf.at[2 * chip_of(sx, sy) + half]

    def rows_of(sx, sy, half, first, count):
        return vall.at[2 * chip_of(sx, sy) + half, pl.ds(first, count)]

    def spread(view, px, py):
        return remote.start(view, view, ctx_of(px, py, core))

    v_half, v_y = [], []
    for number, near, far, half in ((1, left, right, 0), (2, right, left, 1)):
        arrived(0, number, vall, half)
        v_half.append(spread(part(vall, near, y, half), far, y))
        arrived(0, number, vall, 1 - half)
        v_y.append(spread(slot(vall, near, y), x, 1 - y))
    arrived(3, 0, kall, 0)
    arrived(3, 0, kall, 1)
    k_right = spread(slot(kall, x, 1 - y), right, y)
    k_left = spread(slot(kall, x, 1 - y), left, y)

    v_own.wait()
    k_own.wait()
    v_swap.wait_recv()
    k_swap.wait_recv()
    for copy in late_own:
        copy.wait()
    for copy in late:
        copy.wait_recv()

    def own_block(index):
        side, rows = index // 2, slice(index % 2 * BLK, index % 2 * BLK + BLK)
        packet = 2 * chip_of(x, y) + side
        grad_clean, grad_noisy = gg[index, 0], gg[index, 1]
        own_s[index, :, :BLK] = dot(kall[packet, rows, :], qq[index, 0], LAST)
        own_s[index, :, BLK:] = dot(kn[index], qq[index, 1], LAST)
        grads_t[index, :, :BLK] = jnp.transpose(grad_clean.astype(F32))
        grads_t[index, :, BLK:] = jnp.transpose(grad_noisy.astype(F32))

    own_block(0)
    own_block(1)
    k_half = []
    for number, near, far, half in ((1, left, right, 0), (2, right, left, 1)):
        arrived(3, number, kall, half)
        k_half.append(spread(part(kall, near, y, half), far, y))
        arrived(3, number, kall, 1 - half)
    own_block(2)
    own_block(3)
    for half in range(2):
        v_half[half].wait_recv()
        v_y.append(spread(rows_of(opposite, y, half, SHIFT, 512 - SHIFT), x, 1 - y))
    arrived(0, 0, vall, 0)
    arrived(0, 0, vall, 1)
    v_far = []
    for half, near, far in ((0, left, right), (1, right, left)):
        v_y[half].wait_recv()
        v_far.append(spread(rows_of(near, 1 - y, half, 0, SHIFT), far, y))
    k_right.wait_recv()
    k_half.append(spread(part(kall, left, 1 - y, 0), right, y))
    k_left.wait_recv()
    k_half.append(spread(part(kall, right, 1 - y, 1), left, y))

    for copy in v_y[2:] + v_far + k_half:
        copy.wait_recv()
    names = jnp.max(kall[:, 512:, :].astype(F32), axis=1)
    ids_out[...] = names.astype(jnp.int32)
    for copy in remote.started + wide:
        copy.wait_send()


def gather_call(cq, ck, nq, nk, qg, kg, cv, nv, gc, gn, owned):
    return pl.pallas_call(
        gather_kernel,
        name="gather_keys",
        out_shape=(
            jax.ShapeDtypeStruct((16, PACKET, HD), BF16),
            jax.ShapeDtypeStruct((16, 512, HD), BF16),
            jax.ShapeDtypeStruct((4, 2, BLK, HD), BF16),
            jax.ShapeDtypeStruct((4, 2, BLK, HD), BF16),
            jax.ShapeDtypeStruct((4, BLK, HD), BF16),
            jax.ShapeDtypeStruct((4, BLK, HD), BF16),
            jax.ShapeDtypeStruct((4, BLK, 2 * BLK), F32),
            jax.ShapeDtypeStruct((4, HD, 2 * BLK), F32),
            jax.ShapeDtypeStruct((8, 512), F32),
            jax.ShapeDtypeStruct((16, HD), jnp.int32),
        ),
        in_specs=[HBM] * 11,
        out_specs=(VMEM,) * 10,
        scratch_shapes=[
            pltpu.SMEM((2,), jnp.int32),
            pltpu.VMEM((4, 512, 256), BF16),
            pltpu.VMEM((1, 256), F32),
            pltpu.VMEM((1, 256), F32),
            pltpu.VMEM((PACKET, 256), BF16),
            pltpu.VMEM((3, 2, BLK, 2 * HD), BF16),
            pltpu.VMEM((8, 8, 512), F32),
            pltpu.SemaphoreType.DMA((32,)),
            pltpu.SemaphoreType.DMA((32,)),
            pltpu.SemaphoreType.DMA((6, 2)),
            pltpu.SemaphoreType.DMA((6, 2)),
            pltpu.SemaphoreType.DMA((16,)),
        ],
        compiler_params=pltpu.CompilerParams(
            collective_id=0, has_side_effects=True, vmem_limit_bytes=20 * 2**20
        ),
    )(cq, ck, nq, nk, qg, kg, cv, nv, gc, gn, owned)


def attention_kernel(
    ids, docs, kall, vall, qq, gg, kn, vn, own_s, grads_t,
    out_t, dq_t, dk_noisy, dv_noisy, dk_acc, dv_acc,
    where_is, first_of, pair_query, pair_key, pair_bias,
    scores, weights, own_weights, scaled_grads, peaks, sums, deltas,
):
    chip = lax.axis_index("ctx") // 2
    scale = 1.0 / math.sqrt(HD)
    scale2 = scale * math.log2(math.e)

    @pl.loop(0, 16)
    def _(packet):
        where_is[ids[packet, 0]] = packet * 2
        where_is[ids[packet, 1]] = packet * 2 + 1

    first_of[0] = 0

    @pl.loop(1, 32)
    def _(block):
        first_of[block] = jnp.where(docs[block] == docs[block - 1], first_of[block - 1], block)

    @pl.loop(0, 32)
    def _(block):
        dk_acc[block] = jnp.zeros((BLK, HD), F32)
        dv_acc[block] = jnp.zeros((BLK, HD), F32)

    def key_rows(buf, stored):
        start = pl.multiple_of((stored % 2) * BLK, BLK)
        return buf[stored // 2, pl.ds(start, BLK), :]

    def key_pair(buf, pair):
        return jnp.concatenate(
            [key_rows(buf, pair_key[2 * pair]), key_rows(buf, pair_key[2 * pair + 1])], axis=0
        )

    def both(ref, index):
        return ref[index].reshape(2 * BLK, HD)

    def tops(values):
        return jnp.max(values.reshape(-1, 8, values.shape[1]), axis=0)

    def totals(values):
        return jnp.sum(values.reshape(-1, 8, values.shape[1]), axis=0)

    @pl.loop(0, 2)
    def _(side):
        count = 0
        for half in range(2):
            block = ids[chip * 2 + side, half]
            begin = first_of[block]

            def enlist(pair, count, half=half, block=block, begin=begin):
                key = begin + 2 * pair
                pair_query[count] = half
                pair_key[2 * count] = where_is[key]
                pair_key[2 * count + 1] = where_is[jnp.minimum(key + 1, block - 1)]
                pair_bias[count] = jnp.where(key + 1 < block, 0, 1)
                return count + 1

            count = lax.fori_loop(0, (block - begin + 1) // 2, enlist, count)

        def over_pairs(body):
            groups = count // GROUP

            @pl.loop(0, groups)
            def _(group):
                body([group * GROUP + i for i in range(GROUP)])

            @pl.loop(groups * GROUP, count)
            def _(pair):
                body([pair])

        first = 2 * side
        for half in range(2):
            peaks[half] = tops(own_s[first + half])

        def score_pairs(pairs):
            queries = [pair_query[pair] for pair in pairs]
            values = [
                dot(key_pair(kall, pair), both(qq, first + query), LAST)
                for pair, query in zip(pairs, queries)
            ]
            for pair, query, value in zip(pairs, queries, values):
                scores[pair] = value
                peaks[query] = jnp.maximum(peaks[query], tops(value))

        over_pairs(score_pairs)

        for half in range(2):
            index = first + half
            peak = jnp.max(peaks[half], axis=0, keepdims=True) * scale2
            peaks[half] = jnp.broadcast_to(peak, (8, 2 * BLK))
            own = jnp.exp2(own_s[index] * scale2 - peak)
            sums[half] = totals(own)
            own_low = own.astype(BF16)
            own_weights[half] = own_low
            out_t[index, :, :BLK] = dot(key_rows(vall, chip * 4 + index), own_low[:, :BLK], FIRST)
            out_t[index, :, BLK:] = dot(vn[index], own_low[:, BLK:], FIRST)

        def value_pairs(pairs):
            queries = [pair_query[pair] for pair in pairs]
            outs, parts = [], []
            for pair, query in zip(pairs, queries):
                peak = peaks[query, :1]
                hidden = peak + jnp.where(pair_bias[pair] == 1, jnp.inf, 0.0)
                upper = jnp.exp2(scores[pair, :BLK] * scale2 - peak)
                lower = jnp.exp2(scores[pair, BLK:] * scale2 - hidden)
                low = jnp.concatenate([upper.astype(BF16), lower.astype(BF16)], axis=0)
                weights[pair] = low
                outs.append(dot(key_pair(vall, pair), low, FIRST))
                parts.append(totals(upper) + totals(lower))
            for query, out, part in zip(queries, outs, parts):
                sums[query] += part
                out_t[first + query] += out

        over_pairs(value_pairs)

        for half in range(2):
            index = first + half
            stored_own = chip * 4 + index
            inverse_sum = 1.0 / jnp.sum(sums[half], axis=0, keepdims=True)
            out = out_t[index] * inverse_sum
            out_t[index] = out
            grad_rows = (grads_t[index] * inverse_sum).astype(BF16).astype(F32)
            delta = jnp.sum(out * grad_rows, axis=0, keepdims=True)
            deltas[half] = jnp.broadcast_to(delta, (8, 2 * BLK))
            grads = jnp.transpose(grad_rows).astype(BF16)
            scaled_grads[half] = grads
            own_low = own_weights[half]
            own_dp = jnp.concatenate(
                [
                    dot(key_rows(vall, stored_own), grads[:BLK], LAST),
                    dot(vn[index], grads[BLK:], LAST),
                ],
                axis=1,
            )
            own_ds = (own_low.astype(F32) * (own_dp - delta)).astype(BF16)
            dv_acc[stored_own] += dot(own_low[:, :BLK], grads[:BLK], PLAIN)
            dk_acc[stored_own] += dot(own_ds[:, :BLK], qq[index, 0], PLAIN)
            dv_noisy[index] = dot(own_low[:, BLK:], grads[BLK:], PLAIN)
            dk_noisy[index] = dot(own_ds[:, BLK:], qq[index, 1], PLAIN) * scale
            dq_t[index, :, :BLK] = dot(key_rows(kall, stored_own), own_ds[:, :BLK], FIRST)
            dq_t[index, :, BLK:] = dot(kn[index], own_ds[:, BLK:], FIRST)

        def grad_pairs(pairs):
            queries = [pair_query[pair] for pair in pairs]
            results = []
            for pair, query in zip(pairs, queries):
                low = weights[pair]
                dp = dot(key_pair(vall, pair), scaled_grads[query], LAST)
                ds = (low.astype(F32) * (dp - deltas[query, :1])).astype(BF16)
                results.append(
                    (
                        dot(low, scaled_grads[query], PLAIN),
                        dot(ds, both(qq, first + query), PLAIN),
                        dot(key_pair(kall, pair), ds, FIRST),
                    )
                )
            for pair, query, (dv, dk, dq) in zip(pairs, queries, results):
                for place in range(2):
                    rows = slice(place * BLK, place * BLK + BLK)
                    dv_acc[pair_key[2 * pair + place]] += dv[rows]
                    dk_acc[pair_key[2 * pair + place]] += dk[rows]
                dq_t[first + query] += dq

        over_pairs(grad_pairs)


def attention_call(ids, docs, *parts):
    return pl.pallas_call(
        attention_kernel,
        name="attention",
        out_shape=(
            jax.ShapeDtypeStruct((4, HD, 2 * BLK), F32),
            jax.ShapeDtypeStruct((4, HD, 2 * BLK), F32),
            jax.ShapeDtypeStruct((4, BLK, HD), F32),
            jax.ShapeDtypeStruct((4, BLK, HD), F32),
            jax.ShapeDtypeStruct((32, BLK, HD), F32),
            jax.ShapeDtypeStruct((32, BLK, HD), F32),
        ),
        in_specs=[SMEM, SMEM] + [VMEM] * 8,
        out_specs=(VMEM,) * 6,
        scratch_shapes=[
            pltpu.SMEM((32,), jnp.int32),
            pltpu.SMEM((32,), jnp.int32),
            pltpu.SMEM((16,), jnp.int32),
            pltpu.SMEM((32,), jnp.int32),
            pltpu.SMEM((16,), jnp.int32),
            pltpu.VMEM((16, 2 * BLK, 2 * BLK), F32),
            pltpu.VMEM((16, 2 * BLK, 2 * BLK), BF16),
            pltpu.VMEM((2, BLK, 2 * BLK), BF16),
            pltpu.VMEM((2, 2 * BLK, HD), BF16),
            pltpu.VMEM((2, 8, 2 * BLK), F32),
            pltpu.VMEM((2, 8, 2 * BLK), F32),
            pltpu.VMEM((2, 8, 2 * BLK), F32),
        ],
        compiler_params=pltpu.CompilerParams(vmem_limit_bytes=34 * 2**20),
    )(ids, docs, *parts)


def scatter_kernel(
    cq_h, ck_h, nq_h, nk_h, qg_h, kg_h, inv, out_t, dq_t, dk_noisy, dv_noisy, dk, dv,
    back, fin, inner_out,
    raws, qg, kg, stage, k_out, v_out, x_out, vy, vq, vh, vx, kh, kx, ky, away, sums,
    send, recv, lsem,
):
    ctx, head, core, y, x = place()
    right, left = (x + 1) % 4, (x + 3) % 4
    partner = ctx_of(x, y, 1 - core)
    to_right, to_left = ctx_of(right, y, core), ctx_of(left, y, core)
    to_y = ctx_of(x, 1 - y, core)
    score_scale = 1.0 / math.sqrt(HD)
    own_columns = pl.ds(pl.multiple_of(core * HD, HD), HD)
    local = Locals(lsem)
    loads = [local.start(ref, raws.at[i]) for i, ref in enumerate((cq_h, ck_h, nq_h, nk_h))]
    loads += [local.start(qg_h, qg), local.start(kg_h, kg)]
    cq, ck, nq, nk = [raws.at[i] for i in range(4)]
    remote = Copies(send, recv, head)

    def mine(ref, step, row, half):
        chip = chip_of((x + step) % 4, y if row == 0 else 1 - y)
        return ref[pl.ds(chip * 4 + half * 2, 2)].reshape(512, HD)

    def pack_v(step):
        for half in range(2):
            v_out[step, half] = mine(dv, step, 1, half).astype(BF16)

    def pack_k(row, step, half, *others):
        value = mine(dk, step, row, half) * score_scale
        for other in others:
            value = value + other[...].astype(F32)
        k_out[row, step, half] = value.astype(BF16)

    pack_v(2)
    pack_k(1, 2, 0)
    pack_k(1, 2, 1)
    enter(ctx, head, [partner, to_right, to_left, to_y])
    first, rest = pl.ds(0, SHIFT), pl.ds(SHIFT, 512 - SHIFT)
    v_far = [
        remote.start(v_out.at[2, 0, first], vq.at[0], to_left),
        remote.start(v_out.at[2, 1, first], vq.at[1], to_right),
    ]
    v_opposite = [
        remote.start(v_out.at[2, half, rest], vy.at[2, half, rest], to_y) for half in range(2)
    ]
    k_half = {}

    def start_half(row):
        k_half[row, 0] = remote.start(k_out.at[row, 2, 0], kh.at[row, 0], to_left)
        k_half[row, 1] = remote.start(k_out.at[row, 2, 1], kh.at[row, 1], to_right)

    start_half(1)
    pack_k(0, 2, 0)
    pack_k(0, 2, 1)
    start_half(0)
    v_y = {}

    def send_v(step, half):
        pack_v(step)
        if half is not None:
            v_far[half].wait_recv()
            v_out[step, half, :SHIFT] = (
                mine(dv, step, 1, half)[:SHIFT] + vq[half].astype(F32)
            ).astype(BF16)
        v_y[step] = remote.start(v_out.at[step], vy.at[step], to_y)

    send_v(3, 0)
    for row in (1, 0):
        pack_k(row, 3, 1)
        pack_k(row, 1, 0)

    def landing(i):
        return back.at[i, :, own_columns]

    swap = {}
    dk_pair, dv_pair = [
        [ref.at[pl.ds(c * 2, 2)] for c in (core, 1 - core)] for ref in (dk_noisy, dv_noisy)
    ]

    def turn(index, ref, first, factor):
        for part in range(2):
            rows = slice(part * BLK, part * BLK + BLK)
            for c, own in ((core, True), (1 - core, False)):
                values = jnp.transpose(ref[2 * c + part]) * factor
                for kind in range(2):
                    if own:
                        back[first + kind, rows, own_columns] = values[kind * BLK : kind * BLK + BLK]
                    else:
                        stage[first + kind, rows, :] = values[kind * BLK : kind * BLK + BLK]
        for i in (first, first + 1):
            swap[i] = remote.start(stage.at[i], landing(i), partner)

    def turn_noisy(ref, i):
        for part in range(2):
            rows = slice(part * BLK, part * BLK + BLK)
            back[i, rows, own_columns] = ref[2 * core + part]
            stage[i, rows, :] = ref[2 * (1 - core) + part]
        swap[i] = remote.start(stage.at[i], landing(i), partner)

    turn(0, dq_t, 2, score_scale)
    turn_noisy(dk_noisy, 4)

    k_x = {}

    def k_forward(row):
        k_half[row, 0].wait_recv()
        pack_k(row, 3, 0, kh.at[row, 0])
        k_x[row, 0] = remote.start(k_out.at[row, 3], kx.at[row, 0], to_left)
        k_half[row, 1].wait_recv()
        pack_k(row, 1, 1, kh.at[row, 1])
        k_x[row, 1] = remote.start(k_out.at[row, 1], kx.at[row, 1], to_right)

    k_forward(1)

    row = lax.broadcasted_iota(jnp.int32, (8, 512), 0)

    def inner(raw, gain, values):
        return row_sums(raw[...].astype(F32) * (gain[...] * values))

    for copy in loads:
        copy.wait()
    for i in (2, 3, 4):
        swap[i].wait_recv()
    total = jnp.zeros((8, 512), F32)
    normal = ((0, cq, qg, 2), (2, nq, qg, 3), (3, nk, kg, 4))
    for index, raw, gain, i in normal:
        total = jnp.where(row == index, inner(raw, gain, back[i]), total)
    sums[0] = total
    exchange = [
        remote.start(sums.at[0], sums.at[step], ctx, (head + step) % 8) for step in range(1, 8)
    ]

    def pack_x(step, half, *others):
        value = mine(dv, step, 0, half)
        for other in others:
            value = value + other[...].astype(F32)
        x_out[step, half] = value.astype(BF16)

    v_half = []
    for half, target in ((0, to_left), (1, to_right)):
        v_opposite[half].wait_recv()
        pack_x(2, half)
        x_out[2, half, SHIFT:] = (
            mine(dv, 2, 0, half)[SHIFT:] + vy[2, half, SHIFT:].astype(F32)
        ).astype(BF16)
        v_half.append(remote.start(x_out.at[2, half], vh.at[half], target))
    send_v(1, 1)
    k_forward(0)
    turn(0, out_t, 0, 1.0)
    turn_noisy(dv_noisy, 5)
    k_x[1, 0].wait_recv()
    k_x[1, 1].wait_recv()
    for half in range(2):
        pack_k(1, 0, half, kx.at[1, 0, half], kx.at[1, 1, half])
    k_y = remote.start(k_out.at[1, 0], ky, to_y)
    send_v(0, None)

    v_y[3].wait_recv()
    v_half[0].wait_recv()
    pack_x(3, 0, vy.at[3, 0], vh.at[0])
    pack_x(3, 1, vy.at[3, 1])
    v_x = [remote.start(x_out.at[3], vx.at[0], to_left)]
    v_y[1].wait_recv()
    v_half[1].wait_recv()
    pack_x(1, 0, vy.at[1, 0])
    pack_x(1, 1, vy.at[1, 1], vh.at[1])
    v_x.append(remote.start(x_out.at[1], vx.at[1], to_right))

    for copy in exchange:
        copy.wait_recv()
    total = sums[0]
    for step in range(1, 8):
        total = total + sums[step]
    inverses = jnp.transpose(inv[...])
    means = jnp.transpose(total) / FEAT
    for index, raw, gain, i in normal:
        inverse = inverses[:, index : index + 1]
        factor = inverse * inverse * inverse * means[:, index : index + 1]
        back[i] = inverse * (gain[...] * back[i]) - raw[...].astype(F32) * factor

    def finish(index, ref, factor, terms):
        values = []
        for half in range(2):
            value = mine(ref, 0, 0, half) * factor
            for term in terms:
                value = value + term[half].astype(F32)
            values.append(value)
        first_core = core == 0
        fin[index, :, own_columns] = jnp.where(first_core, values[0], values[1])
        away[index] = jnp.where(first_core, values[1], values[0])
        return remote.start(away.at[index], fin.at[index, :, own_columns], partner)

    k_x[0, 0].wait_recv()
    k_x[0, 1].wait_recv()
    k_y.wait_recv()
    k_fin = finish(0, dk, score_scale, (kx.at[0, 0], kx.at[0, 1], ky))
    k_fin.wait_recv()
    sums[8] = inner(ck, kg, fin[0])
    k_exchange = [
        remote.start(sums.at[8], sums.at[8 + step], ctx, (head + step) % 8) for step in range(1, 8)
    ]
    v_y[0].wait_recv()
    v_x[0].wait_recv()
    v_x[1].wait_recv()
    v_fin = finish(1, dv, 1.0, (vy.at[0], vx.at[0], vx.at[1]))

    for copy in k_exchange:
        copy.wait_recv()
    total = sums[8]
    for step in range(1, 8):
        total = total + sums[8 + step]
    inner_out[...] = total
    v_fin.wait_recv()
    for i in (0, 1, 5):
        swap[i].wait_recv()
    for copy in remote.started:
        copy.wait_send()


def scatter_call(*operands):
    return pl.pallas_call(
        scatter_kernel,
        name="scatter_grads",
        out_shape=(
            jax.ShapeDtypeStruct((6, 512, 256), F32),
            jax.ShapeDtypeStruct((2, 512, 256), F32),
            jax.ShapeDtypeStruct((8, 512), F32),
        ),
        in_specs=[HBM] * 6 + [VMEM] * 7,
        out_specs=(VMEM, VMEM, VMEM),
        scratch_shapes=[
            pltpu.VMEM((4, 512, 256), BF16),
            pltpu.VMEM((1, 256), F32),
            pltpu.VMEM((1, 256), F32),
            pltpu.VMEM((6, 512, HD), F32),
            pltpu.VMEM((2, 4, 2, 512, HD), BF16),
            pltpu.VMEM((4, 2, 512, HD), BF16),
            pltpu.VMEM((4, 2, 512, HD), BF16),
            pltpu.VMEM((4, 2, 512, HD), BF16),
            pltpu.VMEM((2, SHIFT, HD), BF16),
            pltpu.VMEM((2, 512, HD), BF16),
            pltpu.VMEM((2, 2, 512, HD), BF16),
            pltpu.VMEM((2, 2, 512, HD), BF16),
            pltpu.VMEM((2, 2, 2, 512, HD), BF16),
            pltpu.VMEM((2, 512, HD), BF16),
            pltpu.VMEM((2, 512, HD), F32),
            pltpu.VMEM((16, 8, 512), F32),
            pltpu.SemaphoreType.DMA((48,)),
            pltpu.SemaphoreType.DMA((48,)),
            pltpu.SemaphoreType.DMA((8,)),
        ],
        compiler_params=pltpu.CompilerParams(
            collective_id=1, has_side_effects=True, vmem_limit_bytes=20 * 2**20
        ),
    )(*operands)


def finish_kernel(
    ck, kg, inv, inner, back, fin,
    out_clean, out_noisy, dq_clean, dk_clean, dv_clean, dq_noisy, dk_noisy, dv_noisy,
    dk, sems,
):
    local = Locals(sems)
    copies = [
        local.start(source, target)
        for source, target in (
            (back.at[0], out_clean),
            (back.at[1], out_noisy),
            (back.at[2], dq_clean),
            (back.at[3], dq_noisy),
            (back.at[4], dk_noisy),
            (back.at[5], dv_noisy),
            (fin.at[1], dv_clean),
        )
    ]
    inverse = jnp.transpose(inv[...])[:, 1:2]
    mean = jnp.transpose(inner[...])[:, :1] / FEAT
    factor = inverse * inverse * inverse * mean
    dk[...] = inverse * (kg[...] * fin[0]) - ck[...].astype(F32) * factor
    copies.append(local.start(dk, dk_clean))
    for copy in copies:
        copy.wait()


def finish_call(*operands):
    return pl.pallas_call(
        finish_kernel,
        name="finish",
        out_shape=tuple(jax.ShapeDtypeStruct((512, 256), F32) for _ in range(8)),
        in_specs=[VMEM] * 6,
        out_specs=(HBM,) * 8,
        scratch_shapes=[pltpu.VMEM((512, 256), F32), pltpu.SemaphoreType.DMA((8,))],
        compiler_params=pltpu.CompilerParams(vmem_limit_bytes=16 * 2**20),
    )(*operands)


def local(
    clean_q, clean_k, clean_v, noisy_q, noisy_k, noisy_v,
    q_gain, k_gain, grad_clean, grad_noisy, owned_blocks, block_doc,
):
    qg = q_gain.reshape(1, 256)
    kg = k_gain.reshape(1, 256)
    blocks = [a.reshape(2, BLK, 2 * HD) for a in (noisy_v, grad_clean, grad_noisy)]
    *pinned, docs = [
        pltpu.with_memory_space_constraint(a, pltpu.HBM)
        for a in (
            clean_q, clean_k, noisy_q, noisy_k, qg, kg, clean_v, *blocks, owned_blocks, block_doc,
        )
    ]
    *parts, inv, ids = gather_call(*pinned)
    grads = attention_call(ids, docs, *parts)
    back, fin, inner = scatter_call(*pinned[:6], inv, *grads)
    return finish_call(clean_k, kg, inv, inner, back, fin)


def solution(mesh):
    placed = (P("ctx", "head"),) * 6 + (P("head"),) * 2 + (P("ctx", "head"),) * 2 + (P("ctx"), P())
    return jax.shard_map(
        local,
        mesh=mesh,
        in_specs=placed,
        out_specs=(P("ctx", "head"),) * 8,
        check_vma=False,
    )
```

```python
import math

import jax
import jax.numpy as jnp
from jax import lax
from jax.experimental import pallas as pl
from jax.experimental.pallas import tpu as pltpu
from jax.sharding import PartitionSpec as P

HD = 128
BLK = 256
FEAT = 2048
EPSILON = 1e-06
NEGATIVE = -1e30
MESH = pl.DeviceIdType.MESH
F32 = jnp.float32
BF16 = jnp.bfloat16
VMEM = pl.BlockSpec(memory_space=pltpu.VMEM)
SMEM = pl.BlockSpec(memory_space=pltpu.SMEM)
ANY = pl.BlockSpec(memory_space=pl.ANY)
HBM = pl.BlockSpec(memory_space=pltpu.HBM)
LAST = (((1,), (1,)), ((), ()))
FIRST = (((0,), (0,)), ((), ()))
PLAIN = (((1,), (0,)), ((), ()))
PACKET = 528
SHIFT = 160
GROUP = 2


def dot(a, b, dims):
    return lax.dot_general(a, b, dims, preferred_element_type=F32)


def row_sums(products):
    high = products.astype(BF16)
    low = (products - high.astype(F32)).astype(BF16)
    ones = jnp.ones((8, products.shape[1]), BF16)
    return dot(ones, high, LAST) + dot(ones, low, LAST)


def place():
    ctx = lax.axis_index("ctx")
    head = lax.axis_index("head")
    core = ctx % 2
    y = (ctx // 2) % 2
    x = ctx // 4
    return ctx, head, core, y, x


def ctx_of(x, y, core):
    return (x * 2 + y) * 2 + core


def chip_of(x, y):
    return x * 2 + y


class Copies:
    def __init__(self, send, recv, head):
        self.send, self.recv, self.head = send, recv, head
        self.started = []
        self.count = 0

    def start(self, src, dst, ctx, head=None):
        copy = pltpu.make_async_remote_copy(
            src_ref=src,
            dst_ref=dst,
            send_sem=self.send.at[self.count],
            recv_sem=self.recv.at[self.count],
            device_id={"ctx": ctx, "head": self.head if head is None else head},
            device_id_type=MESH,
        )
        self.count += 1
        copy.start()
        self.started.append(copy)
        return copy


class Locals:
    def __init__(self, sems):
        self.sems = sems
        self.count = 0

    def start(self, src, dst):
        copy = pltpu.make_async_copy(src, dst, self.sems.at[self.count])
        self.count += 1
        copy.start()
        return copy


def enter(ctx, head, others):
    barrier = pltpu.get_barrier_semaphore()
    for other in others:
        pl.semaphore_signal(barrier, inc=1, device_id={"ctx": other, "head": head}, device_id_type=MESH)
    for step in range(1, 8):
        pl.semaphore_signal(
            barrier, inc=1, device_id={"ctx": ctx, "head": (head + step) % 8}, device_id_type=MESH
        )
    pl.semaphore_wait(barrier, 7 + len(others))


def gather_kernel(
    cq_h, ck_h, nq_h, nk_h, qg_h, kg_h, cv, nv, gc, gn, owned,
    kall, vall, qq, gg, kn, vn, own_s, grads_t, inv_out, ids_out,
    owned_s, raws, qg, kg, k_packet, normed, sums, send, recv, wide_send, wide_recv, lsem,
):
    ctx, head, core, y, x = place()
    right, left = (x + 1) % 4, (x + 3) % 4
    opposite = (x + 2) % 4
    mine = pl.ds(pl.multiple_of(core * HD, HD), HD)
    theirs = pl.ds(pl.multiple_of((1 - core) * HD, HD), HD)
    partner = ctx_of(x, y, 1 - core)
    local = Locals(lsem)
    owned_load = local.start(owned, owned_s)
    loads = [local.start(ref, raws.at[i]) for i, ref in enumerate((cq_h, ck_h, nq_h, nk_h))]
    loads += [local.start(qg_h, qg), local.start(kg_h, kg)]
    remote = Copies(send, recv, head)
    chips = ((x, 1 - y), (right, y), (left, y))
    enter(ctx, head, [partner] + [ctx_of(*chip, c) for chip in chips for c in range(2)])
    wide = []

    def first_hop(base, columns_of, buf):
        for number, chip in enumerate(chips):
            for target in range(2):
                copy = pltpu.make_async_remote_copy(
                    src_ref=columns_of(target),
                    dst_ref=buf.at[ctx],
                    send_sem=wide_send.at[base + number, target],
                    recv_sem=wide_recv.at[base + number, core],
                    device_id={"ctx": ctx_of(*chip, target), "head": head},
                    device_id_type=MESH,
                )
                copy.start()
                wide.append(copy)

    def arrived(base, number, buf, source):
        chip = ((x, 1 - y), (left, y), (right, y))[number]
        pltpu.make_async_remote_copy(
            src_ref=buf.at[ctx],
            dst_ref=buf.at[ctx_of(*chip, source)],
            send_sem=wide_send.at[base + number, source],
            recv_sem=wide_recv.at[base + number, source],
            device_id={"ctx": partner, "head": head},
            device_id_type=MESH,
        ).wait_recv()

    first_hop(0, lambda target: cv.at[:, target * HD : target * HD + HD], vall)
    v_swap = remote.start(cv.at[:, theirs], vall.at[ctx], partner)
    v_own = local.start(cv.at[:, mine], vall.at[ctx])

    for copy in loads:
        copy.wait()
    row = lax.broadcasted_iota(jnp.int32, (8, 512), 0)
    total = jnp.zeros((8, 512), F32)
    for index in range(4):
        raw = raws[index].astype(F32)
        total = jnp.where(row == index, row_sums(raw * raw), total)
    sums[0] = total
    exchange = [
        remote.start(sums.at[0], sums.at[step], ctx, (head + step) % 8) for step in range(1, 8)
    ]
    owned_load.wait()
    lane = lax.broadcasted_iota(jnp.int32, (16, 2 * HD), 1)
    k_packet[512:, :] = jnp.where(lane % HD == 0, owned_s[0], owned_s[1]).astype(F32).astype(BF16)

    pair = pl.ds(core * 2, 2)
    late, late_own = [], []

    def swap(src, dst):
        late.append(remote.start(src.at[:, :, theirs], dst, partner))
        late_own.append(local.start(src.at[:, :, mine], dst))

    swap(gc, gg.at[pair, 0])
    swap(gn, gg.at[pair, 1])
    swap(nv, vn.at[pair])

    for copy in exchange:
        copy.wait_recv()
    total = sums[0]
    for step in range(1, 8):
        total = total + sums[step]
    inverse = lax.rsqrt(total / FEAT + EPSILON)
    inv_out[...] = inverse
    columns = jnp.transpose(inverse)

    def normalized(index, gain):
        values = raws[index].astype(F32) * columns[:, index : index + 1] * gain[...]
        return values.astype(BF16)

    k_packet[:512, :] = normalized(1, kg)
    first_hop(3, lambda target: k_packet.at[:, target * HD : target * HD + HD], kall)
    k_swap = remote.start(k_packet.at[:, theirs], kall.at[ctx], partner)
    k_own = local.start(k_packet.at[:, mine], kall.at[ctx])
    for index, raw, gain, dst in (
        (0, 0, qg, qq.at[pair, 0]),
        (1, 2, qg, qq.at[pair, 1]),
        (2, 3, kg, kn.at[pair]),
    ):
        normed[index] = normalized(raw, gain).reshape(2, BLK, 2 * HD)
        swap(normed.at[index], dst)

    def slot(buf, sx, sy):
        return buf.at[pl.ds(2 * chip_of(sx, sy), 2)]

    def part(buf, sx, sy, half):
        return buf.at[2 * chip_of(sx, sy) + half]

    def rows_of(sx, sy, half, first, count):
        return vall.at[2 * chip_of(sx, sy) + half, pl.ds(first, count)]

    def spread(view, px, py):
        return remote.start(view, view, ctx_of(px, py, core))

    v_half, v_y, k_half = [], [], []
    sides = ((1, left, right, 0), (2, right, left, 1))
    for number, near, far, half in sides:
        arrived(0, number, vall, half)
        v_half.append(spread(part(vall, near, y, half), far, y))
    arrived(3, 0, kall, 0)
    arrived(3, 0, kall, 1)
    k_right = spread(slot(kall, x, 1 - y), right, y)
    k_left = spread(slot(kall, x, 1 - y), left, y)
    arrived(0, 1, vall, 1)
    v_y.append(spread(slot(vall, left, y), x, 1 - y))

    v_own.wait()
    k_own.wait()
    v_swap.wait_recv()
    k_swap.wait_recv()
    for copy in late_own:
        copy.wait()
    for copy in late:
        copy.wait_recv()

    def own_block(index):
        side, rows = index // 2, slice(index % 2 * BLK, index % 2 * BLK + BLK)
        packet = 2 * chip_of(x, y) + side
        own_s[index, :, :BLK] = dot(kall[packet, rows, :], qq[index, 0], LAST)
        own_s[index, :, BLK:] = dot(kn[index], qq[index, 1], LAST)
        for kind in range(2):
            columns = slice(kind * BLK, kind * BLK + BLK)
            grads_t[index, :, columns] = jnp.transpose(gg[index, kind].astype(F32))

    own_block(0)
    for number, near, far, half in sides:
        arrived(3, number, kall, half)
        k_half.append(spread(part(kall, near, y, half), far, y))
        arrived(3, number, kall, 1 - half)
    own_block(1)
    arrived(0, 2, vall, 0)
    v_y.append(spread(slot(vall, right, y), x, 1 - y))
    own_block(2)
    v_half[0].wait_recv()
    v_half[1].wait_recv()
    v_y[0].wait_recv()
    v_far = [spread(rows_of(left, 1 - y, 0, 0, SHIFT), right, y)]
    for half in range(2):
        v_y.append(spread(rows_of(opposite, y, half, SHIFT, 512 - SHIFT), x, 1 - y))
    k_right.wait_recv()
    k_half.append(spread(part(kall, left, 1 - y, 0), right, y))
    k_left.wait_recv()
    k_half.append(spread(part(kall, right, 1 - y, 1), left, y))
    own_block(3)
    v_y[1].wait_recv()
    v_far.append(spread(rows_of(right, 1 - y, 1, 0, SHIFT), left, y))
    arrived(0, 0, vall, 0)
    arrived(0, 0, vall, 1)
    for copy in v_y[2:] + v_far + k_half:
        copy.wait_recv()
    names = jnp.max(kall[:, 512:, :].astype(F32), axis=1)
    ids_out[...] = names.astype(jnp.int32)
    for copy in remote.started + wide:
        copy.wait_send()


def gather_call(cq, ck, nq, nk, qg, kg, cv, nv, gc, gn, owned):
    return pl.pallas_call(
        gather_kernel,
        name="gather_keys",
        out_shape=(
            jax.ShapeDtypeStruct((16, PACKET, HD), BF16),
            jax.ShapeDtypeStruct((16, 512, HD), BF16),
            jax.ShapeDtypeStruct((4, 2, BLK, HD), BF16),
            jax.ShapeDtypeStruct((4, 2, BLK, HD), BF16),
            jax.ShapeDtypeStruct((4, BLK, HD), BF16),
            jax.ShapeDtypeStruct((4, BLK, HD), BF16),
            jax.ShapeDtypeStruct((4, BLK, 2 * BLK), F32),
            jax.ShapeDtypeStruct((4, HD, 2 * BLK), F32),
            jax.ShapeDtypeStruct((8, 512), F32),
            jax.ShapeDtypeStruct((16, HD), jnp.int32),
        ),
        in_specs=[HBM] * 11,
        out_specs=(VMEM,) * 10,
        scratch_shapes=[
            pltpu.SMEM((2,), jnp.int32),
            pltpu.VMEM((4, 512, 256), BF16),
            pltpu.VMEM((1, 256), F32),
            pltpu.VMEM((1, 256), F32),
            pltpu.VMEM((PACKET, 256), BF16),
            pltpu.VMEM((3, 2, BLK, 2 * HD), BF16),
            pltpu.VMEM((8, 8, 512), F32),
            pltpu.SemaphoreType.DMA((32,)),
            pltpu.SemaphoreType.DMA((32,)),
            pltpu.SemaphoreType.DMA((6, 2)),
            pltpu.SemaphoreType.DMA((6, 2)),
            pltpu.SemaphoreType.DMA((16,)),
        ],
        compiler_params=pltpu.CompilerParams(
            collective_id=0, has_side_effects=True, vmem_limit_bytes=20 * 2**20
        ),
    )(cq, ck, nq, nk, qg, kg, cv, nv, gc, gn, owned)


def attention_kernel(
    ids, docs, kall, vall, qq, gg, kn, vn, own_s, grads_t,
    out_t, dq_t, dk_noisy, dv_noisy, dk_acc, dv_acc,
    where_is, first_of, pair_query, pair_key, pair_bias,
    scores, weights, own_weights, scaled_grads, peaks, sums, deltas,
):
    chip = lax.axis_index("ctx") // 2
    scale = 1.0 / math.sqrt(HD)
    scale2 = scale * math.log2(math.e)

    @pl.loop(0, 16)
    def _(packet):
        where_is[ids[packet, 0]] = packet * 2
        where_is[ids[packet, 1]] = packet * 2 + 1

    first_of[0] = 0

    @pl.loop(1, 32)
    def _(block):
        first_of[block] = jnp.where(docs[block] == docs[block - 1], first_of[block - 1], block)

    @pl.loop(0, 32)
    def _(block):
        dk_acc[block] = jnp.zeros((BLK, HD), F32)
        dv_acc[block] = jnp.zeros((BLK, HD), F32)

    def key_rows(buf, stored):
        start = pl.multiple_of((stored % 2) * BLK, BLK)
        return buf[stored // 2, pl.ds(start, BLK), :]

    def key_pair(buf, pair):
        return jnp.concatenate(
            [key_rows(buf, pair_key[2 * pair]), key_rows(buf, pair_key[2 * pair + 1])], axis=0
        )

    def both(ref, index):
        return ref[index].reshape(2 * BLK, HD)

    def tops(values):
        return jnp.max(values.reshape(-1, 8, values.shape[1]), axis=0)

    def totals(values):
        return jnp.sum(values.reshape(-1, 8, values.shape[1]), axis=0)

    @pl.loop(0, 2)
    def _(side):
        count = 0
        for half in range(2):
            block = ids[chip * 2 + side, half]
            begin = first_of[block]

            def enlist(pair, count, half=half, block=block, begin=begin):
                key = begin + 2 * pair
                pair_query[count] = half
                pair_key[2 * count] = where_is[key]
                pair_key[2 * count + 1] = where_is[jnp.minimum(key + 1, block - 1)]
                pair_bias[count] = jnp.where(key + 1 < block, 0, 1)
                return count + 1

            count = lax.fori_loop(0, (block - begin + 1) // 2, enlist, count)

        def over_pairs(body):
            groups = count // GROUP

            @pl.loop(0, groups)
            def _(group):
                body([group * GROUP + i for i in range(GROUP)])

            @pl.loop(groups * GROUP, count)
            def _(pair):
                body([pair])

        first = 2 * side
        for half in range(2):
            peaks[half] = tops(own_s[first + half])

        def score_pairs(pairs):
            queries = [pair_query[pair] for pair in pairs]
            values = [
                dot(key_pair(kall, pair), both(qq, first + query), LAST)
                for pair, query in zip(pairs, queries)
            ]
            for pair, query, value in zip(pairs, queries, values):
                scores[pair] = value
                peaks[query] = jnp.maximum(peaks[query], tops(value))

        over_pairs(score_pairs)

        for half in range(2):
            index = first + half
            peak = jnp.max(peaks[half], axis=0, keepdims=True) * scale2
            peaks[half] = jnp.broadcast_to(peak, (8, 2 * BLK))
            own = jnp.exp2(own_s[index] * scale2 - peak)
            sums[half] = totals(own)
            own_low = own.astype(BF16)
            own_weights[half] = own_low
            out_t[index, :, :BLK] = dot(key_rows(vall, chip * 4 + index), own_low[:, :BLK], FIRST)
            out_t[index, :, BLK:] = dot(vn[index], own_low[:, BLK:], FIRST)

        def value_pairs(pairs):
            queries = [pair_query[pair] for pair in pairs]
            outs, parts = [], []
            for pair, query in zip(pairs, queries):
                peak = peaks[query, :1]
                hidden = peak + jnp.where(pair_bias[pair] == 1, jnp.inf, 0.0)
                upper = jnp.exp2(scores[pair, :BLK] * scale2 - peak)
                lower = jnp.exp2(scores[pair, BLK:] * scale2 - hidden)
                low = jnp.concatenate([upper.astype(BF16), lower.astype(BF16)], axis=0)
                weights[pair] = low
                outs.append(dot(key_pair(vall, pair), low, FIRST))
                parts.append(totals(upper) + totals(lower))
            for query, out, part in zip(queries, outs, parts):
                sums[query] += part
                out_t[first + query] += out

        over_pairs(value_pairs)

        for half in range(2):
            index = first + half
            stored_own = chip * 4 + index
            inverse_sum = 1.0 / jnp.sum(sums[half], axis=0, keepdims=True)
            out = out_t[index] * inverse_sum
            out_t[index] = out
            grad_rows = (grads_t[index] * inverse_sum).astype(BF16).astype(F32)
            delta = jnp.sum(out * grad_rows, axis=0, keepdims=True)
            deltas[half] = jnp.broadcast_to(delta, (8, 2 * BLK))
            grads = jnp.transpose(grad_rows).astype(BF16)
            scaled_grads[half] = grads
            own_low = own_weights[half]
            own_dp = jnp.concatenate(
                [
                    dot(key_rows(vall, stored_own), grads[:BLK], LAST),
                    dot(vn[index], grads[BLK:], LAST),
                ],
                axis=1,
            )
            own_ds = (own_low.astype(F32) * (own_dp - delta)).astype(BF16)
            dv_acc[stored_own] += dot(own_low[:, :BLK], grads[:BLK], PLAIN)
            dk_acc[stored_own] += dot(own_ds[:, :BLK], qq[index, 0], PLAIN)
            dv_noisy[index] = dot(own_low[:, BLK:], grads[BLK:], PLAIN)
            dk_noisy[index] = dot(own_ds[:, BLK:], qq[index, 1], PLAIN) * scale
            dq_t[index, :, :BLK] = dot(key_rows(kall, stored_own), own_ds[:, :BLK], FIRST)
            dq_t[index, :, BLK:] = dot(kn[index], own_ds[:, BLK:], FIRST)

        def grad_pairs(pairs):
            queries = [pair_query[pair] for pair in pairs]
            results = []
            for pair, query in zip(pairs, queries):
                low = weights[pair]
                dp = dot(key_pair(vall, pair), scaled_grads[query], LAST)
                ds = (low.astype(F32) * (dp - deltas[query, :1])).astype(BF16)
                results.append(
                    (
                        dot(low, scaled_grads[query], PLAIN),
                        dot(ds, both(qq, first + query), PLAIN),
                        dot(key_pair(kall, pair), ds, FIRST),
                    )
                )
            for pair, query, (dv, dk, dq) in zip(pairs, queries, results):
                for place in range(2):
                    rows = slice(place * BLK, place * BLK + BLK)
                    dv_acc[pair_key[2 * pair + place]] += dv[rows]
                    dk_acc[pair_key[2 * pair + place]] += dk[rows]
                dq_t[first + query] += dq

        over_pairs(grad_pairs)


def attention_call(ids, docs, *parts):
    return pl.pallas_call(
        attention_kernel,
        name="attention",
        out_shape=(
            jax.ShapeDtypeStruct((4, HD, 2 * BLK), F32),
            jax.ShapeDtypeStruct((4, HD, 2 * BLK), F32),
            jax.ShapeDtypeStruct((4, BLK, HD), F32),
            jax.ShapeDtypeStruct((4, BLK, HD), F32),
            jax.ShapeDtypeStruct((32, BLK, HD), F32),
            jax.ShapeDtypeStruct((32, BLK, HD), F32),
        ),
        in_specs=[SMEM, SMEM] + [VMEM] * 8,
        out_specs=(VMEM,) * 6,
        scratch_shapes=[
            pltpu.SMEM((32,), jnp.int32),
            pltpu.SMEM((32,), jnp.int32),
            pltpu.SMEM((16,), jnp.int32),
            pltpu.SMEM((32,), jnp.int32),
            pltpu.SMEM((16,), jnp.int32),
            pltpu.VMEM((16, 2 * BLK, 2 * BLK), F32),
            pltpu.VMEM((16, 2 * BLK, 2 * BLK), BF16),
            pltpu.VMEM((2, BLK, 2 * BLK), BF16),
            pltpu.VMEM((2, 2 * BLK, HD), BF16),
            pltpu.VMEM((2, 8, 2 * BLK), F32),
            pltpu.VMEM((2, 8, 2 * BLK), F32),
            pltpu.VMEM((2, 8, 2 * BLK), F32),
        ],
        compiler_params=pltpu.CompilerParams(vmem_limit_bytes=34 * 2**20),
    )(ids, docs, *parts)


def scatter_kernel(
    cq_h, ck_h, nq_h, nk_h, qg_h, kg_h, inv, out_t, dq_t, dk_noisy, dv_noisy, dk, dv,
    back, fin, inner_out,
    raws, qg, kg, stage, k_out, v_out, x_out, vy, vq, vh, vx, kh, kx, ky, away, sums,
    send, recv, lsem,
):
    ctx, head, core, y, x = place()
    right, left = (x + 1) % 4, (x + 3) % 4
    partner = ctx_of(x, y, 1 - core)
    to_right, to_left = ctx_of(right, y, core), ctx_of(left, y, core)
    to_y = ctx_of(x, 1 - y, core)
    score_scale = 1.0 / math.sqrt(HD)
    own_columns = pl.ds(pl.multiple_of(core * HD, HD), HD)
    local = Locals(lsem)
    loads = [local.start(ref, raws.at[i]) for i, ref in enumerate((cq_h, ck_h, nq_h, nk_h))]
    loads += [local.start(qg_h, qg), local.start(kg_h, kg)]
    cq, ck, nq, nk = [raws.at[i] for i in range(4)]
    remote = Copies(send, recv, head)

    def mine(ref, step, row, half):
        chip = chip_of((x + step) % 4, y if row == 0 else 1 - y)
        return ref[pl.ds(chip * 4 + half * 2, 2)].reshape(512, HD)

    def pack_v(step):
        for half in range(2):
            v_out[step, half] = mine(dv, step, 1, half).astype(BF16)

    def pack_k(row, step, half, *others):
        value = mine(dk, step, row, half) * score_scale
        for other in others:
            value = value + other[...].astype(F32)
        k_out[row, step, half] = value.astype(BF16)

    pack_k(1, 2, 0)
    pack_k(1, 2, 1)
    enter(ctx, head, [partner, to_right, to_left, to_y])
    k_half = {}

    def start_half(row):
        k_half[row, 0] = remote.start(k_out.at[row, 2, 0], kh.at[row, 0], to_left)
        k_half[row, 1] = remote.start(k_out.at[row, 2, 1], kh.at[row, 1], to_right)

    start_half(1)
    pack_v(2)
    first, rest = pl.ds(0, SHIFT), pl.ds(SHIFT, 512 - SHIFT)
    v_far = [
        remote.start(v_out.at[2, 0, first], vq.at[0], to_left),
        remote.start(v_out.at[2, 1, first], vq.at[1], to_right),
    ]
    v_opposite = [
        remote.start(v_out.at[2, half, rest], vy.at[2, half, rest], to_y) for half in range(2)
    ]
    v_y = {}

    def send_v(step, half):
        pack_v(step)
        if half is not None:
            v_far[half].wait_recv()
            v_out[step, half, :SHIFT] = (
                mine(dv, step, 1, half)[:SHIFT] + vq[half].astype(F32)
            ).astype(BF16)
        v_y[step] = remote.start(v_out.at[step], vy.at[step], to_y)

    for row in (1, 0):
        pack_k(row, 3, 1)
        pack_k(row, 1, 0)
    pack_k(0, 2, 0)
    pack_k(0, 2, 1)

    def landing(i):
        return back.at[i, :, own_columns]

    swap = {}
    dk_pair, dv_pair = [
        [ref.at[pl.ds(c * 2, 2)] for c in (core, 1 - core)] for ref in (dk_noisy, dv_noisy)
    ]

    def turn(index, ref, first, factor):
        for part in range(2):
            rows = slice(part * BLK, part * BLK + BLK)
            for c, own in ((core, True), (1 - core, False)):
                values = jnp.transpose(ref[2 * c + part]) * factor
                for kind in range(2):
                    if own:
                        back[first + kind, rows, own_columns] = values[kind * BLK : kind * BLK + BLK]
                    else:
                        stage[first + kind, rows, :] = values[kind * BLK : kind * BLK + BLK]
        for i in (first, first + 1):
            swap[i] = remote.start(stage.at[i], landing(i), partner)

    def turn_noisy(ref, i):
        for part in range(2):
            rows = slice(part * BLK, part * BLK + BLK)
            back[i, rows, own_columns] = ref[2 * core + part]
            stage[i, rows, :] = ref[2 * (1 - core) + part]
        swap[i] = remote.start(stage.at[i], landing(i), partner)

    k_x = {}

    def k_forward(row):
        k_half[row, 0].wait_recv()
        pack_k(row, 3, 0, kh.at[row, 0])
        k_x[row, 0] = remote.start(k_out.at[row, 3], kx.at[row, 0], to_left)
        k_half[row, 1].wait_recv()
        pack_k(row, 1, 1, kh.at[row, 1])
        k_x[row, 1] = remote.start(k_out.at[row, 1], kx.at[row, 1], to_right)

    turn_noisy(dk_noisy, 4)
    send_v(3, 0)
    k_forward(1)
    start_half(0)

    def pack_x(step, half, *others):
        value = mine(dv, step, 0, half)
        for other in others:
            value = value + other[...].astype(F32)
        x_out[step, half] = value.astype(BF16)

    v_half = []
    for half, target in ((0, to_left), (1, to_right)):
        v_opposite[half].wait_recv()
        pack_x(2, half)
        x_out[2, half, SHIFT:] = (
            mine(dv, 2, 0, half)[SHIFT:] + vy[2, half, SHIFT:].astype(F32)
        ).astype(BF16)
        v_half.append(remote.start(x_out.at[2, half], vh.at[half], target))
    turn(0, dq_t, 2, score_scale)

    row = lax.broadcasted_iota(jnp.int32, (8, 512), 0)

    def inner(raw, gain, values):
        return row_sums(raw[...].astype(F32) * (gain[...] * values))

    for copy in loads:
        copy.wait()
    k_x[1, 0].wait_recv()
    k_x[1, 1].wait_recv()
    for half in range(2):
        pack_k(1, 0, half, kx.at[1, 0, half], kx.at[1, 1, half])
    k_y = remote.start(k_out.at[1, 0], ky, to_y)
    k_forward(0)
    send_v(1, 1)
    for i in (2, 3, 4):
        swap[i].wait_recv()
    total = jnp.zeros((8, 512), F32)
    normal = ((0, cq, qg, 2), (2, nq, qg, 3), (3, nk, kg, 4))
    for index, raw, gain, i in normal:
        total = jnp.where(row == index, inner(raw, gain, back[i]), total)
    sums[0] = total
    exchange = [
        remote.start(sums.at[0], sums.at[step], ctx, (head + step) % 8) for step in range(1, 8)
    ]
    v_y[3].wait_recv()
    v_half[0].wait_recv()
    pack_x(3, 0, vy.at[3, 0], vh.at[0])
    pack_x(3, 1, vy.at[3, 1])
    v_x = [remote.start(x_out.at[3], vx.at[0], to_left)]
    turn(0, out_t, 0, 1.0)
    turn_noisy(dv_noisy, 5)
    send_v(0, None)

    for copy in exchange:
        copy.wait_recv()
    total = sums[0]
    for step in range(1, 8):
        total = total + sums[step]
    inverses = jnp.transpose(inv[...])
    means = jnp.transpose(total) / FEAT
    for index, raw, gain, i in normal:
        inverse = inverses[:, index : index + 1]
        factor = inverse * inverse * inverse * means[:, index : index + 1]
        back[i] = inverse * (gain[...] * back[i]) - raw[...].astype(F32) * factor

    def finish(index, ref, factor, terms):
        values = []
        for half in range(2):
            value = mine(ref, 0, 0, half) * factor
            for term in terms:
                value = value + term[half].astype(F32)
            values.append(value)
        first_core = core == 0
        fin[index, :, own_columns] = jnp.where(first_core, values[0], values[1])
        away[index] = jnp.where(first_core, values[1], values[0])
        return remote.start(away.at[index], fin.at[index, :, own_columns], partner)

    k_y.wait_recv()
    v_y[1].wait_recv()
    v_half[1].wait_recv()
    pack_x(1, 0, vy.at[1, 0])
    pack_x(1, 1, vy.at[1, 1], vh.at[1])
    v_x.append(remote.start(x_out.at[1], vx.at[1], to_right))
    k_x[0, 0].wait_recv()
    k_x[0, 1].wait_recv()
    k_fin = finish(0, dk, score_scale, (kx.at[0, 0], kx.at[0, 1], ky))
    k_fin.wait_recv()
    sums[8] = inner(ck, kg, fin[0])
    k_exchange = [
        remote.start(sums.at[8], sums.at[8 + step], ctx, (head + step) % 8) for step in range(1, 8)
    ]
    v_y[0].wait_recv()
    v_x[0].wait_recv()
    v_x[1].wait_recv()
    v_fin = finish(1, dv, 1.0, (vy.at[0], vx.at[0], vx.at[1]))

    for copy in k_exchange:
        copy.wait_recv()
    total = sums[8]
    for step in range(1, 8):
        total = total + sums[8 + step]
    inner_out[...] = total
    v_fin.wait_recv()
    for i in (0, 1, 5):
        swap[i].wait_recv()
    for copy in remote.started:
        copy.wait_send()


def scatter_call(*operands):
    return pl.pallas_call(
        scatter_kernel,
        name="scatter_grads",
        out_shape=(
            jax.ShapeDtypeStruct((6, 512, 256), F32),
            jax.ShapeDtypeStruct((2, 512, 256), F32),
            jax.ShapeDtypeStruct((8, 512), F32),
        ),
        in_specs=[HBM] * 6 + [VMEM] * 7,
        out_specs=(VMEM, VMEM, VMEM),
        scratch_shapes=[
            pltpu.VMEM((4, 512, 256), BF16),
            pltpu.VMEM((1, 256), F32),
            pltpu.VMEM((1, 256), F32),
            pltpu.VMEM((6, 512, HD), F32),
            pltpu.VMEM((2, 4, 2, 512, HD), BF16),
            pltpu.VMEM((4, 2, 512, HD), BF16),
            pltpu.VMEM((4, 2, 512, HD), BF16),
            pltpu.VMEM((4, 2, 512, HD), BF16),
            pltpu.VMEM((2, SHIFT, HD), BF16),
            pltpu.VMEM((2, 512, HD), BF16),
            pltpu.VMEM((2, 2, 512, HD), BF16),
            pltpu.VMEM((2, 2, 512, HD), BF16),
            pltpu.VMEM((2, 2, 2, 512, HD), BF16),
            pltpu.VMEM((2, 512, HD), BF16),
            pltpu.VMEM((2, 512, HD), F32),
            pltpu.VMEM((16, 8, 512), F32),
            pltpu.SemaphoreType.DMA((48,)),
            pltpu.SemaphoreType.DMA((48,)),
            pltpu.SemaphoreType.DMA((8,)),
        ],
        compiler_params=pltpu.CompilerParams(
            collective_id=1, has_side_effects=True, vmem_limit_bytes=20 * 2**20
        ),
    )(*operands)


def finish_kernel(
    ck, kg, inv, inner, back, fin,
    out_clean, out_noisy, dq_clean, dk_clean, dv_clean, dq_noisy, dk_noisy, dv_noisy,
    dk, sems,
):
    local = Locals(sems)
    copies = [
        local.start(source, target)
        for source, target in (
            (back.at[0], out_clean),
            (back.at[1], out_noisy),
            (back.at[2], dq_clean),
            (back.at[3], dq_noisy),
            (back.at[4], dk_noisy),
            (back.at[5], dv_noisy),
            (fin.at[1], dv_clean),
        )
    ]
    inverse = jnp.transpose(inv[...])[:, 1:2]
    mean = jnp.transpose(inner[...])[:, :1] / FEAT
    factor = inverse * inverse * inverse * mean
    dk[...] = inverse * (kg[...] * fin[0]) - ck[...].astype(F32) * factor
    copies.append(local.start(dk, dk_clean))
    for copy in copies:
        copy.wait()


def finish_call(*operands):
    return pl.pallas_call(
        finish_kernel,
        name="finish",
        out_shape=tuple(jax.ShapeDtypeStruct((512, 256), F32) for _ in range(8)),
        in_specs=[VMEM] * 6,
        out_specs=(HBM,) * 8,
        scratch_shapes=[pltpu.VMEM((512, 256), F32), pltpu.SemaphoreType.DMA((8,))],
        compiler_params=pltpu.CompilerParams(vmem_limit_bytes=16 * 2**20),
    )(*operands)


def local(
    clean_q, clean_k, clean_v, noisy_q, noisy_k, noisy_v,
    q_gain, k_gain, grad_clean, grad_noisy, owned_blocks, block_doc,
):
    qg = q_gain.reshape(1, 256)
    kg = k_gain.reshape(1, 256)
    blocks = [a.reshape(2, BLK, 2 * HD) for a in (noisy_v, grad_clean, grad_noisy)]
    *pinned, docs = [
        pltpu.with_memory_space_constraint(a, pltpu.HBM)
        for a in (
            clean_q, clean_k, noisy_q, noisy_k, qg, kg, clean_v, *blocks, owned_blocks, block_doc,
        )
    ]
    *parts, inv, ids = gather_call(*pinned)
    grads = attention_call(ids, docs, *parts)
    back, fin, inner = scatter_call(*pinned[:6], inv, *grads)
    return finish_call(clean_k, kg, inv, inner, back, fin)


def solution(mesh):
    placed = (P("ctx", "head"),) * 6 + (P("head"),) * 2 + (P("ctx", "head"),) * 2 + (P("ctx"), P())
    return jax.shard_map(
        local,
        mesh=mesh,
        in_specs=placed,
        out_specs=(P("ctx", "head"),) * 8,
        check_vma=False,
    )
```

```python
import math

import jax
import jax.numpy as jnp
from jax import lax
from jax.experimental import pallas as pl
from jax.experimental.pallas import tpu as pltpu
from jax.sharding import PartitionSpec as P

HD = 128
BLK = 256
FEAT = 2048
EPSILON = 1e-06
NEGATIVE = -1e30
MESH = pl.DeviceIdType.MESH
F32 = jnp.float32
BF16 = jnp.bfloat16
VMEM = pl.BlockSpec(memory_space=pltpu.VMEM)
SMEM = pl.BlockSpec(memory_space=pltpu.SMEM)
ANY = pl.BlockSpec(memory_space=pl.ANY)
HBM = pl.BlockSpec(memory_space=pltpu.HBM)
LAST = (((1,), (1,)), ((), ()))
FIRST = (((0,), (0,)), ((), ()))
PLAIN = (((1,), (0,)), ((), ()))
PACKET = 528
SHIFT = 160
GROUP = 2


def dot(a, b, dims):
    return lax.dot_general(a, b, dims, preferred_element_type=F32)


def row_sums(products):
    high = products.astype(BF16)
    low = (products - high.astype(F32)).astype(BF16)
    ones = jnp.ones((8, products.shape[1]), BF16)
    return dot(ones, high, LAST) + dot(ones, low, LAST)


def place():
    ctx = lax.axis_index("ctx")
    head = lax.axis_index("head")
    core = ctx % 2
    y = (ctx // 2) % 2
    x = ctx // 4
    return ctx, head, core, y, x


def ctx_of(x, y, core):
    return (x * 2 + y) * 2 + core


def chip_of(x, y):
    return x * 2 + y


class Copies:
    def __init__(self, send, recv, head):
        self.send, self.recv, self.head = send, recv, head
        self.started = []
        self.count = 0

    def start(self, src, dst, ctx, head=None):
        copy = pltpu.make_async_remote_copy(
            src_ref=src,
            dst_ref=dst,
            send_sem=self.send.at[self.count],
            recv_sem=self.recv.at[self.count],
            device_id={"ctx": ctx, "head": self.head if head is None else head},
            device_id_type=MESH,
        )
        self.count += 1
        copy.start()
        self.started.append(copy)
        return copy


class Locals:
    def __init__(self, sems):
        self.sems = sems
        self.count = 0

    def start(self, src, dst):
        copy = pltpu.make_async_copy(src, dst, self.sems.at[self.count])
        self.count += 1
        copy.start()
        return copy


def enter(ctx, head, others):
    barrier = pltpu.get_barrier_semaphore()
    for other in others:
        pl.semaphore_signal(barrier, inc=1, device_id={"ctx": other, "head": head}, device_id_type=MESH)
    for step in range(1, 8):
        pl.semaphore_signal(
            barrier, inc=1, device_id={"ctx": ctx, "head": (head + step) % 8}, device_id_type=MESH
        )
    pl.semaphore_wait(barrier, 7 + len(others))


def gather_kernel(
    cq_h, ck_h, nq_h, nk_h, qg_h, kg_h, cv, nv, gc, gn, owned,
    kall, vall, qq, gg, kn, vn, own_s, grads_t, inv_out, ids_out,
    owned_s, raws, qg, kg, k_packet, normed, sums, send, recv, wide_send, wide_recv, lsem,
):
    ctx, head, core, y, x = place()
    right, left = (x + 1) % 4, (x + 3) % 4
    opposite = (x + 2) % 4
    mine = pl.ds(pl.multiple_of(core * HD, HD), HD)
    theirs = pl.ds(pl.multiple_of((1 - core) * HD, HD), HD)
    partner = ctx_of(x, y, 1 - core)
    local = Locals(lsem)
    owned_load = local.start(owned, owned_s)
    loads = [local.start(ref, raws.at[i]) for i, ref in enumerate((cq_h, ck_h, nq_h, nk_h))]
    loads += [local.start(qg_h, qg), local.start(kg_h, kg)]
    remote = Copies(send, recv, head)
    chips = ((x, 1 - y), (right, y), (left, y))
    enter(ctx, head, [partner] + [ctx_of(*chip, c) for chip in chips for c in range(2)])
    wide = []

    def first_hop(base, columns_of, buf):
        for number, chip in enumerate(chips):
            for target in range(2):
                copy = pltpu.make_async_remote_copy(
                    src_ref=columns_of(target),
                    dst_ref=buf.at[ctx],
                    send_sem=wide_send.at[base + number, target],
                    recv_sem=wide_recv.at[base + number, core],
                    device_id={"ctx": ctx_of(*chip, target), "head": head},
                    device_id_type=MESH,
                )
                copy.start()
                wide.append(copy)

    def arrived(base, number, buf, source):
        chip = ((x, 1 - y), (left, y), (right, y))[number]
        pltpu.make_async_remote_copy(
            src_ref=buf.at[ctx],
            dst_ref=buf.at[ctx_of(*chip, source)],
            send_sem=wide_send.at[base + number, source],
            recv_sem=wide_recv.at[base + number, source],
            device_id={"ctx": partner, "head": head},
            device_id_type=MESH,
        ).wait_recv()

    first_hop(0, lambda target: cv.at[:, target * HD : target * HD + HD], vall)
    v_swap = remote.start(cv.at[:, theirs], vall.at[ctx], partner)
    v_own = local.start(cv.at[:, mine], vall.at[ctx])

    for copy in loads:
        copy.wait()
    row = lax.broadcasted_iota(jnp.int32, (8, 512), 0)
    total = jnp.zeros((8, 512), F32)
    for index in range(4):
        raw = raws[index].astype(F32)
        total = jnp.where(row == index, row_sums(raw * raw), total)
    sums[0] = total
    exchange = [
        remote.start(sums.at[0], sums.at[step], ctx, (head + step) % 8) for step in range(1, 8)
    ]
    owned_load.wait()
    lane = lax.broadcasted_iota(jnp.int32, (16, 2 * HD), 1)
    k_packet[512:, :] = jnp.where(lane % HD == 0, owned_s[0], owned_s[1]).astype(F32).astype(BF16)

    pair = pl.ds(core * 2, 2)
    late, late_own = [], []

    def swap(src, dst):
        late.append(remote.start(src.at[:, :, theirs], dst, partner))
        late_own.append(local.start(src.at[:, :, mine], dst))

    swap(gc, gg.at[pair, 0])
    swap(gn, gg.at[pair, 1])
    swap(nv, vn.at[pair])

    for copy in exchange:
        copy.wait_recv()
    total = sums[0]
    for step in range(1, 8):
        total = total + sums[step]
    inverse = lax.rsqrt(total / FEAT + EPSILON)
    inv_out[...] = inverse
    columns = jnp.transpose(inverse)

    def normalized(index, gain):
        values = raws[index].astype(F32) * columns[:, index : index + 1] * gain[...]
        return values.astype(BF16)

    k_packet[:512, :] = normalized(1, kg)
    first_hop(3, lambda target: k_packet.at[:, target * HD : target * HD + HD], kall)
    k_swap = remote.start(k_packet.at[:, theirs], kall.at[ctx], partner)
    k_own = local.start(k_packet.at[:, mine], kall.at[ctx])
    for index, raw, gain, dst in (
        (0, 0, qg, qq.at[pair, 0]),
        (1, 2, qg, qq.at[pair, 1]),
        (2, 3, kg, kn.at[pair]),
    ):
        normed[index] = normalized(raw, gain).reshape(2, BLK, 2 * HD)
        swap(normed.at[index], dst)

    def slot(buf, sx, sy):
        return buf.at[pl.ds(2 * chip_of(sx, sy), 2)]

    def part(buf, sx, sy, half):
        return buf.at[2 * chip_of(sx, sy) + half]

    def rows_of(sx, sy, half, first, count):
        return vall.at[2 * chip_of(sx, sy) + half, pl.ds(first, count)]

    def spread(view, px, py):
        return remote.start(view, view, ctx_of(px, py, core))

    v_half, v_y, k_half = [], [], []
    sides = ((1, left, right, 0), (2, right, left, 1))
    for number, near, far, half in sides:
        arrived(0, number, vall, half)
        v_half.append(spread(part(vall, near, y, half), far, y))
    arrived(3, 0, kall, 0)
    arrived(3, 0, kall, 1)
    k_right = spread(slot(kall, x, 1 - y), right, y)
    k_left = spread(slot(kall, x, 1 - y), left, y)
    arrived(0, 1, vall, 1)
    v_y.append(spread(slot(vall, left, y), x, 1 - y))

    v_own.wait()
    k_own.wait()
    v_swap.wait_recv()
    k_swap.wait_recv()
    for copy in late_own:
        copy.wait()
    for copy in late:
        copy.wait_recv()

    def own_block(index):
        side, rows = index // 2, slice(index % 2 * BLK, index % 2 * BLK + BLK)
        packet = 2 * chip_of(x, y) + side
        own_s[index, :, :BLK] = dot(kall[packet, rows, :], qq[index, 0], LAST)
        own_s[index, :, BLK:] = dot(kn[index], qq[index, 1], LAST)
        for kind in range(2):
            columns = slice(kind * BLK, kind * BLK + BLK)
            grads_t[index, :, columns] = jnp.transpose(gg[index, kind].astype(F32))

    own_block(0)
    for number, near, far, half in sides:
        arrived(3, number, kall, half)
        k_half.append(spread(part(kall, near, y, half), far, y))
        arrived(3, number, kall, 1 - half)
    own_block(1)
    arrived(0, 2, vall, 0)
    v_y.append(spread(slot(vall, right, y), x, 1 - y))
    own_block(2)
    v_half[0].wait_recv()
    v_half[1].wait_recv()
    v_y[0].wait_recv()
    v_far = [spread(rows_of(left, 1 - y, 0, 0, SHIFT), right, y)]
    for half in range(2):
        v_y.append(spread(rows_of(opposite, y, half, SHIFT, 512 - SHIFT), x, 1 - y))
    k_right.wait_recv()
    k_half.append(spread(part(kall, left, 1 - y, 0), right, y))
    k_left.wait_recv()
    k_half.append(spread(part(kall, right, 1 - y, 1), left, y))
    own_block(3)
    v_y[1].wait_recv()
    v_far.append(spread(rows_of(right, 1 - y, 1, 0, SHIFT), left, y))
    arrived(0, 0, vall, 0)
    arrived(0, 0, vall, 1)
    for copy in v_y[2:] + v_far + k_half:
        copy.wait_recv()
    names = jnp.max(kall[:, 512:, :].astype(F32), axis=1)
    ids_out[...] = names.astype(jnp.int32)
    for copy in remote.started + wide:
        copy.wait_send()


def gather_call(cq, ck, nq, nk, qg, kg, cv, nv, gc, gn, owned):
    return pl.pallas_call(
        gather_kernel,
        name="gather_keys",
        out_shape=(
            jax.ShapeDtypeStruct((16, PACKET, HD), BF16),
            jax.ShapeDtypeStruct((16, 512, HD), BF16),
            jax.ShapeDtypeStruct((4, 2, BLK, HD), BF16),
            jax.ShapeDtypeStruct((4, 2, BLK, HD), BF16),
            jax.ShapeDtypeStruct((4, BLK, HD), BF16),
            jax.ShapeDtypeStruct((4, BLK, HD), BF16),
            jax.ShapeDtypeStruct((4, BLK, 2 * BLK), F32),
            jax.ShapeDtypeStruct((4, HD, 2 * BLK), F32),
            jax.ShapeDtypeStruct((8, 512), F32),
            jax.ShapeDtypeStruct((16, HD), jnp.int32),
        ),
        in_specs=[HBM] * 11,
        out_specs=(VMEM,) * 10,
        scratch_shapes=[
            pltpu.SMEM((2,), jnp.int32),
            pltpu.VMEM((4, 512, 256), BF16),
            pltpu.VMEM((1, 256), F32),
            pltpu.VMEM((1, 256), F32),
            pltpu.VMEM((PACKET, 256), BF16),
            pltpu.VMEM((3, 2, BLK, 2 * HD), BF16),
            pltpu.VMEM((8, 8, 512), F32),
            pltpu.SemaphoreType.DMA((32,)),
            pltpu.SemaphoreType.DMA((32,)),
            pltpu.SemaphoreType.DMA((6, 2)),
            pltpu.SemaphoreType.DMA((6, 2)),
            pltpu.SemaphoreType.DMA((16,)),
        ],
        compiler_params=pltpu.CompilerParams(
            collective_id=0, has_side_effects=True, vmem_limit_bytes=20 * 2**20
        ),
    )(cq, ck, nq, nk, qg, kg, cv, nv, gc, gn, owned)


def attention_kernel(
    ids, docs, kall, vall, qq, gg, kn, vn, own_s, grads_t,
    out_t, dq_t, dk_noisy, dv_noisy, dk_acc, dv_acc, keys_out, ds_out,
    where_is, first_of, pair_query, pair_key, pair_bias, pair_slot, present,
    weights, zeros, sems, pair_peaks, own_weights, scaled_grads, peaks, sums, deltas,
):
    chip = lax.axis_index("ctx") // 2
    scale = 1.0 / math.sqrt(HD)
    scale2 = scale * math.log2(math.e)

    @pl.loop(0, 16)
    def _(packet):
        where_is[ids[packet, 0]] = packet * 2
        where_is[ids[packet, 1]] = packet * 2 + 1

    first_of[0] = 0

    @pl.loop(1, 32)
    def _(block):
        first_of[block] = jnp.where(docs[block] == docs[block - 1], first_of[block - 1], block)

    @pl.loop(0, 32)
    def _(block):
        dk_acc[block] = jnp.zeros((BLK, HD), F32)
        dv_acc[block] = jnp.zeros((BLK, HD), F32)

    def key_rows(buf, stored):
        start = pl.multiple_of((stored % 2) * BLK, BLK)
        return buf[stored // 2, pl.ds(start, BLK), :]

    def key_pair(buf, pair):
        return jnp.concatenate(
            [key_rows(buf, pair_key[2 * pair]), key_rows(buf, pair_key[2 * pair + 1])], axis=0
        )

    def both(ref, index):
        return ref[index].reshape(2 * BLK, HD)

    def tops(values):
        return jnp.max(values.reshape(-1, 8, values.shape[1]), axis=0)

    def totals(values):
        return jnp.sum(values.reshape(-1, 8, values.shape[1]), axis=0)

    @pl.loop(0, 32)
    def _(slot):
        present[slot] = 0

    zeros[...] = jnp.zeros((2 * BLK, 2 * BLK), BF16)
    count = 0
    for index in range(4):
        block = ids[chip * 2 + index // 2, index % 2]
        begin = first_of[block]

        def enlist(pair, count, index=index, block=block, begin=begin):
            key = begin + 2 * pair
            first = where_is[key]
            second = where_is[jnp.minimum(key + 1, block - 1)]
            slot = index * 8 + pair
            pair_query[count] = index
            pair_key[2 * count] = first
            pair_key[2 * count + 1] = second
            pair_bias[count] = jnp.where(key + 1 < block, 0, 1)
            pair_slot[count] = slot
            present[slot] = 1
            return count + 1

        count = lax.fori_loop(0, (block - begin + 1) // 2, enlist, count)

    @pl.loop(0, 32)
    def _(slot):
        @pl.when(present[slot] == 0)
        def _():
            pltpu.make_async_copy(zeros, ds_out.at[slot], sems.at[slot]).start()
            keys_out[slot] = jnp.zeros((2 * BLK, HD), BF16)

    def over_pairs(body):
        groups = count // GROUP

        @pl.loop(0, groups)
        def _(group):
            body([group * GROUP + i for i in range(GROUP)])

        @pl.loop(groups * GROUP, count)
        def _(pair):
            body([pair])

    def spread_rows(row):
        return jnp.broadcast_to(row, (8, 2 * BLK))

    for index in range(4):
        own = own_s[index]
        peak = jnp.max(own, axis=0, keepdims=True) * scale2
        peaks[index] = spread_rows(peak)
        own = jnp.exp2(own * scale2 - peak)
        sums[index] = totals(own)
        own_low = own.astype(BF16)
        own_weights[index] = own_low
        out_t[index, :, :BLK] = dot(key_rows(vall, chip * 4 + index), own_low[:, :BLK], FIRST)
        out_t[index, :, BLK:] = dot(vn[index], own_low[:, BLK:], FIRST)
        pair_peaks[32 + index] = peaks[index]

    def forward_pairs(pairs):
        queries = [pair_query[pair] for pair in pairs]
        scores = [
            dot(key_pair(kall, pair), both(qq, query), LAST) for pair, query in zip(pairs, queries)
        ]
        tops_of = [jnp.max(tops(score), axis=0, keepdims=True) * scale2 for score in scores]
        results = []
        for pair, query, score, top in zip(pairs, queries, scores, tops_of):
            before = peaks[query]
            now = jnp.maximum(before, spread_rows(top))
            peaks[query] = now
            pair_peaks[pair] = now
            peak = now[:1]
            hidden = peak + jnp.where(pair_bias[pair] == 1, jnp.inf, 0.0)
            upper = jnp.exp2(score[:BLK] * scale2 - peak)
            lower = jnp.exp2(score[BLK:] * scale2 - hidden)
            low = jnp.concatenate([upper.astype(BF16), lower.astype(BF16)], axis=0)
            weights[pair] = low
            results.append(
                (
                    jnp.exp2(before - now),
                    dot(key_pair(vall, pair), low, FIRST),
                    totals(upper) + totals(lower),
                )
            )
        for query, (decay, out, part) in zip(queries, results):
            sums[query] = sums[query] * decay + part
            out_t[query] = out_t[query] * decay[:1] + out

    over_pairs(forward_pairs)

    for index in range(4):
        stored_own = chip * 4 + index
        own_decay = jnp.exp2(pair_peaks[32 + index] - peaks[index])[:1]
        inverse_sum = 1.0 / jnp.sum(sums[index], axis=0, keepdims=True)
        out = out_t[index] * inverse_sum
        out_t[index] = out
        grad_rows = (grads_t[index] * inverse_sum).astype(BF16).astype(F32)
        delta = jnp.sum(out * grad_rows, axis=0, keepdims=True)
        deltas[index] = spread_rows(delta)
        grads = jnp.transpose(grad_rows).astype(BF16)
        scaled_grads[index] = grads
        own = own_weights[index].astype(F32) * own_decay
        own_low = own.astype(BF16)
        own_dp = jnp.concatenate(
            [
                dot(key_rows(vall, stored_own), grads[:BLK], LAST),
                dot(vn[index], grads[BLK:], LAST),
            ],
            axis=1,
        )
        own_ds = (own * (own_dp - delta)).astype(BF16)
        dv_acc[stored_own] += dot(own_low[:, :BLK], grads[:BLK], PLAIN)
        dk_acc[stored_own] += dot(own_ds[:, :BLK], qq[index, 0], PLAIN)
        dv_noisy[index] = dot(own_low[:, BLK:], grads[BLK:], PLAIN)
        dk_noisy[index] = dot(own_ds[:, BLK:], qq[index, 1], PLAIN) * scale
        dq_t[index, :, :BLK] = dot(key_rows(kall, stored_own), own_ds[:, :BLK], FIRST)
        dq_t[index, :, BLK:] = dot(kn[index], own_ds[:, BLK:], FIRST)

    def grad_pairs(pairs):
        queries = [pair_query[pair] for pair in pairs]
        results = []
        for pair, query in zip(pairs, queries):
            decay = jnp.exp2(pair_peaks[pair] - peaks[query])[:1]
            prob = weights[pair].astype(F32) * decay
            dp = dot(key_pair(vall, pair), scaled_grads[query], LAST)
            ds = (prob * (dp - deltas[query, :1])).astype(BF16)
            results.append(
                (ds, dot(prob.astype(BF16), scaled_grads[query], PLAIN), dot(ds, both(qq, query), PLAIN))
            )
        for pair, (ds, dv, dk) in zip(pairs, results):
            weights[pair] = ds
            slot = pair_slot[pair]
            keys_out[slot] = key_pair(kall, pair)
            pltpu.make_async_copy(weights.at[pair], ds_out.at[slot], sems.at[slot]).start()
            for place in range(2):
                rows = slice(place * BLK, place * BLK + BLK)
                dv_acc[pair_key[2 * pair + place]] += dv[rows]
                dk_acc[pair_key[2 * pair + place]] += dk[rows]

    over_pairs(grad_pairs)

    @pl.loop(0, 32)
    def _(slot):
        pltpu.make_async_copy(zeros, ds_out.at[slot], sems.at[slot]).wait()


def attention_call(ids, docs, *parts):
    return pl.pallas_call(
        attention_kernel,
        name="attention",
        out_shape=(
            jax.ShapeDtypeStruct((4, HD, 2 * BLK), F32),
            jax.ShapeDtypeStruct((4, HD, 2 * BLK), F32),
            jax.ShapeDtypeStruct((4, BLK, HD), F32),
            jax.ShapeDtypeStruct((4, BLK, HD), F32),
            jax.ShapeDtypeStruct((32, BLK, HD), F32),
            jax.ShapeDtypeStruct((32, BLK, HD), F32),
            jax.ShapeDtypeStruct((32, 2 * BLK, HD), BF16),
            jax.ShapeDtypeStruct((32, 2 * BLK, 2 * BLK), BF16),
        ),
        in_specs=[SMEM, SMEM] + [VMEM] * 8,
        out_specs=(VMEM,) * 7 + (HBM,),
        scratch_shapes=[
            pltpu.SMEM((32,), jnp.int32),
            pltpu.SMEM((32,), jnp.int32),
            pltpu.SMEM((32,), jnp.int32),
            pltpu.SMEM((64,), jnp.int32),
            pltpu.SMEM((32,), jnp.int32),
            pltpu.SMEM((32,), jnp.int32),
            pltpu.SMEM((32,), jnp.int32),
            pltpu.VMEM((32, 2 * BLK, 2 * BLK), BF16),
            pltpu.VMEM((2 * BLK, 2 * BLK), BF16),
            pltpu.SemaphoreType.DMA((32,)),
            pltpu.VMEM((36, 8, 2 * BLK), F32),
            pltpu.VMEM((4, BLK, 2 * BLK), BF16),
            pltpu.VMEM((4, 2 * BLK, HD), BF16),
            pltpu.VMEM((4, 8, 2 * BLK), F32),
            pltpu.VMEM((4, 8, 2 * BLK), F32),
            pltpu.VMEM((4, 8, 2 * BLK), F32),
        ],
        compiler_params=pltpu.CompilerParams(vmem_limit_bytes=30 * 2**20),
    )(ids, docs, *parts)


def scatter_kernel(
    cq_h, ck_h, nq_h, nk_h, qg_h, kg_h, inv, out_t, dq_t, dk_noisy, dv_noisy, dk, dv,
    pair_keys, ds_h,
    back, fin, inner_out,
    raws, qg, kg, stage, k_out, v_out, x_out, vy, vq, vh, vx, kh, kx, ky, away, sums, dq_acc, ds,
    send, recv, lsem,
):
    ctx, head, core, y, x = place()
    right, left = (x + 1) % 4, (x + 3) % 4
    partner = ctx_of(x, y, 1 - core)
    to_right, to_left = ctx_of(right, y, core), ctx_of(left, y, core)
    to_y = ctx_of(x, 1 - y, core)
    score_scale = 1.0 / math.sqrt(HD)
    own_columns = pl.ds(pl.multiple_of(core * HD, HD), HD)
    local = Locals(lsem)
    loads = [local.start(ref, raws.at[i]) for i, ref in enumerate((cq_h, ck_h, nq_h, nk_h))]
    loads += [local.start(qg_h, qg), local.start(kg_h, kg)]
    cq, ck, nq, nk = [raws.at[i] for i in range(4)]
    ds_loads = [local.start(ds_h.at[pl.ds(8 * i, 8)], ds.at[i]) for i in range(2)]
    remote = Copies(send, recv, head)

    def mine(ref, step, row, half):
        chip = chip_of((x + step) % 4, y if row == 0 else 1 - y)
        return ref[pl.ds(chip * 4 + half * 2, 2)].reshape(512, HD)

    def pack_v(step):
        for half in range(2):
            v_out[step, half] = mine(dv, step, 1, half).astype(BF16)

    def pack_k(row, step, half, *others):
        value = mine(dk, step, row, half) * score_scale
        for other in others:
            value = value + other[...].astype(F32)
        k_out[row, step, half] = value.astype(BF16)

    pack_v(2)
    pack_k(1, 2, 0)
    pack_k(1, 2, 1)
    enter(ctx, head, [partner, to_right, to_left, to_y])
    first, rest = pl.ds(0, SHIFT), pl.ds(SHIFT, 512 - SHIFT)
    v_far = [
        remote.start(v_out.at[2, 0, first], vq.at[0], to_left),
        remote.start(v_out.at[2, 1, first], vq.at[1], to_right),
    ]
    v_opposite = [
        remote.start(v_out.at[2, half, rest], vy.at[2, half, rest], to_y) for half in range(2)
    ]
    k_half = {}

    def start_half(row):
        k_half[row, 0] = remote.start(k_out.at[row, 2, 0], kh.at[row, 0], to_left)
        k_half[row, 1] = remote.start(k_out.at[row, 2, 1], kh.at[row, 1], to_right)

    start_half(1)
    pack_k(0, 2, 0)
    pack_k(0, 2, 1)
    start_half(0)
    v_y = {}

    def send_v(step, half):
        pack_v(step)
        if half is not None:
            v_far[half].wait_recv()
            v_out[step, half, :SHIFT] = (
                mine(dv, step, 1, half)[:SHIFT] + vq[half].astype(F32)
            ).astype(BF16)
        v_y[step] = remote.start(v_out.at[step], vy.at[step], to_y)

    send_v(3, 0)
    for row in (1, 0):
        pack_k(row, 3, 1)
        pack_k(row, 1, 0)

    def landing(i):
        return back.at[i, :, own_columns]

    swap = {}
    def turn(ref, first, factor):
        for part in range(2):
            rows = slice(part * BLK, part * BLK + BLK)
            for c, own in ((core, True), (1 - core, False)):
                values = jnp.transpose(ref[2 * c + part]) * factor
                for kind in range(2):
                    if own:
                        back[first + kind, rows, own_columns] = values[kind * BLK : kind * BLK + BLK]
                    else:
                        stage[first + kind, rows, :] = values[kind * BLK : kind * BLK + BLK]
        for i in (first, first + 1):
            swap[i] = remote.start(stage.at[i], landing(i), partner)

    def turn_noisy(ref, i):
        for part in range(2):
            rows = slice(part * BLK, part * BLK + BLK)
            back[i, rows, own_columns] = ref[2 * core + part]
            stage[i, rows, :] = ref[2 * (1 - core) + part]
        swap[i] = remote.start(stage.at[i], landing(i), partner)

    turn_noisy(dk_noisy, 4)

    k_x = {}

    def k_forward(row):
        k_half[row, 0].wait_recv()
        pack_k(row, 3, 0, kh.at[row, 0])
        k_x[row, 0] = remote.start(k_out.at[row, 3], kx.at[row, 0], to_left)
        k_half[row, 1].wait_recv()
        pack_k(row, 1, 1, kh.at[row, 1])
        k_x[row, 1] = remote.start(k_out.at[row, 1], kx.at[row, 1], to_right)

    k_forward(1)

    def pack_x(step, half, *others):
        value = mine(dv, step, 0, half)
        for other in others:
            value = value + other[...].astype(F32)
        x_out[step, half] = value.astype(BF16)

    v_half = []
    for half, target in ((0, to_left), (1, to_right)):
        v_opposite[half].wait_recv()
        pack_x(2, half)
        x_out[2, half, SHIFT:] = (
            mine(dv, 2, 0, half)[SHIFT:] + vy[2, half, SHIFT:].astype(F32)
        ).astype(BF16)
        v_half.append(remote.start(x_out.at[2, half], vh.at[half], target))
    send_v(1, 1)
    k_forward(0)
    turn(out_t, 0, 1.0)
    turn_noisy(dv_noisy, 5)

    def add_queries(block):
        dq_acc[block] = dq_t[block]
        ds_loads[block].wait()

        @pl.loop(0, 4)
        def _(two):
            keys = pair_keys[pl.ds(block * 8 + two * 2, 2)].reshape(4 * BLK, HD)
            values = ds[block % 2, pl.ds(two * 2, 2)].reshape(4 * BLK, 2 * BLK)
            dq_acc[block] += dot(keys, values, FIRST)

        if block < 2:
            later = block + 2
            ds_loads.append(local.start(ds_h.at[pl.ds(8 * later, 8)], ds.at[block]))

    add_queries(0)
    pack_v(0)
    k_x[1, 0].wait_recv()
    k_x[1, 1].wait_recv()
    for half in range(2):
        pack_k(1, 0, half, kx.at[1, 0, half], kx.at[1, 1, half])
    k_y = remote.start(k_out.at[1, 0], ky, to_y)
    send_v(0, None)
    add_queries(1)

    v_y[3].wait_recv()
    v_half[0].wait_recv()
    pack_x(3, 0, vy.at[3, 0], vh.at[0])
    pack_x(3, 1, vy.at[3, 1])
    v_x = [remote.start(x_out.at[3], vx.at[0], to_left)]
    add_queries(2)
    v_y[1].wait_recv()
    v_half[1].wait_recv()
    pack_x(1, 0, vy.at[1, 0])
    pack_x(1, 1, vy.at[1, 1], vh.at[1])
    v_x.append(remote.start(x_out.at[1], vx.at[1], to_right))
    add_queries(3)
    turn(dq_acc, 2, score_scale)

    row = lax.broadcasted_iota(jnp.int32, (8, 512), 0)

    def inner(raw, gain, values):
        return row_sums(raw[...].astype(F32) * (gain[...] * values))

    for copy in loads:
        copy.wait()
    for i in (2, 3, 4):
        swap[i].wait_recv()
    total = jnp.zeros((8, 512), F32)
    normal = ((0, cq, qg, 2), (2, nq, qg, 3), (3, nk, kg, 4))
    for index, raw, gain, i in normal:
        total = jnp.where(row == index, inner(raw, gain, back[i]), total)
    sums[0] = total
    exchange = [
        remote.start(sums.at[0], sums.at[step], ctx, (head + step) % 8) for step in range(1, 8)
    ]

    def finish(index, ref, factor, terms):
        values = []
        for half in range(2):
            value = mine(ref, 0, 0, half) * factor
            for term in terms:
                value = value + term[half].astype(F32)
            values.append(value)
        first_core = core == 0
        fin[index, :, own_columns] = jnp.where(first_core, values[0], values[1])
        away[index] = jnp.where(first_core, values[1], values[0])
        return remote.start(away.at[index], fin.at[index, :, own_columns], partner)

    k_x[0, 0].wait_recv()
    k_x[0, 1].wait_recv()
    k_y.wait_recv()
    k_fin = finish(0, dk, score_scale, (kx.at[0, 0], kx.at[0, 1], ky))
    k_fin.wait_recv()
    sums[8] = inner(ck, kg, fin[0])
    k_exchange = [
        remote.start(sums.at[8], sums.at[8 + step], ctx, (head + step) % 8) for step in range(1, 8)
    ]
    for copy in exchange:
        copy.wait_recv()
    total = sums[0]
    for step in range(1, 8):
        total = total + sums[step]
    inverses = jnp.transpose(inv[...])
    means = jnp.transpose(total) / FEAT
    for index, raw, gain, i in normal:
        inverse = inverses[:, index : index + 1]
        factor = inverse * inverse * inverse * means[:, index : index + 1]
        back[i] = inverse * (gain[...] * back[i]) - raw[...].astype(F32) * factor

    v_y[0].wait_recv()
    v_x[0].wait_recv()
    v_x[1].wait_recv()
    v_fin = finish(1, dv, 1.0, (vy.at[0], vx.at[0], vx.at[1]))

    for copy in k_exchange:
        copy.wait_recv()
    total = sums[8]
    for step in range(1, 8):
        total = total + sums[8 + step]
    inner_out[...] = total
    v_fin.wait_recv()
    for i in (0, 1, 5):
        swap[i].wait_recv()
    for copy in remote.started:
        copy.wait_send()


def scatter_call(*operands):
    return pl.pallas_call(
        scatter_kernel,
        name="scatter_grads",
        out_shape=(
            jax.ShapeDtypeStruct((6, 512, 256), F32),
            jax.ShapeDtypeStruct((2, 512, 256), F32),
            jax.ShapeDtypeStruct((8, 512), F32),
        ),
        in_specs=[HBM] * 6 + [VMEM] * 8 + [HBM],
        out_specs=(VMEM, VMEM, VMEM),
        scratch_shapes=[
            pltpu.VMEM((4, 512, 256), BF16),
            pltpu.VMEM((1, 256), F32),
            pltpu.VMEM((1, 256), F32),
            pltpu.VMEM((6, 512, HD), F32),
            pltpu.VMEM((2, 4, 2, 512, HD), BF16),
            pltpu.VMEM((4, 2, 512, HD), BF16),
            pltpu.VMEM((4, 2, 512, HD), BF16),
            pltpu.VMEM((4, 2, 512, HD), BF16),
            pltpu.VMEM((2, SHIFT, HD), BF16),
            pltpu.VMEM((2, 512, HD), BF16),
            pltpu.VMEM((2, 2, 512, HD), BF16),
            pltpu.VMEM((2, 2, 512, HD), BF16),
            pltpu.VMEM((2, 2, 2, 512, HD), BF16),
            pltpu.VMEM((2, 512, HD), BF16),
            pltpu.VMEM((2, 512, HD), F32),
            pltpu.VMEM((16, 8, 512), F32),
            pltpu.VMEM((4, HD, 2 * BLK), F32),
            pltpu.VMEM((2, 8, 2 * BLK, 2 * BLK), BF16),
            pltpu.SemaphoreType.DMA((48,)),
            pltpu.SemaphoreType.DMA((48,)),
            pltpu.SemaphoreType.DMA((12,)),
        ],
        compiler_params=pltpu.CompilerParams(
            collective_id=1, has_side_effects=True, vmem_limit_bytes=30 * 2**20
        ),
    )(*operands)


def finish_kernel(
    ck, kg, inv, inner, back, fin,
    out_clean, out_noisy, dq_clean, dk_clean, dv_clean, dq_noisy, dk_noisy, dv_noisy,
    dk, sems,
):
    local = Locals(sems)
    copies = [
        local.start(source, target)
        for source, target in (
            (back.at[0], out_clean),
            (back.at[1], out_noisy),
            (back.at[2], dq_clean),
            (back.at[3], dq_noisy),
            (back.at[4], dk_noisy),
            (back.at[5], dv_noisy),
            (fin.at[1], dv_clean),
        )
    ]
    inverse = jnp.transpose(inv[...])[:, 1:2]
    mean = jnp.transpose(inner[...])[:, :1] / FEAT
    factor = inverse * inverse * inverse * mean
    dk[...] = inverse * (kg[...] * fin[0]) - ck[...].astype(F32) * factor
    copies.append(local.start(dk, dk_clean))
    for copy in copies:
        copy.wait()


def finish_call(*operands):
    return pl.pallas_call(
        finish_kernel,
        name="finish",
        out_shape=tuple(jax.ShapeDtypeStruct((512, 256), F32) for _ in range(8)),
        in_specs=[VMEM] * 6,
        out_specs=(HBM,) * 8,
        scratch_shapes=[pltpu.VMEM((512, 256), F32), pltpu.SemaphoreType.DMA((8,))],
        compiler_params=pltpu.CompilerParams(vmem_limit_bytes=16 * 2**20),
    )(*operands)


def local(
    clean_q, clean_k, clean_v, noisy_q, noisy_k, noisy_v,
    q_gain, k_gain, grad_clean, grad_noisy, owned_blocks, block_doc,
):
    qg = q_gain.reshape(1, 256)
    kg = k_gain.reshape(1, 256)
    blocks = [a.reshape(2, BLK, 2 * HD) for a in (noisy_v, grad_clean, grad_noisy)]
    *pinned, docs = [
        pltpu.with_memory_space_constraint(a, pltpu.HBM)
        for a in (
            clean_q, clean_k, noisy_q, noisy_k, qg, kg, clean_v, *blocks, owned_blocks, block_doc,
        )
    ]
    *parts, inv, ids = gather_call(*pinned)
    grads = attention_call(ids, docs, *parts)
    *grads, ds = grads
    ds = pltpu.with_memory_space_constraint(ds, pltpu.HBM)
    back, fin, inner = scatter_call(*pinned[:6], inv, *grads, ds)
    return finish_call(clean_k, kg, inv, inner, back, fin)


def solution(mesh):
    placed = (P("ctx", "head"),) * 6 + (P("head"),) * 2 + (P("ctx", "head"),) * 2 + (P("ctx"), P())
    return jax.shard_map(
        local,
        mesh=mesh,
        in_specs=placed,
        out_specs=(P("ctx", "head"),) * 8,
        check_vma=False,
    )
```

```python
import math

import jax
import jax.numpy as jnp
from jax import lax
from jax.experimental import pallas as pl
from jax.experimental.pallas import tpu as pltpu
from jax.sharding import PartitionSpec as P

HD = 128
BLK = 256
FEAT = 2048
EPSILON = 1e-06
NEGATIVE = -1e30
MESH = pl.DeviceIdType.MESH
F32 = jnp.float32
BF16 = jnp.bfloat16
VMEM = pl.BlockSpec(memory_space=pltpu.VMEM)
SMEM = pl.BlockSpec(memory_space=pltpu.SMEM)
ANY = pl.BlockSpec(memory_space=pl.ANY)
HBM = pl.BlockSpec(memory_space=pltpu.HBM)
LAST = (((1,), (1,)), ((), ()))
FIRST = (((0,), (0,)), ((), ()))
PLAIN = (((1,), (0,)), ((), ()))
PACKET = 528
SHIFT = 160
GROUP = 2


def dot(a, b, dims):
    return lax.dot_general(a, b, dims, preferred_element_type=F32)


def row_sums(products):
    high = products.astype(BF16)
    low = (products - high.astype(F32)).astype(BF16)
    ones = jnp.ones((8, products.shape[1]), BF16)
    return dot(ones, high, LAST) + dot(ones, low, LAST)


def place():
    ctx = lax.axis_index("ctx")
    head = lax.axis_index("head")
    core = ctx % 2
    y = (ctx // 2) % 2
    x = ctx // 4
    return ctx, head, core, y, x


def ctx_of(x, y, core):
    return (x * 2 + y) * 2 + core


def chip_of(x, y):
    return x * 2 + y


class Copies:
    def __init__(self, send, recv, head):
        self.send, self.recv, self.head = send, recv, head
        self.started = []
        self.count = 0

    def start(self, src, dst, ctx, head=None):
        copy = pltpu.make_async_remote_copy(
            src_ref=src,
            dst_ref=dst,
            send_sem=self.send.at[self.count],
            recv_sem=self.recv.at[self.count],
            device_id={"ctx": ctx, "head": self.head if head is None else head},
            device_id_type=MESH,
        )
        self.count += 1
        copy.start()
        self.started.append(copy)
        return copy


class Locals:
    def __init__(self, sems):
        self.sems = sems
        self.count = 0

    def start(self, src, dst):
        copy = pltpu.make_async_copy(src, dst, self.sems.at[self.count])
        self.count += 1
        copy.start()
        return copy


def enter(ctx, head, others):
    barrier = pltpu.get_barrier_semaphore()
    for other in others:
        pl.semaphore_signal(barrier, inc=1, device_id={"ctx": other, "head": head}, device_id_type=MESH)
    for step in range(1, 8):
        pl.semaphore_signal(
            barrier, inc=1, device_id={"ctx": ctx, "head": (head + step) % 8}, device_id_type=MESH
        )
    pl.semaphore_wait(barrier, 7 + len(others))


def gather_kernel(
    cq_h, ck_h, nq_h, nk_h, qg_h, kg_h, cv, nv, gc, gn, owned,
    kall, vall, qq, gg, kn, vn, own_s, grads_t, inv_out, ids_out,
    owned_s, raws, qg, kg, k_packet, normed, sums, send, recv, wide_send, wide_recv, lsem,
):
    ctx, head, core, y, x = place()
    right, left = (x + 1) % 4, (x + 3) % 4
    opposite = (x + 2) % 4
    mine = pl.ds(pl.multiple_of(core * HD, HD), HD)
    theirs = pl.ds(pl.multiple_of((1 - core) * HD, HD), HD)
    partner = ctx_of(x, y, 1 - core)
    local = Locals(lsem)
    owned_load = local.start(owned, owned_s)
    loads = [local.start(ref, raws.at[i]) for i, ref in enumerate((cq_h, ck_h, nq_h, nk_h))]
    loads += [local.start(qg_h, qg), local.start(kg_h, kg)]
    remote = Copies(send, recv, head)
    chips = ((x, 1 - y), (right, y), (left, y))
    enter(ctx, head, [partner] + [ctx_of(*chip, c) for chip in chips for c in range(2)])
    wide = []

    def first_hop(base, columns_of, buf):
        for number, chip in enumerate(chips):
            for target in range(2):
                copy = pltpu.make_async_remote_copy(
                    src_ref=columns_of(target),
                    dst_ref=buf.at[ctx],
                    send_sem=wide_send.at[base + number, target],
                    recv_sem=wide_recv.at[base + number, core],
                    device_id={"ctx": ctx_of(*chip, target), "head": head},
                    device_id_type=MESH,
                )
                copy.start()
                wide.append(copy)

    def arrived(base, number, buf, source):
        chip = ((x, 1 - y), (left, y), (right, y))[number]
        pltpu.make_async_remote_copy(
            src_ref=buf.at[ctx],
            dst_ref=buf.at[ctx_of(*chip, source)],
            send_sem=wide_send.at[base + number, source],
            recv_sem=wide_recv.at[base + number, source],
            device_id={"ctx": partner, "head": head},
            device_id_type=MESH,
        ).wait_recv()

    first_hop(0, lambda target: cv.at[:, target * HD : target * HD + HD], vall)
    v_swap = remote.start(cv.at[:, theirs], vall.at[ctx], partner)
    v_own = local.start(cv.at[:, mine], vall.at[ctx])

    for copy in loads:
        copy.wait()
    row = lax.broadcasted_iota(jnp.int32, (8, 512), 0)
    total = jnp.zeros((8, 512), F32)
    for index in range(4):
        raw = raws[index].astype(F32)
        total = jnp.where(row == index, row_sums(raw * raw), total)
    sums[0] = total
    exchange = [
        remote.start(sums.at[0], sums.at[step], ctx, (head + step) % 8) for step in range(1, 8)
    ]
    owned_load.wait()
    lane = lax.broadcasted_iota(jnp.int32, (16, 2 * HD), 1)
    k_packet[512:, :] = jnp.where(lane % HD == 0, owned_s[0], owned_s[1]).astype(F32).astype(BF16)

    pair = pl.ds(core * 2, 2)
    late, late_own = [], []

    def swap(src, dst):
        late.append(remote.start(src.at[:, :, theirs], dst, partner))
        late_own.append(local.start(src.at[:, :, mine], dst))

    swap(gc, gg.at[pair, 0])
    swap(gn, gg.at[pair, 1])
    swap(nv, vn.at[pair])

    for copy in exchange:
        copy.wait_recv()
    total = sums[0]
    for step in range(1, 8):
        total = total + sums[step]
    inverse = lax.rsqrt(total / FEAT + EPSILON)
    inv_out[...] = inverse
    columns = jnp.transpose(inverse)

    def normalized(index, gain):
        values = raws[index].astype(F32) * columns[:, index : index + 1] * gain[...]
        return values.astype(BF16)

    k_packet[:512, :] = normalized(1, kg)
    first_hop(3, lambda target: k_packet.at[:, target * HD : target * HD + HD], kall)
    k_swap = remote.start(k_packet.at[:, theirs], kall.at[ctx], partner)
    k_own = local.start(k_packet.at[:, mine], kall.at[ctx])
    for index, raw, gain, dst in (
        (0, 0, qg, qq.at[pair, 0]),
        (1, 2, qg, qq.at[pair, 1]),
        (2, 3, kg, kn.at[pair]),
    ):
        normed[index] = normalized(raw, gain).reshape(2, BLK, 2 * HD)
        swap(normed.at[index], dst)

    def slot(buf, sx, sy):
        return buf.at[pl.ds(2 * chip_of(sx, sy), 2)]

    def part(buf, sx, sy, half):
        return buf.at[2 * chip_of(sx, sy) + half]

    def rows_of(sx, sy, half, first, count):
        return vall.at[2 * chip_of(sx, sy) + half, pl.ds(first, count)]

    def spread(view, px, py):
        return remote.start(view, view, ctx_of(px, py, core))

    v_half, v_y, k_half = [], [], []
    sides = ((1, left, right, 0), (2, right, left, 1))
    for number, near, far, half in sides:
        arrived(0, number, vall, half)
        v_half.append(spread(part(vall, near, y, half), far, y))
    arrived(3, 0, kall, 0)
    arrived(3, 0, kall, 1)
    k_right = spread(slot(kall, x, 1 - y), right, y)
    k_left = spread(slot(kall, x, 1 - y), left, y)
    arrived(0, 1, vall, 1)
    v_y.append(spread(slot(vall, left, y), x, 1 - y))

    v_own.wait()
    k_own.wait()
    v_swap.wait_recv()
    k_swap.wait_recv()
    for copy in late_own:
        copy.wait()
    for copy in late:
        copy.wait_recv()

    def own_block(index):
        side, rows = index // 2, slice(index % 2 * BLK, index % 2 * BLK + BLK)
        packet = 2 * chip_of(x, y) + side
        own_s[index, :, :BLK] = dot(kall[packet, rows, :], qq[index, 0], LAST)
        own_s[index, :, BLK:] = dot(kn[index], qq[index, 1], LAST)
        for kind in range(2):
            columns = slice(kind * BLK, kind * BLK + BLK)
            grads_t[index, :, columns] = jnp.transpose(gg[index, kind].astype(F32))

    own_block(0)
    for number, near, far, half in sides:
        arrived(3, number, kall, half)
        k_half.append(spread(part(kall, near, y, half), far, y))
        arrived(3, number, kall, 1 - half)
    own_block(1)
    arrived(0, 2, vall, 0)
    v_y.append(spread(slot(vall, right, y), x, 1 - y))
    own_block(2)
    v_half[0].wait_recv()
    v_half[1].wait_recv()
    v_y[0].wait_recv()
    v_far = [spread(rows_of(left, 1 - y, 0, 0, SHIFT), right, y)]
    for half in range(2):
        v_y.append(spread(rows_of(opposite, y, half, SHIFT, 512 - SHIFT), x, 1 - y))
    k_right.wait_recv()
    k_half.append(spread(part(kall, left, 1 - y, 0), right, y))
    k_left.wait_recv()
    k_half.append(spread(part(kall, right, 1 - y, 1), left, y))
    own_block(3)
    v_y[1].wait_recv()
    v_far.append(spread(rows_of(right, 1 - y, 1, 0, SHIFT), left, y))
    arrived(0, 0, vall, 0)
    arrived(0, 0, vall, 1)
    for copy in v_y[2:] + v_far + k_half:
        copy.wait_recv()
    names = jnp.max(kall[:, 512:, :].astype(F32), axis=1)
    ids_out[...] = names.astype(jnp.int32)
    for copy in remote.started + wide:
        copy.wait_send()


def gather_call(cq, ck, nq, nk, qg, kg, cv, nv, gc, gn, owned):
    return pl.pallas_call(
        gather_kernel,
        name="gather_keys",
        out_shape=(
            jax.ShapeDtypeStruct((16, PACKET, HD), BF16),
            jax.ShapeDtypeStruct((16, 512, HD), BF16),
            jax.ShapeDtypeStruct((4, 2, BLK, HD), BF16),
            jax.ShapeDtypeStruct((4, 2, BLK, HD), BF16),
            jax.ShapeDtypeStruct((4, BLK, HD), BF16),
            jax.ShapeDtypeStruct((4, BLK, HD), BF16),
            jax.ShapeDtypeStruct((4, BLK, 2 * BLK), F32),
            jax.ShapeDtypeStruct((4, HD, 2 * BLK), F32),
            jax.ShapeDtypeStruct((8, 512), F32),
            jax.ShapeDtypeStruct((16, HD), jnp.int32),
        ),
        in_specs=[HBM] * 11,
        out_specs=(VMEM,) * 10,
        scratch_shapes=[
            pltpu.SMEM((2,), jnp.int32),
            pltpu.VMEM((4, 512, 256), BF16),
            pltpu.VMEM((1, 256), F32),
            pltpu.VMEM((1, 256), F32),
            pltpu.VMEM((PACKET, 256), BF16),
            pltpu.VMEM((3, 2, BLK, 2 * HD), BF16),
            pltpu.VMEM((8, 8, 512), F32),
            pltpu.SemaphoreType.DMA((32,)),
            pltpu.SemaphoreType.DMA((32,)),
            pltpu.SemaphoreType.DMA((6, 2)),
            pltpu.SemaphoreType.DMA((6, 2)),
            pltpu.SemaphoreType.DMA((16,)),
        ],
        compiler_params=pltpu.CompilerParams(
            collective_id=0, has_side_effects=True, vmem_limit_bytes=20 * 2**20
        ),
    )(cq, ck, nq, nk, qg, kg, cv, nv, gc, gn, owned)


def attention_kernel(
    ids, docs, kall, vall, qq, gg, kn, vn, own_s, grads_t,
    out_t, dq_t, dk_noisy, dv_noisy, dk_acc, dv_acc,
    where_is, first_of, pair_query, pair_key, pair_bias,
    weights, pair_peaks, own_weights, scaled_grads, peaks, sums, deltas,
):
    chip = lax.axis_index("ctx") // 2
    scale = 1.0 / math.sqrt(HD)
    scale2 = scale * math.log2(math.e)

    @pl.loop(0, 16)
    def _(packet):
        where_is[ids[packet, 0]] = packet * 2
        where_is[ids[packet, 1]] = packet * 2 + 1

    first_of[0] = 0

    @pl.loop(1, 32)
    def _(block):
        first_of[block] = jnp.where(docs[block] == docs[block - 1], first_of[block - 1], block)

    @pl.loop(0, 32)
    def _(block):
        dk_acc[block] = jnp.zeros((BLK, HD), F32)
        dv_acc[block] = jnp.zeros((BLK, HD), F32)

    def key_rows(buf, stored):
        start = pl.multiple_of((stored % 2) * BLK, BLK)
        return buf[stored // 2, pl.ds(start, BLK), :]

    def key_pair(buf, pair):
        return jnp.concatenate(
            [key_rows(buf, pair_key[2 * pair]), key_rows(buf, pair_key[2 * pair + 1])], axis=0
        )

    def both(ref, index):
        return ref[index].reshape(2 * BLK, HD)

    def tops(values):
        return jnp.max(values.reshape(-1, 8, values.shape[1]), axis=0)

    def totals(values):
        return jnp.sum(values.reshape(-1, 8, values.shape[1]), axis=0)

    count = 0
    for index in range(4):
        block = ids[chip * 2 + index // 2, index % 2]
        begin = first_of[block]

        def enlist(pair, count, index=index, block=block, begin=begin):
            key = begin + 2 * pair
            first = where_is[key]
            second = where_is[jnp.minimum(key + 1, block - 1)]
            pair_query[count] = index
            pair_key[2 * count] = first
            pair_key[2 * count + 1] = second
            pair_bias[count] = jnp.where(key + 1 < block, 0, 1)
            return count + 1

        count = lax.fori_loop(0, (block - begin + 1) // 2, enlist, count)

    def over_pairs(body):
        groups = count // GROUP

        @pl.loop(0, groups)
        def _(group):
            body([group * GROUP + i for i in range(GROUP)])

        @pl.loop(groups * GROUP, count)
        def _(pair):
            body([pair])

    def spread_rows(row):
        return jnp.broadcast_to(row, (8, 2 * BLK))

    for index in range(4):
        own = own_s[index]
        peak = jnp.max(own, axis=0, keepdims=True) * scale2
        peaks[index] = spread_rows(peak)
        own = jnp.exp2(own * scale2 - peak)
        sums[index] = totals(own)
        own_low = own.astype(BF16)
        own_weights[index] = own_low
        out_t[index, :, :BLK] = dot(key_rows(vall, chip * 4 + index), own_low[:, :BLK], FIRST)
        out_t[index, :, BLK:] = dot(vn[index], own_low[:, BLK:], FIRST)
        pair_peaks[32 + index] = peaks[index]

    def forward_pairs(pairs):
        queries = [pair_query[pair] for pair in pairs]
        scores = [
            dot(key_pair(kall, pair), both(qq, query), LAST) for pair, query in zip(pairs, queries)
        ]
        tops_of = [jnp.max(tops(score), axis=0, keepdims=True) * scale2 for score in scores]
        results = []
        for pair, query, score, top in zip(pairs, queries, scores, tops_of):
            before = peaks[query]
            now = jnp.maximum(before, spread_rows(top))
            peaks[query] = now
            pair_peaks[pair] = now
            peak = now[:1]
            hidden = peak + jnp.where(pair_bias[pair] == 1, jnp.inf, 0.0)
            upper = jnp.exp2(score[:BLK] * scale2 - peak)
            lower = jnp.exp2(score[BLK:] * scale2 - hidden)
            low = jnp.concatenate([upper.astype(BF16), lower.astype(BF16)], axis=0)
            weights[pair] = low
            results.append(
                (
                    jnp.exp2(before - now),
                    dot(key_pair(vall, pair), low, FIRST),
                    totals(upper) + totals(lower),
                )
            )
        for query, (decay, out, part) in zip(queries, results):
            sums[query] = sums[query] * decay + part
            out_t[query] = out_t[query] * decay[:1] + out

    over_pairs(forward_pairs)

    for index in range(4):
        stored_own = chip * 4 + index
        own_decay = jnp.exp2(pair_peaks[32 + index] - peaks[index])[:1]
        inverse_sum = 1.0 / jnp.sum(sums[index], axis=0, keepdims=True)
        out = out_t[index] * inverse_sum
        out_t[index] = out
        grad_rows = (grads_t[index] * inverse_sum).astype(BF16).astype(F32)
        delta = jnp.sum(out * grad_rows, axis=0, keepdims=True)
        deltas[index] = spread_rows(delta)
        grads = jnp.transpose(grad_rows).astype(BF16)
        scaled_grads[index] = grads
        own = own_weights[index].astype(F32) * own_decay
        own_low = own.astype(BF16)
        own_dp = jnp.concatenate(
            [
                dot(key_rows(vall, stored_own), grads[:BLK], LAST),
                dot(vn[index], grads[BLK:], LAST),
            ],
            axis=1,
        )
        own_ds = (own * (own_dp - delta)).astype(BF16)
        dv_acc[stored_own] += dot(own_low[:, :BLK], grads[:BLK], PLAIN)
        dk_acc[stored_own] += dot(own_ds[:, :BLK], qq[index, 0], PLAIN)
        dv_noisy[index] = dot(own_low[:, BLK:], grads[BLK:], PLAIN)
        dk_noisy[index] = dot(own_ds[:, BLK:], qq[index, 1], PLAIN) * scale
        dq_t[index, :, :BLK] = dot(key_rows(kall, stored_own), own_ds[:, :BLK], FIRST)
        dq_t[index, :, BLK:] = dot(kn[index], own_ds[:, BLK:], FIRST)

    def grad_pairs(pairs):
        queries = [pair_query[pair] for pair in pairs]
        results = []
        for pair, query in zip(pairs, queries):
            decay = jnp.exp2(pair_peaks[pair] - peaks[query])[:1]
            prob = weights[pair].astype(F32) * decay
            dp = dot(key_pair(vall, pair), scaled_grads[query], LAST)
            ds = (prob * (dp - deltas[query, :1])).astype(BF16)
            results.append(
                (
                    dot(prob.astype(BF16), scaled_grads[query], PLAIN),
                    dot(ds, both(qq, query), PLAIN),
                    dot(key_pair(kall, pair), ds, FIRST),
                )
            )
        for pair, query, (dv, dk, dq) in zip(pairs, queries, results):
            for place in range(2):
                rows = slice(place * BLK, place * BLK + BLK)
                dv_acc[pair_key[2 * pair + place]] += dv[rows]
                dk_acc[pair_key[2 * pair + place]] += dk[rows]
            dq_t[query] += dq

    over_pairs(grad_pairs)


def attention_call(ids, docs, *parts):
    return pl.pallas_call(
        attention_kernel,
        name="attention",
        out_shape=(
            jax.ShapeDtypeStruct((4, HD, 2 * BLK), F32),
            jax.ShapeDtypeStruct((4, HD, 2 * BLK), F32),
            jax.ShapeDtypeStruct((4, BLK, HD), F32),
            jax.ShapeDtypeStruct((4, BLK, HD), F32),
            jax.ShapeDtypeStruct((32, BLK, HD), F32),
            jax.ShapeDtypeStruct((32, BLK, HD), F32),
        ),
        in_specs=[SMEM, SMEM] + [VMEM] * 8,
        out_specs=(VMEM,) * 6,
        scratch_shapes=[
            pltpu.SMEM((32,), jnp.int32),
            pltpu.SMEM((32,), jnp.int32),
            pltpu.SMEM((32,), jnp.int32),
            pltpu.SMEM((64,), jnp.int32),
            pltpu.SMEM((32,), jnp.int32),
            pltpu.VMEM((32, 2 * BLK, 2 * BLK), BF16),
            pltpu.VMEM((36, 8, 2 * BLK), F32),
            pltpu.VMEM((4, BLK, 2 * BLK), BF16),
            pltpu.VMEM((4, 2 * BLK, HD), BF16),
            pltpu.VMEM((4, 8, 2 * BLK), F32),
            pltpu.VMEM((4, 8, 2 * BLK), F32),
            pltpu.VMEM((4, 8, 2 * BLK), F32),
        ],
        compiler_params=pltpu.CompilerParams(vmem_limit_bytes=30 * 2**20),
    )(ids, docs, *parts)


def scatter_kernel(
    cq_h, ck_h, nq_h, nk_h, qg_h, kg_h, inv, out_t, dq_t, dk_noisy, dv_noisy, dk, dv,
    back, fin, inner_out,
    raws, qg, kg, stage, k_out, v_out, x_out, vy, vq, vh, vx, kh, kx, ky, away, sums,
    send, recv, lsem,
):
    ctx, head, core, y, x = place()
    right, left = (x + 1) % 4, (x + 3) % 4
    partner = ctx_of(x, y, 1 - core)
    to_right, to_left = ctx_of(right, y, core), ctx_of(left, y, core)
    to_y = ctx_of(x, 1 - y, core)
    score_scale = 1.0 / math.sqrt(HD)
    own_columns = pl.ds(pl.multiple_of(core * HD, HD), HD)
    local = Locals(lsem)
    loads = [local.start(ref, raws.at[i]) for i, ref in enumerate((cq_h, ck_h, nq_h, nk_h))]
    loads += [local.start(qg_h, qg), local.start(kg_h, kg)]
    cq, ck, nq, nk = [raws.at[i] for i in range(4)]
    remote = Copies(send, recv, head)

    def mine(ref, step, row, half):
        chip = chip_of((x + step) % 4, y if row == 0 else 1 - y)
        return ref[pl.ds(chip * 4 + half * 2, 2)].reshape(512, HD)

    def pack_v(step):
        for half in range(2):
            v_out[step, half] = mine(dv, step, 1, half).astype(BF16)

    def pack_k(row, step, half, *others):
        value = mine(dk, step, row, half) * score_scale
        for other in others:
            value = value + other[...].astype(F32)
        k_out[row, step, half] = value.astype(BF16)

    pack_v(2)
    pack_k(1, 2, 0)
    pack_k(1, 2, 1)
    enter(ctx, head, [partner, to_right, to_left, to_y])
    first, rest = pl.ds(0, SHIFT), pl.ds(SHIFT, 512 - SHIFT)
    v_far = [
        remote.start(v_out.at[2, 0, first], vq.at[0], to_left),
        remote.start(v_out.at[2, 1, first], vq.at[1], to_right),
    ]
    v_opposite = [
        remote.start(v_out.at[2, half, rest], vy.at[2, half, rest], to_y) for half in range(2)
    ]
    k_half = {}

    def start_half(row):
        k_half[row, 0] = remote.start(k_out.at[row, 2, 0], kh.at[row, 0], to_left)
        k_half[row, 1] = remote.start(k_out.at[row, 2, 1], kh.at[row, 1], to_right)

    start_half(1)
    pack_k(0, 2, 0)
    pack_k(0, 2, 1)
    start_half(0)
    v_y = {}

    def send_v(step, half):
        pack_v(step)
        if half is not None:
            v_far[half].wait_recv()
            v_out[step, half, :SHIFT] = (
                mine(dv, step, 1, half)[:SHIFT] + vq[half].astype(F32)
            ).astype(BF16)
        v_y[step] = remote.start(v_out.at[step], vy.at[step], to_y)

    send_v(3, 0)
    for row in (1, 0):
        pack_k(row, 3, 1)
        pack_k(row, 1, 0)

    def landing(i):
        return back.at[i, :, own_columns]

    swap = {}
    dk_pair, dv_pair = [
        [ref.at[pl.ds(c * 2, 2)] for c in (core, 1 - core)] for ref in (dk_noisy, dv_noisy)
    ]

    def turn(index, ref, first, factor):
        for part in range(2):
            rows = slice(part * BLK, part * BLK + BLK)
            for c, own in ((core, True), (1 - core, False)):
                values = jnp.transpose(ref[2 * c + part]) * factor
                for kind in range(2):
                    if own:
                        back[first + kind, rows, own_columns] = values[kind * BLK : kind * BLK + BLK]
                    else:
                        stage[first + kind, rows, :] = values[kind * BLK : kind * BLK + BLK]
        for i in (first, first + 1):
            swap[i] = remote.start(stage.at[i], landing(i), partner)

    def turn_noisy(ref, i):
        for part in range(2):
            rows = slice(part * BLK, part * BLK + BLK)
            back[i, rows, own_columns] = ref[2 * core + part]
            stage[i, rows, :] = ref[2 * (1 - core) + part]
        swap[i] = remote.start(stage.at[i], landing(i), partner)

    turn(0, dq_t, 2, score_scale)
    turn_noisy(dk_noisy, 4)

    k_x = {}

    def k_forward(row):
        k_half[row, 0].wait_recv()
        pack_k(row, 3, 0, kh.at[row, 0])
        k_x[row, 0] = remote.start(k_out.at[row, 3], kx.at[row, 0], to_left)
        k_half[row, 1].wait_recv()
        pack_k(row, 1, 1, kh.at[row, 1])
        k_x[row, 1] = remote.start(k_out.at[row, 1], kx.at[row, 1], to_right)

    k_forward(1)

    row = lax.broadcasted_iota(jnp.int32, (8, 512), 0)

    def inner(raw, gain, values):
        return row_sums(raw[...].astype(F32) * (gain[...] * values))

    for copy in loads:
        copy.wait()
    for i in (2, 3, 4):
        swap[i].wait_recv()
    total = jnp.zeros((8, 512), F32)
    normal = ((0, cq, qg, 2), (2, nq, qg, 3), (3, nk, kg, 4))
    for index, raw, gain, i in normal:
        total = jnp.where(row == index, inner(raw, gain, back[i]), total)
    sums[0] = total
    exchange = [
        remote.start(sums.at[0], sums.at[step], ctx, (head + step) % 8) for step in range(1, 8)
    ]

    def pack_x(step, half, *others):
        value = mine(dv, step, 0, half)
        for other in others:
            value = value + other[...].astype(F32)
        x_out[step, half] = value.astype(BF16)

    v_half = []
    for half, target in ((0, to_left), (1, to_right)):
        v_opposite[half].wait_recv()
        pack_x(2, half)
        x_out[2, half, SHIFT:] = (
            mine(dv, 2, 0, half)[SHIFT:] + vy[2, half, SHIFT:].astype(F32)
        ).astype(BF16)
        v_half.append(remote.start(x_out.at[2, half], vh.at[half], target))
    send_v(1, 1)
    k_forward(0)
    turn(0, out_t, 0, 1.0)
    turn_noisy(dv_noisy, 5)
    k_x[1, 0].wait_recv()
    k_x[1, 1].wait_recv()
    for half in range(2):
        pack_k(1, 0, half, kx.at[1, 0, half], kx.at[1, 1, half])
    k_y = remote.start(k_out.at[1, 0], ky, to_y)
    send_v(0, None)

    v_y[3].wait_recv()
    v_half[0].wait_recv()
    pack_x(3, 0, vy.at[3, 0], vh.at[0])
    pack_x(3, 1, vy.at[3, 1])
    v_x = [remote.start(x_out.at[3], vx.at[0], to_left)]
    v_y[1].wait_recv()
    v_half[1].wait_recv()
    pack_x(1, 0, vy.at[1, 0])
    pack_x(1, 1, vy.at[1, 1], vh.at[1])
    v_x.append(remote.start(x_out.at[1], vx.at[1], to_right))

    for copy in exchange:
        copy.wait_recv()
    total = sums[0]
    for step in range(1, 8):
        total = total + sums[step]
    inverses = jnp.transpose(inv[...])
    means = jnp.transpose(total) / FEAT
    for index, raw, gain, i in normal:
        inverse = inverses[:, index : index + 1]
        factor = inverse * inverse * inverse * means[:, index : index + 1]
        back[i] = inverse * (gain[...] * back[i]) - raw[...].astype(F32) * factor

    def finish(index, ref, factor, terms):
        values = []
        for half in range(2):
            value = mine(ref, 0, 0, half) * factor
            for term in terms:
                value = value + term[half].astype(F32)
            values.append(value)
        first_core = core == 0
        fin[index, :, own_columns] = jnp.where(first_core, values[0], values[1])
        away[index] = jnp.where(first_core, values[1], values[0])
        return remote.start(away.at[index], fin.at[index, :, own_columns], partner)

    k_x[0, 0].wait_recv()
    k_x[0, 1].wait_recv()
    k_y.wait_recv()
    k_fin = finish(0, dk, score_scale, (kx.at[0, 0], kx.at[0, 1], ky))
    k_fin.wait_recv()
    sums[8] = inner(ck, kg, fin[0])
    k_exchange = [
        remote.start(sums.at[8], sums.at[8 + step], ctx, (head + step) % 8) for step in range(1, 8)
    ]
    v_y[0].wait_recv()
    v_x[0].wait_recv()
    v_x[1].wait_recv()
    v_fin = finish(1, dv, 1.0, (vy.at[0], vx.at[0], vx.at[1]))

    for copy in k_exchange:
        copy.wait_recv()
    total = sums[8]
    for step in range(1, 8):
        total = total + sums[8 + step]
    inner_out[...] = total
    v_fin.wait_recv()
    for i in (0, 1, 5):
        swap[i].wait_recv()
    for copy in remote.started:
        copy.wait_send()


def scatter_call(*operands):
    return pl.pallas_call(
        scatter_kernel,
        name="scatter_grads",
        out_shape=(
            jax.ShapeDtypeStruct((6, 512, 256), F32),
            jax.ShapeDtypeStruct((2, 512, 256), F32),
            jax.ShapeDtypeStruct((8, 512), F32),
        ),
        in_specs=[HBM] * 6 + [VMEM] * 7,
        out_specs=(VMEM, VMEM, VMEM),
        scratch_shapes=[
            pltpu.VMEM((4, 512, 256), BF16),
            pltpu.VMEM((1, 256), F32),
            pltpu.VMEM((1, 256), F32),
            pltpu.VMEM((6, 512, HD), F32),
            pltpu.VMEM((2, 4, 2, 512, HD), BF16),
            pltpu.VMEM((4, 2, 512, HD), BF16),
            pltpu.VMEM((4, 2, 512, HD), BF16),
            pltpu.VMEM((4, 2, 512, HD), BF16),
            pltpu.VMEM((2, SHIFT, HD), BF16),
            pltpu.VMEM((2, 512, HD), BF16),
            pltpu.VMEM((2, 2, 512, HD), BF16),
            pltpu.VMEM((2, 2, 512, HD), BF16),
            pltpu.VMEM((2, 2, 2, 512, HD), BF16),
            pltpu.VMEM((2, 512, HD), BF16),
            pltpu.VMEM((2, 512, HD), F32),
            pltpu.VMEM((16, 8, 512), F32),
            pltpu.SemaphoreType.DMA((48,)),
            pltpu.SemaphoreType.DMA((48,)),
            pltpu.SemaphoreType.DMA((8,)),
        ],
        compiler_params=pltpu.CompilerParams(
            collective_id=1, has_side_effects=True, vmem_limit_bytes=20 * 2**20
        ),
    )(*operands)


def finish_kernel(
    ck, kg, inv, inner, back, fin,
    out_clean, out_noisy, dq_clean, dk_clean, dv_clean, dq_noisy, dk_noisy, dv_noisy,
    dk, sems,
):
    local = Locals(sems)
    copies = [
        local.start(source, target)
        for source, target in (
            (back.at[0], out_clean),
            (back.at[1], out_noisy),
            (back.at[2], dq_clean),
            (back.at[3], dq_noisy),
            (back.at[4], dk_noisy),
            (back.at[5], dv_noisy),
            (fin.at[1], dv_clean),
        )
    ]
    inverse = jnp.transpose(inv[...])[:, 1:2]
    mean = jnp.transpose(inner[...])[:, :1] / FEAT
    factor = inverse * inverse * inverse * mean
    dk[...] = inverse * (kg[...] * fin[0]) - ck[...].astype(F32) * factor
    copies.append(local.start(dk, dk_clean))
    for copy in copies:
        copy.wait()


def finish_call(*operands):
    return pl.pallas_call(
        finish_kernel,
        name="finish",
        out_shape=tuple(jax.ShapeDtypeStruct((512, 256), F32) for _ in range(8)),
        in_specs=[VMEM] * 6,
        out_specs=(HBM,) * 8,
        scratch_shapes=[pltpu.VMEM((512, 256), F32), pltpu.SemaphoreType.DMA((8,))],
        compiler_params=pltpu.CompilerParams(vmem_limit_bytes=16 * 2**20),
    )(*operands)


def local(
    clean_q, clean_k, clean_v, noisy_q, noisy_k, noisy_v,
    q_gain, k_gain, grad_clean, grad_noisy, owned_blocks, block_doc,
):
    qg = q_gain.reshape(1, 256)
    kg = k_gain.reshape(1, 256)
    blocks = [a.reshape(2, BLK, 2 * HD) for a in (noisy_v, grad_clean, grad_noisy)]
    *pinned, docs = [
        pltpu.with_memory_space_constraint(a, pltpu.HBM)
        for a in (
            clean_q, clean_k, noisy_q, noisy_k, qg, kg, clean_v, *blocks, owned_blocks, block_doc,
        )
    ]
    *parts, inv, ids = gather_call(*pinned)
    grads = attention_call(ids, docs, *parts)
    back, fin, inner = scatter_call(*pinned[:6], inv, *grads)
    return finish_call(clean_k, kg, inv, inner, back, fin)


def solution(mesh):
    placed = (P("ctx", "head"),) * 6 + (P("head"),) * 2 + (P("ctx", "head"),) * 2 + (P("ctx"), P())
    return jax.shard_map(
        local,
        mesh=mesh,
        in_specs=placed,
        out_specs=(P("ctx", "head"),) * 8,
        check_vma=False,
    )
```

```python
import math

import jax
import jax.numpy as jnp
from jax import lax
from jax.experimental import pallas as pl
from jax.experimental.pallas import tpu as pltpu
from jax.sharding import PartitionSpec as P

HD = 128
BLK = 256
FEAT = 2048
EPSILON = 1e-06
NEGATIVE = -1e30
MESH = pl.DeviceIdType.MESH
F32 = jnp.float32
BF16 = jnp.bfloat16
VMEM = pl.BlockSpec(memory_space=pltpu.VMEM)
SMEM = pl.BlockSpec(memory_space=pltpu.SMEM)
ANY = pl.BlockSpec(memory_space=pl.ANY)
HBM = pl.BlockSpec(memory_space=pltpu.HBM)
LAST = (((1,), (1,)), ((), ()))
FIRST = (((0,), (0,)), ((), ()))
PLAIN = (((1,), (0,)), ((), ()))
PACKET = 528
SHIFT = 32
GROUP = 2
SCALE = 1.0 / math.sqrt(HD)
SCALE2 = SCALE * math.log2(math.e)


def dot(a, b, dims):
    return lax.dot_general(a, b, dims, preferred_element_type=F32)


def row_sums(products):
    high = products.astype(BF16)
    low = (products - high.astype(F32)).astype(BF16)
    ones = jnp.ones((8, products.shape[1]), BF16)
    return dot(ones, high, LAST) + dot(ones, low, LAST)


def place():
    ctx = lax.axis_index("ctx")
    head = lax.axis_index("head")
    core = ctx % 2
    y = (ctx // 2) % 2
    x = ctx // 4
    return ctx, head, core, y, x


def ctx_of(x, y, core):
    return (x * 2 + y) * 2 + core


def chip_of(x, y):
    return x * 2 + y


class Copies:
    def __init__(self, send, recv, head):
        self.send, self.recv, self.head = send, recv, head
        self.started = []
        self.count = 0

    def start(self, src, dst, ctx, head=None):
        copy = pltpu.make_async_remote_copy(
            src_ref=src,
            dst_ref=dst,
            send_sem=self.send.at[self.count],
            recv_sem=self.recv.at[self.count],
            device_id={"ctx": ctx, "head": self.head if head is None else head},
            device_id_type=MESH,
        )
        self.count += 1
        copy.start()
        self.started.append(copy)
        return copy


class Locals:
    def __init__(self, sems):
        self.sems = sems
        self.count = 0

    def start(self, src, dst):
        copy = pltpu.make_async_copy(src, dst, self.sems.at[self.count])
        self.count += 1
        copy.start()
        return copy


def enter(ctx, head, others):
    barrier = pltpu.get_barrier_semaphore()
    for other in others:
        pl.semaphore_signal(barrier, inc=1, device_id={"ctx": other, "head": head}, device_id_type=MESH)
    for step in range(1, 8):
        pl.semaphore_signal(
            barrier, inc=1, device_id={"ctx": ctx, "head": (head + step) % 8}, device_id_type=MESH
        )
    pl.semaphore_wait(barrier, 7 + len(others))


def gather_kernel(
    cq_h, ck_h, nq_h, nk_h, qg_h, kg_h, cv, nv, gc, gn, owned,
    kall, vall, qq, gg, kn, vn, own_w, own_peak, own_sum, out_own, grads_t, inv_out, ids_out,
    owned_s, raws, qg, kg, k_packet, normed, sums, send, recv, wide_send, wide_recv, lsem,
):
    ctx, head, core, y, x = place()
    right, left = (x + 1) % 4, (x + 3) % 4
    opposite = (x + 2) % 4
    mine = pl.ds(pl.multiple_of(core * HD, HD), HD)
    theirs = pl.ds(pl.multiple_of((1 - core) * HD, HD), HD)
    partner = ctx_of(x, y, 1 - core)
    local = Locals(lsem)
    owned_load = local.start(owned, owned_s)
    loads = [local.start(ref, raws.at[i]) for i, ref in enumerate((cq_h, ck_h, nq_h, nk_h))]
    loads += [local.start(qg_h, qg), local.start(kg_h, kg)]
    remote = Copies(send, recv, head)
    chips = ((x, 1 - y), (right, y), (left, y))
    enter(ctx, head, [partner] + [ctx_of(*chip, c) for chip in chips for c in range(2)])
    wide = []

    def first_hop(base, columns_of, buf):
        for number, chip in enumerate(chips):
            for target in range(2):
                copy = pltpu.make_async_remote_copy(
                    src_ref=columns_of(target),
                    dst_ref=buf.at[ctx],
                    send_sem=wide_send.at[base + number, target],
                    recv_sem=wide_recv.at[base + number, core],
                    device_id={"ctx": ctx_of(*chip, target), "head": head},
                    device_id_type=MESH,
                )
                copy.start()
                wide.append(copy)

    def arrived(base, number, buf, source):
        chip = ((x, 1 - y), (left, y), (right, y))[number]
        pltpu.make_async_remote_copy(
            src_ref=buf.at[ctx],
            dst_ref=buf.at[ctx_of(*chip, source)],
            send_sem=wide_send.at[base + number, source],
            recv_sem=wide_recv.at[base + number, source],
            device_id={"ctx": partner, "head": head},
            device_id_type=MESH,
        ).wait_recv()

    first_hop(0, lambda target: cv.at[:, target * HD : target * HD + HD], vall)
    v_swap = remote.start(cv.at[:, theirs], vall.at[ctx], partner)
    v_own = local.start(cv.at[:, mine], vall.at[ctx])

    for copy in loads:
        copy.wait()
    row = lax.broadcasted_iota(jnp.int32, (8, 512), 0)
    total = jnp.zeros((8, 512), F32)
    for index in range(4):
        raw = raws[index].astype(F32)
        total = jnp.where(row == index, row_sums(raw * raw), total)
    sums[0] = total
    exchange = [
        remote.start(sums.at[0], sums.at[step], ctx, (head + step) % 8) for step in range(1, 8)
    ]
    owned_load.wait()
    lane = lax.broadcasted_iota(jnp.int32, (16, 2 * HD), 1)
    k_packet[512:, :] = jnp.where(lane % HD == 0, owned_s[0], owned_s[1]).astype(F32).astype(BF16)

    pair = pl.ds(core * 2, 2)
    late, late_own = [], []

    def swap(src, dst):
        late.append(remote.start(src.at[:, :, theirs], dst, partner))
        late_own.append(local.start(src.at[:, :, mine], dst))

    swap(gc, gg.at[pair, 0])
    swap(gn, gg.at[pair, 1])
    swap(nv, vn.at[pair])

    for copy in exchange:
        copy.wait_recv()
    total = sums[0]
    for step in range(1, 8):
        total = total + sums[step]
    inverse = lax.rsqrt(total / FEAT + EPSILON)
    inv_out[...] = inverse
    columns = jnp.transpose(inverse)

    def normalized(index, gain):
        values = raws[index].astype(F32) * columns[:, index : index + 1] * gain[...]
        return values.astype(BF16)

    k_packet[:512, :] = normalized(1, kg)
    first_hop(3, lambda target: k_packet.at[:, target * HD : target * HD + HD], kall)
    k_swap = remote.start(k_packet.at[:, theirs], kall.at[ctx], partner)
    k_own = local.start(k_packet.at[:, mine], kall.at[ctx])
    for index, raw, gain, dst in (
        (0, 0, qg, qq.at[pair, 0]),
        (1, 2, qg, qq.at[pair, 1]),
        (2, 3, kg, kn.at[pair]),
    ):
        normed[index] = normalized(raw, gain).reshape(2, BLK, 2 * HD)
        swap(normed.at[index], dst)

    def slot(buf, sx, sy):
        return buf.at[pl.ds(2 * chip_of(sx, sy), 2)]

    def part(buf, sx, sy, half):
        return buf.at[2 * chip_of(sx, sy) + half]

    def rows_of(sx, sy, half, first, count):
        return vall.at[2 * chip_of(sx, sy) + half, pl.ds(first, count)]

    def spread(view, px, py):
        return remote.start(view, view, ctx_of(px, py, core))

    v_half, v_y, k_half = [], [], []
    sides = ((1, left, right, 0), (2, right, left, 1))
    for number, near, far, half in sides:
        arrived(0, number, vall, half)
        v_half.append(spread(part(vall, near, y, half), far, y))
    arrived(3, 0, kall, 0)
    arrived(3, 0, kall, 1)
    k_right = spread(slot(kall, x, 1 - y), right, y)
    k_left = spread(slot(kall, x, 1 - y), left, y)
    arrived(0, 1, vall, 1)
    v_y.append(spread(slot(vall, left, y), x, 1 - y))

    v_own.wait()
    k_own.wait()
    v_swap.wait_recv()
    k_swap.wait_recv()
    for copy in late_own:
        copy.wait()
    for copy in late:
        copy.wait_recv()

    def own_block(index):
        side, rows = index // 2, slice(index % 2 * BLK, index % 2 * BLK + BLK)
        packet = 2 * chip_of(x, y) + side
        own = ((kall[packet, rows, :], vall[packet, rows, :]), (kn[index], vn[index]))
        for kind, (keys, values) in enumerate(own):
            columns = slice(kind * BLK, kind * BLK + BLK)
            scores = dot(keys, qq[index, kind], LAST) * SCALE2
            peak = jnp.max(scores, axis=0, keepdims=True)
            weights = jnp.exp2(scores - peak)
            low = weights.astype(BF16)
            own_peak[index, :, columns] = jnp.broadcast_to(peak, (8, BLK))
            own_sum[index, :, columns] = jnp.sum(weights.reshape(BLK // 8, 8, BLK), axis=0)
            own_w[index, :, columns] = low
            out_own[index, :, columns] = dot(values, low, FIRST)
            grads_t[index, :, columns] = jnp.transpose(gg[index, kind].astype(F32))

    own_block(0)
    for number, near, far, half in sides:
        arrived(3, number, kall, half)
        k_half.append(spread(part(kall, near, y, half), far, y))
        arrived(3, number, kall, 1 - half)
    own_block(1)
    arrived(0, 2, vall, 0)
    v_y.append(spread(slot(vall, right, y), x, 1 - y))
    own_block(2)
    v_half[0].wait_recv()
    v_half[1].wait_recv()
    v_y[0].wait_recv()
    v_far = [spread(rows_of(left, 1 - y, 0, 0, SHIFT), right, y)]
    for half in range(2):
        v_y.append(spread(rows_of(opposite, y, half, SHIFT, 512 - SHIFT), x, 1 - y))
    k_right.wait_recv()
    k_half.append(spread(part(kall, left, 1 - y, 0), right, y))
    k_left.wait_recv()
    k_half.append(spread(part(kall, right, 1 - y, 1), left, y))
    own_block(3)
    v_y[1].wait_recv()
    v_far.append(spread(rows_of(right, 1 - y, 1, 0, SHIFT), left, y))
    arrived(0, 0, vall, 0)
    arrived(0, 0, vall, 1)
    for copy in v_y[2:] + v_far + k_half:
        copy.wait_recv()
    names = jnp.max(kall[:, 512:, :].astype(F32), axis=1)
    ids_out[...] = names.astype(jnp.int32)
    for copy in remote.started + wide:
        copy.wait_send()


def gather_call(cq, ck, nq, nk, qg, kg, cv, nv, gc, gn, owned):
    return pl.pallas_call(
        gather_kernel,
        name="gather_keys",
        out_shape=(
            jax.ShapeDtypeStruct((16, PACKET, HD), BF16),
            jax.ShapeDtypeStruct((16, 512, HD), BF16),
            jax.ShapeDtypeStruct((4, 2, BLK, HD), BF16),
            jax.ShapeDtypeStruct((4, 2, BLK, HD), BF16),
            jax.ShapeDtypeStruct((4, BLK, HD), BF16),
            jax.ShapeDtypeStruct((4, BLK, HD), BF16),
            jax.ShapeDtypeStruct((4, BLK, 2 * BLK), BF16),
            jax.ShapeDtypeStruct((4, 8, 2 * BLK), F32),
            jax.ShapeDtypeStruct((4, 8, 2 * BLK), F32),
            jax.ShapeDtypeStruct((4, HD, 2 * BLK), F32),
            jax.ShapeDtypeStruct((4, HD, 2 * BLK), F32),
            jax.ShapeDtypeStruct((8, 512), F32),
            jax.ShapeDtypeStruct((16, HD), jnp.int32),
        ),
        in_specs=[HBM] * 11,
        out_specs=(VMEM,) * 13,
        scratch_shapes=[
            pltpu.SMEM((2,), jnp.int32),
            pltpu.VMEM((4, 512, 256), BF16),
            pltpu.VMEM((1, 256), F32),
            pltpu.VMEM((1, 256), F32),
            pltpu.VMEM((PACKET, 256), BF16),
            pltpu.VMEM((3, 2, BLK, 2 * HD), BF16),
            pltpu.VMEM((8, 8, 512), F32),
            pltpu.SemaphoreType.DMA((32,)),
            pltpu.SemaphoreType.DMA((32,)),
            pltpu.SemaphoreType.DMA((6, 2)),
            pltpu.SemaphoreType.DMA((6, 2)),
            pltpu.SemaphoreType.DMA((16,)),
        ],
        compiler_params=pltpu.CompilerParams(
            collective_id=0, has_side_effects=True, vmem_limit_bytes=20 * 2**20
        ),
    )(cq, ck, nq, nk, qg, kg, cv, nv, gc, gn, owned)


def attention_kernel(
    ids, docs, kall, vall, qq, gg, kn, vn, own_w, own_peak, own_sum, out_own, grads_t,
    out_t, dq_t, dk_noisy, dv_noisy, dk_acc, dv_acc,
    where_is, first_of, pair_query, pair_key, pair_bias,
    weights, pair_peaks, scaled_grads, peaks, sums, deltas,
):
    chip = lax.axis_index("ctx") // 2

    def clear(stored):
        dk_acc[stored] = jnp.zeros((BLK, HD), F32)
        dv_acc[stored] = jnp.zeros((BLK, HD), F32)

    def begin_of(block, begin):
        clear(block)
        where_is[ids[block // 2, block % 2]] = block
        begin = jnp.where(docs[block] == docs[jnp.maximum(block - 1, 0)], begin, block)
        first_of[block] = begin
        return begin

    lax.fori_loop(0, 32, begin_of, 0)

    def key_rows(buf, stored):
        start = pl.multiple_of((stored % 2) * BLK, BLK)
        return buf[stored // 2, pl.ds(start, BLK), :]

    def key_pair(buf, pair):
        return jnp.concatenate(
            [key_rows(buf, pair_key[2 * pair]), key_rows(buf, pair_key[2 * pair + 1])], axis=0
        )

    def both(ref, index):
        return ref[index].reshape(2 * BLK, HD)

    def tops(values):
        return jnp.max(values.reshape(-1, 8, values.shape[1]), axis=0)

    def totals(values):
        return jnp.sum(values.reshape(-1, 8, values.shape[1]), axis=0)

    count = 0
    for index in range(4):
        block = ids[chip * 2 + index // 2, index % 2]
        begin = first_of[block]

        def enlist(pair, count, index=index, block=block, begin=begin):
            key = begin + 2 * pair
            first = where_is[key]
            second = where_is[jnp.minimum(key + 1, block - 1)]
            pair_query[count] = index
            pair_key[2 * count] = first
            pair_key[2 * count + 1] = second
            pair_bias[count] = jnp.where(key + 1 < block, 0, 1)
            return count + 1

        count = lax.fori_loop(0, (block - begin + 1) // 2, enlist, count)

    def over_pairs(body):
        groups = count // GROUP

        @pl.loop(0, groups)
        def _(group):
            body([group * GROUP + i for i in range(GROUP)])

        @pl.loop(groups * GROUP, count)
        def _(pair):
            body([pair])

    def spread_rows(row):
        return jnp.broadcast_to(row, (8, 2 * BLK))

    for index in range(4):
        peaks[index] = own_peak[index]
        sums[index] = own_sum[index]
        out_t[index] = out_own[index]

    def forward_pairs(pairs):
        queries = [pair_query[pair] for pair in pairs]
        scores = [
            dot(key_pair(kall, pair), both(qq, query), LAST) for pair, query in zip(pairs, queries)
        ]
        tops_of = [jnp.max(tops(score), axis=0, keepdims=True) * SCALE2 for score in scores]
        results = []
        for pair, query, score, top in zip(pairs, queries, scores, tops_of):
            before = peaks[query]
            now = jnp.maximum(before, spread_rows(top))
            peaks[query] = now
            pair_peaks[pair] = now
            peak = now[:1]
            hidden = peak + jnp.where(pair_bias[pair] == 1, jnp.inf, 0.0)
            upper = jnp.exp2(score[:BLK] * SCALE2 - peak)
            lower = jnp.exp2(score[BLK:] * SCALE2 - hidden)
            low = jnp.concatenate([upper.astype(BF16), lower.astype(BF16)], axis=0)
            weights[pair] = low
            results.append(
                (
                    jnp.exp2(before - now),
                    dot(key_pair(vall, pair), low, FIRST),
                    totals(upper) + totals(lower),
                )
            )
        for query, (decay, out, part) in zip(queries, results):
            sums[query] = sums[query] * decay + part
            out_t[query] = out_t[query] * decay[:1] + out

    over_pairs(forward_pairs)

    for index in range(4):
        stored_own = chip * 4 + index
        own_decay = jnp.exp2(own_peak[index] - peaks[index])[:1]
        inverse_sum = 1.0 / jnp.sum(sums[index], axis=0, keepdims=True)
        out = out_t[index] * inverse_sum
        out_t[index] = out
        grad_rows = (grads_t[index] * inverse_sum).astype(BF16).astype(F32)
        delta = jnp.sum(out * grad_rows, axis=0, keepdims=True)
        deltas[index] = spread_rows(delta)
        grads = jnp.transpose(grad_rows).astype(BF16)
        scaled_grads[index] = grads
        own = own_w[index].astype(F32) * own_decay
        own_low = own.astype(BF16)
        own_dp = jnp.concatenate(
            [
                dot(key_rows(vall, stored_own), grads[:BLK], LAST),
                dot(vn[index], grads[BLK:], LAST),
            ],
            axis=1,
        )
        own_ds = (own * (own_dp - delta)).astype(BF16)
        dv_acc[stored_own] += dot(own_low[:, :BLK], grads[:BLK], PLAIN)
        dk_acc[stored_own] += dot(own_ds[:, :BLK], qq[index, 0], PLAIN)
        dv_noisy[index] = dot(own_low[:, BLK:], grads[BLK:], PLAIN)
        dk_noisy[index] = dot(own_ds[:, BLK:], qq[index, 1], PLAIN) * SCALE
        dq_t[index, :, :BLK] = dot(key_rows(kall, stored_own), own_ds[:, :BLK], FIRST)
        dq_t[index, :, BLK:] = dot(kn[index], own_ds[:, BLK:], FIRST)

    def grad_pairs(pairs):
        queries = [pair_query[pair] for pair in pairs]
        results = []
        for pair, query in zip(pairs, queries):
            decay = jnp.exp2(pair_peaks[pair] - peaks[query])[:1]
            prob = weights[pair].astype(F32) * decay
            dp = dot(key_pair(vall, pair), scaled_grads[query], LAST)
            ds = (prob * (dp - deltas[query, :1])).astype(BF16)
            results.append(
                (
                    dot(prob.astype(BF16), scaled_grads[query], PLAIN),
                    dot(ds, both(qq, query), PLAIN),
                    dot(key_pair(kall, pair), ds, FIRST),
                )
            )
        for pair, query, (dv, dk, dq) in zip(pairs, queries, results):
            for place in range(2):
                rows = slice(place * BLK, place * BLK + BLK)
                dv_acc[pair_key[2 * pair + place]] += dv[rows]
                dk_acc[pair_key[2 * pair + place]] += dk[rows]
            dq_t[query] += dq

    over_pairs(grad_pairs)


def attention_call(ids, docs, *parts):
    return pl.pallas_call(
        attention_kernel,
        name="attention",
        out_shape=(
            jax.ShapeDtypeStruct((4, HD, 2 * BLK), F32),
            jax.ShapeDtypeStruct((4, HD, 2 * BLK), F32),
            jax.ShapeDtypeStruct((4, BLK, HD), F32),
            jax.ShapeDtypeStruct((4, BLK, HD), F32),
            jax.ShapeDtypeStruct((32, BLK, HD), F32),
            jax.ShapeDtypeStruct((32, BLK, HD), F32),
        ),
        in_specs=[SMEM, SMEM] + [VMEM] * 11,
        out_specs=(VMEM,) * 6,
        scratch_shapes=[
            pltpu.SMEM((32,), jnp.int32),
            pltpu.SMEM((32,), jnp.int32),
            pltpu.SMEM((32,), jnp.int32),
            pltpu.SMEM((64,), jnp.int32),
            pltpu.SMEM((32,), jnp.int32),
            pltpu.VMEM((32, 2 * BLK, 2 * BLK), BF16),
            pltpu.VMEM((32, 8, 2 * BLK), F32),
            pltpu.VMEM((4, 2 * BLK, HD), BF16),
            pltpu.VMEM((4, 8, 2 * BLK), F32),
            pltpu.VMEM((4, 8, 2 * BLK), F32),
            pltpu.VMEM((4, 8, 2 * BLK), F32),
        ],
        compiler_params=pltpu.CompilerParams(vmem_limit_bytes=30 * 2**20),
    )(ids, docs, *parts)


def scatter_kernel(
    cq_h, ck_h, nq_h, nk_h, qg_h, kg_h, inv, out_t, dq_t, dk_noisy, dv_noisy, dk, dv,
    back, fin, inner_out,
    raws, qg, kg, stage, k_out, v_out, x_out, vy, vq, vh, vx, kh, kx, ky, away, sums,
    send, recv, lsem,
):
    ctx, head, core, y, x = place()
    right, left = (x + 1) % 4, (x + 3) % 4
    partner = ctx_of(x, y, 1 - core)
    to_right, to_left = ctx_of(right, y, core), ctx_of(left, y, core)
    to_y = ctx_of(x, 1 - y, core)
    score_scale = 1.0 / math.sqrt(HD)
    own_columns = pl.ds(pl.multiple_of(core * HD, HD), HD)
    local = Locals(lsem)
    loads = [local.start(ref, raws.at[i]) for i, ref in enumerate((cq_h, ck_h, nq_h, nk_h))]
    loads += [local.start(qg_h, qg), local.start(kg_h, kg)]
    cq, ck, nq, nk = [raws.at[i] for i in range(4)]
    remote = Copies(send, recv, head)

    def mine(ref, step, row, half):
        chip = chip_of((x + step) % 4, y if row == 0 else 1 - y)
        return ref[pl.ds(chip * 4 + half * 2, 2)].reshape(512, HD)

    def pack_v(step):
        for half in range(2):
            v_out[step, half] = mine(dv, step, 1, half).astype(BF16)

    def pack_k(row, step, half, *others):
        value = mine(dk, step, row, half) * score_scale
        for other in others:
            value = value + other[...].astype(F32)
        k_out[row, step, half] = value.astype(BF16)

    pack_v(2)
    pack_k(1, 2, 0)
    pack_k(1, 2, 1)
    enter(ctx, head, [partner, to_right, to_left, to_y])
    first, rest = pl.ds(0, SHIFT), pl.ds(SHIFT, 512 - SHIFT)
    v_far = [
        remote.start(v_out.at[2, 0, first], vq.at[0], to_left),
        remote.start(v_out.at[2, 1, first], vq.at[1], to_right),
    ]
    v_opposite = [
        remote.start(v_out.at[2, half, rest], vy.at[2, half, rest], to_y) for half in range(2)
    ]
    k_half = {}

    def start_half(row):
        k_half[row, 0] = remote.start(k_out.at[row, 2, 0], kh.at[row, 0], to_left)
        k_half[row, 1] = remote.start(k_out.at[row, 2, 1], kh.at[row, 1], to_right)

    start_half(1)
    pack_k(0, 2, 0)
    pack_k(0, 2, 1)
    start_half(0)
    v_y = {}

    def send_v(step, half):
        pack_v(step)
        if half is not None:
            v_far[half].wait_recv()
            v_out[step, half, :SHIFT] = (
                mine(dv, step, 1, half)[:SHIFT] + vq[half].astype(F32)
            ).astype(BF16)
        v_y[step] = remote.start(v_out.at[step], vy.at[step], to_y)

    send_v(3, 0)
    for row in (1, 0):
        pack_k(row, 3, 1)
        pack_k(row, 1, 0)

    def landing(i):
        return back.at[i, :, own_columns]

    swap = {}
    dk_pair, dv_pair = [
        [ref.at[pl.ds(c * 2, 2)] for c in (core, 1 - core)] for ref in (dk_noisy, dv_noisy)
    ]

    def turn(index, ref, first, factor):
        for part in range(2):
            rows = slice(part * BLK, part * BLK + BLK)
            for c, own in ((core, True), (1 - core, False)):
                values = jnp.transpose(ref[2 * c + part]) * factor
                for kind in range(2):
                    if own:
                        back[first + kind, rows, own_columns] = values[kind * BLK : kind * BLK + BLK]
                    else:
                        stage[first + kind, rows, :] = values[kind * BLK : kind * BLK + BLK]
        for i in (first, first + 1):
            swap[i] = remote.start(stage.at[i], landing(i), partner)

    def turn_noisy(ref, i):
        for part in range(2):
            rows = slice(part * BLK, part * BLK + BLK)
            back[i, rows, own_columns] = ref[2 * core + part]
            stage[i, rows, :] = ref[2 * (1 - core) + part]
        swap[i] = remote.start(stage.at[i], landing(i), partner)

    turn(0, dq_t, 2, score_scale)
    turn_noisy(dk_noisy, 4)

    k_x = {}

    def k_forward(row):
        k_half[row, 0].wait_recv()
        pack_k(row, 3, 0, kh.at[row, 0])
        k_x[row, 0] = remote.start(k_out.at[row, 3], kx.at[row, 0], to_left)
        k_half[row, 1].wait_recv()
        pack_k(row, 1, 1, kh.at[row, 1])
        k_x[row, 1] = remote.start(k_out.at[row, 1], kx.at[row, 1], to_right)

    k_forward(1)

    row = lax.broadcasted_iota(jnp.int32, (8, 512), 0)

    def inner(raw, gain, values):
        return row_sums(raw[...].astype(F32) * (gain[...] * values))

    for copy in loads:
        copy.wait()
    for i in (2, 3, 4):
        swap[i].wait_recv()
    total = jnp.zeros((8, 512), F32)
    normal = ((0, cq, qg, 2), (2, nq, qg, 3), (3, nk, kg, 4))
    for index, raw, gain, i in normal:
        total = jnp.where(row == index, inner(raw, gain, back[i]), total)
    sums[0] = total
    exchange = [
        remote.start(sums.at[0], sums.at[step], ctx, (head + step) % 8) for step in range(1, 8)
    ]

    def pack_x(step, half, *others):
        value = mine(dv, step, 0, half)
        for other in others:
            value = value + other[...].astype(F32)
        x_out[step, half] = value.astype(BF16)

    v_half = []
    for half, target in ((0, to_left), (1, to_right)):
        v_opposite[half].wait_recv()
        pack_x(2, half)
        x_out[2, half, SHIFT:] = (
            mine(dv, 2, 0, half)[SHIFT:] + vy[2, half, SHIFT:].astype(F32)
        ).astype(BF16)
        v_half.append(remote.start(x_out.at[2, half], vh.at[half], target))
    send_v(1, 1)
    k_forward(0)
    turn(0, out_t, 0, 1.0)
    turn_noisy(dv_noisy, 5)
    k_x[1, 0].wait_recv()
    k_x[1, 1].wait_recv()
    for half in range(2):
        pack_k(1, 0, half, kx.at[1, 0, half], kx.at[1, 1, half])
    k_y = remote.start(k_out.at[1, 0], ky, to_y)
    send_v(0, None)

    v_y[3].wait_recv()
    v_half[0].wait_recv()
    pack_x(3, 0, vy.at[3, 0], vh.at[0])
    pack_x(3, 1, vy.at[3, 1])
    v_x = [remote.start(x_out.at[3], vx.at[0], to_left)]
    v_y[1].wait_recv()
    v_half[1].wait_recv()
    pack_x(1, 0, vy.at[1, 0])
    pack_x(1, 1, vy.at[1, 1], vh.at[1])
    v_x.append(remote.start(x_out.at[1], vx.at[1], to_right))

    for copy in exchange:
        copy.wait_recv()
    total = sums[0]
    for step in range(1, 8):
        total = total + sums[step]
    inverses = jnp.transpose(inv[...])
    means = jnp.transpose(total) / FEAT
    for index, raw, gain, i in normal:
        inverse = inverses[:, index : index + 1]
        factor = inverse * inverse * inverse * means[:, index : index + 1]
        back[i] = inverse * (gain[...] * back[i]) - raw[...].astype(F32) * factor

    def finish(index, ref, factor, terms):
        values = []
        for half in range(2):
            value = mine(ref, 0, 0, half) * factor
            for term in terms:
                value = value + term[half].astype(F32)
            values.append(value)
        first_core = core == 0
        fin[index, :, own_columns] = jnp.where(first_core, values[0], values[1])
        away[index] = jnp.where(first_core, values[1], values[0])
        return remote.start(away.at[index], fin.at[index, :, own_columns], partner)

    k_x[0, 0].wait_recv()
    k_x[0, 1].wait_recv()
    k_y.wait_recv()
    k_fin = finish(0, dk, score_scale, (kx.at[0, 0], kx.at[0, 1], ky))
    k_fin.wait_recv()
    sums[8] = inner(ck, kg, fin[0])
    k_exchange = [
        remote.start(sums.at[8], sums.at[8 + step], ctx, (head + step) % 8) for step in range(1, 8)
    ]
    v_y[0].wait_recv()
    v_x[0].wait_recv()
    v_x[1].wait_recv()
    v_fin = finish(1, dv, 1.0, (vy.at[0], vx.at[0], vx.at[1]))

    for copy in k_exchange:
        copy.wait_recv()
    total = sums[8]
    for step in range(1, 8):
        total = total + sums[8 + step]
    inner_out[...] = total
    v_fin.wait_recv()
    for i in (0, 1, 5):
        swap[i].wait_recv()
    for copy in remote.started:
        copy.wait_send()


def scatter_call(*operands):
    return pl.pallas_call(
        scatter_kernel,
        name="scatter_grads",
        out_shape=(
            jax.ShapeDtypeStruct((6, 512, 256), F32),
            jax.ShapeDtypeStruct((2, 512, 256), F32),
            jax.ShapeDtypeStruct((8, 512), F32),
        ),
        in_specs=[HBM] * 6 + [VMEM] * 7,
        out_specs=(VMEM, VMEM, VMEM),
        scratch_shapes=[
            pltpu.VMEM((4, 512, 256), BF16),
            pltpu.VMEM((1, 256), F32),
            pltpu.VMEM((1, 256), F32),
            pltpu.VMEM((6, 512, HD), F32),
            pltpu.VMEM((2, 4, 2, 512, HD), BF16),
            pltpu.VMEM((4, 2, 512, HD), BF16),
            pltpu.VMEM((4, 2, 512, HD), BF16),
            pltpu.VMEM((4, 2, 512, HD), BF16),
            pltpu.VMEM((2, SHIFT, HD), BF16),
            pltpu.VMEM((2, 512, HD), BF16),
            pltpu.VMEM((2, 2, 512, HD), BF16),
            pltpu.VMEM((2, 2, 512, HD), BF16),
            pltpu.VMEM((2, 2, 2, 512, HD), BF16),
            pltpu.VMEM((2, 512, HD), BF16),
            pltpu.VMEM((2, 512, HD), F32),
            pltpu.VMEM((16, 8, 512), F32),
            pltpu.SemaphoreType.DMA((48,)),
            pltpu.SemaphoreType.DMA((48,)),
            pltpu.SemaphoreType.DMA((8,)),
        ],
        compiler_params=pltpu.CompilerParams(
            collective_id=1, has_side_effects=True, vmem_limit_bytes=20 * 2**20
        ),
    )(*operands)


def finish_kernel(
    ck, kg, inv, inner, back, fin,
    out_clean, out_noisy, dq_clean, dk_clean, dv_clean, dq_noisy, dk_noisy, dv_noisy,
    dk, sems,
):
    local = Locals(sems)
    copies = [
        local.start(source, target)
        for source, target in (
            (back.at[0], out_clean),
            (back.at[1], out_noisy),
            (back.at[2], dq_clean),
            (back.at[3], dq_noisy),
            (back.at[4], dk_noisy),
            (back.at[5], dv_noisy),
            (fin.at[1], dv_clean),
        )
    ]
    inverse = jnp.transpose(inv[...])[:, 1:2]
    mean = jnp.transpose(inner[...])[:, :1] / FEAT
    factor = inverse * inverse * inverse * mean
    dk[...] = inverse * (kg[...] * fin[0]) - ck[...].astype(F32) * factor
    copies.append(local.start(dk, dk_clean))
    for copy in copies:
        copy.wait()


def finish_call(*operands):
    return pl.pallas_call(
        finish_kernel,
        name="finish",
        out_shape=tuple(jax.ShapeDtypeStruct((512, 256), F32) for _ in range(8)),
        in_specs=[VMEM] * 6,
        out_specs=(HBM,) * 8,
        scratch_shapes=[pltpu.VMEM((512, 256), F32), pltpu.SemaphoreType.DMA((8,))],
        compiler_params=pltpu.CompilerParams(vmem_limit_bytes=16 * 2**20),
    )(*operands)


def local(
    clean_q, clean_k, clean_v, noisy_q, noisy_k, noisy_v,
    q_gain, k_gain, grad_clean, grad_noisy, owned_blocks, block_doc,
):
    qg = q_gain.reshape(1, 256)
    kg = k_gain.reshape(1, 256)
    blocks = [a.reshape(2, BLK, 2 * HD) for a in (noisy_v, grad_clean, grad_noisy)]
    *pinned, docs = [
        pltpu.with_memory_space_constraint(a, pltpu.HBM)
        for a in (
            clean_q, clean_k, noisy_q, noisy_k, qg, kg, clean_v, *blocks, owned_blocks, block_doc,
        )
    ]
    *parts, inv, ids = gather_call(*pinned)
    grads = attention_call(ids, docs, *parts)
    back, fin, inner = scatter_call(*pinned[:6], inv, *grads)
    return finish_call(clean_k, kg, inv, inner, back, fin)


def solution(mesh):
    placed = (P("ctx", "head"),) * 6 + (P("head"),) * 2 + (P("ctx", "head"),) * 2 + (P("ctx"), P())
    return jax.shard_map(
        local,
        mesh=mesh,
        in_specs=placed,
        out_specs=(P("ctx", "head"),) * 8,
        check_vma=False,
    )
```

```python
import math

import jax
import jax.numpy as jnp
from jax import lax
from jax.experimental import pallas as pl
from jax.experimental.pallas import tpu as pltpu
from jax.sharding import PartitionSpec as P

HD = 128
BLK = 256
FEAT = 2048
EPSILON = 1e-06
NEGATIVE = -1e30
MESH = pl.DeviceIdType.MESH
F32 = jnp.float32
BF16 = jnp.bfloat16
VMEM = pl.BlockSpec(memory_space=pltpu.VMEM)
SMEM = pl.BlockSpec(memory_space=pltpu.SMEM)
ANY = pl.BlockSpec(memory_space=pl.ANY)
HBM = pl.BlockSpec(memory_space=pltpu.HBM)
LAST = (((1,), (1,)), ((), ()))
FIRST = (((0,), (0,)), ((), ()))
PLAIN = (((1,), (0,)), ((), ()))
PACKET = 528
SHIFT = 160
GROUP = 2
SCALE = 1.0 / math.sqrt(HD)
SCALE2 = SCALE * math.log2(math.e)


def dot(a, b, dims):
    return lax.dot_general(a, b, dims, preferred_element_type=F32)


def row_sums(products):
    high = products.astype(BF16)
    low = (products - high.astype(F32)).astype(BF16)
    ones = jnp.ones((8, products.shape[1]), BF16)
    return dot(ones, high, LAST) + dot(ones, low, LAST)


def place():
    ctx = lax.axis_index("ctx")
    head = lax.axis_index("head")
    core = ctx % 2
    y = (ctx // 2) % 2
    x = ctx // 4
    return ctx, head, core, y, x


def ctx_of(x, y, core):
    return (x * 2 + y) * 2 + core


def chip_of(x, y):
    return x * 2 + y


class Copies:
    def __init__(self, send, recv, head):
        self.send, self.recv, self.head = send, recv, head
        self.started = []
        self.count = 0

    def start(self, src, dst, ctx, head=None):
        copy = pltpu.make_async_remote_copy(
            src_ref=src,
            dst_ref=dst,
            send_sem=self.send.at[self.count],
            recv_sem=self.recv.at[self.count],
            device_id={"ctx": ctx, "head": self.head if head is None else head},
            device_id_type=MESH,
        )
        self.count += 1
        copy.start()
        self.started.append(copy)
        return copy


class Locals:
    def __init__(self, sems):
        self.sems = sems
        self.count = 0

    def start(self, src, dst):
        copy = pltpu.make_async_copy(src, dst, self.sems.at[self.count])
        self.count += 1
        copy.start()
        return copy


def enter(ctx, head, others):
    barrier = pltpu.get_barrier_semaphore()
    for other in others:
        pl.semaphore_signal(barrier, inc=1, device_id={"ctx": other, "head": head}, device_id_type=MESH)
    for step in range(1, 8):
        pl.semaphore_signal(
            barrier, inc=1, device_id={"ctx": ctx, "head": (head + step) % 8}, device_id_type=MESH
        )
    pl.semaphore_wait(barrier, 7 + len(others))


def gather_kernel(
    cq_h, ck_h, nq_h, nk_h, qg_h, kg_h, cv, nv, gc, gn, owned,
    kall, vall, qq, gg, kn, vn, own_w, own_peak, own_sum, out_own, grads_t, inv_out, ids_out,
    owned_s, raws, qg, kg, k_packet, normed, sums, send, recv, wide_send, wide_recv, lsem,
):
    ctx, head, core, y, x = place()
    right, left = (x + 1) % 4, (x + 3) % 4
    opposite = (x + 2) % 4
    mine = pl.ds(pl.multiple_of(core * HD, HD), HD)
    theirs = pl.ds(pl.multiple_of((1 - core) * HD, HD), HD)
    partner = ctx_of(x, y, 1 - core)
    local = Locals(lsem)
    owned_load = local.start(owned, owned_s)
    loads = [local.start(ref, raws.at[i]) for i, ref in enumerate((cq_h, ck_h, nq_h, nk_h))]
    loads += [local.start(qg_h, qg), local.start(kg_h, kg)]
    remote = Copies(send, recv, head)
    chips = ((x, 1 - y), (right, y), (left, y))
    enter(ctx, head, [partner] + [ctx_of(*chip, c) for chip in chips for c in range(2)])
    wide = []

    def first_hop(base, columns_of, buf):
        for number, chip in enumerate(chips):
            for target in range(2):
                copy = pltpu.make_async_remote_copy(
                    src_ref=columns_of(target),
                    dst_ref=buf.at[ctx],
                    send_sem=wide_send.at[base + number, target],
                    recv_sem=wide_recv.at[base + number, core],
                    device_id={"ctx": ctx_of(*chip, target), "head": head},
                    device_id_type=MESH,
                )
                copy.start()
                wide.append(copy)

    def arrived(base, number, buf, source):
        chip = ((x, 1 - y), (left, y), (right, y))[number]
        pltpu.make_async_remote_copy(
            src_ref=buf.at[ctx],
            dst_ref=buf.at[ctx_of(*chip, source)],
            send_sem=wide_send.at[base + number, source],
            recv_sem=wide_recv.at[base + number, source],
            device_id={"ctx": partner, "head": head},
            device_id_type=MESH,
        ).wait_recv()

    first_hop(0, lambda target: cv.at[:, target * HD : target * HD + HD], vall)
    v_swap = remote.start(cv.at[:, theirs], vall.at[ctx], partner)
    v_own = local.start(cv.at[:, mine], vall.at[ctx])

    for copy in loads:
        copy.wait()
    row = lax.broadcasted_iota(jnp.int32, (8, 512), 0)
    total = jnp.zeros((8, 512), F32)
    for index in range(4):
        raw = raws[index].astype(F32)
        total = jnp.where(row == index, row_sums(raw * raw), total)
    sums[0] = total
    exchange = [
        remote.start(sums.at[0], sums.at[step], ctx, (head + step) % 8) for step in range(1, 8)
    ]
    owned_load.wait()
    lane = lax.broadcasted_iota(jnp.int32, (16, 2 * HD), 1)
    k_packet[512:, :] = jnp.where(lane % HD == 0, owned_s[0], owned_s[1]).astype(F32).astype(BF16)

    pair = pl.ds(core * 2, 2)
    late, late_own = [], []

    def swap(src, dst):
        late.append(remote.start(src.at[:, :, theirs], dst, partner))
        late_own.append(local.start(src.at[:, :, mine], dst))

    swap(gc, gg.at[pair, 0])
    swap(gn, gg.at[pair, 1])
    swap(nv, vn.at[pair])

    for copy in exchange:
        copy.wait_recv()
    total = sums[0]
    for step in range(1, 8):
        total = total + sums[step]
    inverse = lax.rsqrt(total / FEAT + EPSILON)
    inv_out[...] = inverse
    columns = jnp.transpose(inverse)

    def normalized(index, gain):
        values = raws[index].astype(F32) * columns[:, index : index + 1] * gain[...]
        return values.astype(BF16)

    k_packet[:512, :] = normalized(1, kg)
    first_hop(3, lambda target: k_packet.at[:, target * HD : target * HD + HD], kall)
    k_swap = remote.start(k_packet.at[:, theirs], kall.at[ctx], partner)
    k_own = local.start(k_packet.at[:, mine], kall.at[ctx])
    for index, raw, gain, dst in (
        (0, 0, qg, qq.at[pair, 0]),
        (1, 2, qg, qq.at[pair, 1]),
        (2, 3, kg, kn.at[pair]),
    ):
        normed[index] = normalized(raw, gain).reshape(2, BLK, 2 * HD)
        swap(normed.at[index], dst)

    def slot(buf, sx, sy):
        return buf.at[pl.ds(2 * chip_of(sx, sy), 2)]

    def part(buf, sx, sy, half):
        return buf.at[2 * chip_of(sx, sy) + half]

    def rows_of(sx, sy, half, first, count):
        return vall.at[2 * chip_of(sx, sy) + half, pl.ds(first, count)]

    def spread(view, px, py):
        return remote.start(view, view, ctx_of(px, py, core))

    v_half, v_y, k_half = [], [], []
    sides = ((1, left, right, 0), (2, right, left, 1))
    for number, near, far, half in sides:
        arrived(0, number, vall, half)
        v_half.append(spread(part(vall, near, y, half), far, y))
    arrived(3, 0, kall, 0)
    arrived(3, 0, kall, 1)
    k_right = spread(slot(kall, x, 1 - y), right, y)
    k_left = spread(slot(kall, x, 1 - y), left, y)
    arrived(0, 1, vall, 1)
    v_y.append(spread(slot(vall, left, y), x, 1 - y))

    v_own.wait()
    k_own.wait()
    v_swap.wait_recv()
    k_swap.wait_recv()
    for copy in late_own:
        copy.wait()
    for copy in late:
        copy.wait_recv()

    def own_block(index):
        side, rows = index // 2, slice(index % 2 * BLK, index % 2 * BLK + BLK)
        packet = 2 * chip_of(x, y) + side
        own = ((kall[packet, rows, :], vall[packet, rows, :]), (kn[index], vn[index]))
        for kind, (keys, values) in enumerate(own):
            columns = slice(kind * BLK, kind * BLK + BLK)
            scores = dot(keys, qq[index, kind], LAST) * SCALE2
            peak = jnp.max(scores, axis=0, keepdims=True)
            weights = jnp.exp2(scores - peak)
            low = weights.astype(BF16)
            own_peak[index, :, columns] = jnp.broadcast_to(peak, (8, BLK))
            own_sum[index, :, columns] = jnp.sum(weights.reshape(BLK // 8, 8, BLK), axis=0)
            own_w[index, :, columns] = low
            out_own[index, :, columns] = dot(values, low, FIRST)
            grads_t[index, :, columns] = jnp.transpose(gg[index, kind].astype(F32))

    own_block(0)
    for number, near, far, half in sides:
        arrived(3, number, kall, half)
        k_half.append(spread(part(kall, near, y, half), far, y))
        arrived(3, number, kall, 1 - half)
    own_block(1)
    arrived(0, 2, vall, 0)
    v_y.append(spread(slot(vall, right, y), x, 1 - y))
    own_block(2)
    v_half[0].wait_recv()
    v_half[1].wait_recv()
    v_y[0].wait_recv()
    v_far = [spread(rows_of(left, 1 - y, 0, 0, SHIFT), right, y)]
    for half in range(2):
        v_y.append(spread(rows_of(opposite, y, half, SHIFT, 512 - SHIFT), x, 1 - y))
    k_right.wait_recv()
    k_half.append(spread(part(kall, left, 1 - y, 0), right, y))
    k_left.wait_recv()
    k_half.append(spread(part(kall, right, 1 - y, 1), left, y))
    own_block(3)
    v_y[1].wait_recv()
    v_far.append(spread(rows_of(right, 1 - y, 1, 0, SHIFT), left, y))
    arrived(0, 0, vall, 0)
    arrived(0, 0, vall, 1)
    for copy in v_y[2:] + v_far + k_half:
        copy.wait_recv()
    names = jnp.max(kall[:, 512:, :].astype(F32), axis=1)
    ids_out[...] = names.astype(jnp.int32)
    for copy in remote.started + wide:
        copy.wait_send()


def gather_call(cq, ck, nq, nk, qg, kg, cv, nv, gc, gn, owned):
    return pl.pallas_call(
        gather_kernel,
        name="gather_keys",
        out_shape=(
            jax.ShapeDtypeStruct((16, PACKET, HD), BF16),
            jax.ShapeDtypeStruct((16, 512, HD), BF16),
            jax.ShapeDtypeStruct((4, 2, BLK, HD), BF16),
            jax.ShapeDtypeStruct((4, 2, BLK, HD), BF16),
            jax.ShapeDtypeStruct((4, BLK, HD), BF16),
            jax.ShapeDtypeStruct((4, BLK, HD), BF16),
            jax.ShapeDtypeStruct((4, BLK, 2 * BLK), BF16),
            jax.ShapeDtypeStruct((4, 8, 2 * BLK), F32),
            jax.ShapeDtypeStruct((4, 8, 2 * BLK), F32),
            jax.ShapeDtypeStruct((4, HD, 2 * BLK), F32),
            jax.ShapeDtypeStruct((4, HD, 2 * BLK), F32),
            jax.ShapeDtypeStruct((8, 512), F32),
            jax.ShapeDtypeStruct((16, HD), jnp.int32),
        ),
        in_specs=[HBM] * 11,
        out_specs=(VMEM,) * 13,
        scratch_shapes=[
            pltpu.SMEM((2,), jnp.int32),
            pltpu.VMEM((4, 512, 256), BF16),
            pltpu.VMEM((1, 256), F32),
            pltpu.VMEM((1, 256), F32),
            pltpu.VMEM((PACKET, 256), BF16),
            pltpu.VMEM((3, 2, BLK, 2 * HD), BF16),
            pltpu.VMEM((8, 8, 512), F32),
            pltpu.SemaphoreType.DMA((32,)),
            pltpu.SemaphoreType.DMA((32,)),
            pltpu.SemaphoreType.DMA((6, 2)),
            pltpu.SemaphoreType.DMA((6, 2)),
            pltpu.SemaphoreType.DMA((16,)),
        ],
        compiler_params=pltpu.CompilerParams(
            collective_id=0, has_side_effects=True, vmem_limit_bytes=20 * 2**20
        ),
    )(cq, ck, nq, nk, qg, kg, cv, nv, gc, gn, owned)


def attention_kernel(
    ids, docs, kall, vall, qq, gg, kn, vn, own_w, own_peak, own_sum, out_own, grads_t,
    out_t, dq_t, dk_noisy, dv_noisy, dk_acc, dv_acc,
    where_is, first_of, pair_query, pair_key, pair_bias,
    scores, weights, scaled_grads, peaks, sums, decays, deltas,
):
    chip = lax.axis_index("ctx") // 2

    def clear(stored):
        dk_acc[stored] = jnp.zeros((BLK, HD), F32)
        dv_acc[stored] = jnp.zeros((BLK, HD), F32)

    def begin_of(block, begin):
        clear(block)
        where_is[ids[block // 2, block % 2]] = block
        begin = jnp.where(docs[block] == docs[jnp.maximum(block - 1, 0)], begin, block)
        first_of[block] = begin
        return begin

    lax.fori_loop(0, 32, begin_of, 0)

    def key_rows(buf, stored):
        start = pl.multiple_of((stored % 2) * BLK, BLK)
        return buf[stored // 2, pl.ds(start, BLK), :]

    def key_pair(buf, pair):
        return jnp.concatenate(
            [key_rows(buf, pair_key[2 * pair]), key_rows(buf, pair_key[2 * pair + 1])], axis=0
        )

    def both(ref, index):
        return ref[index].reshape(2 * BLK, HD)

    def tops(values):
        return jnp.max(values.reshape(-1, 8, values.shape[1]), axis=0)

    def totals(values):
        return jnp.sum(values.reshape(-1, 8, values.shape[1]), axis=0)

    @pl.loop(0, 2)
    def _(side):
        count = 0
        for half in range(2):
            block = ids[chip * 2 + side, half]
            begin = first_of[block]

            def enlist(pair, count, half=half, block=block, begin=begin):
                key = begin + 2 * pair
                pair_query[count] = half
                pair_key[2 * count] = where_is[key]
                pair_key[2 * count + 1] = where_is[jnp.minimum(key + 1, block - 1)]
                pair_bias[count] = jnp.where(key + 1 < block, 0, 1)
                return count + 1

            count = lax.fori_loop(0, (block - begin + 1) // 2, enlist, count)

        def over_pairs(body):
            groups = count // GROUP

            @pl.loop(0, groups)
            def _(group):
                body([group * GROUP + i for i in range(GROUP)])

            @pl.loop(groups * GROUP, count)
            def _(pair):
                body([pair])

        first = 2 * side
        for half in range(2):
            peaks[half] = own_peak[first + half]

        def score_pairs(pairs):
            queries = [pair_query[pair] for pair in pairs]
            values = [
                dot(key_pair(kall, pair), both(qq, first + query), LAST)
                for pair, query in zip(pairs, queries)
            ]
            for pair, query, value in zip(pairs, queries, values):
                scores[pair] = value
                peaks[query] = jnp.maximum(peaks[query], tops(value) * SCALE2)

        over_pairs(score_pairs)

        for half in range(2):
            index = first + half
            peak = jnp.max(peaks[half], axis=0, keepdims=True)
            decay = jnp.exp2(own_peak[index] - peak)
            peaks[half] = jnp.broadcast_to(peak, (8, 2 * BLK))
            decays[half] = decay
            sums[half] = own_sum[index] * decay
            out_t[index] = out_own[index] * decay[:1]

        def value_pairs(pairs):
            queries = [pair_query[pair] for pair in pairs]
            outs, parts = [], []
            for pair, query in zip(pairs, queries):
                peak = peaks[query, :1]
                hidden = peak + jnp.where(pair_bias[pair] == 1, jnp.inf, 0.0)
                upper = jnp.exp2(scores[pair, :BLK] * SCALE2 - peak)
                lower = jnp.exp2(scores[pair, BLK:] * SCALE2 - hidden)
                low = jnp.concatenate([upper.astype(BF16), lower.astype(BF16)], axis=0)
                weights[pair] = low
                outs.append(dot(key_pair(vall, pair), low, FIRST))
                parts.append(totals(upper) + totals(lower))
            for query, out, part in zip(queries, outs, parts):
                sums[query] += part
                out_t[first + query] += out

        over_pairs(value_pairs)

        for half in range(2):
            index = first + half
            stored_own = chip * 4 + index
            inverse_sum = 1.0 / jnp.sum(sums[half], axis=0, keepdims=True)
            out = out_t[index] * inverse_sum
            out_t[index] = out
            grad_rows = (grads_t[index] * inverse_sum).astype(BF16).astype(F32)
            delta = jnp.sum(out * grad_rows, axis=0, keepdims=True)
            deltas[half] = jnp.broadcast_to(delta, (8, 2 * BLK))
            grads = jnp.transpose(grad_rows).astype(BF16)
            scaled_grads[half] = grads
            own = own_w[index].astype(F32) * decays[half, :1]
            own_low = own.astype(BF16)
            own_dp = jnp.concatenate(
                [
                    dot(key_rows(vall, stored_own), grads[:BLK], LAST),
                    dot(vn[index], grads[BLK:], LAST),
                ],
                axis=1,
            )
            own_ds = (own * (own_dp - delta)).astype(BF16)
            dv_acc[stored_own] += dot(own_low[:, :BLK], grads[:BLK], PLAIN)
            dk_acc[stored_own] += dot(own_ds[:, :BLK], qq[index, 0], PLAIN)
            dv_noisy[index] = dot(own_low[:, BLK:], grads[BLK:], PLAIN)
            dk_noisy[index] = dot(own_ds[:, BLK:], qq[index, 1], PLAIN) * SCALE
            dq_t[index, :, :BLK] = dot(key_rows(kall, stored_own), own_ds[:, :BLK], FIRST)
            dq_t[index, :, BLK:] = dot(kn[index], own_ds[:, BLK:], FIRST)

        def grad_pairs(pairs):
            queries = [pair_query[pair] for pair in pairs]
            results = []
            for pair, query in zip(pairs, queries):
                low = weights[pair]
                dp = dot(key_pair(vall, pair), scaled_grads[query], LAST)
                ds = (low.astype(F32) * (dp - deltas[query, :1])).astype(BF16)
                results.append(
                    (
                        dot(low, scaled_grads[query], PLAIN),
                        dot(ds, both(qq, first + query), PLAIN),
                        dot(key_pair(kall, pair), ds, FIRST),
                    )
                )
            for pair, query, (dv, dk, dq) in zip(pairs, queries, results):
                for place in range(2):
                    rows = slice(place * BLK, place * BLK + BLK)
                    dv_acc[pair_key[2 * pair + place]] += dv[rows]
                    dk_acc[pair_key[2 * pair + place]] += dk[rows]
                dq_t[first + query] += dq

        over_pairs(grad_pairs)


def attention_call(ids, docs, *parts):
    return pl.pallas_call(
        attention_kernel,
        name="attention",
        out_shape=(
            jax.ShapeDtypeStruct((4, HD, 2 * BLK), F32),
            jax.ShapeDtypeStruct((4, HD, 2 * BLK), F32),
            jax.ShapeDtypeStruct((4, BLK, HD), F32),
            jax.ShapeDtypeStruct((4, BLK, HD), F32),
            jax.ShapeDtypeStruct((32, BLK, HD), F32),
            jax.ShapeDtypeStruct((32, BLK, HD), F32),
        ),
        in_specs=[SMEM, SMEM] + [VMEM] * 11,
        out_specs=(VMEM,) * 6,
        scratch_shapes=[
            pltpu.SMEM((32,), jnp.int32),
            pltpu.SMEM((32,), jnp.int32),
            pltpu.SMEM((32,), jnp.int32),
            pltpu.SMEM((32,), jnp.int32),
            pltpu.SMEM((16,), jnp.int32),
            pltpu.VMEM((16, 2 * BLK, 2 * BLK), F32),
            pltpu.VMEM((16, 2 * BLK, 2 * BLK), BF16),
            pltpu.VMEM((2, 2 * BLK, HD), BF16),
            pltpu.VMEM((2, 8, 2 * BLK), F32),
            pltpu.VMEM((2, 8, 2 * BLK), F32),
            pltpu.VMEM((2, 8, 2 * BLK), F32),
            pltpu.VMEM((2, 8, 2 * BLK), F32),
        ],
        compiler_params=pltpu.CompilerParams(vmem_limit_bytes=34 * 2**20),
    )(ids, docs, *parts)


def scatter_kernel(
    cq_h, ck_h, nq_h, nk_h, qg_h, kg_h, inv, out_t, dq_t, dk_noisy, dv_noisy, dk, dv,
    back, fin, inner_out,
    raws, qg, kg, stage, k_out, v_out, x_out, vy, vq, vh, vx, kh, kx, ky, away, sums,
    send, recv, lsem,
):
    ctx, head, core, y, x = place()
    right, left = (x + 1) % 4, (x + 3) % 4
    partner = ctx_of(x, y, 1 - core)
    to_right, to_left = ctx_of(right, y, core), ctx_of(left, y, core)
    to_y = ctx_of(x, 1 - y, core)
    score_scale = 1.0 / math.sqrt(HD)
    own_columns = pl.ds(pl.multiple_of(core * HD, HD), HD)
    local = Locals(lsem)
    loads = [local.start(ref, raws.at[i]) for i, ref in enumerate((cq_h, ck_h, nq_h, nk_h))]
    loads += [local.start(qg_h, qg), local.start(kg_h, kg)]
    cq, ck, nq, nk = [raws.at[i] for i in range(4)]
    remote = Copies(send, recv, head)

    def mine(ref, step, row, half):
        chip = chip_of((x + step) % 4, y if row == 0 else 1 - y)
        return ref[pl.ds(chip * 4 + half * 2, 2)].reshape(512, HD)

    def pack_v(step):
        for half in range(2):
            v_out[step, half] = mine(dv, step, 1, half).astype(BF16)

    def pack_k(row, step, half, *others):
        value = mine(dk, step, row, half) * score_scale
        for other in others:
            value = value + other[...].astype(F32)
        k_out[row, step, half] = value.astype(BF16)

    pack_v(2)
    pack_k(1, 2, 0)
    pack_k(1, 2, 1)
    enter(ctx, head, [partner, to_right, to_left, to_y])
    first, rest = pl.ds(0, SHIFT), pl.ds(SHIFT, 512 - SHIFT)
    v_far = [
        remote.start(v_out.at[2, 0, first], vq.at[0], to_left),
        remote.start(v_out.at[2, 1, first], vq.at[1], to_right),
    ]
    v_opposite = [
        remote.start(v_out.at[2, half, rest], vy.at[2, half, rest], to_y) for half in range(2)
    ]
    k_half = {}

    def start_half(row):
        k_half[row, 0] = remote.start(k_out.at[row, 2, 0], kh.at[row, 0], to_left)
        k_half[row, 1] = remote.start(k_out.at[row, 2, 1], kh.at[row, 1], to_right)

    start_half(1)
    pack_k(0, 2, 0)
    pack_k(0, 2, 1)
    start_half(0)
    v_y = {}

    def send_v(step, half):
        pack_v(step)
        if half is not None:
            v_far[half].wait_recv()
            v_out[step, half, :SHIFT] = (
                mine(dv, step, 1, half)[:SHIFT] + vq[half].astype(F32)
            ).astype(BF16)
        v_y[step] = remote.start(v_out.at[step], vy.at[step], to_y)

    send_v(3, 0)
    for row in (1, 0):
        pack_k(row, 3, 1)
        pack_k(row, 1, 0)

    def landing(i):
        return back.at[i, :, own_columns]

    swap = {}
    dk_pair, dv_pair = [
        [ref.at[pl.ds(c * 2, 2)] for c in (core, 1 - core)] for ref in (dk_noisy, dv_noisy)
    ]

    def turn(index, ref, first, factor):
        for part in range(2):
            rows = slice(part * BLK, part * BLK + BLK)
            for c, own in ((core, True), (1 - core, False)):
                values = jnp.transpose(ref[2 * c + part]) * factor
                for kind in range(2):
                    if own:
                        back[first + kind, rows, own_columns] = values[kind * BLK : kind * BLK + BLK]
                    else:
                        stage[first + kind, rows, :] = values[kind * BLK : kind * BLK + BLK]
        for i in (first, first + 1):
            swap[i] = remote.start(stage.at[i], landing(i), partner)

    def turn_noisy(ref, i):
        for part in range(2):
            rows = slice(part * BLK, part * BLK + BLK)
            back[i, rows, own_columns] = ref[2 * core + part]
            stage[i, rows, :] = ref[2 * (1 - core) + part]
        swap[i] = remote.start(stage.at[i], landing(i), partner)

    turn(0, dq_t, 2, score_scale)
    turn_noisy(dk_noisy, 4)

    k_x = {}

    def k_forward(row):
        k_half[row, 0].wait_recv()
        pack_k(row, 3, 0, kh.at[row, 0])
        k_x[row, 0] = remote.start(k_out.at[row, 3], kx.at[row, 0], to_left)
        k_half[row, 1].wait_recv()
        pack_k(row, 1, 1, kh.at[row, 1])
        k_x[row, 1] = remote.start(k_out.at[row, 1], kx.at[row, 1], to_right)

    k_forward(1)

    row = lax.broadcasted_iota(jnp.int32, (8, 512), 0)

    def inner(raw, gain, values):
        return row_sums(raw[...].astype(F32) * (gain[...] * values))

    for copy in loads:
        copy.wait()
    for i in (2, 3, 4):
        swap[i].wait_recv()
    total = jnp.zeros((8, 512), F32)
    normal = ((0, cq, qg, 2), (2, nq, qg, 3), (3, nk, kg, 4))
    for index, raw, gain, i in normal:
        total = jnp.where(row == index, inner(raw, gain, back[i]), total)
    sums[0] = total
    exchange = [
        remote.start(sums.at[0], sums.at[step], ctx, (head + step) % 8) for step in range(1, 8)
    ]

    def pack_x(step, half, *others):
        value = mine(dv, step, 0, half)
        for other in others:
            value = value + other[...].astype(F32)
        x_out[step, half] = value.astype(BF16)

    v_half = []
    for half, target in ((0, to_left), (1, to_right)):
        v_opposite[half].wait_recv()
        pack_x(2, half)
        x_out[2, half, SHIFT:] = (
            mine(dv, 2, 0, half)[SHIFT:] + vy[2, half, SHIFT:].astype(F32)
        ).astype(BF16)
        v_half.append(remote.start(x_out.at[2, half], vh.at[half], target))
    send_v(1, 1)
    k_forward(0)
    turn(0, out_t, 0, 1.0)
    turn_noisy(dv_noisy, 5)
    k_x[1, 0].wait_recv()
    k_x[1, 1].wait_recv()
    for half in range(2):
        pack_k(1, 0, half, kx.at[1, 0, half], kx.at[1, 1, half])
    k_y = remote.start(k_out.at[1, 0], ky, to_y)
    send_v(0, None)

    v_y[3].wait_recv()
    v_half[0].wait_recv()
    pack_x(3, 0, vy.at[3, 0], vh.at[0])
    pack_x(3, 1, vy.at[3, 1])
    v_x = [remote.start(x_out.at[3], vx.at[0], to_left)]
    v_y[1].wait_recv()
    v_half[1].wait_recv()
    pack_x(1, 0, vy.at[1, 0])
    pack_x(1, 1, vy.at[1, 1], vh.at[1])
    v_x.append(remote.start(x_out.at[1], vx.at[1], to_right))

    for copy in exchange:
        copy.wait_recv()
    total = sums[0]
    for step in range(1, 8):
        total = total + sums[step]
    inverses = jnp.transpose(inv[...])
    means = jnp.transpose(total) / FEAT
    for index, raw, gain, i in normal:
        inverse = inverses[:, index : index + 1]
        factor = inverse * inverse * inverse * means[:, index : index + 1]
        back[i] = inverse * (gain[...] * back[i]) - raw[...].astype(F32) * factor

    def finish(index, ref, factor, terms):
        values = []
        for half in range(2):
            value = mine(ref, 0, 0, half) * factor
            for term in terms:
                value = value + term[half].astype(F32)
            values.append(value)
        first_core = core == 0
        fin[index, :, own_columns] = jnp.where(first_core, values[0], values[1])
        away[index] = jnp.where(first_core, values[1], values[0])
        return remote.start(away.at[index], fin.at[index, :, own_columns], partner)

    k_x[0, 0].wait_recv()
    k_x[0, 1].wait_recv()
    k_y.wait_recv()
    k_fin = finish(0, dk, score_scale, (kx.at[0, 0], kx.at[0, 1], ky))
    k_fin.wait_recv()
    sums[8] = inner(ck, kg, fin[0])
    k_exchange = [
        remote.start(sums.at[8], sums.at[8 + step], ctx, (head + step) % 8) for step in range(1, 8)
    ]
    v_y[0].wait_recv()
    v_x[0].wait_recv()
    v_x[1].wait_recv()
    v_fin = finish(1, dv, 1.0, (vy.at[0], vx.at[0], vx.at[1]))

    for copy in k_exchange:
        copy.wait_recv()
    total = sums[8]
    for step in range(1, 8):
        total = total + sums[8 + step]
    inner_out[...] = total
    v_fin.wait_recv()
    for i in (0, 1, 5):
        swap[i].wait_recv()
    for copy in remote.started:
        copy.wait_send()


def scatter_call(*operands):
    return pl.pallas_call(
        scatter_kernel,
        name="scatter_grads",
        out_shape=(
            jax.ShapeDtypeStruct((6, 512, 256), F32),
            jax.ShapeDtypeStruct((2, 512, 256), F32),
            jax.ShapeDtypeStruct((8, 512), F32),
        ),
        in_specs=[HBM] * 6 + [VMEM] * 7,
        out_specs=(VMEM, VMEM, VMEM),
        scratch_shapes=[
            pltpu.VMEM((4, 512, 256), BF16),
            pltpu.VMEM((1, 256), F32),
            pltpu.VMEM((1, 256), F32),
            pltpu.VMEM((6, 512, HD), F32),
            pltpu.VMEM((2, 4, 2, 512, HD), BF16),
            pltpu.VMEM((4, 2, 512, HD), BF16),
            pltpu.VMEM((4, 2, 512, HD), BF16),
            pltpu.VMEM((4, 2, 512, HD), BF16),
            pltpu.VMEM((2, SHIFT, HD), BF16),
            pltpu.VMEM((2, 512, HD), BF16),
            pltpu.VMEM((2, 2, 512, HD), BF16),
            pltpu.VMEM((2, 2, 512, HD), BF16),
            pltpu.VMEM((2, 2, 2, 512, HD), BF16),
            pltpu.VMEM((2, 512, HD), BF16),
            pltpu.VMEM((2, 512, HD), F32),
            pltpu.VMEM((16, 8, 512), F32),
            pltpu.SemaphoreType.DMA((48,)),
            pltpu.SemaphoreType.DMA((48,)),
            pltpu.SemaphoreType.DMA((8,)),
        ],
        compiler_params=pltpu.CompilerParams(
            collective_id=1, has_side_effects=True, vmem_limit_bytes=20 * 2**20
        ),
    )(*operands)


def finish_kernel(
    ck, kg, inv, inner, back, fin,
    out_clean, out_noisy, dq_clean, dk_clean, dv_clean, dq_noisy, dk_noisy, dv_noisy,
    dk, sems,
):
    local = Locals(sems)
    copies = [
        local.start(source, target)
        for source, target in (
            (back.at[0], out_clean),
            (back.at[1], out_noisy),
            (back.at[2], dq_clean),
            (back.at[3], dq_noisy),
            (back.at[4], dk_noisy),
            (back.at[5], dv_noisy),
            (fin.at[1], dv_clean),
        )
    ]
    inverse = jnp.transpose(inv[...])[:, 1:2]
    mean = jnp.transpose(inner[...])[:, :1] / FEAT
    factor = inverse * inverse * inverse * mean
    dk[...] = inverse * (kg[...] * fin[0]) - ck[...].astype(F32) * factor
    copies.append(local.start(dk, dk_clean))
    for copy in copies:
        copy.wait()


def finish_call(*operands):
    return pl.pallas_call(
        finish_kernel,
        name="finish",
        out_shape=tuple(jax.ShapeDtypeStruct((512, 256), F32) for _ in range(8)),
        in_specs=[VMEM] * 6,
        out_specs=(HBM,) * 8,
        scratch_shapes=[pltpu.VMEM((512, 256), F32), pltpu.SemaphoreType.DMA((8,))],
        compiler_params=pltpu.CompilerParams(vmem_limit_bytes=16 * 2**20),
    )(*operands)


def local(
    clean_q, clean_k, clean_v, noisy_q, noisy_k, noisy_v,
    q_gain, k_gain, grad_clean, grad_noisy, owned_blocks, block_doc,
):
    qg = q_gain.reshape(1, 256)
    kg = k_gain.reshape(1, 256)
    blocks = [a.reshape(2, BLK, 2 * HD) for a in (noisy_v, grad_clean, grad_noisy)]
    *pinned, docs = [
        pltpu.with_memory_space_constraint(a, pltpu.HBM)
        for a in (
            clean_q, clean_k, noisy_q, noisy_k, qg, kg, clean_v, *blocks, owned_blocks, block_doc,
        )
    ]
    *parts, inv, ids = gather_call(*pinned)
    grads = attention_call(ids, docs, *parts)
    back, fin, inner = scatter_call(*pinned[:6], inv, *grads)
    return finish_call(clean_k, kg, inv, inner, back, fin)


def solution(mesh):
    placed = (P("ctx", "head"),) * 6 + (P("head"),) * 2 + (P("ctx", "head"),) * 2 + (P("ctx"), P())
    return jax.shard_map(
        local,
        mesh=mesh,
        in_specs=placed,
        out_specs=(P("ctx", "head"),) * 8,
        check_vma=False,
    )
```

```python
import math

import jax
import jax.numpy as jnp
from jax import lax
from jax.experimental import pallas as pl
from jax.experimental.pallas import tpu as pltpu
from jax.sharding import PartitionSpec as P

HD = 128
BLK = 256
FEAT = 2048
EPSILON = 1e-06
NEGATIVE = -1e30
MESH = pl.DeviceIdType.MESH
F32 = jnp.float32
BF16 = jnp.bfloat16
VMEM = pl.BlockSpec(memory_space=pltpu.VMEM)
SMEM = pl.BlockSpec(memory_space=pltpu.SMEM)
ANY = pl.BlockSpec(memory_space=pl.ANY)
HBM = pl.BlockSpec(memory_space=pltpu.HBM)
LAST = (((1,), (1,)), ((), ()))
FIRST = (((0,), (0,)), ((), ()))
PLAIN = (((1,), (0,)), ((), ()))
PACKET = 528
SHIFT = 160
GROUP = 1
SCALE = 1.0 / math.sqrt(HD)
SCALE2 = SCALE * math.log2(math.e)


def dot(a, b, dims):
    return lax.dot_general(a, b, dims, preferred_element_type=F32)


def row_sums(products):
    high = products.astype(BF16)
    low = (products - high.astype(F32)).astype(BF16)
    ones = jnp.ones((8, products.shape[1]), BF16)
    return dot(ones, high, LAST) + dot(ones, low, LAST)


def place():
    ctx = lax.axis_index("ctx")
    head = lax.axis_index("head")
    core = ctx % 2
    y = (ctx // 2) % 2
    x = ctx // 4
    return ctx, head, core, y, x


def ctx_of(x, y, core):
    return (x * 2 + y) * 2 + core


def chip_of(x, y):
    return x * 2 + y


class Copies:
    def __init__(self, send, recv, head):
        self.send, self.recv, self.head = send, recv, head
        self.started = []
        self.count = 0

    def start(self, src, dst, ctx, head=None):
        copy = pltpu.make_async_remote_copy(
            src_ref=src,
            dst_ref=dst,
            send_sem=self.send.at[self.count],
            recv_sem=self.recv.at[self.count],
            device_id={"ctx": ctx, "head": self.head if head is None else head},
            device_id_type=MESH,
        )
        self.count += 1
        copy.start()
        self.started.append(copy)
        return copy


class Locals:
    def __init__(self, sems):
        self.sems = sems
        self.count = 0

    def start(self, src, dst):
        copy = pltpu.make_async_copy(src, dst, self.sems.at[self.count])
        self.count += 1
        copy.start()
        return copy


def enter(ctx, head, others):
    barrier = pltpu.get_barrier_semaphore()
    for other in others:
        pl.semaphore_signal(barrier, inc=1, device_id={"ctx": other, "head": head}, device_id_type=MESH)
    for step in range(1, 8):
        pl.semaphore_signal(
            barrier, inc=1, device_id={"ctx": ctx, "head": (head + step) % 8}, device_id_type=MESH
        )
    pl.semaphore_wait(barrier, 7 + len(others))


def gather_kernel(
    cq_h, ck_h, nq_h, nk_h, qg_h, kg_h, cv, nv, gc, gn, owned,
    kall, vall, qq, gg, kn, vn, own_w, own_peak, own_sum, out_own, grads_t, inv_out, ids_out,
    owned_s, raws, qg, kg, k_packet, normed, sums, send, recv, wide_send, wide_recv, lsem,
):
    ctx, head, core, y, x = place()
    right, left = (x + 1) % 4, (x + 3) % 4
    opposite = (x + 2) % 4
    mine = pl.ds(pl.multiple_of(core * HD, HD), HD)
    theirs = pl.ds(pl.multiple_of((1 - core) * HD, HD), HD)
    partner = ctx_of(x, y, 1 - core)
    local = Locals(lsem)
    owned_load = local.start(owned, owned_s)
    loads = [local.start(ref, raws.at[i]) for i, ref in enumerate((cq_h, ck_h, nq_h, nk_h))]
    loads += [local.start(qg_h, qg), local.start(kg_h, kg)]
    remote = Copies(send, recv, head)
    chips = ((x, 1 - y), (right, y), (left, y))
    enter(ctx, head, [partner] + [ctx_of(*chip, c) for chip in chips for c in range(2)])
    wide = []

    def first_hop(base, columns_of, buf):
        for number, chip in enumerate(chips):
            for target in range(2):
                copy = pltpu.make_async_remote_copy(
                    src_ref=columns_of(target),
                    dst_ref=buf.at[ctx],
                    send_sem=wide_send.at[base + number, target],
                    recv_sem=wide_recv.at[base + number, core],
                    device_id={"ctx": ctx_of(*chip, target), "head": head},
                    device_id_type=MESH,
                )
                copy.start()
                wide.append(copy)

    def arrived(base, number, buf, source):
        chip = ((x, 1 - y), (left, y), (right, y))[number]
        pltpu.make_async_remote_copy(
            src_ref=buf.at[ctx],
            dst_ref=buf.at[ctx_of(*chip, source)],
            send_sem=wide_send.at[base + number, source],
            recv_sem=wide_recv.at[base + number, source],
            device_id={"ctx": partner, "head": head},
            device_id_type=MESH,
        ).wait_recv()

    first_hop(0, lambda target: cv.at[:, target * HD : target * HD + HD], vall)
    v_swap = remote.start(cv.at[:, theirs], vall.at[ctx], partner)
    v_own = local.start(cv.at[:, mine], vall.at[ctx])

    for copy in loads:
        copy.wait()
    row = lax.broadcasted_iota(jnp.int32, (8, 512), 0)
    total = jnp.zeros((8, 512), F32)
    for index in range(4):
        raw = raws[index].astype(F32)
        total = jnp.where(row == index, row_sums(raw * raw), total)
    sums[0] = total
    exchange = [
        remote.start(sums.at[0], sums.at[step], ctx, (head + step) % 8) for step in range(1, 8)
    ]
    owned_load.wait()
    lane = lax.broadcasted_iota(jnp.int32, (16, 2 * HD), 1)
    k_packet[512:, :] = jnp.where(lane % HD == 0, owned_s[0], owned_s[1]).astype(F32).astype(BF16)

    pair = pl.ds(core * 2, 2)
    late, late_own = [], []

    def swap(src, dst):
        late.append(remote.start(src.at[:, :, theirs], dst, partner))
        late_own.append(local.start(src.at[:, :, mine], dst))

    swap(gc, gg.at[pair, 0])
    swap(gn, gg.at[pair, 1])
    swap(nv, vn.at[pair])

    for copy in exchange:
        copy.wait_recv()
    total = sums[0]
    for step in range(1, 8):
        total = total + sums[step]
    inverse = lax.rsqrt(total / FEAT + EPSILON)
    inv_out[...] = inverse
    columns = jnp.transpose(inverse)

    def normalized(index, gain):
        values = raws[index].astype(F32) * columns[:, index : index + 1] * gain[...]
        return values.astype(BF16)

    k_packet[:512, :] = normalized(1, kg)
    first_hop(3, lambda target: k_packet.at[:, target * HD : target * HD + HD], kall)
    k_swap = remote.start(k_packet.at[:, theirs], kall.at[ctx], partner)
    k_own = local.start(k_packet.at[:, mine], kall.at[ctx])
    for index, raw, gain, dst in (
        (0, 0, qg, qq.at[pair, 0]),
        (1, 2, qg, qq.at[pair, 1]),
        (2, 3, kg, kn.at[pair]),
    ):
        normed[index] = normalized(raw, gain).reshape(2, BLK, 2 * HD)
        swap(normed.at[index], dst)

    def slot(buf, sx, sy):
        return buf.at[pl.ds(2 * chip_of(sx, sy), 2)]

    def part(buf, sx, sy, half):
        return buf.at[2 * chip_of(sx, sy) + half]

    def rows_of(sx, sy, half, first, count):
        return vall.at[2 * chip_of(sx, sy) + half, pl.ds(first, count)]

    def spread(view, px, py):
        return remote.start(view, view, ctx_of(px, py, core))

    v_half, v_y, k_half = [], [], []
    sides = ((1, left, right, 0), (2, right, left, 1))
    for number, near, far, half in sides:
        arrived(0, number, vall, half)
        v_half.append(spread(part(vall, near, y, half), far, y))
    arrived(3, 0, kall, 0)
    arrived(3, 0, kall, 1)
    k_right = spread(slot(kall, x, 1 - y), right, y)
    k_left = spread(slot(kall, x, 1 - y), left, y)
    arrived(0, 1, vall, 1)
    v_y.append(spread(slot(vall, left, y), x, 1 - y))

    v_own.wait()
    k_own.wait()
    v_swap.wait_recv()
    k_swap.wait_recv()
    for copy in late_own:
        copy.wait()
    for copy in late:
        copy.wait_recv()

    def own_block(index):
        side, rows = index // 2, slice(index % 2 * BLK, index % 2 * BLK + BLK)
        packet = 2 * chip_of(x, y) + side
        own = ((kall[packet, rows, :], vall[packet, rows, :]), (kn[index], vn[index]))
        for kind, (keys, values) in enumerate(own):
            columns = slice(kind * BLK, kind * BLK + BLK)
            scores = dot(keys, qq[index, kind], LAST) * SCALE2
            peak = jnp.max(scores, axis=0, keepdims=True)
            weights = jnp.exp2(scores - peak)
            low = weights.astype(BF16)
            own_peak[index, :, columns] = jnp.broadcast_to(peak, (8, BLK))
            own_sum[index, :, columns] = jnp.sum(weights.reshape(BLK // 8, 8, BLK), axis=0)
            own_w[index, :, columns] = low
            out_own[index, :, columns] = dot(values, low, FIRST)
            grads_t[index, :, columns] = jnp.transpose(gg[index, kind].astype(F32))

    own_block(0)
    for number, near, far, half in sides:
        arrived(3, number, kall, half)
        k_half.append(spread(part(kall, near, y, half), far, y))
        arrived(3, number, kall, 1 - half)
    own_block(1)
    arrived(0, 2, vall, 0)
    v_y.append(spread(slot(vall, right, y), x, 1 - y))
    own_block(2)
    v_half[0].wait_recv()
    v_half[1].wait_recv()
    v_y[0].wait_recv()
    v_far = [spread(rows_of(left, 1 - y, 0, 0, SHIFT), right, y)]
    for half in range(2):
        v_y.append(spread(rows_of(opposite, y, half, SHIFT, 512 - SHIFT), x, 1 - y))
    k_right.wait_recv()
    k_half.append(spread(part(kall, left, 1 - y, 0), right, y))
    k_left.wait_recv()
    k_half.append(spread(part(kall, right, 1 - y, 1), left, y))
    own_block(3)
    v_y[1].wait_recv()
    v_far.append(spread(rows_of(right, 1 - y, 1, 0, SHIFT), left, y))
    arrived(0, 0, vall, 0)
    arrived(0, 0, vall, 1)
    for copy in v_y[2:] + v_far + k_half:
        copy.wait_recv()
    names = jnp.max(kall[:, 512:, :].astype(F32), axis=1)
    ids_out[...] = names.astype(jnp.int32)
    for copy in remote.started + wide:
        copy.wait_send()


def gather_call(cq, ck, nq, nk, qg, kg, cv, nv, gc, gn, owned):
    return pl.pallas_call(
        gather_kernel,
        name="gather_keys",
        out_shape=(
            jax.ShapeDtypeStruct((16, PACKET, HD), BF16),
            jax.ShapeDtypeStruct((16, 512, HD), BF16),
            jax.ShapeDtypeStruct((4, 2, BLK, HD), BF16),
            jax.ShapeDtypeStruct((4, 2, BLK, HD), BF16),
            jax.ShapeDtypeStruct((4, BLK, HD), BF16),
            jax.ShapeDtypeStruct((4, BLK, HD), BF16),
            jax.ShapeDtypeStruct((4, BLK, 2 * BLK), BF16),
            jax.ShapeDtypeStruct((4, 8, 2 * BLK), F32),
            jax.ShapeDtypeStruct((4, 8, 2 * BLK), F32),
            jax.ShapeDtypeStruct((4, HD, 2 * BLK), F32),
            jax.ShapeDtypeStruct((4, HD, 2 * BLK), F32),
            jax.ShapeDtypeStruct((8, 512), F32),
            jax.ShapeDtypeStruct((16, HD), jnp.int32),
        ),
        in_specs=[HBM] * 11,
        out_specs=(VMEM,) * 13,
        scratch_shapes=[
            pltpu.SMEM((2,), jnp.int32),
            pltpu.VMEM((4, 512, 256), BF16),
            pltpu.VMEM((1, 256), F32),
            pltpu.VMEM((1, 256), F32),
            pltpu.VMEM((PACKET, 256), BF16),
            pltpu.VMEM((3, 2, BLK, 2 * HD), BF16),
            pltpu.VMEM((8, 8, 512), F32),
            pltpu.SemaphoreType.DMA((32,)),
            pltpu.SemaphoreType.DMA((32,)),
            pltpu.SemaphoreType.DMA((6, 2)),
            pltpu.SemaphoreType.DMA((6, 2)),
            pltpu.SemaphoreType.DMA((16,)),
        ],
        compiler_params=pltpu.CompilerParams(
            collective_id=0, has_side_effects=True, vmem_limit_bytes=20 * 2**20
        ),
    )(cq, ck, nq, nk, qg, kg, cv, nv, gc, gn, owned)


def attention_kernel(
    ids, docs, kall, vall, qq, gg, kn, vn, own_w, own_peak, own_sum, out_own, grads_t,
    out_t, dq_t, dk_noisy, dv_noisy, dk_acc, dv_acc,
    where_is, first_of, pair_query, pair_key, pair_bias,
    scores, weights, scaled_grads, peaks, sums, decays, deltas,
):
    chip = lax.axis_index("ctx") // 2

    def clear(stored):
        dk_acc[stored] = jnp.zeros((BLK, HD), F32)
        dv_acc[stored] = jnp.zeros((BLK, HD), F32)

    def begin_of(block, begin):
        clear(block)
        where_is[ids[block // 2, block % 2]] = block
        begin = jnp.where(docs[block] == docs[jnp.maximum(block - 1, 0)], begin, block)
        first_of[block] = begin
        return begin

    lax.fori_loop(0, 32, begin_of, 0)

    def key_rows(buf, stored):
        start = pl.multiple_of((stored % 2) * BLK, BLK)
        return buf[stored // 2, pl.ds(start, BLK), :]

    def key_pair(buf, pair):
        return jnp.concatenate(
            [key_rows(buf, pair_key[2 * pair]), key_rows(buf, pair_key[2 * pair + 1])], axis=0
        )

    def both(ref, index):
        return ref[index].reshape(2 * BLK, HD)

    def tops(values):
        return jnp.max(values.reshape(-1, 8, values.shape[1]), axis=0)

    def totals(values):
        return jnp.sum(values.reshape(-1, 8, values.shape[1]), axis=0)

    @pl.loop(0, 2)
    def _(side):
        count = 0
        for half in range(2):
            block = ids[chip * 2 + side, half]
            begin = first_of[block]

            def enlist(pair, count, half=half, block=block, begin=begin):
                key = begin + 2 * pair
                pair_query[count] = half
                pair_key[2 * count] = where_is[key]
                pair_key[2 * count + 1] = where_is[jnp.minimum(key + 1, block - 1)]
                pair_bias[count] = jnp.where(key + 1 < block, 0, 1)
                return count + 1

            count = lax.fori_loop(0, (block - begin + 1) // 2, enlist, count)

        def over_pairs(body):
            groups = count // GROUP

            @pl.loop(0, groups)
            def _(group):
                body([group * GROUP + i for i in range(GROUP)])

            @pl.loop(groups * GROUP, count)
            def _(pair):
                body([pair])

        first = 2 * side
        for half in range(2):
            peaks[half] = own_peak[first + half]

        def score_pairs(pairs):
            queries = [pair_query[pair] for pair in pairs]
            values = [
                dot(key_pair(kall, pair), both(qq, first + query), LAST)
                for pair, query in zip(pairs, queries)
            ]
            for pair, query, value in zip(pairs, queries, values):
                scores[pair] = value
                peaks[query] = jnp.maximum(peaks[query], tops(value) * SCALE2)

        over_pairs(score_pairs)

        for half in range(2):
            index = first + half
            peak = jnp.max(peaks[half], axis=0, keepdims=True)
            decay = jnp.exp2(own_peak[index] - peak)
            peaks[half] = jnp.broadcast_to(peak, (8, 2 * BLK))
            decays[half] = decay
            sums[half] = own_sum[index] * decay
            out_t[index] = out_own[index] * decay[:1]

        def value_pairs(pairs):
            queries = [pair_query[pair] for pair in pairs]
            outs, parts = [], []
            for pair, query in zip(pairs, queries):
                peak = peaks[query, :1]
                hidden = peak + jnp.where(pair_bias[pair] == 1, jnp.inf, 0.0)
                upper = jnp.exp2(scores[pair, :BLK] * SCALE2 - peak)
                lower = jnp.exp2(scores[pair, BLK:] * SCALE2 - hidden)
                low = jnp.concatenate([upper.astype(BF16), lower.astype(BF16)], axis=0)
                weights[pair] = low
                outs.append(dot(key_pair(vall, pair), low, FIRST))
                parts.append(totals(upper) + totals(lower))
            for query, out, part in zip(queries, outs, parts):
                sums[query] += part
                out_t[first + query] += out

        over_pairs(value_pairs)

        for half in range(2):
            index = first + half
            stored_own = chip * 4 + index
            inverse_sum = 1.0 / jnp.sum(sums[half], axis=0, keepdims=True)
            out = out_t[index] * inverse_sum
            out_t[index] = out
            grad_rows = (grads_t[index] * inverse_sum).astype(BF16).astype(F32)
            delta = jnp.sum(out * grad_rows, axis=0, keepdims=True)
            deltas[half] = jnp.broadcast_to(delta, (8, 2 * BLK))
            grads = jnp.transpose(grad_rows).astype(BF16)
            scaled_grads[half] = grads
            own = own_w[index].astype(F32) * decays[half, :1]
            own_low = own.astype(BF16)
            own_dp = jnp.concatenate(
                [
                    dot(key_rows(vall, stored_own), grads[:BLK], LAST),
                    dot(vn[index], grads[BLK:], LAST),
                ],
                axis=1,
            )
            own_ds = (own * (own_dp - delta)).astype(BF16)
            dv_acc[stored_own] += dot(own_low[:, :BLK], grads[:BLK], PLAIN)
            dk_acc[stored_own] += dot(own_ds[:, :BLK], qq[index, 0], PLAIN)
            dv_noisy[index] = dot(own_low[:, BLK:], grads[BLK:], PLAIN)
            dk_noisy[index] = dot(own_ds[:, BLK:], qq[index, 1], PLAIN) * SCALE
            dq_t[index, :, :BLK] = dot(key_rows(kall, stored_own), own_ds[:, :BLK], FIRST)
            dq_t[index, :, BLK:] = dot(kn[index], own_ds[:, BLK:], FIRST)

        def grad_pairs(pairs):
            queries = [pair_query[pair] for pair in pairs]
            results = []
            for pair, query in zip(pairs, queries):
                low = weights[pair]
                dp = dot(key_pair(vall, pair), scaled_grads[query], LAST)
                ds = (low.astype(F32) * (dp - deltas[query, :1])).astype(BF16)
                results.append(
                    (
                        dot(low, scaled_grads[query], PLAIN),
                        dot(ds, both(qq, first + query), PLAIN),
                        dot(key_pair(kall, pair), ds, FIRST),
                    )
                )
            for pair, query, (dv, dk, dq) in zip(pairs, queries, results):
                for place in range(2):
                    rows = slice(place * BLK, place * BLK + BLK)
                    dv_acc[pair_key[2 * pair + place]] += dv[rows]
                    dk_acc[pair_key[2 * pair + place]] += dk[rows]
                dq_t[first + query] += dq

        over_pairs(grad_pairs)


def attention_call(ids, docs, *parts):
    return pl.pallas_call(
        attention_kernel,
        name="attention",
        out_shape=(
            jax.ShapeDtypeStruct((4, HD, 2 * BLK), F32),
            jax.ShapeDtypeStruct((4, HD, 2 * BLK), F32),
            jax.ShapeDtypeStruct((4, BLK, HD), F32),
            jax.ShapeDtypeStruct((4, BLK, HD), F32),
            jax.ShapeDtypeStruct((32, BLK, HD), F32),
            jax.ShapeDtypeStruct((32, BLK, HD), F32),
        ),
        in_specs=[SMEM, SMEM] + [VMEM] * 11,
        out_specs=(VMEM,) * 6,
        scratch_shapes=[
            pltpu.SMEM((32,), jnp.int32),
            pltpu.SMEM((32,), jnp.int32),
            pltpu.SMEM((32,), jnp.int32),
            pltpu.SMEM((32,), jnp.int32),
            pltpu.SMEM((16,), jnp.int32),
            pltpu.VMEM((16, 2 * BLK, 2 * BLK), F32),
            pltpu.VMEM((16, 2 * BLK, 2 * BLK), BF16),
            pltpu.VMEM((2, 2 * BLK, HD), BF16),
            pltpu.VMEM((2, 8, 2 * BLK), F32),
            pltpu.VMEM((2, 8, 2 * BLK), F32),
            pltpu.VMEM((2, 8, 2 * BLK), F32),
            pltpu.VMEM((2, 8, 2 * BLK), F32),
        ],
        compiler_params=pltpu.CompilerParams(vmem_limit_bytes=34 * 2**20),
    )(ids, docs, *parts)


def scatter_kernel(
    cq_h, ck_h, nq_h, nk_h, qg_h, kg_h, inv, out_t, dq_t, dk_noisy, dv_noisy, dk, dv,
    back, fin, inner_out,
    raws, qg, kg, stage, k_out, v_out, x_out, vy, vq, vh, vx, kh, kx, ky, away, sums,
    send, recv, lsem,
):
    ctx, head, core, y, x = place()
    right, left = (x + 1) % 4, (x + 3) % 4
    partner = ctx_of(x, y, 1 - core)
    to_right, to_left = ctx_of(right, y, core), ctx_of(left, y, core)
    to_y = ctx_of(x, 1 - y, core)
    score_scale = 1.0 / math.sqrt(HD)
    own_columns = pl.ds(pl.multiple_of(core * HD, HD), HD)
    local = Locals(lsem)
    loads = [local.start(ref, raws.at[i]) for i, ref in enumerate((cq_h, ck_h, nq_h, nk_h))]
    loads += [local.start(qg_h, qg), local.start(kg_h, kg)]
    cq, ck, nq, nk = [raws.at[i] for i in range(4)]
    remote = Copies(send, recv, head)

    def mine(ref, step, row, half):
        chip = chip_of((x + step) % 4, y if row == 0 else 1 - y)
        return ref[pl.ds(chip * 4 + half * 2, 2)].reshape(512, HD)

    def pack_v(step):
        for half in range(2):
            v_out[step, half] = mine(dv, step, 1, half).astype(BF16)

    def pack_k(row, step, half, *others):
        value = mine(dk, step, row, half) * score_scale
        for other in others:
            value = value + other[...].astype(F32)
        k_out[row, step, half] = value.astype(BF16)

    pack_v(2)
    pack_k(1, 2, 0)
    pack_k(1, 2, 1)
    enter(ctx, head, [partner, to_right, to_left, to_y])
    first, rest = pl.ds(0, SHIFT), pl.ds(SHIFT, 512 - SHIFT)
    v_far = [
        remote.start(v_out.at[2, 0, first], vq.at[0], to_left),
        remote.start(v_out.at[2, 1, first], vq.at[1], to_right),
    ]
    v_opposite = [
        remote.start(v_out.at[2, half, rest], vy.at[2, half, rest], to_y) for half in range(2)
    ]
    k_half = {}

    def start_half(row):
        k_half[row, 0] = remote.start(k_out.at[row, 2, 0], kh.at[row, 0], to_left)
        k_half[row, 1] = remote.start(k_out.at[row, 2, 1], kh.at[row, 1], to_right)

    start_half(1)
    pack_k(0, 2, 0)
    pack_k(0, 2, 1)
    start_half(0)
    v_y = {}

    def send_v(step, half):
        pack_v(step)
        if half is not None:
            v_far[half].wait_recv()
            v_out[step, half, :SHIFT] = (
                mine(dv, step, 1, half)[:SHIFT] + vq[half].astype(F32)
            ).astype(BF16)
        v_y[step] = remote.start(v_out.at[step], vy.at[step], to_y)

    send_v(3, 0)
    for row in (1, 0):
        pack_k(row, 3, 1)
        pack_k(row, 1, 0)

    def landing(i):
        return back.at[i, :, own_columns]

    swap = {}
    dk_pair, dv_pair = [
        [ref.at[pl.ds(c * 2, 2)] for c in (core, 1 - core)] for ref in (dk_noisy, dv_noisy)
    ]

    def turn(index, ref, first, factor):
        for part in range(2):
            rows = slice(part * BLK, part * BLK + BLK)
            for c, own in ((core, True), (1 - core, False)):
                values = jnp.transpose(ref[2 * c + part]) * factor
                for kind in range(2):
                    if own:
                        back[first + kind, rows, own_columns] = values[kind * BLK : kind * BLK + BLK]
                    else:
                        stage[first + kind, rows, :] = values[kind * BLK : kind * BLK + BLK]
        for i in (first, first + 1):
            swap[i] = remote.start(stage.at[i], landing(i), partner)

    def turn_noisy(ref, i):
        for part in range(2):
            rows = slice(part * BLK, part * BLK + BLK)
            back[i, rows, own_columns] = ref[2 * core + part]
            stage[i, rows, :] = ref[2 * (1 - core) + part]
        swap[i] = remote.start(stage.at[i], landing(i), partner)

    turn(0, dq_t, 2, score_scale)
    turn_noisy(dk_noisy, 4)

    k_x = {}

    def k_forward(row):
        k_half[row, 0].wait_recv()
        pack_k(row, 3, 0, kh.at[row, 0])
        k_x[row, 0] = remote.start(k_out.at[row, 3], kx.at[row, 0], to_left)
        k_half[row, 1].wait_recv()
        pack_k(row, 1, 1, kh.at[row, 1])
        k_x[row, 1] = remote.start(k_out.at[row, 1], kx.at[row, 1], to_right)

    k_forward(1)

    row = lax.broadcasted_iota(jnp.int32, (8, 512), 0)

    def inner(raw, gain, values):
        return row_sums(raw[...].astype(F32) * (gain[...] * values))

    for copy in loads:
        copy.wait()
    for i in (2, 3, 4):
        swap[i].wait_recv()
    total = jnp.zeros((8, 512), F32)
    normal = ((0, cq, qg, 2), (2, nq, qg, 3), (3, nk, kg, 4))
    for index, raw, gain, i in normal:
        total = jnp.where(row == index, inner(raw, gain, back[i]), total)
    sums[0] = total
    exchange = [
        remote.start(sums.at[0], sums.at[step], ctx, (head + step) % 8) for step in range(1, 8)
    ]

    def pack_x(step, half, *others):
        value = mine(dv, step, 0, half)
        for other in others:
            value = value + other[...].astype(F32)
        x_out[step, half] = value.astype(BF16)

    v_half = []
    for half, target in ((0, to_left), (1, to_right)):
        v_opposite[half].wait_recv()
        pack_x(2, half)
        x_out[2, half, SHIFT:] = (
            mine(dv, 2, 0, half)[SHIFT:] + vy[2, half, SHIFT:].astype(F32)
        ).astype(BF16)
        v_half.append(remote.start(x_out.at[2, half], vh.at[half], target))
    send_v(1, 1)
    k_forward(0)
    turn(0, out_t, 0, 1.0)
    turn_noisy(dv_noisy, 5)
    k_x[1, 0].wait_recv()
    k_x[1, 1].wait_recv()
    for half in range(2):
        pack_k(1, 0, half, kx.at[1, 0, half], kx.at[1, 1, half])
    k_y = remote.start(k_out.at[1, 0], ky, to_y)
    send_v(0, None)

    v_y[3].wait_recv()
    v_half[0].wait_recv()
    pack_x(3, 0, vy.at[3, 0], vh.at[0])
    pack_x(3, 1, vy.at[3, 1])
    v_x = [remote.start(x_out.at[3], vx.at[0], to_left)]
    v_y[1].wait_recv()
    v_half[1].wait_recv()
    pack_x(1, 0, vy.at[1, 0])
    pack_x(1, 1, vy.at[1, 1], vh.at[1])
    v_x.append(remote.start(x_out.at[1], vx.at[1], to_right))

    for copy in exchange:
        copy.wait_recv()
    total = sums[0]
    for step in range(1, 8):
        total = total + sums[step]
    inverses = jnp.transpose(inv[...])
    means = jnp.transpose(total) / FEAT
    for index, raw, gain, i in normal:
        inverse = inverses[:, index : index + 1]
        factor = inverse * inverse * inverse * means[:, index : index + 1]
        back[i] = inverse * (gain[...] * back[i]) - raw[...].astype(F32) * factor

    def finish(index, ref, factor, terms):
        values = []
        for half in range(2):
            value = mine(ref, 0, 0, half) * factor
            for term in terms:
                value = value + term[half].astype(F32)
            values.append(value)
        first_core = core == 0
        fin[index, :, own_columns] = jnp.where(first_core, values[0], values[1])
        away[index] = jnp.where(first_core, values[1], values[0])
        return remote.start(away.at[index], fin.at[index, :, own_columns], partner)

    k_x[0, 0].wait_recv()
    k_x[0, 1].wait_recv()
    k_y.wait_recv()
    k_fin = finish(0, dk, score_scale, (kx.at[0, 0], kx.at[0, 1], ky))
    k_fin.wait_recv()
    sums[8] = inner(ck, kg, fin[0])
    k_exchange = [
        remote.start(sums.at[8], sums.at[8 + step], ctx, (head + step) % 8) for step in range(1, 8)
    ]
    v_y[0].wait_recv()
    v_x[0].wait_recv()
    v_x[1].wait_recv()
    v_fin = finish(1, dv, 1.0, (vy.at[0], vx.at[0], vx.at[1]))

    for copy in k_exchange:
        copy.wait_recv()
    total = sums[8]
    for step in range(1, 8):
        total = total + sums[8 + step]
    inner_out[...] = total
    v_fin.wait_recv()
    for i in (0, 1, 5):
        swap[i].wait_recv()
    for copy in remote.started:
        copy.wait_send()


def scatter_call(*operands):
    return pl.pallas_call(
        scatter_kernel,
        name="scatter_grads",
        out_shape=(
            jax.ShapeDtypeStruct((6, 512, 256), F32),
            jax.ShapeDtypeStruct((2, 512, 256), F32),
            jax.ShapeDtypeStruct((8, 512), F32),
        ),
        in_specs=[HBM] * 6 + [VMEM] * 7,
        out_specs=(VMEM, VMEM, VMEM),
        scratch_shapes=[
            pltpu.VMEM((4, 512, 256), BF16),
            pltpu.VMEM((1, 256), F32),
            pltpu.VMEM((1, 256), F32),
            pltpu.VMEM((6, 512, HD), F32),
            pltpu.VMEM((2, 4, 2, 512, HD), BF16),
            pltpu.VMEM((4, 2, 512, HD), BF16),
            pltpu.VMEM((4, 2, 512, HD), BF16),
            pltpu.VMEM((4, 2, 512, HD), BF16),
            pltpu.VMEM((2, SHIFT, HD), BF16),
            pltpu.VMEM((2, 512, HD), BF16),
            pltpu.VMEM((2, 2, 512, HD), BF16),
            pltpu.VMEM((2, 2, 512, HD), BF16),
            pltpu.VMEM((2, 2, 2, 512, HD), BF16),
            pltpu.VMEM((2, 512, HD), BF16),
            pltpu.VMEM((2, 512, HD), F32),
            pltpu.VMEM((16, 8, 512), F32),
            pltpu.SemaphoreType.DMA((48,)),
            pltpu.SemaphoreType.DMA((48,)),
            pltpu.SemaphoreType.DMA((8,)),
        ],
        compiler_params=pltpu.CompilerParams(
            collective_id=1, has_side_effects=True, vmem_limit_bytes=20 * 2**20
        ),
    )(*operands)


def finish_kernel(
    ck, kg, inv, inner, back, fin,
    out_clean, out_noisy, dq_clean, dk_clean, dv_clean, dq_noisy, dk_noisy, dv_noisy,
    dk, sems,
):
    local = Locals(sems)
    copies = [
        local.start(source, target)
        for source, target in (
            (back.at[0], out_clean),
            (back.at[1], out_noisy),
            (back.at[2], dq_clean),
            (back.at[3], dq_noisy),
            (back.at[4], dk_noisy),
            (back.at[5], dv_noisy),
            (fin.at[1], dv_clean),
        )
    ]
    inverse = jnp.transpose(inv[...])[:, 1:2]
    mean = jnp.transpose(inner[...])[:, :1] / FEAT
    factor = inverse * inverse * inverse * mean
    dk[...] = inverse * (kg[...] * fin[0]) - ck[...].astype(F32) * factor
    copies.append(local.start(dk, dk_clean))
    for copy in copies:
        copy.wait()


def finish_call(*operands):
    return pl.pallas_call(
        finish_kernel,
        name="finish",
        out_shape=tuple(jax.ShapeDtypeStruct((512, 256), F32) for _ in range(8)),
        in_specs=[VMEM] * 6,
        out_specs=(HBM,) * 8,
        scratch_shapes=[pltpu.VMEM((512, 256), F32), pltpu.SemaphoreType.DMA((8,))],
        compiler_params=pltpu.CompilerParams(vmem_limit_bytes=16 * 2**20),
    )(*operands)


def local(
    clean_q, clean_k, clean_v, noisy_q, noisy_k, noisy_v,
    q_gain, k_gain, grad_clean, grad_noisy, owned_blocks, block_doc,
):
    qg = q_gain.reshape(1, 256)
    kg = k_gain.reshape(1, 256)
    blocks = [a.reshape(2, BLK, 2 * HD) for a in (noisy_v, grad_clean, grad_noisy)]
    *pinned, docs = [
        pltpu.with_memory_space_constraint(a, pltpu.HBM)
        for a in (
            clean_q, clean_k, noisy_q, noisy_k, qg, kg, clean_v, *blocks, owned_blocks, block_doc,
        )
    ]
    *parts, inv, ids = gather_call(*pinned)
    grads = attention_call(ids, docs, *parts)
    back, fin, inner = scatter_call(*pinned[:6], inv, *grads)
    return finish_call(clean_k, kg, inv, inner, back, fin)


def solution(mesh):
    placed = (P("ctx", "head"),) * 6 + (P("head"),) * 2 + (P("ctx", "head"),) * 2 + (P("ctx"), P())
    return jax.shard_map(
        local,
        mesh=mesh,
        in_specs=placed,
        out_specs=(P("ctx", "head"),) * 8,
        check_vma=False,
    )
```

```python
import math

import jax
import jax.numpy as jnp
from jax import lax
from jax.experimental import pallas as pl
from jax.experimental.pallas import tpu as pltpu
from jax.sharding import PartitionSpec as P

HD = 128
BLK = 256
FEAT = 2048
EPSILON = 1e-06
NEGATIVE = -1e30
MESH = pl.DeviceIdType.MESH
F32 = jnp.float32
BF16 = jnp.bfloat16
VMEM = pl.BlockSpec(memory_space=pltpu.VMEM)
SMEM = pl.BlockSpec(memory_space=pltpu.SMEM)
ANY = pl.BlockSpec(memory_space=pl.ANY)
HBM = pl.BlockSpec(memory_space=pltpu.HBM)
LAST = (((1,), (1,)), ((), ()))
FIRST = (((0,), (0,)), ((), ()))
PLAIN = (((1,), (0,)), ((), ()))
PACKET = 528
SHIFT = 160
GROUPS = (4, 2, 1)
SCALE = 1.0 / math.sqrt(HD)
SCALE2 = SCALE * math.log2(math.e)


def dot(a, b, dims):
    return lax.dot_general(a, b, dims, preferred_element_type=F32)


def row_sums(products):
    high = products.astype(BF16)
    low = (products - high.astype(F32)).astype(BF16)
    ones = jnp.ones((8, products.shape[1]), BF16)
    return dot(ones, high, LAST) + dot(ones, low, LAST)


def place():
    ctx = lax.axis_index("ctx")
    head = lax.axis_index("head")
    core = ctx % 2
    y = (ctx // 2) % 2
    x = ctx // 4
    return ctx, head, core, y, x


def ctx_of(x, y, core):
    return (x * 2 + y) * 2 + core


def chip_of(x, y):
    return x * 2 + y


class Copies:
    def __init__(self, send, recv, head):
        self.send, self.recv, self.head = send, recv, head
        self.started = []
        self.count = 0

    def start(self, src, dst, ctx, head=None):
        copy = pltpu.make_async_remote_copy(
            src_ref=src,
            dst_ref=dst,
            send_sem=self.send.at[self.count],
            recv_sem=self.recv.at[self.count],
            device_id={"ctx": ctx, "head": self.head if head is None else head},
            device_id_type=MESH,
        )
        self.count += 1
        copy.start()
        self.started.append(copy)
        return copy


class Locals:
    def __init__(self, sems):
        self.sems = sems
        self.count = 0

    def start(self, src, dst):
        copy = pltpu.make_async_copy(src, dst, self.sems.at[self.count])
        self.count += 1
        copy.start()
        return copy


def enter(ctx, head, others):
    barrier = pltpu.get_barrier_semaphore()
    for other in others:
        pl.semaphore_signal(barrier, inc=1, device_id={"ctx": other, "head": head}, device_id_type=MESH)
    for step in range(1, 8):
        pl.semaphore_signal(
            barrier, inc=1, device_id={"ctx": ctx, "head": (head + step) % 8}, device_id_type=MESH
        )
    pl.semaphore_wait(barrier, 7 + len(others))


def gather_kernel(
    cq_h, ck_h, nq_h, nk_h, qg_h, kg_h, cv, nv, gc, gn, owned,
    kall, vall, qq, gg, kn, vn, own_w, own_peak, own_sum, out_own, grads_t, inv_out, ids_out,
    owned_s, raws, qg, kg, k_packet, normed, sums, send, recv, wide_send, wide_recv, lsem,
):
    ctx, head, core, y, x = place()
    right, left = (x + 1) % 4, (x + 3) % 4
    opposite = (x + 2) % 4
    mine = pl.ds(pl.multiple_of(core * HD, HD), HD)
    theirs = pl.ds(pl.multiple_of((1 - core) * HD, HD), HD)
    partner = ctx_of(x, y, 1 - core)
    local = Locals(lsem)
    owned_load = local.start(owned, owned_s)
    loads = [local.start(ref, raws.at[i]) for i, ref in enumerate((cq_h, ck_h, nq_h, nk_h))]
    loads += [local.start(qg_h, qg), local.start(kg_h, kg)]
    remote = Copies(send, recv, head)
    chips = ((x, 1 - y), (right, y), (left, y))
    enter(ctx, head, [partner] + [ctx_of(*chip, c) for chip in chips for c in range(2)])
    wide = []

    def first_hop(base, columns_of, buf):
        for number, chip in enumerate(chips):
            for target in range(2):
                copy = pltpu.make_async_remote_copy(
                    src_ref=columns_of(target),
                    dst_ref=buf.at[ctx],
                    send_sem=wide_send.at[base + number, target],
                    recv_sem=wide_recv.at[base + number, core],
                    device_id={"ctx": ctx_of(*chip, target), "head": head},
                    device_id_type=MESH,
                )
                copy.start()
                wide.append(copy)

    def arrived(base, number, buf, source):
        chip = ((x, 1 - y), (left, y), (right, y))[number]
        pltpu.make_async_remote_copy(
            src_ref=buf.at[ctx],
            dst_ref=buf.at[ctx_of(*chip, source)],
            send_sem=wide_send.at[base + number, source],
            recv_sem=wide_recv.at[base + number, source],
            device_id={"ctx": partner, "head": head},
            device_id_type=MESH,
        ).wait_recv()

    first_hop(0, lambda target: cv.at[:, target * HD : target * HD + HD], vall)
    v_swap = remote.start(cv.at[:, theirs], vall.at[ctx], partner)
    v_own = local.start(cv.at[:, mine], vall.at[ctx])

    for copy in loads:
        copy.wait()
    row = lax.broadcasted_iota(jnp.int32, (8, 512), 0)
    total = jnp.zeros((8, 512), F32)
    for index in range(4):
        raw = raws[index].astype(F32)
        total = jnp.where(row == index, row_sums(raw * raw), total)
    sums[0] = total
    exchange = [
        remote.start(sums.at[0], sums.at[step], ctx, (head + step) % 8) for step in range(1, 8)
    ]
    owned_load.wait()
    lane = lax.broadcasted_iota(jnp.int32, (16, 2 * HD), 1)
    k_packet[512:, :] = jnp.where(lane % HD == 0, owned_s[0], owned_s[1]).astype(F32).astype(BF16)

    pair = pl.ds(core * 2, 2)
    late, late_own = [], []

    def swap(src, dst):
        late.append(remote.start(src.at[:, :, theirs], dst, partner))
        late_own.append(local.start(src.at[:, :, mine], dst))

    swap(gc, gg.at[pair, 0])
    swap(gn, gg.at[pair, 1])
    swap(nv, vn.at[pair])

    for copy in exchange:
        copy.wait_recv()
    total = sums[0]
    for step in range(1, 8):
        total = total + sums[step]
    inverse = lax.rsqrt(total / FEAT + EPSILON)
    inv_out[...] = inverse
    columns = jnp.transpose(inverse)

    def normalized(index, gain):
        values = raws[index].astype(F32) * columns[:, index : index + 1] * gain[...]
        return values.astype(BF16)

    k_packet[:512, :] = normalized(1, kg)
    first_hop(3, lambda target: k_packet.at[:, target * HD : target * HD + HD], kall)
    k_swap = remote.start(k_packet.at[:, theirs], kall.at[ctx], partner)
    k_own = local.start(k_packet.at[:, mine], kall.at[ctx])
    for index, raw, gain, dst in (
        (0, 0, qg, qq.at[pair, 0]),
        (1, 2, qg, qq.at[pair, 1]),
        (2, 3, kg, kn.at[pair]),
    ):
        normed[index] = normalized(raw, gain).reshape(2, BLK, 2 * HD)
        swap(normed.at[index], dst)

    def slot(buf, sx, sy):
        return buf.at[pl.ds(2 * chip_of(sx, sy), 2)]

    def part(buf, sx, sy, half):
        return buf.at[2 * chip_of(sx, sy) + half]

    def rows_of(sx, sy, half, first, count):
        return vall.at[2 * chip_of(sx, sy) + half, pl.ds(first, count)]

    def spread(view, px, py):
        return remote.start(view, view, ctx_of(px, py, core))

    v_half, v_y, k_half = [], [], []
    sides = ((1, left, right, 0), (2, right, left, 1))
    for number, near, far, half in sides:
        arrived(0, number, vall, half)
        v_half.append(spread(part(vall, near, y, half), far, y))
    arrived(3, 0, kall, 0)
    arrived(3, 0, kall, 1)
    k_right = spread(slot(kall, x, 1 - y), right, y)
    k_left = spread(slot(kall, x, 1 - y), left, y)
    arrived(0, 1, vall, 1)
    v_y.append(spread(slot(vall, left, y), x, 1 - y))

    v_own.wait()
    k_own.wait()
    v_swap.wait_recv()
    k_swap.wait_recv()
    for copy in late_own:
        copy.wait()
    for copy in late:
        copy.wait_recv()

    def own_block(index):
        side, rows = index // 2, slice(index % 2 * BLK, index % 2 * BLK + BLK)
        packet = 2 * chip_of(x, y) + side
        own = ((kall[packet, rows, :], vall[packet, rows, :]), (kn[index], vn[index]))
        for kind, (keys, values) in enumerate(own):
            columns = slice(kind * BLK, kind * BLK + BLK)
            scores = dot(keys, qq[index, kind], LAST) * SCALE2
            peak = jnp.max(scores, axis=0, keepdims=True)
            weights = jnp.exp2(scores - peak)
            low = weights.astype(BF16)
            own_peak[index, :, columns] = jnp.broadcast_to(peak, (8, BLK))
            own_sum[index, :, columns] = jnp.sum(weights.reshape(BLK // 8, 8, BLK), axis=0)
            own_w[index, :, columns] = low
            out_own[index, :, columns] = dot(values, low, FIRST)
            grads_t[index, :, columns] = jnp.transpose(gg[index, kind].astype(F32))

    own_block(0)
    for number, near, far, half in sides:
        arrived(3, number, kall, half)
        k_half.append(spread(part(kall, near, y, half), far, y))
        arrived(3, number, kall, 1 - half)
    own_block(1)
    arrived(0, 2, vall, 0)
    v_y.append(spread(slot(vall, right, y), x, 1 - y))
    own_block(2)
    v_half[0].wait_recv()
    v_half[1].wait_recv()
    v_y[0].wait_recv()
    v_far = [spread(rows_of(left, 1 - y, 0, 0, SHIFT), right, y)]
    for half in range(2):
        v_y.append(spread(rows_of(opposite, y, half, SHIFT, 512 - SHIFT), x, 1 - y))
    k_right.wait_recv()
    k_half.append(spread(part(kall, left, 1 - y, 0), right, y))
    k_left.wait_recv()
    k_half.append(spread(part(kall, right, 1 - y, 1), left, y))
    own_block(3)
    v_y[1].wait_recv()
    v_far.append(spread(rows_of(right, 1 - y, 1, 0, SHIFT), left, y))
    arrived(0, 0, vall, 0)
    arrived(0, 0, vall, 1)
    for copy in v_y[2:] + v_far + k_half:
        copy.wait_recv()
    names = jnp.max(kall[:, 512:, :].astype(F32), axis=1)
    ids_out[...] = names.astype(jnp.int32)
    for copy in remote.started + wide:
        copy.wait_send()


def gather_call(cq, ck, nq, nk, qg, kg, cv, nv, gc, gn, owned):
    return pl.pallas_call(
        gather_kernel,
        name="gather_keys",
        out_shape=(
            jax.ShapeDtypeStruct((16, PACKET, HD), BF16),
            jax.ShapeDtypeStruct((16, 512, HD), BF16),
            jax.ShapeDtypeStruct((4, 2, BLK, HD), BF16),
            jax.ShapeDtypeStruct((4, 2, BLK, HD), BF16),
            jax.ShapeDtypeStruct((4, BLK, HD), BF16),
            jax.ShapeDtypeStruct((4, BLK, HD), BF16),
            jax.ShapeDtypeStruct((4, BLK, 2 * BLK), BF16),
            jax.ShapeDtypeStruct((4, 8, 2 * BLK), F32),
            jax.ShapeDtypeStruct((4, 8, 2 * BLK), F32),
            jax.ShapeDtypeStruct((4, HD, 2 * BLK), F32),
            jax.ShapeDtypeStruct((4, HD, 2 * BLK), F32),
            jax.ShapeDtypeStruct((8, 512), F32),
            jax.ShapeDtypeStruct((16, HD), jnp.int32),
        ),
        in_specs=[HBM] * 11,
        out_specs=(VMEM,) * 13,
        scratch_shapes=[
            pltpu.SMEM((2,), jnp.int32),
            pltpu.VMEM((4, 512, 256), BF16),
            pltpu.VMEM((1, 256), F32),
            pltpu.VMEM((1, 256), F32),
            pltpu.VMEM((PACKET, 256), BF16),
            pltpu.VMEM((3, 2, BLK, 2 * HD), BF16),
            pltpu.VMEM((8, 8, 512), F32),
            pltpu.SemaphoreType.DMA((32,)),
            pltpu.SemaphoreType.DMA((32,)),
            pltpu.SemaphoreType.DMA((6, 2)),
            pltpu.SemaphoreType.DMA((6, 2)),
            pltpu.SemaphoreType.DMA((16,)),
        ],
        compiler_params=pltpu.CompilerParams(
            collective_id=0, has_side_effects=True, vmem_limit_bytes=20 * 2**20
        ),
    )(cq, ck, nq, nk, qg, kg, cv, nv, gc, gn, owned)


def attention_kernel(
    ids, docs, kall, vall, qq, gg, kn, vn, own_w, own_peak, own_sum, out_own, grads_t,
    out_t, dq_t, dk_noisy, dv_noisy, dk_acc, dv_acc,
    where_is, first_of, pair_query, pair_key, pair_bias,
    scores, weights, scaled_grads, peaks, sums, decays, deltas,
):
    chip = lax.axis_index("ctx") // 2

    def clear(stored):
        dk_acc[stored] = jnp.zeros((BLK, HD), F32)
        dv_acc[stored] = jnp.zeros((BLK, HD), F32)

    def begin_of(block, begin):
        clear(block)
        where_is[ids[block // 2, block % 2]] = block
        begin = jnp.where(docs[block] == docs[jnp.maximum(block - 1, 0)], begin, block)
        first_of[block] = begin
        return begin

    lax.fori_loop(0, 32, begin_of, 0)

    def key_rows(buf, stored):
        start = pl.multiple_of((stored % 2) * BLK, BLK)
        return buf[stored // 2, pl.ds(start, BLK), :]

    def key_pair(buf, pair):
        return jnp.concatenate(
            [key_rows(buf, pair_key[2 * pair]), key_rows(buf, pair_key[2 * pair + 1])], axis=0
        )

    def both(ref, index):
        return ref[index].reshape(2 * BLK, HD)

    def tops(values):
        return jnp.max(values.reshape(-1, 8, values.shape[1]), axis=0)

    def totals(values):
        return jnp.sum(values.reshape(-1, 8, values.shape[1]), axis=0)

    @pl.loop(0, 2)
    def _(side):
        count = 0
        for half in range(2):
            block = ids[chip * 2 + side, half]
            begin = first_of[block]

            def enlist(pair, count, half=half, block=block, begin=begin):
                key = begin + 2 * pair
                pair_query[count] = half
                pair_key[2 * count] = where_is[key]
                pair_key[2 * count + 1] = where_is[jnp.minimum(key + 1, block - 1)]
                pair_bias[count] = jnp.where(key + 1 < block, 0, 1)
                return count + 1

            count = lax.fori_loop(0, (block - begin + 1) // 2, enlist, count)

        def over_pairs(body):
            begin = 0
            for size in GROUPS:
                end = begin + (count - begin) // size

                def step(group, carry, size=size, base=begin):
                    body([base + (group - base) * size + i for i in range(size)])
                    return carry

                lax.fori_loop(begin, end, step, 0)
                begin = begin + (end - begin) * size

        first = 2 * side
        for half in range(2):
            peaks[half] = own_peak[first + half]

        def score_pairs(pairs):
            queries = [pair_query[pair] for pair in pairs]
            values = [
                dot(key_pair(kall, pair), both(qq, first + query), LAST)
                for pair, query in zip(pairs, queries)
            ]
            for pair, query, value in zip(pairs, queries, values):
                scores[pair] = value
                peaks[query] = jnp.maximum(peaks[query], tops(value) * SCALE2)

        over_pairs(score_pairs)

        for half in range(2):
            index = first + half
            peak = jnp.max(peaks[half], axis=0, keepdims=True)
            decay = jnp.exp2(own_peak[index] - peak)
            peaks[half] = jnp.broadcast_to(peak, (8, 2 * BLK))
            decays[half] = decay
            sums[half] = own_sum[index] * decay
            out_t[index] = out_own[index] * decay[:1]

        def value_pairs(pairs):
            queries = [pair_query[pair] for pair in pairs]
            outs, parts = [], []
            for pair, query in zip(pairs, queries):
                peak = peaks[query, :1]
                hidden = peak + jnp.where(pair_bias[pair] == 1, jnp.inf, 0.0)
                upper = jnp.exp2(scores[pair, :BLK] * SCALE2 - peak)
                lower = jnp.exp2(scores[pair, BLK:] * SCALE2 - hidden)
                low = jnp.concatenate([upper.astype(BF16), lower.astype(BF16)], axis=0)
                weights[pair] = low
                outs.append(dot(key_pair(vall, pair), low, FIRST))
                parts.append(totals(upper) + totals(lower))
            for query, out, part in zip(queries, outs, parts):
                sums[query] += part
                out_t[first + query] += out

        over_pairs(value_pairs)

        for half in range(2):
            index = first + half
            stored_own = chip * 4 + index
            inverse_sum = 1.0 / jnp.sum(sums[half], axis=0, keepdims=True)
            out = out_t[index] * inverse_sum
            out_t[index] = out
            grad_rows = (grads_t[index] * inverse_sum).astype(BF16).astype(F32)
            delta = jnp.sum(out * grad_rows, axis=0, keepdims=True)
            deltas[half] = jnp.broadcast_to(delta, (8, 2 * BLK))
            grads = jnp.transpose(grad_rows).astype(BF16)
            scaled_grads[half] = grads
            own = own_w[index].astype(F32) * decays[half, :1]
            own_low = own.astype(BF16)
            own_dp = jnp.concatenate(
                [
                    dot(key_rows(vall, stored_own), grads[:BLK], LAST),
                    dot(vn[index], grads[BLK:], LAST),
                ],
                axis=1,
            )
            own_ds = (own * (own_dp - delta)).astype(BF16)
            dv_acc[stored_own] += dot(own_low[:, :BLK], grads[:BLK], PLAIN)
            dk_acc[stored_own] += dot(own_ds[:, :BLK], qq[index, 0], PLAIN)
            dv_noisy[index] = dot(own_low[:, BLK:], grads[BLK:], PLAIN)
            dk_noisy[index] = dot(own_ds[:, BLK:], qq[index, 1], PLAIN) * SCALE
            dq_t[index, :, :BLK] = dot(key_rows(kall, stored_own), own_ds[:, :BLK], FIRST)
            dq_t[index, :, BLK:] = dot(kn[index], own_ds[:, BLK:], FIRST)

        def grad_pairs(pairs):
            queries = [pair_query[pair] for pair in pairs]
            results = []
            for pair, query in zip(pairs, queries):
                low = weights[pair]
                dp = dot(key_pair(vall, pair), scaled_grads[query], LAST)
                ds = (low.astype(F32) * (dp - deltas[query, :1])).astype(BF16)
                results.append(
                    (
                        dot(low, scaled_grads[query], PLAIN),
                        dot(ds, both(qq, first + query), PLAIN),
                        dot(key_pair(kall, pair), ds, FIRST),
                    )
                )
            for pair, query, (dv, dk, dq) in zip(pairs, queries, results):
                for place in range(2):
                    rows = slice(place * BLK, place * BLK + BLK)
                    dv_acc[pair_key[2 * pair + place]] += dv[rows]
                    dk_acc[pair_key[2 * pair + place]] += dk[rows]
                dq_t[first + query] += dq

        over_pairs(grad_pairs)


def attention_call(ids, docs, *parts):
    return pl.pallas_call(
        attention_kernel,
        name="attention",
        out_shape=(
            jax.ShapeDtypeStruct((4, HD, 2 * BLK), F32),
            jax.ShapeDtypeStruct((4, HD, 2 * BLK), F32),
            jax.ShapeDtypeStruct((4, BLK, HD), F32),
            jax.ShapeDtypeStruct((4, BLK, HD), F32),
            jax.ShapeDtypeStruct((32, BLK, HD), F32),
            jax.ShapeDtypeStruct((32, BLK, HD), F32),
        ),
        in_specs=[SMEM, SMEM] + [VMEM] * 11,
        out_specs=(VMEM,) * 6,
        scratch_shapes=[
            pltpu.SMEM((32,), jnp.int32),
            pltpu.SMEM((32,), jnp.int32),
            pltpu.SMEM((32,), jnp.int32),
            pltpu.SMEM((32,), jnp.int32),
            pltpu.SMEM((16,), jnp.int32),
            pltpu.VMEM((16, 2 * BLK, 2 * BLK), F32),
            pltpu.VMEM((16, 2 * BLK, 2 * BLK), BF16),
            pltpu.VMEM((2, 2 * BLK, HD), BF16),
            pltpu.VMEM((2, 8, 2 * BLK), F32),
            pltpu.VMEM((2, 8, 2 * BLK), F32),
            pltpu.VMEM((2, 8, 2 * BLK), F32),
            pltpu.VMEM((2, 8, 2 * BLK), F32),
        ],
        compiler_params=pltpu.CompilerParams(vmem_limit_bytes=34 * 2**20),
    )(ids, docs, *parts)


def scatter_kernel(
    cq_h, ck_h, nq_h, nk_h, qg_h, kg_h, inv, out_t, dq_t, dk_noisy, dv_noisy, dk, dv,
    back, fin, inner_out,
    raws, qg, kg, stage, k_out, v_out, x_out, vy, vq, vh, vx, kh, kx, ky, away, sums,
    send, recv, lsem,
):
    ctx, head, core, y, x = place()
    right, left = (x + 1) % 4, (x + 3) % 4
    partner = ctx_of(x, y, 1 - core)
    to_right, to_left = ctx_of(right, y, core), ctx_of(left, y, core)
    to_y = ctx_of(x, 1 - y, core)
    score_scale = 1.0 / math.sqrt(HD)
    own_columns = pl.ds(pl.multiple_of(core * HD, HD), HD)
    local = Locals(lsem)
    loads = [local.start(ref, raws.at[i]) for i, ref in enumerate((cq_h, ck_h, nq_h, nk_h))]
    loads += [local.start(qg_h, qg), local.start(kg_h, kg)]
    cq, ck, nq, nk = [raws.at[i] for i in range(4)]
    remote = Copies(send, recv, head)

    def mine(ref, step, row, half):
        chip = chip_of((x + step) % 4, y if row == 0 else 1 - y)
        return ref[pl.ds(chip * 4 + half * 2, 2)].reshape(512, HD)

    def pack_v(step):
        for half in range(2):
            v_out[step, half] = mine(dv, step, 1, half).astype(BF16)

    def pack_k(row, step, half, *others):
        value = mine(dk, step, row, half) * score_scale
        for other in others:
            value = value + other[...].astype(F32)
        k_out[row, step, half] = value.astype(BF16)

    pack_v(2)
    pack_k(1, 2, 0)
    pack_k(1, 2, 1)
    enter(ctx, head, [partner, to_right, to_left, to_y])
    first, rest = pl.ds(0, SHIFT), pl.ds(SHIFT, 512 - SHIFT)
    v_far = [
        remote.start(v_out.at[2, 0, first], vq.at[0], to_left),
        remote.start(v_out.at[2, 1, first], vq.at[1], to_right),
    ]
    v_opposite = [
        remote.start(v_out.at[2, half, rest], vy.at[2, half, rest], to_y) for half in range(2)
    ]
    k_half = {}

    def start_half(row):
        k_half[row, 0] = remote.start(k_out.at[row, 2, 0], kh.at[row, 0], to_left)
        k_half[row, 1] = remote.start(k_out.at[row, 2, 1], kh.at[row, 1], to_right)

    start_half(1)
    pack_k(0, 2, 0)
    pack_k(0, 2, 1)
    start_half(0)
    v_y = {}

    def send_v(step, half):
        pack_v(step)
        if half is not None:
            v_far[half].wait_recv()
            v_out[step, half, :SHIFT] = (
                mine(dv, step, 1, half)[:SHIFT] + vq[half].astype(F32)
            ).astype(BF16)
        v_y[step] = remote.start(v_out.at[step], vy.at[step], to_y)

    send_v(3, 0)
    for row in (1, 0):
        pack_k(row, 3, 1)
        pack_k(row, 1, 0)

    def landing(i):
        return back.at[i, :, own_columns]

    swap = {}
    dk_pair, dv_pair = [
        [ref.at[pl.ds(c * 2, 2)] for c in (core, 1 - core)] for ref in (dk_noisy, dv_noisy)
    ]

    def turn(index, ref, first, factor):
        for part in range(2):
            rows = slice(part * BLK, part * BLK + BLK)
            for c, own in ((core, True), (1 - core, False)):
                values = jnp.transpose(ref[2 * c + part]) * factor
                for kind in range(2):
                    if own:
                        back[first + kind, rows, own_columns] = values[kind * BLK : kind * BLK + BLK]
                    else:
                        stage[first + kind, rows, :] = values[kind * BLK : kind * BLK + BLK]
        for i in (first, first + 1):
            swap[i] = remote.start(stage.at[i], landing(i), partner)

    def turn_noisy(ref, i):
        for part in range(2):
            rows = slice(part * BLK, part * BLK + BLK)
            back[i, rows, own_columns] = ref[2 * core + part]
            stage[i, rows, :] = ref[2 * (1 - core) + part]
        swap[i] = remote.start(stage.at[i], landing(i), partner)

    turn(0, dq_t, 2, score_scale)
    turn_noisy(dk_noisy, 4)

    k_x = {}

    def k_forward(row):
        k_half[row, 0].wait_recv()
        pack_k(row, 3, 0, kh.at[row, 0])
        k_x[row, 0] = remote.start(k_out.at[row, 3], kx.at[row, 0], to_left)
        k_half[row, 1].wait_recv()
        pack_k(row, 1, 1, kh.at[row, 1])
        k_x[row, 1] = remote.start(k_out.at[row, 1], kx.at[row, 1], to_right)

    k_forward(1)

    row = lax.broadcasted_iota(jnp.int32, (8, 512), 0)

    def inner(raw, gain, values):
        return row_sums(raw[...].astype(F32) * (gain[...] * values))

    for copy in loads:
        copy.wait()
    for i in (2, 3, 4):
        swap[i].wait_recv()
    total = jnp.zeros((8, 512), F32)
    normal = ((0, cq, qg, 2), (2, nq, qg, 3), (3, nk, kg, 4))
    for index, raw, gain, i in normal:
        total = jnp.where(row == index, inner(raw, gain, back[i]), total)
    sums[0] = total
    exchange = [
        remote.start(sums.at[0], sums.at[step], ctx, (head + step) % 8) for step in range(1, 8)
    ]

    def pack_x(step, half, *others):
        value = mine(dv, step, 0, half)
        for other in others:
            value = value + other[...].astype(F32)
        x_out[step, half] = value.astype(BF16)

    v_half = []
    for half, target in ((0, to_left), (1, to_right)):
        v_opposite[half].wait_recv()
        pack_x(2, half)
        x_out[2, half, SHIFT:] = (
            mine(dv, 2, 0, half)[SHIFT:] + vy[2, half, SHIFT:].astype(F32)
        ).astype(BF16)
        v_half.append(remote.start(x_out.at[2, half], vh.at[half], target))
    send_v(1, 1)
    k_forward(0)
    turn(0, out_t, 0, 1.0)
    turn_noisy(dv_noisy, 5)
    k_x[1, 0].wait_recv()
    k_x[1, 1].wait_recv()
    for half in range(2):
        pack_k(1, 0, half, kx.at[1, 0, half], kx.at[1, 1, half])
    k_y = remote.start(k_out.at[1, 0], ky, to_y)
    send_v(0, None)

    v_y[3].wait_recv()
    v_half[0].wait_recv()
    pack_x(3, 0, vy.at[3, 0], vh.at[0])
    pack_x(3, 1, vy.at[3, 1])
    v_x = [remote.start(x_out.at[3], vx.at[0], to_left)]
    v_y[1].wait_recv()
    v_half[1].wait_recv()
    pack_x(1, 0, vy.at[1, 0])
    pack_x(1, 1, vy.at[1, 1], vh.at[1])
    v_x.append(remote.start(x_out.at[1], vx.at[1], to_right))

    for copy in exchange:
        copy.wait_recv()
    total = sums[0]
    for step in range(1, 8):
        total = total + sums[step]
    inverses = jnp.transpose(inv[...])
    means = jnp.transpose(total) / FEAT
    for index, raw, gain, i in normal:
        inverse = inverses[:, index : index + 1]
        factor = inverse * inverse * inverse * means[:, index : index + 1]
        back[i] = inverse * (gain[...] * back[i]) - raw[...].astype(F32) * factor

    def finish(index, ref, factor, terms):
        values = []
        for half in range(2):
            value = mine(ref, 0, 0, half) * factor
            for term in terms:
                value = value + term[half].astype(F32)
            values.append(value)
        first_core = core == 0
        fin[index, :, own_columns] = jnp.where(first_core, values[0], values[1])
        away[index] = jnp.where(first_core, values[1], values[0])
        return remote.start(away.at[index], fin.at[index, :, own_columns], partner)

    k_x[0, 0].wait_recv()
    k_x[0, 1].wait_recv()
    k_y.wait_recv()
    k_fin = finish(0, dk, score_scale, (kx.at[0, 0], kx.at[0, 1], ky))
    k_fin.wait_recv()
    sums[8] = inner(ck, kg, fin[0])
    k_exchange = [
        remote.start(sums.at[8], sums.at[8 + step], ctx, (head + step) % 8) for step in range(1, 8)
    ]
    v_y[0].wait_recv()
    v_x[0].wait_recv()
    v_x[1].wait_recv()
    v_fin = finish(1, dv, 1.0, (vy.at[0], vx.at[0], vx.at[1]))

    for copy in k_exchange:
        copy.wait_recv()
    total = sums[8]
    for step in range(1, 8):
        total = total + sums[8 + step]
    inner_out[...] = total
    v_fin.wait_recv()
    for i in (0, 1, 5):
        swap[i].wait_recv()
    for copy in remote.started:
        copy.wait_send()


def scatter_call(*operands):
    return pl.pallas_call(
        scatter_kernel,
        name="scatter_grads",
        out_shape=(
            jax.ShapeDtypeStruct((6, 512, 256), F32),
            jax.ShapeDtypeStruct((2, 512, 256), F32),
            jax.ShapeDtypeStruct((8, 512), F32),
        ),
        in_specs=[HBM] * 6 + [VMEM] * 7,
        out_specs=(VMEM, VMEM, VMEM),
        scratch_shapes=[
            pltpu.VMEM((4, 512, 256), BF16),
            pltpu.VMEM((1, 256), F32),
            pltpu.VMEM((1, 256), F32),
            pltpu.VMEM((6, 512, HD), F32),
            pltpu.VMEM((2, 4, 2, 512, HD), BF16),
            pltpu.VMEM((4, 2, 512, HD), BF16),
            pltpu.VMEM((4, 2, 512, HD), BF16),
            pltpu.VMEM((4, 2, 512, HD), BF16),
            pltpu.VMEM((2, SHIFT, HD), BF16),
            pltpu.VMEM((2, 512, HD), BF16),
            pltpu.VMEM((2, 2, 512, HD), BF16),
            pltpu.VMEM((2, 2, 512, HD), BF16),
            pltpu.VMEM((2, 2, 2, 512, HD), BF16),
            pltpu.VMEM((2, 512, HD), BF16),
            pltpu.VMEM((2, 512, HD), F32),
            pltpu.VMEM((16, 8, 512), F32),
            pltpu.SemaphoreType.DMA((48,)),
            pltpu.SemaphoreType.DMA((48,)),
            pltpu.SemaphoreType.DMA((8,)),
        ],
        compiler_params=pltpu.CompilerParams(
            collective_id=1, has_side_effects=True, vmem_limit_bytes=20 * 2**20
        ),
    )(*operands)


def finish_kernel(
    ck, kg, inv, inner, back, fin,
    out_clean, out_noisy, dq_clean, dk_clean, dv_clean, dq_noisy, dk_noisy, dv_noisy,
    dk, sems,
):
    local = Locals(sems)
    copies = [
        local.start(source, target)
        for source, target in (
            (back.at[0], out_clean),
            (back.at[1], out_noisy),
            (back.at[2], dq_clean),
            (back.at[3], dq_noisy),
            (back.at[4], dk_noisy),
            (back.at[5], dv_noisy),
            (fin.at[1], dv_clean),
        )
    ]
    inverse = jnp.transpose(inv[...])[:, 1:2]
    mean = jnp.transpose(inner[...])[:, :1] / FEAT
    factor = inverse * inverse * inverse * mean
    dk[...] = inverse * (kg[...] * fin[0]) - ck[...].astype(F32) * factor
    copies.append(local.start(dk, dk_clean))
    for copy in copies:
        copy.wait()


def finish_call(*operands):
    return pl.pallas_call(
        finish_kernel,
        name="finish",
        out_shape=tuple(jax.ShapeDtypeStruct((512, 256), F32) for _ in range(8)),
        in_specs=[VMEM] * 6,
        out_specs=(HBM,) * 8,
        scratch_shapes=[pltpu.VMEM((512, 256), F32), pltpu.SemaphoreType.DMA((8,))],
        compiler_params=pltpu.CompilerParams(vmem_limit_bytes=16 * 2**20),
    )(*operands)


def local(
    clean_q, clean_k, clean_v, noisy_q, noisy_k, noisy_v,
    q_gain, k_gain, grad_clean, grad_noisy, owned_blocks, block_doc,
):
    qg = q_gain.reshape(1, 256)
    kg = k_gain.reshape(1, 256)
    blocks = [a.reshape(2, BLK, 2 * HD) for a in (noisy_v, grad_clean, grad_noisy)]
    *pinned, docs = [
        pltpu.with_memory_space_constraint(a, pltpu.HBM)
        for a in (
            clean_q, clean_k, noisy_q, noisy_k, qg, kg, clean_v, *blocks, owned_blocks, block_doc,
        )
    ]
    *parts, inv, ids = gather_call(*pinned)
    grads = attention_call(ids, docs, *parts)
    back, fin, inner = scatter_call(*pinned[:6], inv, *grads)
    return finish_call(clean_k, kg, inv, inner, back, fin)


def solution(mesh):
    placed = (P("ctx", "head"),) * 6 + (P("head"),) * 2 + (P("ctx", "head"),) * 2 + (P("ctx"), P())
    return jax.shard_map(
        local,
        mesh=mesh,
        in_specs=placed,
        out_specs=(P("ctx", "head"),) * 8,
        check_vma=False,
    )
```

```python
import math

import jax
import jax.numpy as jnp
from jax import lax
from jax.experimental import pallas as pl
from jax.experimental.pallas import tpu as pltpu
from jax.sharding import PartitionSpec as P

HD = 128
BLK = 256
FEAT = 2048
EPSILON = 1e-06
NEGATIVE = -1e30
MESH = pl.DeviceIdType.MESH
F32 = jnp.float32
BF16 = jnp.bfloat16
VMEM = pl.BlockSpec(memory_space=pltpu.VMEM)
SMEM = pl.BlockSpec(memory_space=pltpu.SMEM)
ANY = pl.BlockSpec(memory_space=pl.ANY)
HBM = pl.BlockSpec(memory_space=pltpu.HBM)
LAST = (((1,), (1,)), ((), ()))
FIRST = (((0,), (0,)), ((), ()))
PLAIN = (((1,), (0,)), ((), ()))
PACKET = 528
SHIFT = 160
GROUPS = (4, 2, 1)
SCALE = 1.0 / math.sqrt(HD)
SCALE2 = SCALE * math.log2(math.e)


def dot(a, b, dims):
    return lax.dot_general(a, b, dims, preferred_element_type=F32)


def row_sums(products):
    high = products.astype(BF16)
    low = (products - high.astype(F32)).astype(BF16)
    ones = jnp.ones((8, products.shape[1]), BF16)
    return dot(ones, high, LAST) + dot(ones, low, LAST)


def place():
    ctx = lax.axis_index("ctx")
    head = lax.axis_index("head")
    core = ctx % 2
    y = (ctx // 2) % 2
    x = ctx // 4
    return ctx, head, core, y, x


def ctx_of(x, y, core):
    return (x * 2 + y) * 2 + core


def chip_of(x, y):
    return x * 2 + y


class Copies:
    def __init__(self, send, recv, head):
        self.send, self.recv, self.head = send, recv, head
        self.started = []
        self.count = 0

    def start(self, src, dst, ctx, head=None):
        copy = pltpu.make_async_remote_copy(
            src_ref=src,
            dst_ref=dst,
            send_sem=self.send.at[self.count],
            recv_sem=self.recv.at[self.count],
            device_id={"ctx": ctx, "head": self.head if head is None else head},
            device_id_type=MESH,
        )
        self.count += 1
        copy.start()
        self.started.append(copy)
        return copy


class Locals:
    def __init__(self, sems):
        self.sems = sems
        self.count = 0

    def start(self, src, dst):
        copy = pltpu.make_async_copy(src, dst, self.sems.at[self.count])
        self.count += 1
        copy.start()
        return copy


def enter(ctx, head, others):
    barrier = pltpu.get_barrier_semaphore()
    for other in others:
        pl.semaphore_signal(barrier, inc=1, device_id={"ctx": other, "head": head}, device_id_type=MESH)
    for step in range(1, 8):
        pl.semaphore_signal(
            barrier, inc=1, device_id={"ctx": ctx, "head": (head + step) % 8}, device_id_type=MESH
        )
    pl.semaphore_wait(barrier, 7 + len(others))


def gather_kernel(
    cq_h, ck_h, nq_h, nk_h, qg_h, kg_h, cv, nv, gc, gn, owned,
    kall, vall, qq, gg, kn, vn, own_w, own_peak, own_sum, out_own, grads_t, inv_out, ids_out,
    owned_s, raws, qg, kg, k_packet, normed, sums, send, recv, wide_send, wide_recv, lsem,
):
    ctx, head, core, y, x = place()
    right, left = (x + 1) % 4, (x + 3) % 4
    opposite = (x + 2) % 4
    mine = pl.ds(pl.multiple_of(core * HD, HD), HD)
    theirs = pl.ds(pl.multiple_of((1 - core) * HD, HD), HD)
    partner = ctx_of(x, y, 1 - core)
    local = Locals(lsem)
    owned_load = local.start(owned, owned_s)
    loads = [local.start(ref, raws.at[i]) for i, ref in enumerate((cq_h, ck_h, nq_h, nk_h))]
    loads += [local.start(qg_h, qg), local.start(kg_h, kg)]
    remote = Copies(send, recv, head)
    chips = ((x, 1 - y), (right, y), (left, y))
    enter(ctx, head, [partner] + [ctx_of(*chip, c) for chip in chips for c in range(2)])
    wide = []

    def first_hop(base, columns_of, buf):
        for number, chip in enumerate(chips):
            for target in range(2):
                copy = pltpu.make_async_remote_copy(
                    src_ref=columns_of(target),
                    dst_ref=buf.at[ctx],
                    send_sem=wide_send.at[base + number, target],
                    recv_sem=wide_recv.at[base + number, core],
                    device_id={"ctx": ctx_of(*chip, target), "head": head},
                    device_id_type=MESH,
                )
                copy.start()
                wide.append(copy)

    def arrived(base, number, buf, source):
        chip = ((x, 1 - y), (left, y), (right, y))[number]
        pltpu.make_async_remote_copy(
            src_ref=buf.at[ctx],
            dst_ref=buf.at[ctx_of(*chip, source)],
            send_sem=wide_send.at[base + number, source],
            recv_sem=wide_recv.at[base + number, source],
            device_id={"ctx": partner, "head": head},
            device_id_type=MESH,
        ).wait_recv()

    first_hop(0, lambda target: cv.at[:, target * HD : target * HD + HD], vall)
    v_swap = remote.start(cv.at[:, theirs], vall.at[ctx], partner)
    v_own = local.start(cv.at[:, mine], vall.at[ctx])

    for copy in loads:
        copy.wait()
    row = lax.broadcasted_iota(jnp.int32, (8, 512), 0)
    total = jnp.zeros((8, 512), F32)
    for index in range(4):
        raw = raws[index].astype(F32)
        total = jnp.where(row == index, row_sums(raw * raw), total)
    sums[0] = total
    exchange = [
        remote.start(sums.at[0], sums.at[step], ctx, (head + step) % 8) for step in range(1, 8)
    ]
    owned_load.wait()
    lane = lax.broadcasted_iota(jnp.int32, (16, 2 * HD), 1)
    k_packet[512:, :] = jnp.where(lane % HD == 0, owned_s[0], owned_s[1]).astype(F32).astype(BF16)

    pair = pl.ds(core * 2, 2)
    late, late_own = [], []

    def swap(src, dst):
        late.append(remote.start(src.at[:, :, theirs], dst, partner))
        late_own.append(local.start(src.at[:, :, mine], dst))

    swap(gc, gg.at[pair, 0])
    swap(gn, gg.at[pair, 1])
    swap(nv, vn.at[pair])

    for copy in exchange:
        copy.wait_recv()
    total = sums[0]
    for step in range(1, 8):
        total = total + sums[step]
    inverse = lax.rsqrt(total / FEAT + EPSILON)
    inv_out[...] = inverse
    columns = jnp.transpose(inverse)

    def normalized(index, gain):
        values = raws[index].astype(F32) * columns[:, index : index + 1] * gain[...]
        return values.astype(BF16)

    k_packet[:512, :] = normalized(1, kg)
    first_hop(3, lambda target: k_packet.at[:, target * HD : target * HD + HD], kall)
    k_swap = remote.start(k_packet.at[:, theirs], kall.at[ctx], partner)
    k_own = local.start(k_packet.at[:, mine], kall.at[ctx])
    for index, raw, gain, dst in (
        (0, 0, qg, qq.at[pair, 0]),
        (1, 2, qg, qq.at[pair, 1]),
        (2, 3, kg, kn.at[pair]),
    ):
        normed[index] = normalized(raw, gain).reshape(2, BLK, 2 * HD)
        swap(normed.at[index], dst)

    def slot(buf, sx, sy):
        return buf.at[pl.ds(2 * chip_of(sx, sy), 2)]

    def part(buf, sx, sy, half):
        return buf.at[2 * chip_of(sx, sy) + half]

    def rows_of(sx, sy, half, first, count):
        return vall.at[2 * chip_of(sx, sy) + half, pl.ds(first, count)]

    def spread(view, px, py):
        return remote.start(view, view, ctx_of(px, py, core))

    v_half, v_y, k_half = [], [], []
    sides = ((1, left, right, 0), (2, right, left, 1))
    for number, near, far, half in sides:
        arrived(0, number, vall, half)
        v_half.append(spread(part(vall, near, y, half), far, y))
    arrived(3, 0, kall, 0)
    arrived(3, 0, kall, 1)
    k_right = spread(slot(kall, x, 1 - y), right, y)
    k_left = spread(slot(kall, x, 1 - y), left, y)
    arrived(0, 1, vall, 1)
    v_y.append(spread(slot(vall, left, y), x, 1 - y))

    v_own.wait()
    k_own.wait()
    v_swap.wait_recv()
    k_swap.wait_recv()
    for copy in late_own:
        copy.wait()
    for copy in late:
        copy.wait_recv()

    def own_block(index):
        side, rows = index // 2, slice(index % 2 * BLK, index % 2 * BLK + BLK)
        packet = 2 * chip_of(x, y) + side
        own = ((kall[packet, rows, :], vall[packet, rows, :]), (kn[index], vn[index]))
        for kind, (keys, values) in enumerate(own):
            columns = slice(kind * BLK, kind * BLK + BLK)
            scores = dot(keys, qq[index, kind], LAST) * SCALE2
            peak = jnp.max(scores, axis=0, keepdims=True)
            weights = jnp.exp2(scores - peak)
            low = weights.astype(BF16)
            own_peak[index, :, columns] = jnp.broadcast_to(peak, (8, BLK))
            own_sum[index, :, columns] = jnp.sum(weights.reshape(BLK // 8, 8, BLK), axis=0)
            own_w[index, :, columns] = low
            out_own[index, :, columns] = dot(values, low, FIRST)
            grads_t[index, :, columns] = jnp.transpose(gg[index, kind].astype(F32))

    own_block(0)
    for number, near, far, half in sides:
        arrived(3, number, kall, half)
        k_half.append(spread(part(kall, near, y, half), far, y))
        arrived(3, number, kall, 1 - half)
    own_block(1)
    arrived(0, 2, vall, 0)
    v_y.append(spread(slot(vall, right, y), x, 1 - y))
    own_block(2)
    v_half[0].wait_recv()
    v_half[1].wait_recv()
    v_y[0].wait_recv()
    v_far = [spread(rows_of(left, 1 - y, 0, 0, SHIFT), right, y)]
    for half in range(2):
        v_y.append(spread(rows_of(opposite, y, half, SHIFT, 512 - SHIFT), x, 1 - y))
    k_right.wait_recv()
    k_half.append(spread(part(kall, left, 1 - y, 0), right, y))
    k_left.wait_recv()
    k_half.append(spread(part(kall, right, 1 - y, 1), left, y))
    own_block(3)
    v_y[1].wait_recv()
    v_far.append(spread(rows_of(right, 1 - y, 1, 0, SHIFT), left, y))
    arrived(0, 0, vall, 0)
    arrived(0, 0, vall, 1)
    for copy in v_y[2:] + v_far + k_half:
        copy.wait_recv()
    names = jnp.max(kall[:, 512:, :].astype(F32), axis=1)
    ids_out[...] = names.astype(jnp.int32)
    for copy in remote.started + wide:
        copy.wait_send()


def gather_call(cq, ck, nq, nk, qg, kg, cv, nv, gc, gn, owned):
    return pl.pallas_call(
        gather_kernel,
        name="gather_keys",
        out_shape=(
            jax.ShapeDtypeStruct((16, PACKET, HD), BF16),
            jax.ShapeDtypeStruct((16, 512, HD), BF16),
            jax.ShapeDtypeStruct((4, 2, BLK, HD), BF16),
            jax.ShapeDtypeStruct((4, 2, BLK, HD), BF16),
            jax.ShapeDtypeStruct((4, BLK, HD), BF16),
            jax.ShapeDtypeStruct((4, BLK, HD), BF16),
            jax.ShapeDtypeStruct((4, BLK, 2 * BLK), BF16),
            jax.ShapeDtypeStruct((4, 8, 2 * BLK), F32),
            jax.ShapeDtypeStruct((4, 8, 2 * BLK), F32),
            jax.ShapeDtypeStruct((4, HD, 2 * BLK), F32),
            jax.ShapeDtypeStruct((4, HD, 2 * BLK), F32),
            jax.ShapeDtypeStruct((8, 512), F32),
            jax.ShapeDtypeStruct((16, HD), jnp.int32),
        ),
        in_specs=[HBM] * 11,
        out_specs=(VMEM,) * 13,
        scratch_shapes=[
            pltpu.SMEM((2,), jnp.int32),
            pltpu.VMEM((4, 512, 256), BF16),
            pltpu.VMEM((1, 256), F32),
            pltpu.VMEM((1, 256), F32),
            pltpu.VMEM((PACKET, 256), BF16),
            pltpu.VMEM((3, 2, BLK, 2 * HD), BF16),
            pltpu.VMEM((8, 8, 512), F32),
            pltpu.SemaphoreType.DMA((32,)),
            pltpu.SemaphoreType.DMA((32,)),
            pltpu.SemaphoreType.DMA((6, 2)),
            pltpu.SemaphoreType.DMA((6, 2)),
            pltpu.SemaphoreType.DMA((16,)),
        ],
        compiler_params=pltpu.CompilerParams(
            collective_id=0, has_side_effects=True, vmem_limit_bytes=20 * 2**20
        ),
    )(cq, ck, nq, nk, qg, kg, cv, nv, gc, gn, owned)


def attention_kernel(
    ids, docs, kall, vall, qq, gg, kn, vn, own_w, own_peak, own_sum, out_own, grads_t,
    out_t, dq_t, dk_noisy, dv_noisy, dk_acc, dv_acc,
    where_is, first_of, pair_query, pair_key, pair_bias,
    scores, weights, scaled_grads, peaks, sums, decays, deltas,
):
    chip = lax.axis_index("ctx") // 2

    def clear(stored):
        dk_acc[stored] = jnp.zeros((BLK, HD), F32)
        dv_acc[stored] = jnp.zeros((BLK, HD), F32)

    def begin_of(block, begin):
        clear(block)
        where_is[ids[block // 2, block % 2]] = block
        begin = jnp.where(docs[block] == docs[jnp.maximum(block - 1, 0)], begin, block)
        first_of[block] = begin
        return begin

    lax.fori_loop(0, 32, begin_of, 0)

    def key_rows(buf, stored):
        start = pl.multiple_of((stored % 2) * BLK, BLK)
        return buf[stored // 2, pl.ds(start, BLK), :]

    def key_pair(buf, pair):
        return jnp.concatenate(
            [key_rows(buf, pair_key[2 * pair]), key_rows(buf, pair_key[2 * pair + 1])], axis=0
        )

    def both(ref, index):
        return ref[index].reshape(2 * BLK, HD)

    def tops(values):
        return jnp.max(values.reshape(-1, 8, values.shape[1]), axis=0)

    def totals(values):
        return jnp.sum(values.reshape(-1, 8, values.shape[1]), axis=0)

    @pl.loop(0, 2)
    def _(side):
        count = 0
        for half in range(2):
            block = ids[chip * 2 + side, half]
            begin = first_of[block]

            def enlist(pair, count, half=half, block=block, begin=begin):
                key = begin + 2 * pair
                pair_query[count] = half
                pair_key[2 * count] = where_is[key]
                pair_key[2 * count + 1] = where_is[jnp.minimum(key + 1, block - 1)]
                pair_bias[count] = jnp.where(key + 1 < block, 0, 1)
                return count + 1

            count = lax.fori_loop(0, (block - begin + 1) // 2, enlist, count)

        def over_pairs(body):
            begin = 0
            for size in GROUPS:
                end = begin + (count - begin) // size

                def step(group, carry, size=size, base=begin):
                    body([base + (group - base) * size + i for i in range(size)])
                    return carry

                lax.fori_loop(begin, end, step, 0)
                begin = begin + (end - begin) * size

        first = 2 * side
        for half in range(2):
            peaks[half] = own_peak[first + half]

        def score_pairs(pairs):
            queries = [pair_query[pair] for pair in pairs]
            values = [
                dot(key_pair(kall, pair), both(qq, first + query), LAST)
                for pair, query in zip(pairs, queries)
            ]
            for pair, query, value in zip(pairs, queries, values):
                scores[pair] = value
                peaks[query] = jnp.maximum(peaks[query], tops(value) * SCALE2)

        over_pairs(score_pairs)

        for half in range(2):
            index = first + half
            peak = jnp.max(peaks[half], axis=0, keepdims=True)
            decay = jnp.exp2(own_peak[index] - peak)
            peaks[half] = jnp.broadcast_to(peak, (8, 2 * BLK))
            decays[half] = decay
            sums[half] = own_sum[index] * decay
            out_t[index] = out_own[index] * decay[:1]

        def value_pairs(pairs):
            queries = [pair_query[pair] for pair in pairs]
            outs, parts = [], []
            for pair, query in zip(pairs, queries):
                peak = peaks[query, :1]
                hidden = peak + jnp.where(pair_bias[pair] == 1, jnp.inf, 0.0)
                upper = jnp.exp2(scores[pair, :BLK] * SCALE2 - peak)
                lower = jnp.exp2(scores[pair, BLK:] * SCALE2 - hidden)
                low = jnp.concatenate([upper.astype(BF16), lower.astype(BF16)], axis=0)
                weights[pair] = low
                outs.append(dot(key_pair(vall, pair), low, FIRST))
                parts.append(totals(upper) + totals(lower))
            for query, out, part in zip(queries, outs, parts):
                sums[query] += part
                out_t[first + query] += out

        over_pairs(value_pairs)

        for half in range(2):
            index = first + half
            stored_own = chip * 4 + index
            inverse_sum = 1.0 / jnp.sum(sums[half], axis=0, keepdims=True)
            out = out_t[index] * inverse_sum
            out_t[index] = out
            grad_rows = (grads_t[index] * inverse_sum).astype(BF16).astype(F32)
            delta = jnp.sum(out * grad_rows, axis=0, keepdims=True)
            deltas[half] = jnp.broadcast_to(delta, (8, 2 * BLK))
            grads = jnp.transpose(grad_rows).astype(BF16)
            scaled_grads[half] = grads
            own = own_w[index].astype(F32) * decays[half, :1]
            own_low = own.astype(BF16)
            own_dp = jnp.concatenate(
                [
                    dot(key_rows(vall, stored_own), grads[:BLK], LAST),
                    dot(vn[index], grads[BLK:], LAST),
                ],
                axis=1,
            )
            own_ds = (own * (own_dp - delta)).astype(BF16)
            dv_acc[stored_own] += dot(own_low[:, :BLK], grads[:BLK], PLAIN)
            dk_acc[stored_own] += dot(own_ds[:, :BLK], qq[index, 0], PLAIN)
            dv_noisy[index] = dot(own_low[:, BLK:], grads[BLK:], PLAIN)
            dk_noisy[index] = dot(own_ds[:, BLK:], qq[index, 1], PLAIN) * SCALE
            dq_t[index, :, :BLK] = dot(key_rows(kall, stored_own), own_ds[:, :BLK], FIRST)
            dq_t[index, :, BLK:] = dot(kn[index], own_ds[:, BLK:], FIRST)

        def grad_pairs(pairs):
            queries = [pair_query[pair] for pair in pairs]
            results = []
            for pair, query in zip(pairs, queries):
                low = weights[pair]
                dp = dot(key_pair(vall, pair), scaled_grads[query], LAST)
                ds = low * (dp - deltas[query, :1]).astype(BF16)
                results.append(
                    (
                        dot(low, scaled_grads[query], PLAIN),
                        dot(ds, both(qq, first + query), PLAIN),
                        dot(key_pair(kall, pair), ds, FIRST),
                    )
                )
            for pair, query, (dv, dk, dq) in zip(pairs, queries, results):
                for place in range(2):
                    rows = slice(place * BLK, place * BLK + BLK)
                    dv_acc[pair_key[2 * pair + place]] += dv[rows]
                    dk_acc[pair_key[2 * pair + place]] += dk[rows]
                dq_t[first + query] += dq

        over_pairs(grad_pairs)


def attention_call(ids, docs, *parts):
    return pl.pallas_call(
        attention_kernel,
        name="attention",
        out_shape=(
            jax.ShapeDtypeStruct((4, HD, 2 * BLK), F32),
            jax.ShapeDtypeStruct((4, HD, 2 * BLK), F32),
            jax.ShapeDtypeStruct((4, BLK, HD), F32),
            jax.ShapeDtypeStruct((4, BLK, HD), F32),
            jax.ShapeDtypeStruct((32, BLK, HD), F32),
            jax.ShapeDtypeStruct((32, BLK, HD), F32),
        ),
        in_specs=[SMEM, SMEM] + [VMEM] * 11,
        out_specs=(VMEM,) * 6,
        scratch_shapes=[
            pltpu.SMEM((32,), jnp.int32),
            pltpu.SMEM((32,), jnp.int32),
            pltpu.SMEM((32,), jnp.int32),
            pltpu.SMEM((32,), jnp.int32),
            pltpu.SMEM((16,), jnp.int32),
            pltpu.VMEM((16, 2 * BLK, 2 * BLK), F32),
            pltpu.VMEM((16, 2 * BLK, 2 * BLK), BF16),
            pltpu.VMEM((2, 2 * BLK, HD), BF16),
            pltpu.VMEM((2, 8, 2 * BLK), F32),
            pltpu.VMEM((2, 8, 2 * BLK), F32),
            pltpu.VMEM((2, 8, 2 * BLK), F32),
            pltpu.VMEM((2, 8, 2 * BLK), F32),
        ],
        compiler_params=pltpu.CompilerParams(vmem_limit_bytes=34 * 2**20),
    )(ids, docs, *parts)


def scatter_kernel(
    cq_h, ck_h, nq_h, nk_h, qg_h, kg_h, inv, out_t, dq_t, dk_noisy, dv_noisy, dk, dv,
    back, fin, inner_out,
    raws, qg, kg, stage, k_out, v_out, x_out, vy, vq, vh, vx, kh, kx, ky, away, sums,
    send, recv, lsem,
):
    ctx, head, core, y, x = place()
    right, left = (x + 1) % 4, (x + 3) % 4
    partner = ctx_of(x, y, 1 - core)
    to_right, to_left = ctx_of(right, y, core), ctx_of(left, y, core)
    to_y = ctx_of(x, 1 - y, core)
    score_scale = 1.0 / math.sqrt(HD)
    own_columns = pl.ds(pl.multiple_of(core * HD, HD), HD)
    local = Locals(lsem)
    loads = [local.start(ref, raws.at[i]) for i, ref in enumerate((cq_h, ck_h, nq_h, nk_h))]
    loads += [local.start(qg_h, qg), local.start(kg_h, kg)]
    cq, ck, nq, nk = [raws.at[i] for i in range(4)]
    remote = Copies(send, recv, head)

    def mine(ref, step, row, half):
        chip = chip_of((x + step) % 4, y if row == 0 else 1 - y)
        return ref[pl.ds(chip * 4 + half * 2, 2)].reshape(512, HD)

    def pack_v(step):
        for half in range(2):
            v_out[step, half] = mine(dv, step, 1, half).astype(BF16)

    def pack_k(row, step, half, *others):
        value = mine(dk, step, row, half) * score_scale
        for other in others:
            value = value + other[...].astype(F32)
        k_out[row, step, half] = value.astype(BF16)

    pack_v(2)
    pack_k(1, 2, 0)
    pack_k(1, 2, 1)
    enter(ctx, head, [partner, to_right, to_left, to_y])
    first, rest = pl.ds(0, SHIFT), pl.ds(SHIFT, 512 - SHIFT)
    v_far = [
        remote.start(v_out.at[2, 0, first], vq.at[0], to_left),
        remote.start(v_out.at[2, 1, first], vq.at[1], to_right),
    ]
    v_opposite = [
        remote.start(v_out.at[2, half, rest], vy.at[2, half, rest], to_y) for half in range(2)
    ]
    k_half = {}

    def start_half(row):
        k_half[row, 0] = remote.start(k_out.at[row, 2, 0], kh.at[row, 0], to_left)
        k_half[row, 1] = remote.start(k_out.at[row, 2, 1], kh.at[row, 1], to_right)

    start_half(1)
    pack_k(0, 2, 0)
    pack_k(0, 2, 1)
    start_half(0)
    v_y = {}

    def send_v(step, half):
        pack_v(step)
        if half is not None:
            v_far[half].wait_recv()
            v_out[step, half, :SHIFT] = (
                mine(dv, step, 1, half)[:SHIFT] + vq[half].astype(F32)
            ).astype(BF16)
        v_y[step] = remote.start(v_out.at[step], vy.at[step], to_y)

    send_v(3, 0)
    for row in (1, 0):
        pack_k(row, 3, 1)
        pack_k(row, 1, 0)

    def landing(i):
        return back.at[i, :, own_columns]

    swap = {}
    dk_pair, dv_pair = [
        [ref.at[pl.ds(c * 2, 2)] for c in (core, 1 - core)] for ref in (dk_noisy, dv_noisy)
    ]

    def turn(index, ref, first, factor):
        for part in range(2):
            rows = slice(part * BLK, part * BLK + BLK)
            for c, own in ((core, True), (1 - core, False)):
                values = jnp.transpose(ref[2 * c + part]) * factor
                for kind in range(2):
                    if own:
                        back[first + kind, rows, own_columns] = values[kind * BLK : kind * BLK + BLK]
                    else:
                        stage[first + kind, rows, :] = values[kind * BLK : kind * BLK + BLK]
        for i in (first, first + 1):
            swap[i] = remote.start(stage.at[i], landing(i), partner)

    def turn_noisy(ref, i):
        for part in range(2):
            rows = slice(part * BLK, part * BLK + BLK)
            back[i, rows, own_columns] = ref[2 * core + part]
            stage[i, rows, :] = ref[2 * (1 - core) + part]
        swap[i] = remote.start(stage.at[i], landing(i), partner)

    turn(0, dq_t, 2, score_scale)
    turn_noisy(dk_noisy, 4)

    k_x = {}

    def k_forward(row):
        k_half[row, 0].wait_recv()
        pack_k(row, 3, 0, kh.at[row, 0])
        k_x[row, 0] = remote.start(k_out.at[row, 3], kx.at[row, 0], to_left)
        k_half[row, 1].wait_recv()
        pack_k(row, 1, 1, kh.at[row, 1])
        k_x[row, 1] = remote.start(k_out.at[row, 1], kx.at[row, 1], to_right)

    k_forward(1)

    row = lax.broadcasted_iota(jnp.int32, (8, 512), 0)

    def inner(raw, gain, values):
        return row_sums(raw[...].astype(F32) * (gain[...] * values))

    for copy in loads:
        copy.wait()
    for i in (2, 3, 4):
        swap[i].wait_recv()
    total = jnp.zeros((8, 512), F32)
    normal = ((0, cq, qg, 2), (2, nq, qg, 3), (3, nk, kg, 4))
    for index, raw, gain, i in normal:
        total = jnp.where(row == index, inner(raw, gain, back[i]), total)
    sums[0] = total
    exchange = [
        remote.start(sums.at[0], sums.at[step], ctx, (head + step) % 8) for step in range(1, 8)
    ]

    def pack_x(step, half, *others):
        value = mine(dv, step, 0, half)
        for other in others:
            value = value + other[...].astype(F32)
        x_out[step, half] = value.astype(BF16)

    v_half = []
    for half, target in ((0, to_left), (1, to_right)):
        v_opposite[half].wait_recv()
        pack_x(2, half)
        x_out[2, half, SHIFT:] = (
            mine(dv, 2, 0, half)[SHIFT:] + vy[2, half, SHIFT:].astype(F32)
        ).astype(BF16)
        v_half.append(remote.start(x_out.at[2, half], vh.at[half], target))
    send_v(1, 1)
    k_forward(0)
    turn(0, out_t, 0, 1.0)
    turn_noisy(dv_noisy, 5)
    k_x[1, 0].wait_recv()
    k_x[1, 1].wait_recv()
    for half in range(2):
        pack_k(1, 0, half, kx.at[1, 0, half], kx.at[1, 1, half])
    k_y = remote.start(k_out.at[1, 0], ky, to_y)
    send_v(0, None)

    v_y[3].wait_recv()
    v_half[0].wait_recv()
    pack_x(3, 0, vy.at[3, 0], vh.at[0])
    pack_x(3, 1, vy.at[3, 1])
    v_x = [remote.start(x_out.at[3], vx.at[0], to_left)]
    v_y[1].wait_recv()
    v_half[1].wait_recv()
    pack_x(1, 0, vy.at[1, 0])
    pack_x(1, 1, vy.at[1, 1], vh.at[1])
    v_x.append(remote.start(x_out.at[1], vx.at[1], to_right))

    for copy in exchange:
        copy.wait_recv()
    total = sums[0]
    for step in range(1, 8):
        total = total + sums[step]
    inverses = jnp.transpose(inv[...])
    means = jnp.transpose(total) / FEAT
    for index, raw, gain, i in normal:
        inverse = inverses[:, index : index + 1]
        factor = inverse * inverse * inverse * means[:, index : index + 1]
        back[i] = inverse * (gain[...] * back[i]) - raw[...].astype(F32) * factor

    def finish(index, ref, factor, terms):
        values = []
        for half in range(2):
            value = mine(ref, 0, 0, half) * factor
            for term in terms:
                value = value + term[half].astype(F32)
            values.append(value)
        first_core = core == 0
        fin[index, :, own_columns] = jnp.where(first_core, values[0], values[1])
        away[index] = jnp.where(first_core, values[1], values[0])
        return remote.start(away.at[index], fin.at[index, :, own_columns], partner)

    k_x[0, 0].wait_recv()
    k_x[0, 1].wait_recv()
    k_y.wait_recv()
    k_fin = finish(0, dk, score_scale, (kx.at[0, 0], kx.at[0, 1], ky))
    k_fin.wait_recv()
    sums[8] = inner(ck, kg, fin[0])
    k_exchange = [
        remote.start(sums.at[8], sums.at[8 + step], ctx, (head + step) % 8) for step in range(1, 8)
    ]
    v_y[0].wait_recv()
    v_x[0].wait_recv()
    v_x[1].wait_recv()
    v_fin = finish(1, dv, 1.0, (vy.at[0], vx.at[0], vx.at[1]))

    for copy in k_exchange:
        copy.wait_recv()
    total = sums[8]
    for step in range(1, 8):
        total = total + sums[8 + step]
    inner_out[...] = total
    v_fin.wait_recv()
    for i in (0, 1, 5):
        swap[i].wait_recv()
    for copy in remote.started:
        copy.wait_send()


def scatter_call(*operands):
    return pl.pallas_call(
        scatter_kernel,
        name="scatter_grads",
        out_shape=(
            jax.ShapeDtypeStruct((6, 512, 256), F32),
            jax.ShapeDtypeStruct((2, 512, 256), F32),
            jax.ShapeDtypeStruct((8, 512), F32),
        ),
        in_specs=[HBM] * 6 + [VMEM] * 7,
        out_specs=(VMEM, VMEM, VMEM),
        scratch_shapes=[
            pltpu.VMEM((4, 512, 256), BF16),
            pltpu.VMEM((1, 256), F32),
            pltpu.VMEM((1, 256), F32),
            pltpu.VMEM((6, 512, HD), F32),
            pltpu.VMEM((2, 4, 2, 512, HD), BF16),
            pltpu.VMEM((4, 2, 512, HD), BF16),
            pltpu.VMEM((4, 2, 512, HD), BF16),
            pltpu.VMEM((4, 2, 512, HD), BF16),
            pltpu.VMEM((2, SHIFT, HD), BF16),
            pltpu.VMEM((2, 512, HD), BF16),
            pltpu.VMEM((2, 2, 512, HD), BF16),
            pltpu.VMEM((2, 2, 512, HD), BF16),
            pltpu.VMEM((2, 2, 2, 512, HD), BF16),
            pltpu.VMEM((2, 512, HD), BF16),
            pltpu.VMEM((2, 512, HD), F32),
            pltpu.VMEM((16, 8, 512), F32),
            pltpu.SemaphoreType.DMA((48,)),
            pltpu.SemaphoreType.DMA((48,)),
            pltpu.SemaphoreType.DMA((8,)),
        ],
        compiler_params=pltpu.CompilerParams(
            collective_id=1, has_side_effects=True, vmem_limit_bytes=20 * 2**20
        ),
    )(*operands)


def finish_kernel(
    ck, kg, inv, inner, back, fin,
    out_clean, out_noisy, dq_clean, dk_clean, dv_clean, dq_noisy, dk_noisy, dv_noisy,
    dk, sems,
):
    local = Locals(sems)
    copies = [
        local.start(source, target)
        for source, target in (
            (back.at[0], out_clean),
            (back.at[1], out_noisy),
            (back.at[2], dq_clean),
            (back.at[3], dq_noisy),
            (back.at[4], dk_noisy),
            (back.at[5], dv_noisy),
            (fin.at[1], dv_clean),
        )
    ]
    inverse = jnp.transpose(inv[...])[:, 1:2]
    mean = jnp.transpose(inner[...])[:, :1] / FEAT
    factor = inverse * inverse * inverse * mean
    dk[...] = inverse * (kg[...] * fin[0]) - ck[...].astype(F32) * factor
    copies.append(local.start(dk, dk_clean))
    for copy in copies:
        copy.wait()


def finish_call(*operands):
    return pl.pallas_call(
        finish_kernel,
        name="finish",
        out_shape=tuple(jax.ShapeDtypeStruct((512, 256), F32) for _ in range(8)),
        in_specs=[VMEM] * 6,
        out_specs=(HBM,) * 8,
        scratch_shapes=[pltpu.VMEM((512, 256), F32), pltpu.SemaphoreType.DMA((8,))],
        compiler_params=pltpu.CompilerParams(vmem_limit_bytes=16 * 2**20),
    )(*operands)


def local(
    clean_q, clean_k, clean_v, noisy_q, noisy_k, noisy_v,
    q_gain, k_gain, grad_clean, grad_noisy, owned_blocks, block_doc,
):
    qg = q_gain.reshape(1, 256)
    kg = k_gain.reshape(1, 256)
    blocks = [a.reshape(2, BLK, 2 * HD) for a in (noisy_v, grad_clean, grad_noisy)]
    *pinned, docs = [
        pltpu.with_memory_space_constraint(a, pltpu.HBM)
        for a in (
            clean_q, clean_k, noisy_q, noisy_k, qg, kg, clean_v, *blocks, owned_blocks, block_doc,
        )
    ]
    *parts, inv, ids = gather_call(*pinned)
    grads = attention_call(ids, docs, *parts)
    back, fin, inner = scatter_call(*pinned[:6], inv, *grads)
    return finish_call(clean_k, kg, inv, inner, back, fin)


def solution(mesh):
    placed = (P("ctx", "head"),) * 6 + (P("head"),) * 2 + (P("ctx", "head"),) * 2 + (P("ctx"), P())
    return jax.shard_map(
        local,
        mesh=mesh,
        in_specs=placed,
        out_specs=(P("ctx", "head"),) * 8,
        check_vma=False,
    )
```
